32 devices in a mesh: batch: 4 (over z), chan: 8 (over y, x, core).
Axes of the slice: x: 2, y: 2, z: 4, core: 2. Of those that a mesh axis runs over, the one named last changes fastest.
Arguments:
- teacher_images: bfloat16 [64, 32, 32, 256], P(('batch', 'chan')), may hold values from -6 to 6
- student_images: bfloat16 [64, 16, 16, 256], P(('batch', 'chan')), may hold values from -6 to 6
- pair_index: int32 [64], P(('batch', 'chan')), may hold values from 0 to 63
- labels: int32 [64], P(('batch', 'chan')), may hold values from 0 to 99
- teacher_first: bfloat16 [3, 3, 256, 256], replicated, may hold values from -0.125 to 0.125
- teacher_second: bfloat16 [3, 3, 256, 256], replicated, may hold values from -0.125 to 0.125
- teacher_head: bfloat16 [256, 100], replicated, may hold values from -3 to 3
- teacher_bias: float32 [100], replicated, may hold values from -3 to 3
- conv_first: bfloat16 [3, 3, 256, 256], P(None, None, None, 'chan'), may hold values from -0.125 to 0.125
- gain_first: float32 [256], P('chan'), may hold values from 0.5 to 1.5
- shift_first: float32 [256], P('chan'), may hold values from -3 to 3
- conv_second: bfloat16 [3, 3, 256, 256], P(None, None, None, 'chan'), may hold values from -0.125 to 0.125
- gain_second: float32 [256], P('chan'), may hold values from 0.5 to 1.5
- shift_second: float32 [256], P('chan'), may hold values from -3 to 3
- head_weight: bfloat16 [256, 100], P('chan'), may hold values from -3 to 3
- head_bias: float32 [100], replicated, may hold values from -3 to 3
Outputs:
- student_logits: float32 [64, 100], P('batch')
- images_grad: float32 [64, 16, 16, 256], P(('batch', 'chan'))
- grad_conv_first: float32 [3, 3, 256, 256], P(None, None, None, 'chan')
- grad_gain_first: float32 [256], P('chan')
- grad_shift_first: float32 [256], P('chan')
- grad_conv_second: float32 [3, 3, 256, 256], P(None, None, None, 'chan')
- grad_gain_second: float32 [256], P('chan')
- grad_shift_second: float32 [256], P('chan')
- grad_head_weight: float32 [256, 100], P('chan')
- grad_head_bias: float32 [100], replicated
The draws below stay inside these ranges and needn't reach their ends.
All inputs are finite; a program needn't handle non-finite values.
Results may differ from the reference program's by a relative error of at most 0.0034.
Values may be sent and summed in bfloat16 or wider, within the bound.
A program may use at most 256 MiB of HBM per device.

```python
import jax
import jax.numpy as jnp
from jax import lax

C = 256
CLASSES = 100
HS = 16
HT = 32
MICRO = 2
MB_IMG = 1
IMG_DEV = 2
IMGS = 64


def place_ends(drawn, own_key, least, high):
    index_at = [jax.random.randint(jax.random.fold_in(own_key, axis), (), 0, length) for axis, length in enumerate(drawn.shape)]
    longest = drawn.shape.index(max(drawn.shape))
    beside = index_at[:longest] + [(index_at[longest] + 1) % drawn.shape[longest]] + index_at[longest + 1:]
    return drawn.at[tuple(index_at)].set(least).at[tuple(beside)].set(high)


def steps_of(rng, dims, pieces, low, high):
    level, own = 1.0, jax.random.fold_in(rng, 6)
    for position, parts in pieces:
        steps = jnp.exp(jax.random.uniform(jax.random.fold_in(own, position), (parts,), jnp.float32, low / len(pieces), high / len(pieces)))
        level = level * jnp.repeat(steps, dims[position] // parts).reshape([-1 if axis == position else 1 for axis in range(len(dims))])
    return level


def bell_draw(key, dims, scale, bound, cuts=(), kind=jnp.bfloat16):
    result = scale * jax.random.normal(key, dims, jnp.float32)
    if cuts:
        result = result * steps_of(key, dims, cuts, -0.22, 0.18)
    return jnp.clip(result, -bound, bound).astype(kind)


def setup_inputs(seed: int = 0) -> dict:
    arg_keys = jax.random.split(jax.random.key(seed), 17)
    return {
        "teacher_images": bell_draw(arg_keys[0], (IMGS, HT, HT, C), 1.0, 6.0, ((0, 32),)),
        "student_images": bell_draw(arg_keys[1], (IMGS, HS, HS, C), 1.0, 6.0, ((0, 32),)),
        "pair_index": place_ends(jax.random.randint(arg_keys[2], (IMGS,), 0, IMGS), jax.random.fold_in(arg_keys[2], 1), 0, IMGS - 1).astype(jnp.int32),
        "labels": place_ends(jax.random.randint(arg_keys[3], (IMGS,), 0, CLASSES), jax.random.fold_in(arg_keys[3], 1), 0, CLASSES - 1).astype(jnp.int32),
        "teacher_first": bell_draw(arg_keys[4], (3, 3, C, C), (9 * C) ** -0.5, 0.125),
        "teacher_second": bell_draw(arg_keys[5], (3, 3, C, C), (9 * C) ** -0.5, 0.125),
        "teacher_head": bell_draw(arg_keys[6], (C, CLASSES), 0.5, 3.0),
        "teacher_bias": bell_draw(arg_keys[7], (CLASSES,), 0.5, 3.0, (), jnp.float32),
        "conv_first": bell_draw(arg_keys[8], (3, 3, C, C), (9 * C) ** -0.5, 0.125, ((3, 8),)),
        "gain_first": jnp.clip(1.0 + 0.1 * jax.random.normal(arg_keys[9], (C,), jnp.float32), 0.5, 1.5),
        "shift_first": bell_draw(arg_keys[10], (C,), 0.5, 3.0, ((0, 8),), jnp.float32),
        "conv_second": bell_draw(arg_keys[11], (3, 3, C, C), (9 * C) ** -0.5, 0.125, ((3, 8),)),
        "gain_second": jnp.clip(1.0 + 0.1 * jax.random.normal(arg_keys[12], (C,), jnp.float32), 0.5, 1.5),
        "shift_second": bell_draw(arg_keys[13], (C,), 0.5, 3.0, ((0, 8),), jnp.float32),
        "head_weight": bell_draw(arg_keys[14], (C, CLASSES), 0.5, 3.0, ((0, 8),)),
        "head_bias": bell_draw(arg_keys[15], (CLASSES,), 0.5, 3.0, (), jnp.float32),
    }


EPS = 1e-05
TARGET_WEIGHT = 1.0
NONTARGET_WEIGHT = 8.0
SOFTEN_FACTOR = 4.0
HIGHEST = lax.Precision.HIGHEST
LAYOUT = ('NHWC', 'HWIO', 'NHWC')

@jax.custom_vjp
def low(v):
    return lax.optimization_barrier(v.astype(jnp.bfloat16)).astype(jnp.float32)

@jax.custom_vjp
def low_back(v):
    return v

def low_keep(v):
    return (low(v), None)

def low_pass(kept, grad):
    return (grad,)

def back_keep(v):
    return (v, None)

def back_low(kept, grad):
    return (low(grad),)
low.defvjp(low_keep, low_pass)
low_back.defvjp(back_keep, back_low)

def convolve(inputs, kernel):
    return lax.conv_general_dilated(inputs, kernel, (1, 1), 'SAME', dimension_numbers=LAYOUT, precision=HIGHEST)

def normalize(values, gain_row, shift_row):
    center = lax.optimization_barrier(jnp.mean(values, axis=(0, 1, 2)))
    spread = lax.optimization_barrier(jnp.mean(values * values, axis=(0, 1, 2))) - center * center
    return (values - center) * lax.rsqrt(spread + EPS) * gain_row + shift_row

def distill_rows(student_output, teacher_output, label_rows):
    classes = student_output.shape[-1]
    onehot = (jnp.arange(classes, dtype=jnp.int32)[None, :] == label_rows[:, None]).astype(jnp.float32)
    softened_student = student_output / SOFTEN_FACTOR
    softened_teacher = teacher_output / SOFTEN_FACTOR
    whole_student = jax.nn.logsumexp(softened_student, axis=-1)
    whole_teacher = jax.nn.logsumexp(softened_teacher, axis=-1)
    rest_student = jax.nn.logsumexp(softened_student - 1000.0 * onehot, axis=-1)
    rest_teacher = jax.nn.logsumexp(softened_teacher - 1000.0 * onehot, axis=-1)
    true_student = lax.optimization_barrier(jnp.sum(onehot * softened_student, axis=-1))
    true_teacher = lax.optimization_barrier(jnp.sum(onehot * softened_teacher, axis=-1))
    log_ps = true_student - whole_student
    log_pt = true_teacher - whole_teacher
    log_rs = rest_student - whole_student
    log_rt = rest_teacher - whole_teacher
    binary_split = jnp.exp(log_pt) * (log_pt - log_ps) + jnp.exp(log_rt) * (log_rt - log_rs)
    inner_teacher = softened_teacher - 1000.0 * onehot - rest_teacher[:, None]
    inner_student = softened_student - 1000.0 * onehot - rest_student[:, None]
    nontarget_part = lax.optimization_barrier(jnp.sum(jnp.exp(inner_teacher) * (inner_teacher - inner_student), axis=-1))
    return (TARGET_WEIGHT * binary_split + NONTARGET_WEIGHT * nontarget_part) * SOFTEN_FACTOR * SOFTEN_FACTOR

def teacher_block(images, teacher_first, teacher_second, teacher_head, teacher_bias):
    conv_one = convolve(images, teacher_first)
    hidden = low(jax.nn.gelu(conv_one))
    conv_two = convolve(hidden, teacher_second)
    activated = jax.nn.gelu(conv_two + images)
    pooled = lax.optimization_barrier(jnp.mean(activated, axis=(1, 2)))
    return jnp.dot(pooled, teacher_head, precision=HIGHEST) + teacher_bias

def student_block(images, conv_first, gain_first, shift_first, conv_second, gain_second, shift_second):
    conv_one = low_back(convolve(images, conv_first))
    hidden = low(jax.nn.gelu(normalize(conv_one, gain_first, shift_first)))
    conv_two = low_back(convolve(hidden, conv_second))
    activated = jax.nn.gelu(normalize(conv_two, gain_second, shift_second) + images)
    return lax.optimization_barrier(jnp.mean(activated, axis=(1, 2)))

def reference(teacher_images, student_images, pair_index, labels, teacher_first, teacher_second, teacher_head, teacher_bias, conv_first, gain_first, shift_first, conv_second, gain_second, shift_second, head_weight, head_bias):
    f32 = jnp.float32
    pair_groups = pair_index.reshape(-1, MICRO, MB_IMG)
    label_groups = labels.reshape(-1, MICRO, MB_IMG)

    def window_loss(images, w_one, g_one, s_one, w_two, g_two, s_two, head, bias):
        tw_one = teacher_first.astype(f32)
        tw_two = teacher_second.astype(f32)
        tw_head = teacher_head.astype(f32)
        blocks = teacher_images.reshape(IMGS // IMG_DEV, IMG_DEV, HT, HT, C)
        teacher_all = lax.map(lambda block: teacher_block(block.astype(f32), tw_one, tw_two, tw_head, teacher_bias), blocks)
        teacher_all = teacher_all.reshape(IMGS, CLASSES)
        groups = images.reshape(-1, MICRO, MB_IMG, HS, HS, C)
        total = jnp.zeros((), f32)
        outputs = []
        for micro_step in range(MICRO):
            batch_images = groups[:, micro_step].reshape(-1, HS, HS, C)
            pooled = student_block(batch_images, w_one, g_one, s_one, w_two, g_two, s_two)
            logits = jnp.dot(pooled, head, precision=HIGHEST) + bias
            pair_rows = pair_groups[:, micro_step].reshape(-1).astype(jnp.int32)
            label_rows = label_groups[:, micro_step].reshape(-1).astype(jnp.int32)
            paired = jnp.take(teacher_all, pair_rows, axis=0)
            total = total + jnp.sum(distill_rows(logits, paired, label_rows))
            outputs.append(logits.reshape(-1, MB_IMG, CLASSES))
        return (total, jnp.stack(outputs, axis=1).reshape(IMGS, CLASSES))
    params = (student_images.astype(f32), conv_first.astype(f32), gain_first, shift_first, conv_second.astype(f32), gain_second, shift_second, head_weight.astype(f32), head_bias)
    total, puller, student_logits = jax.vjp(window_loss, *params, has_aux=True)
    grads = puller(jnp.ones((), f32))
    return (student_logits, grads[0], grads[1], grads[2], grads[3], grads[4], grads[5], grads[6], grads[7], grads[8])
```

```python
import functools

import jax
import jax.numpy as jnp
from jax import lax
from jax.experimental import pallas as pl
from jax.experimental.pallas import tpu as pltpu
from jax.sharding import PartitionSpec as P

MESH = pl.DeviceIdType.MESH
F32 = jnp.float32
BF16 = jnp.bfloat16
HIGHEST = lax.Precision.HIGHEST
MICRO = 2
EPS = 1e-05
TARGET_WEIGHT = 1.0
NONTARGET_WEIGHT = 8.0
SOFTEN = 4.0
GELU_A = 0.7978845608028654
GELU_B = 0.044715
LANES = 128


def gelu(x):
    return x * (0.5 + 0.5 * jnp.tanh(GELU_A * (x + GELU_B * (x * x * x))))


def gelu_slope(x):
    square = x * x
    t = jnp.tanh(GELU_A * (x + GELU_B * (x * square)))
    return 0.5 + 0.5 * t + (0.5 * x) * (1.0 - t * t) * (GELU_A + (3.0 * GELU_A * GELU_B) * square)


def column(shape, width):
    return lax.rem(lax.broadcasted_iota(jnp.int32, shape, 0), width)


def spread_columns(dest, lead, top, values, width):
    rows, depth = values.shape
    col = column(values.shape, width)
    left = jnp.where(col == 0, 0.0, pltpu.roll(values, 1, 0))
    right = jnp.where(col == width - 1, 0.0, pltpu.roll(values, rows - 1, 0))
    high = rows // width
    for place, part in enumerate((left, values, right)):
        dest[lead, pl.ds(top, high), :, place * depth : (place + 1) * depth] = part.astype(BF16).reshape(
            high, width, depth
        )


def halves(row):
    return (row[:, :LANES], row[:, LANES:])


def distill_grad(student, teacher, label, classes):
    lane = lax.broadcasted_iota(jnp.int32, student.shape, 1)
    live = lane < classes
    target = lane == label
    other = jnp.logical_and(live, jnp.logical_not(target))
    low = -1e30

    def parts(logits):
        soft = logits / SOFTEN
        whole_top = jnp.max(jnp.where(live, soft, low), axis=1, keepdims=True)
        rest_top = jnp.max(jnp.where(other, soft, low), axis=1, keepdims=True)
        whole_exp = jnp.where(live, jnp.exp(jnp.where(live, soft, whole_top) - whole_top), 0.0)
        rest_exp = jnp.where(other, jnp.exp(jnp.where(other, soft, rest_top) - rest_top), 0.0)
        whole_sum = jnp.sum(whole_exp, axis=1, keepdims=True)
        rest_sum = jnp.sum(rest_exp, axis=1, keepdims=True)
        whole = whole_top + jnp.log(whole_sum)
        rest = rest_top + jnp.log(rest_sum)
        true = jnp.sum(jnp.where(target, soft, 0.0), axis=1, keepdims=True)
        return (whole_exp / whole_sum, rest_exp / rest_sum, true - whole, rest - whole)

    probs, inner, _, _ = parts(student)
    _, inner_t, log_pt, log_rt = parts(teacher)
    p_true, p_rest = jnp.exp(log_pt), jnp.exp(log_rt)
    split_grad = (p_true + p_rest) * probs - jnp.where(target, p_true, 0.0) - p_rest * inner
    inner_grad = jnp.sum(inner_t, axis=1, keepdims=True) * inner - inner_t
    return SOFTEN * (TARGET_WEIGHT * split_grad + NONTARGET_WEIGHT * inner_grad)


def body(
    sizes,
    teacher_hbm,
    images,
    pair_index,
    labels,
    teacher_first_hbm,
    teacher_second_hbm,
    teacher_head,
    teacher_bias,
    first_own,
    gain_first,
    shift_first,
    second_own,
    gain_second,
    shift_second,
    head_own,
    head_bias,
    logits_out,
    images_grad,
    first_grad,
    gain_first_grad,
    shift_first_grad,
    second_grad,
    gain_second_grad,
    shift_second_grad,
    head_grad,
    bias_grad,
    teacher_in,
    teacher_w1,
    teacher_w2,
    teacher_x,
    teacher_h,
    teacher_head_pad,
    image_x,
    hidden_x,
    grad_x,
    w_first,
    w_second,
    own_first,
    own_second,
    y_first,
    y_second,
    d_res,
    d_hid,
    image_all,
    hidden_all,
    turned_send,
    turned_all,
    part_send,
    part_recv,
    sum_send,
    sum_recv,
    param_send,
    param_all,
    head_send,
    head_all,
    tile_send,
    tile_all_0,
    tile_all_1,
    tile_all_2,
    tile_all_3,
    tile_all_4,
    tile_all_5,
    head_sum,
    local_sem,
    gather_send,
    gather_recv,
    tile_ssem,
    tile_rsem,
    plane_ssem,
    plane_rsem,
    line_ssem,
    line_rsem,
):
    groups, chans, own, own_pad, classes = sizes
    tile_all = (tile_all_0, tile_all_1, tile_all_2, tile_all_3, tile_all_4, tile_all_5)
    b = lax.axis_index("batch")
    c = lax.axis_index("chan")
    me = b * chans + c
    devices = groups * chans
    sibling = c + 1 - 2 * lax.rem(c, 2)
    extent = images.shape[1]
    cells = extent * extent
    depth = images.shape[3]
    wide = teacher_hbm.shape[1]
    samples = float(devices * cells)
    rows_part = part_send.shape[2]
    own_rows = own_first.shape[0]

    def far_order():
        return [db for db in range(1, groups)] + [0]

    def each_device(fn):
        for db in far_order():
            peer_b = lax.rem(b + db, groups)

            def one(i, carry, peer_b=peer_b):
                fn(peer_b, lax.rem(c + (chans - i), chans))
                return carry

            lax.fori_loop(1 if db == 0 else 0, chans, one, 0, unroll=chans <= 8)

    def each_plane(fn):
        def one(i, carry):
            fn(lax.rem(c + i, chans))
            return carry

        lax.fori_loop(1, chans, one, 0, unroll=chans <= 8)

    barrier = pltpu.get_barrier_semaphore()
    each_device(lambda pb, pc: pl.semaphore_signal(barrier, inc=1, device_id=(pb, pc), device_id_type=MESH))

    loads = [
        pltpu.make_async_copy(teacher_hbm, teacher_in, local_sem.at[0]),
        pltpu.make_async_copy(teacher_first_hbm, teacher_w1, local_sem.at[1]),
        pltpu.make_async_copy(teacher_second_hbm, teacher_w2, local_sem.at[2]),
    ]
    for load in loads:
        load.start()

    def place_own(param_row):
        at = c * own
        lane0 = lax.rem(at, LANES)
        padded = jnp.concatenate([param_row, jnp.zeros((1, LANES - own), F32)], axis=1)
        moved = pltpu.roll(jnp.broadcast_to(padded, (8, LANES)), lane0, 1)[0:1]
        upper = at >= LANES
        return (jnp.where(upper, 0.0, moved), jnp.where(upper, moved, 0.0))

    for i, ref in enumerate((gain_first, shift_first, gain_second, shift_second)):
        low_half, high_half = place_own(ref[...])
        param_send[2 * i : 2 * i + 1, :] = low_half
        param_send[2 * i + 1 : 2 * i + 2, :] = high_half
    head_send[...] = jnp.zeros(head_send.shape, BF16)
    head_send[0:own, 0:classes] = head_own[...]
    for src, dst in ((first_own, own_first), (second_own, own_second)):
        if own_rows != 9 * own:
            dst[...] = jnp.zeros(dst.shape, BF16)
        dst[0 : 9 * own, :] = src[...]

    for ref in (image_x, hidden_x, grad_x, teacher_x, teacher_h):
        high = ref.shape[1]
        for lead in range(ref.shape[0]):
            ref[lead, 0] = jnp.zeros(ref.shape[2:], BF16)
            ref[lead, high - 1] = jnp.zeros(ref.shape[2:], BF16)
    for lead in range(MICRO):
        spread_columns(image_x, lead, 1, images[lead].astype(F32).reshape(cells, depth), extent)

    t_high = 16
    t_steps = wide // t_high
    t_rows = t_high * wide

    def teacher_conv(source, kernel, top):
        total = None
        for row_off in range(3):
            window = source[0, pl.ds(top + row_off, t_high)].reshape(t_rows, 3 * depth)
            term = jnp.dot(
                window, kernel[row_off * 3 * depth : (row_off + 1) * 3 * depth, :], preferred_element_type=F32
            )
            total = term if total is None else total + term
        return total

    def teacher_block(lead):
        def fill(i, carry):
            top = i * t_high
            values = teacher_in[lead, pl.ds(top, t_high)].astype(F32).reshape(t_rows, depth)
            spread_columns(teacher_x, 0, top + 1, values, wide)
            return carry

        def one(i, carry):
            top = i * t_high
            spread_columns(teacher_h, 0, top + 1, gelu(teacher_conv(teacher_x, teacher_w1, top)), wide)
            return carry

        def two(i, total):
            top = i * t_high
            values = teacher_in[lead, pl.ds(top, t_high)].astype(F32).reshape(t_rows, depth)
            act = gelu(teacher_conv(teacher_h, teacher_w2, top) + values)
            return total + jnp.sum(act, axis=0, keepdims=True)

        lax.fori_loop(0, t_steps, fill, 0)
        lax.fori_loop(0, t_steps, one, 0)
        return lax.fori_loop(0, t_steps, two, jnp.zeros((1, depth), F32))

    for load in loads:
        load.wait()
    teacher_rows = [teacher_block(0)]

    pl.semaphore_wait(barrier, devices - 1)

    def gather_start(k, source, slot):
        def push(target, shard):
            pltpu.make_async_remote_copy(
                src_ref=source if shard is None else slot(shard),
                dst_ref=slot(c if shard is None else shard),
                send_sem=gather_send.at[k],
                recv_sem=gather_recv.at[k, c if shard is None else shard],
                device_id=(b, target),
                device_id_type=MESH,
            ).start()

        push(sibling, None)

        def one(i, carry):
            push(lax.rem(c + 2 * i, chans), None)
            return carry

        lax.fori_loop(1, chans // 2, one, 0, unroll=chans <= 8)
        return push

    def gather_wait(k, slot, shard):
        pltpu.make_async_remote_copy(
            src_ref=slot(shard),
            dst_ref=slot(shard),
            send_sem=gather_send.at[k],
            recv_sem=gather_recv.at[k, shard],
            device_id=(b, sibling),
            device_id_type=MESH,
        ).wait_recv()

    def gather_forward(k, slot, push):
        def one(i, carry):
            shard = lax.rem(c + 2 * i, chans)
            gather_wait(k, slot, shard)
            push(sibling, shard)
            return carry

        lax.fori_loop(1, chans // 2, one, 0, unroll=chans <= 8)

    def gather_finish(k, slot):
        def one(i, carry):
            gather_wait(k, slot, lax.rem(sibling + 2 * i, chans))
            return carry

        lax.fori_loop(0, chans // 2, one, 0, unroll=chans <= 8)

    def gather_drain(k, many):
        pltpu.make_async_copy(many, many, gather_send.at[k]).wait()

    slot_first = lambda s: w_first.at[s]
    slot_second = lambda s: w_second.at[s]
    slot_image = lambda s: image_all.at[s]
    slot_hidden = lambda s: hidden_all.at[s]

    def tile_start(k):
        def one(pb, pc):
            pltpu.make_async_remote_copy(
                src_ref=tile_send.at[k],
                dst_ref=tile_all[k].at[me],
                send_sem=tile_ssem.at[k],
                recv_sem=tile_rsem.at[k],
                device_id=(pb, pc),
                device_id_type=MESH,
            ).start()

        each_device(one)
        tile_all[k][me] = tile_send[k]

    def tile_wait(k):
        many = tile_all[k].at[pl.ds(0, devices - 1)]
        pltpu.make_async_copy(many, many, tile_rsem.at[k]).wait()

    def tile_drain(k):
        many = tile_all[k].at[pl.ds(0, devices - 1)]
        pltpu.make_async_copy(many, many, tile_ssem.at[k]).wait()

    def plane_start(k, source, slot):
        def one(pc):
            pltpu.make_async_remote_copy(
                src_ref=source(pc),
                dst_ref=slot(c),
                send_sem=plane_ssem.at[k],
                recv_sem=plane_rsem.at[k],
                device_id=(b, pc),
                device_id_type=MESH,
            ).start()

        each_plane(one)

    def plane_wait(k, many):
        pltpu.make_async_copy(many, many, plane_rsem.at[k]).wait()

    def plane_drain(k, many):
        pltpu.make_async_copy(many, many, plane_ssem.at[k]).wait()

    plane_start(0, lambda pc: param_send, lambda s: param_all.at[s])
    plane_start(1, lambda pc: head_send, lambda s: head_all.at[s])
    param_all[c] = param_send[...]
    head_all[c] = head_send[...]
    w_first[c] = own_first[...]
    w_second[c] = own_second[...]
    push_first = gather_start(0, own_first, slot_first)

    teacher_rows.append(teacher_block(1))
    which_t = lax.broadcasted_iota(jnp.int32, (8, depth), 0)
    pooled_t = jnp.zeros((8, depth), F32)
    for m in range(MICRO):
        pooled_t = jnp.where(which_t == m, teacher_rows[m] / float(wide * wide), pooled_t)
    teacher_head_pad[...] = jnp.zeros(teacher_head_pad.shape, F32)
    teacher_head_pad[0:classes, :] = teacher_head[...].astype(F32)
    teacher_logits = lax.dot_general(
        pooled_t, teacher_head_pad[...], (((1,), (1,)), ((), ())), precision=HIGHEST, preferred_element_type=F32
    )
    lane_pad = jnp.zeros((1, LANES - classes), F32)
    tile_send[0] = teacher_logits + jnp.concatenate([teacher_bias[...], lane_pad], axis=1)
    tile_start(0)

    gather_forward(0, slot_first, push_first)
    push_second = gather_start(1, own_second, slot_second)
    gather_finish(0, slot_first)

    def picker(shard, block, offset):
        at_row = lax.broadcasted_iota(jnp.int32, (depth, block), 0)
        place = lax.broadcasted_iota(jnp.int32, (depth, block), 1) - offset
        wanted = jnp.logical_and(place >= 0, place < own)
        return jnp.logical_and(wanted, at_row == shard * own + place).astype(BF16)

    def unpack(ref, block, offset):
        def one(shard, total):
            return total + jnp.dot(picker(shard, block, offset), ref[shard], preferred_element_type=F32)

        return lax.fori_loop(0, chans, one, jnp.zeros((depth, ref.shape[2]), F32)).astype(BF16)

    def weights(ref, tap):
        if own_pad == own:
            return ref[:, tap * own : (tap + 1) * own, :].reshape(depth, depth)
        return unpack(ref, own_rows, tap * own)

    def window(source, row_off, col_off):
        return source[:, row_off : row_off + extent, :, col_off * depth : (col_off + 1) * depth].reshape(
            MICRO * cells, depth
        )

    def student_conv(source, ref):
        total = None
        for row_off in range(3):
            for col_off in range(3):
                term = lax.dot_general(
                    window(source, row_off, col_off),
                    weights(ref, row_off * 3 + col_off),
                    (((1,), (1,)), ((), ())),
                    preferred_element_type=F32,
                )
                total = term if total is None else total + term
        return total

    def student_back(source, ref):
        total = None
        for row_off in range(3):
            for col_off in range(3):
                term = jnp.dot(
                    window(source, row_off, col_off),
                    weights(ref, (2 - row_off) * 3 + 2 - col_off),
                    preferred_element_type=F32,
                )
                total = term if total is None else total + term
        return total

    def put_sums(k, micro, first_sum, second_sum):
        for i, row in enumerate((first_sum, second_sum)):
            for j, half in enumerate(halves(row)):
                at = micro * 4 + i * 2 + j
                tile_send[k, at : at + 1, :] = half

    def total_sums(k):
        total = jnp.sum(tile_all[k][...], axis=0)
        return [
            [
                jnp.concatenate([total[m * 4 + i * 2 : m * 4 + i * 2 + 1], total[m * 4 + i * 2 + 1 : m * 4 + i * 2 + 2]], axis=1)
                for i in range(2)
            ]
            for m in range(MICRO)
        ]

    def rows_of(m):
        return slice(m * cells, (m + 1) * cells)

    def col_sum(values):
        return jnp.sum(values, axis=0, keepdims=True)

    def put_moments(k, ref):
        for m in range(MICRO):
            values = ref[rows_of(m), :]
            put_sums(k, m, col_sum(values), col_sum(values * values))

    def moments(k):
        found = []
        for total, square in total_sums(k):
            center = total / samples
            spread = square / samples - center * center
            found.append((center, lax.rsqrt(spread + EPS)))
        return found

    y_first[...] = student_conv(image_x, w_first)
    put_moments(1, y_first)
    tile_start(1)

    plane_wait(0, param_all.at[pl.ds(0, chans - 1)])
    plane_wait(1, head_all.at[pl.ds(0, chans - 1)])
    params = jnp.sum(param_all[...], axis=0)
    gain1, shift1, gain2, shift2 = (
        jnp.concatenate([params[2 * i : 2 * i + 1], params[2 * i + 1 : 2 * i + 2]], axis=1) for i in range(4)
    )
    if own_pad == own:
        head = head_all[...].reshape(depth, LANES).astype(F32)
    else:
        head = unpack(head_all, own_pad, 0).astype(F32)
    gather_forward(1, slot_second, push_second)
    push_image = gather_start(2, images, slot_image)
    image_all[c] = images[...]

    tile_wait(1)
    norm1 = moments(1)
    for m in range(MICRO):
        center, inv = norm1[m]
        normed = (y_first[rows_of(m), :] - center) * inv * gain1 + shift1
        spread_columns(hidden_x, m, 1, gelu(normed), extent)
    gather_finish(1, slot_second)

    y_second[...] = student_conv(hidden_x, w_second)
    put_moments(2, y_second)
    tile_start(2)
    for m in range(MICRO):
        hidden_all[c, m] = hidden_x[m, 1 : extent + 1, :, depth : 2 * depth]
    gather_forward(2, slot_image, push_image)
    push_hidden = gather_start(3, hidden_all.at[c], slot_hidden)

    tile_wait(2)
    norm2 = moments(2)

    def residual(m):
        center, inv = norm2[m]
        normal = (y_second[rows_of(m), :] - center) * inv
        return (normal, normal * gain2 + shift2 + images[m].astype(F32).reshape(cells, depth))

    pooled_rows = [col_sum(gelu(residual(m)[1])) / float(cells) for m in range(MICRO)]
    which = lax.broadcasted_iota(jnp.int32, (8, depth), 0)
    pooled = jnp.zeros((8, depth), F32)
    for m in range(MICRO):
        pooled = jnp.where(which == m, pooled_rows[m], pooled)
    logits = jnp.dot(pooled, head, precision=HIGHEST, preferred_element_type=F32) + jnp.concatenate(
        [head_bias[...], lane_pad], axis=1
    )

    tile_wait(0)
    per_device = pair_index.shape[0]
    grads = []
    for m in range(MICRO):
        paired = pair_index[m]
        teacher_row = tile_all[0][pl.ds(paired // per_device, 1), pl.ds(lax.rem(paired, per_device), 1), :].reshape(1, LANES)
        grads.append(distill_grad(logits[m : m + 1], teacher_row, labels[m], classes))
    which_lane = lax.broadcasted_iota(jnp.int32, (8, LANES), 0)
    logit_grad = jnp.zeros((8, LANES), F32)
    for m in range(MICRO):
        logit_grad = jnp.where(which_lane == m, grads[m], logit_grad)
    pooled_grad = lax.dot_general(
        logit_grad, head, (((1,), (1,)), ((), ())), precision=HIGHEST, preferred_element_type=F32
    ) / float(cells)
    for m in range(MICRO):
        normal, res = residual(m)
        grad = pooled_grad[m : m + 1] * gelu_slope(res)
        d_res[rows_of(m), :] = grad
        put_sums(3, m, col_sum(grad * normal), col_sum(grad))
    tile_start(3)
    for m in range(MICRO):
        for j, half in enumerate(halves(pooled_rows[m])):
            tile_send[4, m * 4 + j : m * 4 + j + 1, :] = half
        tile_send[4, m * 4 + 2 : m * 4 + 3, :] = grads[m]
        tile_send[4, m * 4 + 3 : m * 4 + 4, :] = logits[m : m + 1]
    tile_start(4)

    def own_lanes(low_row, high_row):
        at = c * own
        row = jnp.where(at >= LANES, high_row, low_row)
        turn = lax.rem(LANES - lax.rem(at, LANES), LANES)
        return pltpu.roll(jnp.broadcast_to(row, (8, LANES)), turn, 1)[0:1, 0:own]

    def norm_back(k, gain, norms, grad_ref, y_ref, gain_out, shift_out):
        totals = total_sums(k)
        for out, i in ((gain_out, 0), (shift_out, 1)):
            row = totals[0][i]
            for m in range(1, MICRO):
                row = row + totals[m][i]
            out[...] = own_lanes(*halves(row))
        found = []
        for m in range(MICRO):
            center, inv = norms[m]
            normal = (y_ref[rows_of(m), :] - center) * inv
            found.append(
                gain * inv * (grad_ref[rows_of(m), :] - totals[m][1] / samples - normal * (totals[m][0] / samples))
            )
        return found

    def send_turned(k, found):
        whole = jnp.concatenate([jnp.transpose(part) for part in found], axis=1).astype(BF16)
        if own_pad == own:
            turned_send[k] = whole.reshape(chans, own, MICRO * cells)
        else:

            def one(shard, carry):
                turned_send[k, shard] = lax.dot_general(
                    picker(shard, own_pad, 0), whole, (((0,), (0,)), ((), ())), preferred_element_type=F32
                ).astype(BF16)
                return carry

            lax.fori_loop(0, chans, one, 0)
        plane_start(2 + k, lambda pc: turned_send.at[k, pc], lambda s: turned_all.at[k, s])
        turned_all[k, c] = turned_send[k, c]

    def kernel_grad(k, inputs_all):
        plane_wait(2 + k, turned_all.at[k, pl.ds(0, chans - 1)])
        count = MICRO * cells
        lane = lax.broadcasted_iota(jnp.int32, (own_pad, count), 1)
        high, wide_at = lax.rem(lane, cells) // extent, lax.rem(lane, extent)

        def one(s, total):
            turned = turned_all[k, s].astype(F32)
            taps = []
            for row_off in range(3):
                for col_off in range(3):
                    up, over = row_off - 1, col_off - 1
                    shift = (up * extent + over) % count
                    moved = turned if shift == 0 else pltpu.roll(turned, shift, 1)
                    good = jnp.logical_and(
                        jnp.logical_and(high - up >= 0, high - up < extent),
                        jnp.logical_and(wide_at - over >= 0, wide_at - over < extent),
                    )
                    taps.append(jnp.where(good, moved, 0.0).astype(BF16))
            return total + jnp.dot(
                jnp.concatenate(taps, axis=0), inputs_all[s].reshape(count, depth), preferred_element_type=F32
            )

        return lax.fori_loop(0, chans, one, jnp.zeros((9 * own_pad, depth), F32))

    def line_start(k, source, slot):
        for db in range(1, groups):
            peer = lax.rem(b + db, groups)
            pltpu.make_async_remote_copy(
                src_ref=source(peer),
                dst_ref=slot(b),
                send_sem=line_ssem.at[k],
                recv_sem=line_rsem.at[k],
                device_id=(peer, c),
                device_id_type=MESH,
            ).start()

    def line_wait(k, many):
        pltpu.make_async_copy(many, many, line_rsem.at[k]).wait()

    def line_drain(k, many):
        pltpu.make_async_copy(many, many, line_ssem.at[k]).wait()

    def sum_start(k, total):
        flat = total.astype(BF16)
        padding = groups * rows_part - flat.shape[0]
        if padding:
            flat = jnp.concatenate([flat, jnp.zeros((padding, depth), BF16)], axis=0)
        part_send[k] = flat.reshape(groups, rows_part, depth)
        line_start(2 * k, lambda peer: part_send.at[k, peer], lambda s: part_recv.at[k, s])
        part_recv[k, b] = part_send[k, b]

    def sum_middle(k):
        line_wait(2 * k, part_recv.at[k, pl.ds(0, groups - 1)])
        sum_send[k] = jnp.sum(part_recv[k].astype(F32), axis=0).astype(BF16)
        line_start(2 * k + 1, lambda peer: sum_send.at[k], lambda s: sum_recv.at[k, s])
        sum_recv[k, b] = sum_send[k]

    def sum_finish(k, out):
        line_wait(2 * k + 1, sum_recv.at[k, pl.ds(0, groups - 1)])
        flat = sum_recv[k].reshape(groups * rows_part, depth)[0 : 9 * own_pad]
        out[...] = flat.astype(F32).reshape(9, own_pad, depth)

    gather_forward(3, slot_hidden, push_hidden)
    tile_wait(3)
    found = norm_back(3, gain2, norm2, d_res, y_second, gain_second_grad, shift_second_grad)
    send_turned(0, found)
    for m in range(MICRO):
        spread_columns(grad_x, m, 1, found[m].astype(BF16).astype(F32), extent)
    d_hid[...] = student_back(grad_x, w_second)
    for m in range(MICRO):
        center, inv = norm1[m]
        normal = (y_first[rows_of(m), :] - center) * inv
        grad = d_hid[rows_of(m), :] * gelu_slope(normal * gain1 + shift1)
        d_hid[rows_of(m), :] = grad
        put_sums(5, m, col_sum(grad * normal), col_sum(grad))
    tile_start(5)
    gather_finish(2, slot_image)
    gather_finish(3, slot_hidden)
    sum_start(0, kernel_grad(0, hidden_all))

    tile_wait(5)
    found = norm_back(5, gain1, norm1, d_hid, y_first, gain_first_grad, shift_first_grad)
    send_turned(1, found)
    for m in range(MICRO):
        spread_columns(grad_x, m, 1, found[m].astype(BF16).astype(F32), extent)
    images_grad[...] = (student_back(grad_x, w_first) + d_res[...]).reshape(images_grad.shape)
    sum_start(1, kernel_grad(1, image_all))
    sum_middle(0)

    tile_wait(4)
    totals = [jnp.zeros((LANES, LANES), F32) for _ in range(2)]
    bias_row = jnp.zeros((1, LANES), F32)
    for m in range(MICRO):
        per_image = tile_all[4][:, m * 4 + 2, :]
        bias_row = bias_row + col_sum(per_image)
        for j in range(2):
            totals[j] = totals[j] + lax.dot_general(
                tile_all[4][:, m * 4 + j, :],
                per_image,
                (((0,), (0,)), ((), ())),
                precision=HIGHEST,
                preferred_element_type=F32,
            )
        shown = tile_all[4][pl.ds(b * chans, chans), m * 4 + 3, :]
        logits_out[pl.ds(m, chans, stride=MICRO), :] = shown[:, 0:classes]
    for j in range(2):
        head_sum[j * LANES : (j + 1) * LANES, :] = totals[j]
    head_grad[...] = head_sum[pl.ds(c * own, own), :][:, 0:classes]
    bias_grad[...] = bias_row[:, 0:classes]

    sum_middle(1)
    sum_finish(0, second_grad)
    sum_finish(1, first_grad)

    for k in range(6):
        tile_drain(k)
    gather_drain(0, w_first.at[pl.ds(0, chans - 1)])
    gather_drain(1, w_second.at[pl.ds(0, chans - 1)])
    gather_drain(2, image_all.at[pl.ds(0, chans - 1)])
    gather_drain(3, hidden_all.at[pl.ds(0, chans - 1)])
    plane_drain(0, param_all.at[pl.ds(0, chans - 1)])
    plane_drain(1, head_all.at[pl.ds(0, chans - 1)])
    for k in range(2):
        plane_drain(2 + k, turned_all.at[k, pl.ds(0, chans - 1)])
        line_drain(2 * k, part_recv.at[k, pl.ds(0, groups - 1)])
        line_drain(2 * k + 1, sum_recv.at[k, pl.ds(0, groups - 1)])


def shards(
    teacher_images,
    student_images,
    pair_index,
    labels,
    teacher_first,
    teacher_second,
    teacher_head,
    teacher_bias,
    conv_first,
    gain_first,
    shift_first,
    conv_second,
    gain_second,
    shift_second,
    head_weight,
    head_bias,
):
    groups, chans = lax.axis_size("batch"), lax.axis_size("chan")
    devices = groups * chans
    count, extent, _, depth = student_images.shape
    wide = teacher_images.shape[1]
    own = conv_first.shape[3]
    own_pad = max(own, 16)
    own_rows = -(-9 * own // 16) * 16
    classes = head_bias.shape[0]
    cells = extent * extent
    rows = count * cells
    rows_part = -(-9 * own_pad // (groups * 16)) * 16

    def turned(kernel):
        return jnp.transpose(kernel, (0, 1, 3, 2)).reshape(9 * own, depth)

    def row(vector):
        return vector.reshape(1, -1)

    vmem = pl.BlockSpec(memory_space=pltpu.VMEM)
    smem = pl.BlockSpec(memory_space=pltpu.SMEM)
    hbm = pl.BlockSpec(memory_space=pl.ANY)
    out_shape = [
        jax.ShapeDtypeStruct((chans * count, classes), F32),
        jax.ShapeDtypeStruct(student_images.shape, F32),
        jax.ShapeDtypeStruct((9, own_pad, depth), F32),
        jax.ShapeDtypeStruct((1, own), F32),
        jax.ShapeDtypeStruct((1, own), F32),
        jax.ShapeDtypeStruct((9, own_pad, depth), F32),
        jax.ShapeDtypeStruct((1, own), F32),
        jax.ShapeDtypeStruct((1, own), F32),
        jax.ShapeDtypeStruct((own, classes), F32),
        jax.ShapeDtypeStruct((1, classes), F32),
    ]
    scratch = [
        pltpu.VMEM(teacher_images.shape, BF16),
        pltpu.VMEM((9 * depth, depth), BF16),
        pltpu.VMEM((9 * depth, depth), BF16),
        pltpu.VMEM((1, wide + 2, wide, 3 * depth), BF16),
        pltpu.VMEM((1, wide + 2, wide, 3 * depth), BF16),
        pltpu.VMEM((LANES, depth), F32),
        pltpu.VMEM((count, extent + 2, extent, 3 * depth), BF16),
        pltpu.VMEM((count, extent + 2, extent, 3 * depth), BF16),
        pltpu.VMEM((count, extent + 2, extent, 3 * depth), BF16),
        pltpu.VMEM((chans, own_rows, depth), BF16),
        pltpu.VMEM((chans, own_rows, depth), BF16),
        pltpu.VMEM((own_rows, depth), BF16),
        pltpu.VMEM((own_rows, depth), BF16),
        pltpu.VMEM((rows, depth), F32),
        pltpu.VMEM((rows, depth), F32),
        pltpu.VMEM((rows, depth), F32),
        pltpu.VMEM((rows, depth), F32),
        pltpu.VMEM((chans,) + student_images.shape, BF16),
        pltpu.VMEM((chans,) + student_images.shape, BF16),
        pltpu.VMEM((2, chans, own_pad, rows), BF16),
        pltpu.VMEM((2, chans, own_pad, rows), BF16),
        pltpu.VMEM((2, groups, rows_part, depth), BF16),
        pltpu.VMEM((2, groups, rows_part, depth), BF16),
        pltpu.VMEM((2, rows_part, depth), BF16),
        pltpu.VMEM((2, groups, rows_part, depth), BF16),
        pltpu.VMEM((8, LANES), F32),
        pltpu.VMEM((chans, 8, LANES), F32),
        pltpu.VMEM((own_pad, LANES), BF16),
        pltpu.VMEM((chans, own_pad, LANES), BF16),
        pltpu.VMEM((6, 8, LANES), F32),
        pltpu.VMEM((devices, 8, LANES), F32),
        pltpu.VMEM((devices, 8, LANES), F32),
        pltpu.VMEM((devices, 8, LANES), F32),
        pltpu.VMEM((devices, 8, LANES), F32),
        pltpu.VMEM((devices, 8, LANES), F32),
        pltpu.VMEM((devices, 8, LANES), F32),
        pltpu.VMEM((depth, LANES), F32),
        pltpu.SemaphoreType.DMA((3,)),
        pltpu.SemaphoreType.DMA((4,)),
        pltpu.SemaphoreType.DMA((4, chans)),
        pltpu.SemaphoreType.DMA((6,)),
        pltpu.SemaphoreType.DMA((6,)),
        pltpu.SemaphoreType.DMA((4,)),
        pltpu.SemaphoreType.DMA((4,)),
        pltpu.SemaphoreType.DMA((4,)),
        pltpu.SemaphoreType.DMA((4,)),
    ]
    found = pl.pallas_call(
        functools.partial(body, (groups, chans, own, own_pad, classes)),
        out_shape=out_shape,
        in_specs=[hbm, vmem, smem, smem, hbm, hbm] + [vmem] * 10,
        out_specs=[vmem] * 10,
        scratch_shapes=scratch,
        compiler_params=pltpu.CompilerParams(
            collective_id=0, has_side_effects=True, vmem_limit_bytes=62 * 2**20
        ),
    )(
        teacher_images,
        student_images,
        pair_index,
        labels,
        teacher_first.reshape(9 * depth, depth),
        teacher_second.reshape(9 * depth, depth),
        teacher_head.T,
        row(teacher_bias),
        turned(conv_first),
        row(gain_first),
        row(shift_first),
        turned(conv_second),
        row(gain_second),
        row(shift_second),
        head_weight,
        row(head_bias),
    )
    logits, images_grad, first, gain1, shift1, second, gain2, shift2, head, bias = found

    def back(grad):
        return jnp.transpose(grad[:, :own].reshape(3, 3, own, depth), (0, 1, 3, 2))

    return (
        logits,
        images_grad,
        back(first),
        gain1.reshape(-1),
        shift1.reshape(-1),
        back(second),
        gain2.reshape(-1),
        shift2.reshape(-1),
        head,
        bias.reshape(-1),
    )


def solution(mesh):
    in_specs = (
        P(("batch", "chan"), None, None, None),
        P(("batch", "chan"), None, None, None),
        P(("batch", "chan")),
        P(("batch", "chan")),
        P(),
        P(),
        P(),
        P(),
        P(None, None, None, "chan"),
        P("chan"),
        P("chan"),
        P(None, None, None, "chan"),
        P("chan"),
        P("chan"),
        P("chan", None),
        P(),
    )
    out_specs = (
        P("batch", None),
        P(("batch", "chan"), None, None, None),
        P(None, None, None, "chan"),
        P("chan"),
        P("chan"),
        P(None, None, None, "chan"),
        P("chan"),
        P("chan"),
        P("chan", None),
        P(),
    )
    return jax.shard_map(shards, mesh=mesh, in_specs=in_specs, out_specs=out_specs, check_vma=False)
```

```python
import functools

import jax
import jax.numpy as jnp
from jax import lax
from jax.experimental import pallas as pl
from jax.experimental.pallas import tpu as pltpu
from jax.sharding import PartitionSpec as P

MESH = pl.DeviceIdType.MESH
F32 = jnp.float32
BF16 = jnp.bfloat16
HIGHEST = lax.Precision.HIGHEST
MICRO = 2
EPS = 1e-05
TARGET_WEIGHT = 1.0
NONTARGET_WEIGHT = 8.0
SOFTEN = 4.0
GELU_A = 0.7978845608028654
GELU_B = 0.044715
LANES = 128


def gelu(x):
    return x * (0.5 + 0.5 * jnp.tanh(GELU_A * (x + GELU_B * (x * x * x))))


def gelu_slope(x):
    square = x * x
    t = jnp.tanh(GELU_A * (x + GELU_B * (x * square)))
    return 0.5 + 0.5 * t + (0.5 * x) * (1.0 - t * t) * (GELU_A + (3.0 * GELU_A * GELU_B) * square)


def column(shape, width):
    return lax.rem(lax.broadcasted_iota(jnp.int32, shape, 0), width)


def spread_columns(dest, lead, top, values, width):
    rows, depth = values.shape
    col = column(values.shape, width)
    left = jnp.where(col == 0, 0.0, pltpu.roll(values, 1, 0))
    right = jnp.where(col == width - 1, 0.0, pltpu.roll(values, rows - 1, 0))
    high = rows // width
    for place, part in enumerate((left, values, right)):
        dest[lead, pl.ds(top, high), :, place * depth : (place + 1) * depth] = part.astype(BF16).reshape(
            high, width, depth
        )


def halves(row):
    return (row[:, :LANES], row[:, LANES:])


def distill_grad(student, teacher, label, classes):
    lane = lax.broadcasted_iota(jnp.int32, student.shape, 1)
    live = lane < classes
    target = lane == label
    other = jnp.logical_and(live, jnp.logical_not(target))
    low = -1e30

    def parts(logits):
        soft = logits / SOFTEN
        whole_top = jnp.max(jnp.where(live, soft, low), axis=1, keepdims=True)
        rest_top = jnp.max(jnp.where(other, soft, low), axis=1, keepdims=True)
        whole_exp = jnp.where(live, jnp.exp(jnp.where(live, soft, whole_top) - whole_top), 0.0)
        rest_exp = jnp.where(other, jnp.exp(jnp.where(other, soft, rest_top) - rest_top), 0.0)
        whole_sum = jnp.sum(whole_exp, axis=1, keepdims=True)
        rest_sum = jnp.sum(rest_exp, axis=1, keepdims=True)
        whole = whole_top + jnp.log(whole_sum)
        rest = rest_top + jnp.log(rest_sum)
        true = jnp.sum(jnp.where(target, soft, 0.0), axis=1, keepdims=True)
        return (whole_exp / whole_sum, rest_exp / rest_sum, true - whole, rest - whole)

    probs, inner, _, _ = parts(student)
    _, inner_t, log_pt, log_rt = parts(teacher)
    p_true, p_rest = jnp.exp(log_pt), jnp.exp(log_rt)
    split_grad = (p_true + p_rest) * probs - jnp.where(target, p_true, 0.0) - p_rest * inner
    inner_grad = jnp.sum(inner_t, axis=1, keepdims=True) * inner - inner_t
    return SOFTEN * (TARGET_WEIGHT * split_grad + NONTARGET_WEIGHT * inner_grad)


def body(
    sizes,
    teacher_hbm,
    images,
    pair_index,
    labels,
    teacher_first_hbm,
    teacher_second_hbm,
    teacher_head,
    teacher_bias,
    first_own,
    gain_first,
    shift_first,
    second_own,
    gain_second,
    shift_second,
    head_own,
    head_bias,
    logits_out,
    images_grad,
    first_grad,
    gain_first_grad,
    shift_first_grad,
    second_grad,
    gain_second_grad,
    shift_second_grad,
    head_grad,
    bias_grad,
    teacher_in,
    teacher_w1,
    teacher_w2,
    teacher_x,
    teacher_h,
    teacher_head_pad,
    image_x,
    hidden_x,
    grad_x,
    w_first,
    w_second,
    own_first,
    own_second,
    y_first,
    y_second,
    d_res,
    d_hid,
    image_sib,
    hidden_sib,
    turned,
    turned_sib,
    part_all,
    part_own,
    part_send,
    part_recv,
    line_own,
    line_send,
    line_recv_first,
    line_recv_second,
    sum_send,
    sum_recv,
    param_send,
    param_all,
    head_send,
    head_all,
    tile_send,
    tile_all_0,
    tile_all_1,
    tile_all_2,
    tile_all_3,
    tile_all_4,
    tile_all_5,
    head_sum,
    local_sem,
    gather_send,
    gather_recv,
    tile_ssem,
    tile_rsem,
    plane_ssem,
    plane_rsem,
    swap_ssem,
    swap_rsem,
    part_ssem,
    part_rsem,
    line_ssem,
    line_rsem,
    sum_ssem,
    sum_rsem,
):
    groups, chans, own, own_pad, classes = sizes
    tile_all = (tile_all_0, tile_all_1, tile_all_2, tile_all_3, tile_all_4, tile_all_5)
    b = lax.axis_index("batch")
    c = lax.axis_index("chan")
    me = b * chans + c
    devices = groups * chans
    sibling = c + 1 - 2 * lax.rem(c, 2)
    extent = images.shape[1]
    cells = extent * extent
    depth = images.shape[3]
    wide = teacher_hbm.shape[1]
    samples = float(devices * cells)
    chips = chans // 2
    chip, core = c // 2, lax.rem(c, 2)
    own_rows = own_first.shape[0]

    def far_order():
        return [db for db in range(1, groups)] + [0]

    def each_device(fn):
        for db in far_order():
            peer_b = lax.rem(b + db, groups)

            def one(i, carry, peer_b=peer_b):
                fn(peer_b, lax.rem(c + (chans - i), chans))
                return carry

            lax.fori_loop(1 if db == 0 else 0, chans, one, 0, unroll=chans <= 8)

    def each_plane(fn):
        def one(i, carry):
            fn(lax.rem(c + i, chans))
            return carry

        lax.fori_loop(1, chans, one, 0, unroll=chans <= 8)

    barrier = pltpu.get_barrier_semaphore()
    each_device(lambda pb, pc: pl.semaphore_signal(barrier, inc=1, device_id=(pb, pc), device_id_type=MESH))

    loads = [
        pltpu.make_async_copy(teacher_hbm, teacher_in, local_sem.at[0]),
        pltpu.make_async_copy(teacher_first_hbm, teacher_w1, local_sem.at[1]),
        pltpu.make_async_copy(teacher_second_hbm, teacher_w2, local_sem.at[2]),
    ]
    for load in loads:
        load.start()

    def place_own(param_row):
        at = c * own
        lane0 = lax.rem(at, LANES)
        padded = jnp.concatenate([param_row, jnp.zeros((1, LANES - own), F32)], axis=1)
        moved = pltpu.roll(jnp.broadcast_to(padded, (8, LANES)), lane0, 1)[0:1]
        upper = at >= LANES
        return (jnp.where(upper, 0.0, moved), jnp.where(upper, moved, 0.0))

    for i, ref in enumerate((gain_first, shift_first, gain_second, shift_second)):
        low_half, high_half = place_own(ref[...])
        param_send[2 * i : 2 * i + 1, :] = low_half
        param_send[2 * i + 1 : 2 * i + 2, :] = high_half
    head_send[...] = jnp.zeros(head_send.shape, BF16)
    head_send[0:own, 0:classes] = head_own[...]
    for src, dst in ((first_own, own_first), (second_own, own_second)):
        if own_rows != 9 * own:
            dst[...] = jnp.zeros(dst.shape, BF16)
        dst[0 : 9 * own, :] = src[...]

    for ref in (image_x, hidden_x, grad_x, teacher_x, teacher_h):
        high = ref.shape[1]
        for lead in range(ref.shape[0]):
            ref[lead, 0] = jnp.zeros(ref.shape[2:], BF16)
            ref[lead, high - 1] = jnp.zeros(ref.shape[2:], BF16)
    for lead in range(MICRO):
        spread_columns(image_x, lead, 1, images[lead].astype(F32).reshape(cells, depth), extent)

    t_high = 16
    t_steps = wide // t_high
    t_rows = t_high * wide

    def teacher_conv(source, kernel, top):
        total = None
        for row_off in range(3):
            window = source[0, pl.ds(top + row_off, t_high)].reshape(t_rows, 3 * depth)
            term = jnp.dot(
                window, kernel[row_off * 3 * depth : (row_off + 1) * 3 * depth, :], preferred_element_type=F32
            )
            total = term if total is None else total + term
        return total

    def teacher_block(lead):
        def fill(i, carry):
            top = i * t_high
            values = teacher_in[lead, pl.ds(top, t_high)].astype(F32).reshape(t_rows, depth)
            spread_columns(teacher_x, 0, top + 1, values, wide)
            return carry

        def one(i, carry):
            top = i * t_high
            spread_columns(teacher_h, 0, top + 1, gelu(teacher_conv(teacher_x, teacher_w1, top)), wide)
            return carry

        def two(i, total):
            top = i * t_high
            values = teacher_in[lead, pl.ds(top, t_high)].astype(F32).reshape(t_rows, depth)
            act = gelu(teacher_conv(teacher_h, teacher_w2, top) + values)
            return total + jnp.sum(act, axis=0, keepdims=True)

        lax.fori_loop(0, t_steps, fill, 0)
        lax.fori_loop(0, t_steps, one, 0)
        return lax.fori_loop(0, t_steps, two, jnp.zeros((1, depth), F32))

    for load in loads:
        load.wait()
    teacher_rows = [teacher_block(0)]

    pl.semaphore_wait(barrier, devices - 1)

    def gather_start(k, source, slot):
        def push(target, shard):
            pltpu.make_async_remote_copy(
                src_ref=source if shard is None else slot(shard),
                dst_ref=slot(c if shard is None else shard),
                send_sem=gather_send.at[k],
                recv_sem=gather_recv.at[k, c if shard is None else shard],
                device_id=(b, target),
                device_id_type=MESH,
            ).start()

        push(sibling, None)

        def one(i, carry):
            push(lax.rem(c + 2 * i, chans), None)
            return carry

        lax.fori_loop(1, chans // 2, one, 0, unroll=chans <= 8)
        return push

    def gather_wait(k, slot, shard):
        pltpu.make_async_remote_copy(
            src_ref=slot(shard),
            dst_ref=slot(shard),
            send_sem=gather_send.at[k],
            recv_sem=gather_recv.at[k, shard],
            device_id=(b, sibling),
            device_id_type=MESH,
        ).wait_recv()

    def gather_forward(k, slot, push):
        def one(i, carry):
            shard = lax.rem(c + 2 * i, chans)
            gather_wait(k, slot, shard)
            push(sibling, shard)
            return carry

        lax.fori_loop(1, chans // 2, one, 0, unroll=chans <= 8)

    def gather_finish(k, slot):
        def one(i, carry):
            gather_wait(k, slot, lax.rem(sibling + 2 * i, chans))
            return carry

        lax.fori_loop(0, chans // 2, one, 0, unroll=chans <= 8)

    def gather_drain(k, many):
        pltpu.make_async_copy(many, many, gather_send.at[k]).wait()

    slot_first = lambda s: w_first.at[s]
    slot_second = lambda s: w_second.at[s]

    def swap(k, source, dest):
        return pltpu.make_async_remote_copy(
            src_ref=source,
            dst_ref=dest,
            send_sem=swap_ssem.at[k],
            recv_sem=swap_rsem.at[k],
            device_id=(b, sibling),
            device_id_type=MESH,
        )

    def tile_start(k):
        def one(pb, pc):
            pltpu.make_async_remote_copy(
                src_ref=tile_send.at[k],
                dst_ref=tile_all[k].at[me],
                send_sem=tile_ssem.at[k],
                recv_sem=tile_rsem.at[k],
                device_id=(pb, pc),
                device_id_type=MESH,
            ).start()

        each_device(one)
        tile_all[k][me] = tile_send[k]

    def tile_wait(k):
        many = tile_all[k].at[pl.ds(0, devices - 1)]
        pltpu.make_async_copy(many, many, tile_rsem.at[k]).wait()

    def tile_drain(k):
        many = tile_all[k].at[pl.ds(0, devices - 1)]
        pltpu.make_async_copy(many, many, tile_ssem.at[k]).wait()

    def plane_start(k, source, slot):
        def one(pc):
            pltpu.make_async_remote_copy(
                src_ref=source(pc),
                dst_ref=slot(c),
                send_sem=plane_ssem.at[k],
                recv_sem=plane_rsem.at[k],
                device_id=(b, pc),
                device_id_type=MESH,
            ).start()

        each_plane(one)

    def plane_wait(k, many):
        pltpu.make_async_copy(many, many, plane_rsem.at[k]).wait()

    def plane_drain(k, many):
        pltpu.make_async_copy(many, many, plane_ssem.at[k]).wait()

    w_first[c] = own_first[...]
    w_second[c] = own_second[...]
    push_first = gather_start(0, own_first, slot_first)
    swaps = [swap(0, image_x, image_sib)]
    swaps[0].start()
    plane_start(0, lambda pc: param_send, lambda s: param_all.at[s])
    plane_start(1, lambda pc: head_send, lambda s: head_all.at[s])
    param_all[c] = param_send[...]
    head_all[c] = head_send[...]

    teacher_rows.append(teacher_block(1))
    which_t = lax.broadcasted_iota(jnp.int32, (8, depth), 0)
    pooled_t = jnp.zeros((8, depth), F32)
    for m in range(MICRO):
        pooled_t = jnp.where(which_t == m, teacher_rows[m] / float(wide * wide), pooled_t)
    teacher_head_pad[...] = jnp.zeros(teacher_head_pad.shape, F32)
    teacher_head_pad[0:classes, :] = teacher_head[...].astype(F32)
    teacher_logits = lax.dot_general(
        pooled_t, teacher_head_pad[...], (((1,), (1,)), ((), ())), precision=HIGHEST, preferred_element_type=F32
    )
    lane_pad = jnp.zeros((1, LANES - classes), F32)
    tile_send[0] = teacher_logits + jnp.concatenate([teacher_bias[...], lane_pad], axis=1)
    tile_start(0)

    gather_forward(0, slot_first, push_first)
    push_second = gather_start(1, own_second, slot_second)
    gather_finish(0, slot_first)

    def picker(shard, block, offset):
        at_row = lax.broadcasted_iota(jnp.int32, (depth, block), 0)
        place = lax.broadcasted_iota(jnp.int32, (depth, block), 1) - offset
        wanted = jnp.logical_and(place >= 0, place < own)
        return jnp.logical_and(wanted, at_row == shard * own + place).astype(BF16)

    def unpack(ref, block, offset):
        def one(shard, total):
            return total + jnp.dot(picker(shard, block, offset), ref[shard], preferred_element_type=F32)

        return lax.fori_loop(0, chans, one, jnp.zeros((depth, ref.shape[2]), F32)).astype(BF16)

    def weights(ref, tap):
        if own_pad == own:
            return ref[:, tap * own : (tap + 1) * own, :].reshape(depth, depth)
        return unpack(ref, own_rows, tap * own)

    def window(source, row_off, col_off):
        return source[:, row_off : row_off + extent, :, col_off * depth : (col_off + 1) * depth].reshape(
            MICRO * cells, depth
        )

    def student_conv(source, ref):
        total = None
        for row_off in range(3):
            for col_off in range(3):
                term = lax.dot_general(
                    window(source, row_off, col_off),
                    weights(ref, row_off * 3 + col_off),
                    (((1,), (1,)), ((), ())),
                    preferred_element_type=F32,
                )
                total = term if total is None else total + term
        return total

    def student_back(source, ref):
        total = None
        for row_off in range(3):
            for col_off in range(3):
                term = jnp.dot(
                    window(source, row_off, col_off),
                    weights(ref, (2 - row_off) * 3 + 2 - col_off),
                    preferred_element_type=F32,
                )
                total = term if total is None else total + term
        return total

    def put_sums(k, micro, first_sum, second_sum):
        for i, row in enumerate((first_sum, second_sum)):
            for j, half in enumerate(halves(row)):
                at = micro * 4 + i * 2 + j
                tile_send[k, at : at + 1, :] = half

    def total_sums(k):
        total = jnp.sum(tile_all[k][...], axis=0)
        return [
            [
                jnp.concatenate([total[m * 4 + i * 2 : m * 4 + i * 2 + 1], total[m * 4 + i * 2 + 1 : m * 4 + i * 2 + 2]], axis=1)
                for i in range(2)
            ]
            for m in range(MICRO)
        ]

    def rows_of(m):
        return slice(m * cells, (m + 1) * cells)

    def col_sum(values):
        return jnp.sum(values, axis=0, keepdims=True)

    def put_moments(k, ref):
        for m in range(MICRO):
            values = ref[rows_of(m), :]
            put_sums(k, m, col_sum(values), col_sum(values * values))

    def moments(k):
        found = []
        for total, square in total_sums(k):
            center = total / samples
            spread = square / samples - center * center
            found.append((center, lax.rsqrt(spread + EPS)))
        return found

    y_first[...] = student_conv(image_x, w_first)
    put_moments(1, y_first)
    tile_start(1)

    plane_wait(0, param_all.at[pl.ds(0, chans - 1)])
    plane_wait(1, head_all.at[pl.ds(0, chans - 1)])
    params = jnp.sum(param_all[...], axis=0)
    gain1, shift1, gain2, shift2 = (
        jnp.concatenate([params[2 * i : 2 * i + 1], params[2 * i + 1 : 2 * i + 2]], axis=1) for i in range(4)
    )
    if own_pad == own:
        head = head_all[...].reshape(depth, LANES).astype(F32)
    else:
        head = unpack(head_all, own_pad, 0).astype(F32)
    gather_forward(1, slot_second, push_second)

    tile_wait(1)
    norm1 = moments(1)
    for m in range(MICRO):
        center, inv = norm1[m]
        normed = (y_first[rows_of(m), :] - center) * inv * gain1 + shift1
        spread_columns(hidden_x, m, 1, gelu(normed), extent)
    swaps.append(swap(1, hidden_x, hidden_sib))
    swaps[1].start()
    gather_finish(1, slot_second)

    y_second[...] = student_conv(hidden_x, w_second)
    put_moments(2, y_second)
    tile_start(2)

    tile_wait(2)
    norm2 = moments(2)

    def residual(m):
        center, inv = norm2[m]
        normal = (y_second[rows_of(m), :] - center) * inv
        return (normal, normal * gain2 + shift2 + images[m].astype(F32).reshape(cells, depth))

    pooled_rows = [col_sum(gelu(residual(m)[1])) / float(cells) for m in range(MICRO)]
    which = lax.broadcasted_iota(jnp.int32, (8, depth), 0)
    pooled = jnp.zeros((8, depth), F32)
    for m in range(MICRO):
        pooled = jnp.where(which == m, pooled_rows[m], pooled)
    logits = jnp.dot(pooled, head, precision=HIGHEST, preferred_element_type=F32) + jnp.concatenate(
        [head_bias[...], lane_pad], axis=1
    )

    tile_wait(0)
    per_device = pair_index.shape[0]
    grads = []
    for m in range(MICRO):
        paired = pair_index[m]
        teacher_row = tile_all[0][pl.ds(paired // per_device, 1), pl.ds(lax.rem(paired, per_device), 1), :].reshape(1, LANES)
        grads.append(distill_grad(logits[m : m + 1], teacher_row, labels[m], classes))
    which_lane = lax.broadcasted_iota(jnp.int32, (8, LANES), 0)
    logit_grad = jnp.zeros((8, LANES), F32)
    for m in range(MICRO):
        logit_grad = jnp.where(which_lane == m, grads[m], logit_grad)
    pooled_grad = lax.dot_general(
        logit_grad, head, (((1,), (1,)), ((), ())), precision=HIGHEST, preferred_element_type=F32
    ) / float(cells)
    for m in range(MICRO):
        normal, res = residual(m)
        grad = pooled_grad[m : m + 1] * gelu_slope(res)
        d_res[rows_of(m), :] = grad
        put_sums(3, m, col_sum(grad * normal), col_sum(grad))
    tile_start(3)
    for m in range(MICRO):
        for j, half in enumerate(halves(pooled_rows[m])):
            tile_send[4, m * 4 + j : m * 4 + j + 1, :] = half
        tile_send[4, m * 4 + 2 : m * 4 + 3, :] = grads[m]
        tile_send[4, m * 4 + 3 : m * 4 + 4, :] = logits[m : m + 1]
    tile_start(4)

    def own_lanes(low_row, high_row):
        at = c * own
        row = jnp.where(at >= LANES, high_row, low_row)
        turn = lax.rem(LANES - lax.rem(at, LANES), LANES)
        return pltpu.roll(jnp.broadcast_to(row, (8, LANES)), turn, 1)[0:1, 0:own]

    def norm_back(k, gain, norms, grad_ref, y_ref, gain_out, shift_out):
        totals = total_sums(k)
        for out, i in ((gain_out, 0), (shift_out, 1)):
            row = totals[0][i]
            for m in range(1, MICRO):
                row = row + totals[m][i]
            out[...] = own_lanes(*halves(row))
        found = []
        for m in range(MICRO):
            center, inv = norms[m]
            normal = (y_ref[rows_of(m), :] - center) * inv
            found.append(
                gain * inv * (grad_ref[rows_of(m), :] - totals[m][1] / samples - normal * (totals[m][0] / samples))
            )
        return found

    def turn(k, found):
        whole = jnp.concatenate([jnp.transpose(part) for part in found], axis=1).astype(BF16)
        if own_pad == own:
            turned[k] = whole.reshape(chips, 2, own, MICRO * cells)
        else:

            def one(shard, carry):
                turned[k, shard // 2, lax.rem(shard, 2)] = lax.dot_general(
                    picker(shard, own_pad, 0), whole, (((0,), (0,)), ((), ())), preferred_element_type=F32
                ).astype(BF16)
                return carry

            lax.fori_loop(0, chans, one, 0)
        swaps.append(swap(2 + k, turned.at[k, :, 1 - core], turned_sib.at[k]))
        swaps[-1].start()

    taps = 3 * own_pad

    def part_copy(k, row_off, peer_chip):
        return pltpu.make_async_remote_copy(
            src_ref=part_send.at[k, row_off, peer_chip],
            dst_ref=part_recv.at[k, row_off, chip],
            send_sem=part_ssem.at[k, row_off],
            recv_sem=part_rsem.at[k, row_off],
            device_id=(b, 2 * peer_chip + core),
            device_id_type=MESH,
        )

    def each_chip(fn):
        def one(i, carry):
            fn(lax.rem(chip + i, chips))
            return carry

        lax.fori_loop(1, chips, one, 0, unroll=chips <= 4)

    def kernel_grad(k, source, source_sib):
        count = MICRO * cells
        mine = turned[k, :, pl.ds(core, 1)].reshape(chips * own_pad, count)
        theirs = None
        for row_off in range(3):
            total = jnp.dot(
                mine,
                source[:, row_off : row_off + extent].reshape(count, 3 * depth),
                preferred_element_type=F32,
            )
            if theirs is None:
                swaps[2 + k].wait_recv()
                theirs = turned_sib[k].reshape(chips * own_pad, count)
            total = total + jnp.dot(
                theirs,
                source_sib[:, row_off : row_off + extent].reshape(count, 3 * depth),
                preferred_element_type=F32,
            )
            for i in range(chips):
                for col_off in range(3):
                    part_all[i, col_off * own_pad : (col_off + 1) * own_pad, :] = total[
                        i * own_pad : (i + 1) * own_pad, col_off * depth : (col_off + 1) * depth
                    ]
            part_send[k, row_off] = part_all[...].astype(BF16)
            part_own[k, row_off] = part_all[pl.ds(chip, 1)].reshape(taps, depth)
            each_chip(lambda peer, row_off=row_off: part_copy(k, row_off, peer).start())
            part_recv[k, row_off, chip] = jnp.zeros((taps, depth), BF16)

    per_half = groups // 2
    part_rows = taps // per_half
    part_pad = sum_send.shape[2]

    def line_copy(k, row_off, peer):
        if k == 0:
            source, dest = line_own.at[k, row_off, peer], line_recv_second.at[row_off, b]
        else:
            source, dest = line_send.at[row_off, peer], line_recv_first.at[row_off, b]
        return pltpu.make_async_remote_copy(
            src_ref=source,
            dst_ref=dest,
            send_sem=line_ssem.at[k, row_off],
            recv_sem=line_rsem.at[k, row_off],
            device_id=(peer, c),
            device_id_type=MESH,
        )

    def sum_copy(k, row_off, peer):
        return pltpu.make_async_remote_copy(
            src_ref=sum_send.at[k, row_off],
            dst_ref=sum_recv.at[k, row_off, b],
            send_sem=sum_ssem.at[k, row_off],
            recv_sem=sum_rsem.at[k, row_off],
            device_id=(peer, c),
            device_id_type=MESH,
        )

    def each_line(fn):
        for db in range(1, groups):
            fn(lax.rem(b + db, groups))

    def bytes_of(sem, many):
        pltpu.make_async_copy(many, many, sem).wait()

    def line_start(k):
        recv = line_recv_second if k == 0 else line_recv_first
        for row_off in range(3):
            bytes_of(part_rsem.at[k, row_off], part_recv.at[k, row_off, pl.ds(0, chips - 1)])
            total = part_own[k, row_off] + jnp.sum(
                part_recv[k, row_off].astype(F32), axis=0
            )
            for p in range(groups):
                half, row = p // per_half, (p % per_half) * part_rows
                line_own[k, row_off, p, 0:part_rows] = total[
                    row : row + part_rows, half * LANES : (half + 1) * LANES
                ]
                if part_pad != part_rows:
                    line_own[k, row_off, p, part_rows:part_pad] = jnp.zeros((part_pad - part_rows, LANES), F32)
            if k == 1:
                line_send[row_off] = line_own[k, row_off].astype(BF16)
            each_line(lambda peer, row_off=row_off: line_copy(k, row_off, peer).start())
            recv[row_off, b] = jnp.zeros((part_pad, LANES), recv.dtype)

    def sum_start(k):
        recv = line_recv_second if k == 0 else line_recv_first
        for row_off in range(3):
            bytes_of(line_rsem.at[k, row_off], recv.at[row_off, pl.ds(0, groups - 1)])
            total = line_own[k, row_off, pl.ds(b, 1)].reshape(part_pad, LANES) + jnp.sum(
                recv[row_off].astype(F32), axis=0
            )
            sum_send[k, row_off] = total.astype(BF16)
            each_line(lambda peer, row_off=row_off: sum_copy(k, row_off, peer).start())
            sum_recv[k, row_off, b] = sum_send[k, row_off]

    def sum_finish(k, out):
        for row_off in range(3):
            bytes_of(sum_rsem.at[k, row_off], sum_recv.at[k, row_off, pl.ds(0, groups - 1)])
            for half in range(2):
                rows = sum_recv[k, row_off, half * per_half : (half + 1) * per_half, 0:part_rows].astype(F32)
                out[row_off * 3 : row_off * 3 + 3, :, half * LANES : (half + 1) * LANES] = rows.reshape(
                    3, own_pad, LANES
                )

    tile_wait(3)
    found = norm_back(3, gain2, norm2, d_res, y_second, gain_second_grad, shift_second_grad)
    for m in range(MICRO):
        spread_columns(grad_x, m, 1, found[m].astype(BF16).astype(F32), extent)
    d_hid[...] = student_back(grad_x, w_second)
    for m in range(MICRO):
        center, inv = norm1[m]
        normal = (y_first[rows_of(m), :] - center) * inv
        grad = d_hid[rows_of(m), :] * gelu_slope(normal * gain1 + shift1)
        d_hid[rows_of(m), :] = grad
        put_sums(5, m, col_sum(grad * normal), col_sum(grad))
    tile_start(5)
    turn(0, [grad_x[m, 1 : extent + 1, :, depth : 2 * depth].astype(F32).reshape(cells, depth) for m in range(MICRO)])
    swaps[0].wait_recv()
    swaps[1].wait_recv()
    kernel_grad(0, hidden_x, hidden_sib)

    tile_wait(5)
    found = norm_back(5, gain1, norm1, d_hid, y_first, gain_first_grad, shift_first_grad)
    turn(1, found)
    for m in range(MICRO):
        spread_columns(grad_x, m, 1, found[m].astype(BF16).astype(F32), extent)
    kernel_grad(1, image_x, image_sib)
    images_grad[...] = (student_back(grad_x, w_first) + d_res[...]).reshape(images_grad.shape)
    line_start(0)

    tile_wait(4)
    totals = [jnp.zeros((LANES, LANES), F32) for _ in range(2)]
    bias_row = jnp.zeros((1, LANES), F32)
    for m in range(MICRO):
        per_image = tile_all[4][:, m * 4 + 2, :]
        bias_row = bias_row + col_sum(per_image)
        for j in range(2):
            totals[j] = totals[j] + lax.dot_general(
                tile_all[4][:, m * 4 + j, :],
                per_image,
                (((0,), (0,)), ((), ())),
                precision=HIGHEST,
                preferred_element_type=F32,
            )
        shown = tile_all[4][pl.ds(b * chans, chans), m * 4 + 3, :]
        logits_out[pl.ds(m, chans, stride=MICRO), :] = shown[:, 0:classes]
    for j in range(2):
        head_sum[j * LANES : (j + 1) * LANES, :] = totals[j]
    head_grad[...] = head_sum[pl.ds(c * own, own), :][:, 0:classes]
    bias_grad[...] = bias_row[:, 0:classes]

    line_start(1)
    sum_start(0)
    sum_start(1)
    sum_finish(0, second_grad)
    sum_finish(1, first_grad)

    for k in range(6):
        tile_drain(k)
    gather_drain(0, w_first.at[pl.ds(0, chans - 1)])
    gather_drain(1, w_second.at[pl.ds(0, chans - 1)])
    plane_drain(0, param_all.at[pl.ds(0, chans - 1)])
    plane_drain(1, head_all.at[pl.ds(0, chans - 1)])
    for copy in swaps:
        copy.wait_send()
    for k in range(2):
        recv = line_recv_second if k == 0 else line_recv_first
        for row_off in range(3):
            bytes_of(part_ssem.at[k, row_off], part_recv.at[k, row_off, pl.ds(0, chips - 1)])
            bytes_of(line_ssem.at[k, row_off], recv.at[row_off, pl.ds(0, groups - 1)])
            bytes_of(sum_ssem.at[k, row_off], sum_recv.at[k, row_off, pl.ds(0, groups - 1)])


def hand_on(*refs):
    count = (len(refs) - 2) // 3
    source, dest, held = refs[:count], refs[count : 2 * count], refs[2 * count : 3 * count]
    in_sem, out_sem = refs[3 * count :]
    loads = [pltpu.make_async_copy(source[i], held[i], in_sem.at[i]) for i in range(count)]
    stores = [pltpu.make_async_copy(held[i], dest[i], out_sem.at[i]) for i in range(count)]
    for load in loads:
        load.start()
    for load, store in zip(loads, stores):
        load.wait()
        store.start()
    for store in stores:
        store.wait()


def shards(
    teacher_images,
    student_images,
    pair_index,
    labels,
    teacher_first,
    teacher_second,
    teacher_head,
    teacher_bias,
    conv_first,
    gain_first,
    shift_first,
    conv_second,
    gain_second,
    shift_second,
    head_weight,
    head_bias,
):
    groups, chans = lax.axis_size("batch"), lax.axis_size("chan")
    devices = groups * chans
    count, extent, _, depth = student_images.shape
    wide = teacher_images.shape[1]
    own = conv_first.shape[3]
    own_pad = max(own, 16)
    own_rows = -(-9 * own // 16) * 16
    classes = head_bias.shape[0]
    cells = extent * extent
    rows = count * cells
    chips = chans // 2
    taps = 3 * own_pad
    part_rows = 2 * taps // groups
    part_pad = -(-part_rows // 16) * 16

    def turned(kernel):
        return jnp.transpose(kernel, (0, 1, 3, 2)).reshape(9 * own, depth)

    def row(vector):
        return vector.reshape(1, -1)

    vmem = pl.BlockSpec(memory_space=pltpu.VMEM)
    smem = pl.BlockSpec(memory_space=pltpu.SMEM)
    hbm = pl.BlockSpec(memory_space=pl.ANY)
    out_shape = [
        jax.ShapeDtypeStruct((chans * count, classes), F32),
        jax.ShapeDtypeStruct(student_images.shape, F32),
        jax.ShapeDtypeStruct((9, own_pad, depth), F32),
        jax.ShapeDtypeStruct((1, own), F32),
        jax.ShapeDtypeStruct((1, own), F32),
        jax.ShapeDtypeStruct((9, own_pad, depth), F32),
        jax.ShapeDtypeStruct((1, own), F32),
        jax.ShapeDtypeStruct((1, own), F32),
        jax.ShapeDtypeStruct((own, classes), F32),
        jax.ShapeDtypeStruct((1, classes), F32),
    ]
    scratch = [
        pltpu.VMEM(teacher_images.shape, BF16),
        pltpu.VMEM((9 * depth, depth), BF16),
        pltpu.VMEM((9 * depth, depth), BF16),
        pltpu.VMEM((1, wide + 2, wide, 3 * depth), BF16),
        pltpu.VMEM((1, wide + 2, wide, 3 * depth), BF16),
        pltpu.VMEM((LANES, depth), F32),
        pltpu.VMEM((count, extent + 2, extent, 3 * depth), BF16),
        pltpu.VMEM((count, extent + 2, extent, 3 * depth), BF16),
        pltpu.VMEM((count, extent + 2, extent, 3 * depth), BF16),
        pltpu.VMEM((chans, own_rows, depth), BF16),
        pltpu.VMEM((chans, own_rows, depth), BF16),
        pltpu.VMEM((own_rows, depth), BF16),
        pltpu.VMEM((own_rows, depth), BF16),
        pltpu.VMEM((rows, depth), F32),
        pltpu.VMEM((rows, depth), F32),
        pltpu.VMEM((rows, depth), F32),
        pltpu.VMEM((rows, depth), F32),
        pltpu.VMEM((count, extent + 2, extent, 3 * depth), BF16),
        pltpu.VMEM((count, extent + 2, extent, 3 * depth), BF16),
        pltpu.VMEM((2, chips, 2, own_pad, rows), BF16),
        pltpu.VMEM((2, chips, own_pad, rows), BF16),
        pltpu.VMEM((chips, taps, depth), F32),
        pltpu.VMEM((2, 3, taps, depth), F32),
        pltpu.VMEM((2, 3, chips, taps, depth), BF16),
        pltpu.VMEM((2, 3, chips, taps, depth), BF16),
        pltpu.VMEM((2, 3, groups, part_pad, LANES), F32),
        pltpu.VMEM((3, groups, part_pad, LANES), BF16),
        pltpu.VMEM((3, groups, part_pad, LANES), BF16),
        pltpu.VMEM((3, groups, part_pad, LANES), F32),
        pltpu.VMEM((2, 3, part_pad, LANES), BF16),
        pltpu.VMEM((2, 3, groups, part_pad, LANES), BF16),
        pltpu.VMEM((8, LANES), F32),
        pltpu.VMEM((chans, 8, LANES), F32),
        pltpu.VMEM((own_pad, LANES), BF16),
        pltpu.VMEM((chans, own_pad, LANES), BF16),
        pltpu.VMEM((6, 8, LANES), F32),
        pltpu.VMEM((devices, 8, LANES), F32),
        pltpu.VMEM((devices, 8, LANES), F32),
        pltpu.VMEM((devices, 8, LANES), F32),
        pltpu.VMEM((devices, 8, LANES), F32),
        pltpu.VMEM((devices, 8, LANES), F32),
        pltpu.VMEM((devices, 8, LANES), F32),
        pltpu.VMEM((depth, LANES), F32),
        pltpu.SemaphoreType.DMA((3,)),
        pltpu.SemaphoreType.DMA((2,)),
        pltpu.SemaphoreType.DMA((2, chans)),
        pltpu.SemaphoreType.DMA((6,)),
        pltpu.SemaphoreType.DMA((6,)),
        pltpu.SemaphoreType.DMA((2,)),
        pltpu.SemaphoreType.DMA((2,)),
        pltpu.SemaphoreType.DMA((4,)),
        pltpu.SemaphoreType.DMA((4,)),
        pltpu.SemaphoreType.DMA((2, 3)),
        pltpu.SemaphoreType.DMA((2, 3)),
        pltpu.SemaphoreType.DMA((2, 3)),
        pltpu.SemaphoreType.DMA((2, 3)),
        pltpu.SemaphoreType.DMA((2, 3)),
        pltpu.SemaphoreType.DMA((2, 3)),
    ]
    found = pl.pallas_call(
        functools.partial(body, (groups, chans, own, own_pad, classes)),
        out_shape=out_shape,
        in_specs=[hbm, vmem, smem, smem, hbm, hbm] + [vmem] * 10,
        out_specs=[vmem] * 10,
        scratch_shapes=scratch,
        compiler_params=pltpu.CompilerParams(
            collective_id=0, has_side_effects=True, vmem_limit_bytes=62 * 2**20
        ),
    )(
        teacher_images,
        student_images,
        pair_index,
        labels,
        teacher_first.reshape(9 * depth, depth),
        teacher_second.reshape(9 * depth, depth),
        teacher_head.T,
        row(teacher_bias),
        turned(conv_first),
        row(gain_first),
        row(shift_first),
        turned(conv_second),
        row(gain_second),
        row(shift_second),
        head_weight,
        row(head_bias),
    )
    found = pl.pallas_call(
        hand_on,
        out_shape=out_shape,
        in_specs=[hbm] * len(out_shape),
        out_specs=[hbm] * len(out_shape),
        scratch_shapes=[pltpu.VMEM(out.shape, out.dtype) for out in out_shape]
        + [pltpu.SemaphoreType.DMA((len(out_shape),))] * 2,
    )(*found)
    logits, images_grad, first, gain1, shift1, second, gain2, shift2, head, bias = found

    def back(grad):
        return jnp.transpose(grad[:, :own].reshape(3, 3, own, depth), (0, 1, 3, 2))

    return (
        logits,
        images_grad,
        back(first),
        gain1.reshape(-1),
        shift1.reshape(-1),
        back(second),
        gain2.reshape(-1),
        shift2.reshape(-1),
        head,
        bias.reshape(-1),
    )


def solution(mesh):
    in_specs = (
        P(("batch", "chan"), None, None, None),
        P(("batch", "chan"), None, None, None),
        P(("batch", "chan")),
        P(("batch", "chan")),
        P(),
        P(),
        P(),
        P(),
        P(None, None, None, "chan"),
        P("chan"),
        P("chan"),
        P(None, None, None, "chan"),
        P("chan"),
        P("chan"),
        P("chan", None),
        P(),
    )
    out_specs = (
        P("batch", None),
        P(("batch", "chan"), None, None, None),
        P(None, None, None, "chan"),
        P("chan"),
        P("chan"),
        P(None, None, None, "chan"),
        P("chan"),
        P("chan"),
        P("chan", None),
        P(),
    )
    return jax.shard_map(shards, mesh=mesh, in_specs=in_specs, out_specs=out_specs, check_vma=False)
```

```python
import functools

import jax
import jax.numpy as jnp
from jax import lax
from jax.experimental import pallas as pl
from jax.experimental.pallas import tpu as pltpu
from jax.sharding import PartitionSpec as P

MESH = pl.DeviceIdType.MESH
F32 = jnp.float32
BF16 = jnp.bfloat16
HIGHEST = lax.Precision.HIGHEST
MICRO = 2
EPS = 1e-05
TARGET_WEIGHT = 1.0
NONTARGET_WEIGHT = 8.0
SOFTEN = 4.0
GELU_A = 0.7978845608028654
GELU_B = 0.044715
LANES = 128


def gelu(x):
    return x * (0.5 + 0.5 * jnp.tanh(GELU_A * (x + GELU_B * (x * x * x))))


def gelu_slope(x):
    square = x * x
    t = jnp.tanh(GELU_A * (x + GELU_B * (x * square)))
    return 0.5 + 0.5 * t + (0.5 * x) * (1.0 - t * t) * (GELU_A + (3.0 * GELU_A * GELU_B) * square)


def column(shape, width):
    return lax.rem(lax.broadcasted_iota(jnp.int32, shape, 0), width)


def spread_columns(dest, lead, top, values, width):
    rows, depth = values.shape
    col = column(values.shape, width)
    left = jnp.where(col == 0, 0.0, pltpu.roll(values, 1, 0))
    right = jnp.where(col == width - 1, 0.0, pltpu.roll(values, rows - 1, 0))
    high = rows // width
    for place, part in enumerate((left, values, right)):
        dest[lead, pl.ds(top, high), :, place * depth : (place + 1) * depth] = part.astype(BF16).reshape(
            high, width, depth
        )


def halves(row):
    return (row[:, :LANES], row[:, LANES:])


def distill_grad(student, teacher, label, classes):
    lane = lax.broadcasted_iota(jnp.int32, student.shape, 1)
    live = lane < classes
    target = lane == label
    other = jnp.logical_and(live, jnp.logical_not(target))
    low = -1e30

    def parts(logits):
        soft = logits / SOFTEN
        whole_top = jnp.max(jnp.where(live, soft, low), axis=1, keepdims=True)
        rest_top = jnp.max(jnp.where(other, soft, low), axis=1, keepdims=True)
        whole_exp = jnp.where(live, jnp.exp(jnp.where(live, soft, whole_top) - whole_top), 0.0)
        rest_exp = jnp.where(other, jnp.exp(jnp.where(other, soft, rest_top) - rest_top), 0.0)
        whole_sum = jnp.sum(whole_exp, axis=1, keepdims=True)
        rest_sum = jnp.sum(rest_exp, axis=1, keepdims=True)
        whole = whole_top + jnp.log(whole_sum)
        rest = rest_top + jnp.log(rest_sum)
        true = jnp.sum(jnp.where(target, soft, 0.0), axis=1, keepdims=True)
        return (whole_exp / whole_sum, rest_exp / rest_sum, true - whole, rest - whole)

    probs, inner, _, _ = parts(student)
    _, inner_t, log_pt, log_rt = parts(teacher)
    p_true, p_rest = jnp.exp(log_pt), jnp.exp(log_rt)
    split_grad = (p_true + p_rest) * probs - jnp.where(target, p_true, 0.0) - p_rest * inner
    inner_grad = jnp.sum(inner_t, axis=1, keepdims=True) * inner - inner_t
    return SOFTEN * (TARGET_WEIGHT * split_grad + NONTARGET_WEIGHT * inner_grad)


def body(
    sizes,
    teacher_hbm,
    images,
    pair_index,
    labels,
    teacher_first_hbm,
    teacher_second_hbm,
    teacher_head,
    teacher_bias,
    first_own,
    gain_first,
    shift_first,
    second_own,
    gain_second,
    shift_second,
    head_own,
    head_bias,
    logits_out,
    images_grad,
    first_grad,
    gain_first_grad,
    shift_first_grad,
    second_grad,
    gain_second_grad,
    shift_second_grad,
    head_grad,
    bias_grad,
    teacher_in,
    teacher_w1,
    teacher_w2,
    teacher_x,
    teacher_h,
    teacher_head_pad,
    image_x,
    hidden_x,
    grad_x,
    w_first,
    w_second,
    own_first,
    own_second,
    y_first,
    y_second,
    slope_first,
    slope_second,
    d_hid,
    image_sib,
    hidden_sib,
    turned,
    turned_sib,
    part_all,
    part_own,
    part_send,
    part_recv,
    line_own,
    line_send,
    line_recv_first,
    line_recv_second,
    sum_send,
    sum_recv,
    param_send,
    param_all,
    head_send,
    head_all,
    wide_send,
    wide_all_0,
    wide_all_1,
    sync_send,
    sync_all_0,
    sync_all_1,
    sync_all_2,
    sync_all_3,
    sync_all_4,
    sync_all_5,
    sync_all_6,
    sync_all_7,
    head_sum,
    local_sem,
    gather_send,
    gather_recv,
    wide_ssem,
    wide_rsem,
    sync_ssem,
    sync_rsem,
    known,
    plane_ssem,
    plane_rsem,
    swap_ssem,
    swap_rsem,
    part_ssem,
    part_rsem,
    line_ssem,
    line_rsem,
    sum_ssem,
    sum_rsem,
):
    groups, chans, own, own_pad, classes = sizes
    wide_all = (wide_all_0, wide_all_1)
    sync_all = (
        sync_all_0,
        sync_all_1,
        sync_all_2,
        sync_all_3,
        sync_all_4,
        sync_all_5,
        sync_all_6,
        sync_all_7,
    )
    b = lax.axis_index("batch")
    c = lax.axis_index("chan")
    me = b * chans + c
    devices = groups * chans
    sibling = c + 1 - 2 * lax.rem(c, 2)
    extent = images.shape[1]
    cells = extent * extent
    depth = images.shape[3]
    wide = teacher_hbm.shape[1]
    samples = float(devices * cells)
    chips = chans // 2
    chip, core = c // 2, lax.rem(c, 2)
    own_rows = own_first.shape[0]

    if groups == 4:
        far_first = [groups - 1 - b, lax.rem(b + 2, groups), b + 1 - 2 * lax.rem(b, 2)]
    else:
        far_first = [lax.rem(b + i, groups) for i in range(1, groups)]

    def each_device(fn):
        for peer_b in far_first + [b]:

            def one(i, carry, peer_b=peer_b):
                fn(peer_b, lax.rem(c + (chans - i), chans))
                return carry

            lax.fori_loop(1 if peer_b is b else 0, chans, one, 0, unroll=chans <= 8)

    def each_chip(fn):
        def one(i, carry):
            fn(lax.rem(chip + i, chips))
            return carry

        lax.fori_loop(1, chips, one, 0, unroll=chips <= 4)

    def each_line(fn):
        for peer_b in far_first:
            fn(peer_b)

    def signal(sem, peer_b, peer_c):
        pl.semaphore_signal(sem, inc=1, device_id=(peer_b, peer_c), device_id_type=MESH)

    def each_plane(fn):
        def one(i, carry):
            fn(lax.rem(c + i, chans))
            return carry

        lax.fori_loop(1, chans, one, 0, unroll=chans <= 8)

    barrier = pltpu.get_barrier_semaphore()
    each_line(lambda pb: signal(barrier, pb, c))
    each_chip(lambda peer: signal(barrier, b, 2 * peer + core))
    signal(barrier, b, sibling)

    loads = [
        pltpu.make_async_copy(teacher_hbm, teacher_in, local_sem.at[0]),
        pltpu.make_async_copy(teacher_first_hbm, teacher_w1, local_sem.at[1]),
        pltpu.make_async_copy(teacher_second_hbm, teacher_w2, local_sem.at[2]),
    ]
    for load in loads:
        load.start()

    def place_own(param_row):
        at = c * own
        lane0 = lax.rem(at, LANES)
        padded = jnp.concatenate([param_row, jnp.zeros((1, LANES - own), F32)], axis=1)
        moved = pltpu.roll(jnp.broadcast_to(padded, (8, LANES)), lane0, 1)[0:1]
        upper = at >= LANES
        return (jnp.where(upper, 0.0, moved), jnp.where(upper, moved, 0.0))

    for i, ref in enumerate((gain_first, shift_first, gain_second, shift_second)):
        low_half, high_half = place_own(ref[...])
        param_send[2 * i : 2 * i + 1, :] = low_half
        param_send[2 * i + 1 : 2 * i + 2, :] = high_half
    head_send[...] = jnp.zeros(head_send.shape, BF16)
    head_send[0:own, 0:classes] = head_own[...]
    for src, dst in ((first_own, own_first), (second_own, own_second)):
        if own_rows != 9 * own:
            dst[...] = jnp.zeros(dst.shape, BF16)
        dst[0 : 9 * own, :] = src[...]

    for ref in (image_x, hidden_x, grad_x, teacher_x, teacher_h):
        high = ref.shape[1]
        for lead in range(ref.shape[0]):
            ref[lead, 0] = jnp.zeros(ref.shape[2:], BF16)
            ref[lead, high - 1] = jnp.zeros(ref.shape[2:], BF16)
    for lead in range(MICRO):
        spread_columns(image_x, lead, 1, images[lead].astype(F32).reshape(cells, depth), extent)

    t_high = 16
    t_steps = wide // t_high
    t_rows = t_high * wide

    def teacher_conv(source, kernel, top):
        total = None
        for row_off in range(3):
            window = source[0, pl.ds(top + row_off, t_high)].reshape(t_rows, 3 * depth)
            term = jnp.dot(
                window, kernel[row_off * 3 * depth : (row_off + 1) * 3 * depth, :], preferred_element_type=F32
            )
            total = term if total is None else total + term
        return total

    def teacher_fill(lead):
        def fill(i, carry):
            top = i * t_high
            values = teacher_in[lead, pl.ds(top, t_high)].astype(F32).reshape(t_rows, depth)
            spread_columns(teacher_x, 0, top + 1, values, wide)
            return carry

        lax.fori_loop(0, t_steps, fill, 0)

    def teacher_one():
        def one(i, carry):
            top = i * t_high
            spread_columns(teacher_h, 0, top + 1, gelu(teacher_conv(teacher_x, teacher_w1, top)), wide)
            return carry

        lax.fori_loop(0, t_steps, one, 0)

    def teacher_two(lead):
        def two(i, total):
            top = i * t_high
            values = teacher_in[lead, pl.ds(top, t_high)].astype(F32).reshape(t_rows, depth)
            act = gelu(teacher_conv(teacher_h, teacher_w2, top) + values)
            return total + jnp.sum(act, axis=0, keepdims=True)

        return lax.fori_loop(0, t_steps, two, jnp.zeros((1, depth), F32))

    loads[0].wait()
    teacher_fill(0)
    loads[1].wait()
    teacher_one()

    pl.semaphore_wait(barrier, groups - 1 + chips - 1 + 1)
    signal(known.at[0], b, sibling)

    pieces = 3 if 3 * own % 16 == 0 else 1
    piece_rows = own_rows // pieces
    held = (w_first, w_second)
    offered = (own_first, own_second)

    def gather_copy(k, piece, shard, target, source=None):
        rows = pl.ds(piece * piece_rows, piece_rows)
        slot = held[k].at[shard, rows]
        return pltpu.make_async_remote_copy(
            src_ref=slot if source is None else source.at[rows],
            dst_ref=slot,
            send_sem=gather_send.at[k],
            recv_sem=gather_recv.at[k, piece, shard],
            device_id=(b, target),
            device_id_type=MESH,
        )

    def gather_start(k):
        for piece in range(pieces):
            each_chip(lambda peer, piece=piece: gather_copy(k, piece, c, 2 * peer + core, offered[k]).start())
            gather_copy(k, piece, c, sibling, offered[k]).start()
        held[k][c] = offered[k][...]

    def gather_forward(k, piece):
        def one(peer):
            shard = 2 * peer + core
            gather_copy(k, piece, shard, sibling).wait_recv()
            gather_copy(k, piece, shard, sibling).start()

        each_chip(one)

    def gather_finish(k, piece):
        def one(i, carry):
            gather_copy(k, piece, 2 * lax.rem(chip + i, chips) + 1 - core, sibling).wait_recv()
            return carry

        lax.fori_loop(0, chips, one, 0, unroll=chips <= 4)

    def bytes_of(sem, many):
        pltpu.make_async_copy(many, many, sem).wait()

    def swap(k, source, dest):
        return pltpu.make_async_remote_copy(
            src_ref=source,
            dst_ref=dest,
            send_sem=swap_ssem.at[k],
            recv_sem=swap_rsem.at[k],
            device_id=(b, sibling),
            device_id_type=MESH,
        )

    def tile_start(send, recv, ssem, rsem):
        def one(pb, pc):
            pltpu.make_async_remote_copy(
                src_ref=send, dst_ref=recv.at[me], send_sem=ssem, recv_sem=rsem, device_id=(pb, pc), device_id_type=MESH
            ).start()

        each_device(one)
        recv[me] = send[...]

    def tile_bytes(sem, recv):
        bytes_of(sem, recv.at[pl.ds(0, devices - 1)])

    def wide_start(k):
        tile_start(wide_send.at[k], wide_all[k], wide_ssem.at[k], wide_rsem.at[k])

    def wide_wait(k):
        tile_bytes(wide_rsem.at[k], wide_all[k])

    def sync_start(stage, micro, rows):
        k = stage * MICRO + micro
        for i, row in enumerate(rows):
            for j, half in enumerate(halves(row)):
                sync_send[k, 2 * i + j : 2 * i + j + 1, :] = half
        tile_start(sync_send.at[k], sync_all[k], sync_ssem.at[k], sync_rsem.at[k])

    def sync_wait(stage, micro):
        k = stage * MICRO + micro
        tile_bytes(sync_rsem.at[k], sync_all[k])
        total = jnp.sum(sync_all[k][...], axis=0)
        return [jnp.concatenate([total[2 * i : 2 * i + 1], total[2 * i + 1 : 2 * i + 2]], axis=1) for i in range(2)]

    def plane_start(k, source, slot):
        def one(pc):
            pltpu.make_async_remote_copy(
                src_ref=source(pc),
                dst_ref=slot(c),
                send_sem=plane_ssem.at[k],
                recv_sem=plane_rsem.at[k],
                device_id=(b, pc),
                device_id_type=MESH,
            ).start()

        each_plane(one)

    def plane_wait(k, many):
        pltpu.make_async_copy(many, many, plane_rsem.at[k]).wait()

    def plane_drain(k, many):
        pltpu.make_async_copy(many, many, plane_ssem.at[k]).wait()

    gather_start(0)
    swaps = [swap(0, image_x, image_sib)]
    swaps[0].start()
    loads[2].wait()
    teacher_rows = [teacher_two(0)]

    pl.semaphore_wait(known.at[0], 1)
    each_line(lambda pb: signal(known.at[1], pb, c))
    plane_start(0, lambda pc: param_send, lambda s: param_all.at[s])
    plane_start(1, lambda pc: head_send, lambda s: head_all.at[s])
    param_all[c] = param_send[...]
    head_all[c] = head_send[...]

    teacher_fill(1)
    teacher_one()
    teacher_rows.append(teacher_two(1))
    which_t = lax.broadcasted_iota(jnp.int32, (8, depth), 0)
    pooled_t = jnp.zeros((8, depth), F32)
    for m in range(MICRO):
        pooled_t = jnp.where(which_t == m, teacher_rows[m] / float(wide * wide), pooled_t)
    teacher_head_pad[...] = jnp.zeros(teacher_head_pad.shape, F32)
    teacher_head_pad[0:classes, :] = teacher_head[...].astype(F32)
    teacher_logits = lax.dot_general(
        pooled_t, teacher_head_pad[...], (((1,), (1,)), ((), ())), precision=HIGHEST, preferred_element_type=F32
    )
    lane_pad = jnp.zeros((1, LANES - classes), F32)
    wide_send[0] = teacher_logits + jnp.concatenate([teacher_bias[...], lane_pad], axis=1)
    pl.semaphore_wait(known.at[1], groups - 1)
    wide_start(0)
    gather_start(1)

    def picker(shard, block, offset):
        at_row = lax.broadcasted_iota(jnp.int32, (depth, block), 0)
        place = lax.broadcasted_iota(jnp.int32, (depth, block), 1) - offset
        wanted = jnp.logical_and(place >= 0, place < own)
        return jnp.logical_and(wanted, at_row == shard * own + place).astype(BF16)

    def unpack(ref, block, offset):
        def one(shard, total):
            return total + jnp.dot(picker(shard, block, offset), ref[shard], preferred_element_type=F32)

        return lax.fori_loop(0, chans, one, jnp.zeros((depth, ref.shape[2]), F32)).astype(BF16)

    def weights(ref, tap):
        if own_pad == own:
            return ref[:, tap * own : (tap + 1) * own, :].reshape(depth, depth)
        return unpack(ref, own_rows, tap * own)

    def window(source, micro, row_off, col_off):
        return source[micro, row_off : row_off + extent, :, col_off * depth : (col_off + 1) * depth].reshape(
            cells, depth
        )

    def student_conv(source, micro, ref, row_offs):
        total = None
        for row_off in row_offs:
            for col_off in range(3):
                term = lax.dot_general(
                    window(source, micro, row_off, col_off),
                    weights(ref, row_off * 3 + col_off),
                    (((1,), (1,)), ((), ())),
                    preferred_element_type=F32,
                )
                total = term if total is None else total + term
        return total

    def student_back(source, micro, ref):
        total = None
        for row_off in range(3):
            for col_off in range(3):
                term = jnp.dot(
                    window(source, micro, row_off, col_off),
                    weights(ref, (2 - row_off) * 3 + 2 - col_off),
                    preferred_element_type=F32,
                )
                total = term if total is None else total + term
        return total

    def rows_of(m):
        return slice(m * cells, (m + 1) * cells)

    def col_sum(values):
        return jnp.sum(values, axis=0, keepdims=True)

    def moments_start(stage, m, values):
        sync_start(stage, m, (col_sum(values), col_sum(values * values)))

    def moments(stage, m):
        total, square = sync_wait(stage, m)
        center = total / samples
        spread = square / samples - center * center
        return (center, lax.rsqrt(spread + EPS))

    if pieces == 3:
        gather_forward(0, 0)
        gather_forward(0, 1)
        gather_finish(0, 0)
        for m in range(MICRO):
            y_first[rows_of(m), :] = student_conv(image_x, m, w_first, (0,))
        gather_forward(0, 2)
        gather_finish(0, 1)
        for m in range(MICRO):
            y_first[rows_of(m), :] += student_conv(image_x, m, w_first, (1,))
        gather_finish(0, 2)
        for m in range(MICRO):
            values = y_first[rows_of(m), :] + student_conv(image_x, m, w_first, (2,))
            y_first[rows_of(m), :] = values
            moments_start(0, m, values)
    else:
        gather_forward(0, 0)
        gather_finish(0, 0)
        for m in range(MICRO):
            values = student_conv(image_x, m, w_first, range(3))
            y_first[rows_of(m), :] = values
            moments_start(0, m, values)

    plane_wait(0, param_all.at[pl.ds(0, chans - 1)])
    plane_wait(1, head_all.at[pl.ds(0, chans - 1)])
    params = jnp.sum(param_all[...], axis=0)
    gain1, shift1, gain2, shift2 = (
        jnp.concatenate([params[2 * i : 2 * i + 1], params[2 * i + 1 : 2 * i + 2]], axis=1) for i in range(4)
    )
    if own_pad == own:
        head = head_all[...].reshape(depth, LANES)
    else:
        head = unpack(head_all, own_pad, 0)
    for piece in range(pieces):
        gather_forward(1, piece)
    for piece in range(pieces):
        gather_finish(1, piece)

    def three_parts(values):
        first = values.astype(BF16)
        rest = values - first.astype(F32)
        second = rest.astype(BF16)
        third = (rest - second.astype(F32)).astype(BF16)
        return jnp.concatenate([first, second, third], axis=0)

    def sum_parts(product):
        return product[0:8] + product[8:16] + product[16:24]

    norm1 = []
    for m in range(MICRO):
        center, inv = moments(0, m)
        norm1.append((center, inv))
        normed = (y_first[rows_of(m), :] - center) * (inv * gain1) + shift1
        spread_columns(hidden_x, m, 1, gelu(normed), extent)
        values = student_conv(hidden_x, m, w_second, range(3))
        y_second[rows_of(m), :] = values
        moments_start(1, m, values)
    swaps.append(swap(1, hidden_x, hidden_sib))
    swaps[1].start()
    for m in range(MICRO):
        center, inv = norm1[m]
        slope_first[rows_of(m), :] = gelu_slope((y_first[rows_of(m), :] - center) * (inv * gain1) + shift1)

    per_device = pair_index.shape[0]
    norm2, slope_scale = [], []
    which = lax.broadcasted_iota(jnp.int32, (8, depth), 0)
    which_lane = lax.broadcasted_iota(jnp.int32, (8, LANES), 0)
    for m in range(MICRO):
        center, inv = moments(1, m)
        norm2.append((center, inv))
        spread = y_second[rows_of(m), :] - center
        res = spread * (inv * gain2) + shift2 + images[m].astype(F32).reshape(cells, depth)
        square = res * res
        t = jnp.tanh(GELU_A * (res + GELU_B * (res * square)))
        half = 0.5 + 0.5 * t
        slope = half + (0.5 * res) * (1.0 - t * t) * (GELU_A + (3.0 * GELU_A * GELU_B) * square)
        slope_second[rows_of(m), :] = slope
        pooled = col_sum(res * half) / float(cells)
        slope_sum = col_sum(slope)
        slope_dot = col_sum(slope * spread) * inv
        product = jnp.dot(
            three_parts(jnp.where(which == 0, pooled, 0.0)), head, preferred_element_type=F32
        )
        logits = sum_parts(product)[0:1] + jnp.concatenate([head_bias[...], lane_pad], axis=1)
        if m == 0:
            wide_wait(0)
        paired = pair_index[m]
        teacher_row = wide_all[0][pl.ds(paired // per_device, 1), pl.ds(lax.rem(paired, per_device), 1), :].reshape(1, LANES)
        grad = distill_grad(logits, teacher_row, labels[m], classes)
        product = lax.dot_general(
            three_parts(jnp.where(which_lane == 0, grad, 0.0)),
            head,
            (((1,), (1,)), ((), ())),
            preferred_element_type=F32,
        )
        scale = sum_parts(product)[0:1] / float(cells)
        slope_scale.append(scale)
        sync_start(2, m, (scale * slope_dot, scale * slope_sum))
        for j, part in enumerate(halves(pooled)):
            wide_send[1, m * 4 + j : m * 4 + j + 1, :] = part
        wide_send[1, m * 4 + 2 : m * 4 + 3, :] = grad
        wide_send[1, m * 4 + 3 : m * 4 + 4, :] = logits
    wide_start(1)

    def own_lanes(low_row, high_row):
        at = c * own
        row = jnp.where(at >= LANES, high_row, low_row)
        turn = lax.rem(LANES - lax.rem(at, LANES), LANES)
        return pltpu.roll(jnp.broadcast_to(row, (8, LANES)), turn, 1)[0:1, 0:own]

    def norm_back(stage, m, gain, norm, grad, y_ref):
        center, inv = norm
        totals = sync_wait(stage, m)
        scale = gain * inv
        slant = scale * inv * (totals[0] / samples)
        level = scale * (totals[1] / samples)
        return (grad * scale - (y_ref[rows_of(m), :] - center) * slant - level, totals)

    def norm_out(totals, gain_out, shift_out):
        for out, i in ((gain_out, 0), (shift_out, 1)):
            row = totals[0][i]
            for m in range(1, MICRO):
                row = row + totals[m][i]
            out[...] = own_lanes(*halves(row))

    def turn(k, found):
        whole = jnp.concatenate([jnp.transpose(part) for part in found], axis=1).astype(BF16)
        if own_pad == own:
            turned[k] = whole.reshape(chips, 2, own, MICRO * cells)
        else:

            def one(shard, carry):
                turned[k, shard // 2, lax.rem(shard, 2)] = lax.dot_general(
                    picker(shard, own_pad, 0), whole, (((0,), (0,)), ((), ())), preferred_element_type=F32
                ).astype(BF16)
                return carry

            lax.fori_loop(0, chans, one, 0)
        swaps.append(swap(2 + k, turned.at[k, :, 1 - core], turned_sib.at[k]))
        swaps[-1].start()

    taps = 3 * own_pad

    def part_copy(k, row_off, peer_chip):
        return pltpu.make_async_remote_copy(
            src_ref=part_send.at[k, row_off, peer_chip],
            dst_ref=part_recv.at[k, row_off, chip],
            send_sem=part_ssem.at[k, row_off],
            recv_sem=part_rsem.at[k, row_off],
            device_id=(b, 2 * peer_chip + core),
            device_id_type=MESH,
        )

    def kernel_grad(k, source, source_sib):
        count = MICRO * cells
        mine = turned[k, :, pl.ds(core, 1)].reshape(chips * own_pad, count)
        theirs = None
        for row_off in range(3):
            total = jnp.dot(
                mine,
                source[:, row_off : row_off + extent].reshape(count, 3 * depth),
                preferred_element_type=F32,
            )
            if theirs is None:
                swaps[2 + k].wait_recv()
                theirs = turned_sib[k].reshape(chips * own_pad, count)
            total = total + jnp.dot(
                theirs,
                source_sib[:, row_off : row_off + extent].reshape(count, 3 * depth),
                preferred_element_type=F32,
            )
            for i in range(chips):
                for col_off in range(3):
                    part_all[i, col_off * own_pad : (col_off + 1) * own_pad, :] = total[
                        i * own_pad : (i + 1) * own_pad, col_off * depth : (col_off + 1) * depth
                    ]
            part_send[k, row_off] = part_all[...].astype(BF16)
            part_own[k, row_off] = part_all[pl.ds(chip, 1)].reshape(taps, depth)
            each_chip(lambda peer, row_off=row_off: part_copy(k, row_off, peer).start())
            part_recv[k, row_off, chip] = jnp.zeros((taps, depth), BF16)

    per_half = groups // 2
    part_rows = taps // per_half
    part_pad = sum_send.shape[2]

    def line_copy(k, row_off, peer):
        if k == 0:
            source, dest = line_own.at[k, row_off, peer], line_recv_second.at[row_off, b]
        else:
            source, dest = line_send.at[row_off, peer], line_recv_first.at[row_off, b]
        return pltpu.make_async_remote_copy(
            src_ref=source,
            dst_ref=dest,
            send_sem=line_ssem.at[k, row_off],
            recv_sem=line_rsem.at[k, row_off],
            device_id=(peer, c),
            device_id_type=MESH,
        )

    def sum_copy(k, row_off, peer):
        return pltpu.make_async_remote_copy(
            src_ref=sum_send.at[k, row_off],
            dst_ref=sum_recv.at[k, row_off, b],
            send_sem=sum_ssem.at[k, row_off],
            recv_sem=sum_rsem.at[k, row_off],
            device_id=(peer, c),
            device_id_type=MESH,
        )

    def line_start(k):
        recv = line_recv_second if k == 0 else line_recv_first
        for row_off in range(3):
            bytes_of(part_rsem.at[k, row_off], part_recv.at[k, row_off, pl.ds(0, chips - 1)])
            total = part_own[k, row_off] + jnp.sum(
                part_recv[k, row_off].astype(F32), axis=0
            )
            for p in range(groups):
                half, row = p // per_half, (p % per_half) * part_rows
                line_own[k, row_off, p, 0:part_rows] = total[
                    row : row + part_rows, half * LANES : (half + 1) * LANES
                ]
                if part_pad != part_rows:
                    line_own[k, row_off, p, part_rows:part_pad] = jnp.zeros((part_pad - part_rows, LANES), F32)
            if k == 1:
                line_send[row_off] = line_own[k, row_off].astype(BF16)
            each_line(lambda peer, row_off=row_off: line_copy(k, row_off, peer).start())
            recv[row_off, b] = jnp.zeros((part_pad, LANES), recv.dtype)

    def sum_start(k):
        recv = line_recv_second if k == 0 else line_recv_first
        for row_off in range(3):
            bytes_of(line_rsem.at[k, row_off], recv.at[row_off, pl.ds(0, groups - 1)])
            total = line_own[k, row_off, pl.ds(b, 1)].reshape(part_pad, LANES) + jnp.sum(
                recv[row_off].astype(F32), axis=0
            )
            sum_send[k, row_off] = total.astype(BF16)
            each_line(lambda peer, row_off=row_off: sum_copy(k, row_off, peer).start())
            sum_recv[k, row_off, b] = sum_send[k, row_off]

    def sum_finish(k, out):
        for row_off in range(3):
            bytes_of(sum_rsem.at[k, row_off], sum_recv.at[k, row_off, pl.ds(0, groups - 1)])
            for half in range(2):
                rows = sum_recv[k, row_off, half * per_half : (half + 1) * per_half, 0:part_rows].astype(F32)
                out[row_off * 3 : row_off * 3 + 3, :, half * LANES : (half + 1) * LANES] = rows.reshape(
                    3, own_pad, LANES
                )

    totals2 = []
    for m in range(MICRO):
        found, totals = norm_back(2, m, gain2, norm2[m], slope_second[rows_of(m), :] * slope_scale[m], y_second)
        totals2.append(totals)
        spread_columns(grad_x, m, 1, found, extent)
        grad = student_back(grad_x, m, w_second) * slope_first[rows_of(m), :]
        d_hid[rows_of(m), :] = grad
        center, inv = norm1[m]
        sync_start(3, m, (col_sum(grad * (y_first[rows_of(m), :] - center)) * inv, col_sum(grad)))
    turn(0, [grad_x[m, 1 : extent + 1, :, depth : 2 * depth].astype(F32).reshape(cells, depth) for m in range(MICRO)])
    norm_out(totals2, gain_second_grad, shift_second_grad)
    swaps[0].wait_recv()
    swaps[1].wait_recv()
    kernel_grad(0, hidden_x, hidden_sib)

    found, totals1 = [], []
    for m in range(MICRO):
        one, totals = norm_back(3, m, gain1, norm1[m], d_hid[rows_of(m), :], y_first)
        found.append(one)
        totals1.append(totals)
        spread_columns(grad_x, m, 1, one, extent)
    turn(1, found)
    kernel_grad(1, image_x, image_sib)
    for m in range(MICRO):
        images_grad[m] = (
            student_back(grad_x, m, w_first) + slope_second[rows_of(m), :] * slope_scale[m]
        ).reshape(images_grad.shape[1:])
    norm_out(totals1, gain_first_grad, shift_first_grad)
    line_start(0)

    wide_wait(1)
    totals = [jnp.zeros((LANES, LANES), F32) for _ in range(2)]
    bias_row = jnp.zeros((1, LANES), F32)
    for m in range(MICRO):
        per_image = wide_all[1][:, m * 4 + 2, :]
        bias_row = bias_row + col_sum(per_image)
        for j in range(2):
            totals[j] = totals[j] + lax.dot_general(
                wide_all[1][:, m * 4 + j, :],
                per_image,
                (((0,), (0,)), ((), ())),
                precision=HIGHEST,
                preferred_element_type=F32,
            )
        shown = wide_all[1][pl.ds(b * chans, chans), m * 4 + 3, :]
        logits_out[pl.ds(m, chans, stride=MICRO), :] = shown[:, 0:classes]
    for j in range(2):
        head_sum[j * LANES : (j + 1) * LANES, :] = totals[j]
    head_grad[...] = head_sum[pl.ds(c * own, own), :][:, 0:classes]
    bias_grad[...] = bias_row[:, 0:classes]

    line_start(1)
    sum_start(0)
    sum_start(1)
    sum_finish(0, second_grad)
    sum_finish(1, first_grad)

    for k in range(2):
        tile_bytes(wide_ssem.at[k], wide_all[k])
        bytes_of(gather_send.at[k], held[k].at[pl.ds(0, chans - 1)])
    for k in range(4 * MICRO):
        tile_bytes(sync_ssem.at[k], sync_all[k])
    plane_drain(0, param_all.at[pl.ds(0, chans - 1)])
    plane_drain(1, head_all.at[pl.ds(0, chans - 1)])
    for copy in swaps:
        copy.wait_send()
    for k in range(2):
        recv = line_recv_second if k == 0 else line_recv_first
        for row_off in range(3):
            bytes_of(part_ssem.at[k, row_off], part_recv.at[k, row_off, pl.ds(0, chips - 1)])
            bytes_of(line_ssem.at[k, row_off], recv.at[row_off, pl.ds(0, groups - 1)])
            bytes_of(sum_ssem.at[k, row_off], sum_recv.at[k, row_off, pl.ds(0, groups - 1)])


def hand_on(*refs):
    count = len(refs) // 2
    copies = [pltpu.make_async_copy(refs[i], refs[count + i], refs[-1].at[i]) for i in range(count)]
    for copy in copies:
        copy.start()
    for copy in copies:
        copy.wait()


def shards(
    teacher_images,
    student_images,
    pair_index,
    labels,
    teacher_first,
    teacher_second,
    teacher_head,
    teacher_bias,
    conv_first,
    gain_first,
    shift_first,
    conv_second,
    gain_second,
    shift_second,
    head_weight,
    head_bias,
):
    groups, chans = lax.axis_size("batch"), lax.axis_size("chan")
    devices = groups * chans
    count, extent, _, depth = student_images.shape
    wide = teacher_images.shape[1]
    own = conv_first.shape[3]
    own_pad = max(own, 16)
    own_rows = -(-9 * own // 16) * 16
    classes = head_bias.shape[0]
    cells = extent * extent
    rows = count * cells
    chips = chans // 2
    taps = 3 * own_pad
    part_rows = 2 * taps // groups
    part_pad = -(-part_rows // 16) * 16

    def turned(kernel):
        return jnp.transpose(kernel, (0, 1, 3, 2)).reshape(9 * own, depth)

    def row(vector):
        return vector.reshape(1, -1)

    vmem = pl.BlockSpec(memory_space=pltpu.VMEM)
    smem = pl.BlockSpec(memory_space=pltpu.SMEM)
    hbm = pl.BlockSpec(memory_space=pl.ANY)
    out_shape = [
        jax.ShapeDtypeStruct((chans * count, classes), F32),
        jax.ShapeDtypeStruct(student_images.shape, F32),
        jax.ShapeDtypeStruct((9, own_pad, depth), F32),
        jax.ShapeDtypeStruct((1, own), F32),
        jax.ShapeDtypeStruct((1, own), F32),
        jax.ShapeDtypeStruct((9, own_pad, depth), F32),
        jax.ShapeDtypeStruct((1, own), F32),
        jax.ShapeDtypeStruct((1, own), F32),
        jax.ShapeDtypeStruct((own, classes), F32),
        jax.ShapeDtypeStruct((1, classes), F32),
    ]
    scratch = [
        pltpu.VMEM(teacher_images.shape, BF16),
        pltpu.VMEM((9 * depth, depth), BF16),
        pltpu.VMEM((9 * depth, depth), BF16),
        pltpu.VMEM((1, wide + 2, wide, 3 * depth), BF16),
        pltpu.VMEM((1, wide + 2, wide, 3 * depth), BF16),
        pltpu.VMEM((LANES, depth), F32),
        pltpu.VMEM((count, extent + 2, extent, 3 * depth), BF16),
        pltpu.VMEM((count, extent + 2, extent, 3 * depth), BF16),
        pltpu.VMEM((count, extent + 2, extent, 3 * depth), BF16),
        pltpu.VMEM((chans, own_rows, depth), BF16),
        pltpu.VMEM((chans, own_rows, depth), BF16),
        pltpu.VMEM((own_rows, depth), BF16),
        pltpu.VMEM((own_rows, depth), BF16),
        pltpu.VMEM((rows, depth), F32),
        pltpu.VMEM((rows, depth), F32),
        pltpu.VMEM((rows, depth), F32),
        pltpu.VMEM((rows, depth), F32),
        pltpu.VMEM((rows, depth), F32),
        pltpu.VMEM((count, extent + 2, extent, 3 * depth), BF16),
        pltpu.VMEM((count, extent + 2, extent, 3 * depth), BF16),
        pltpu.VMEM((2, chips, 2, own_pad, rows), BF16),
        pltpu.VMEM((2, chips, own_pad, rows), BF16),
        pltpu.VMEM((chips, taps, depth), F32),
        pltpu.VMEM((2, 3, taps, depth), F32),
        pltpu.VMEM((2, 3, chips, taps, depth), BF16),
        pltpu.VMEM((2, 3, chips, taps, depth), BF16),
        pltpu.VMEM((2, 3, groups, part_pad, LANES), F32),
        pltpu.VMEM((3, groups, part_pad, LANES), BF16),
        pltpu.VMEM((3, groups, part_pad, LANES), BF16),
        pltpu.VMEM((3, groups, part_pad, LANES), F32),
        pltpu.VMEM((2, 3, part_pad, LANES), BF16),
        pltpu.VMEM((2, 3, groups, part_pad, LANES), BF16),
        pltpu.VMEM((8, LANES), F32),
        pltpu.VMEM((chans, 8, LANES), F32),
        pltpu.VMEM((own_pad, LANES), BF16),
        pltpu.VMEM((chans, own_pad, LANES), BF16),
        pltpu.VMEM((2, 8, LANES), F32),
        pltpu.VMEM((devices, 8, LANES), F32),
        pltpu.VMEM((devices, 8, LANES), F32),
        pltpu.VMEM((4 * MICRO, 4, LANES), F32),
        pltpu.VMEM((devices, 4, LANES), F32),
        pltpu.VMEM((devices, 4, LANES), F32),
        pltpu.VMEM((devices, 4, LANES), F32),
        pltpu.VMEM((devices, 4, LANES), F32),
        pltpu.VMEM((devices, 4, LANES), F32),
        pltpu.VMEM((devices, 4, LANES), F32),
        pltpu.VMEM((devices, 4, LANES), F32),
        pltpu.VMEM((devices, 4, LANES), F32),
        pltpu.VMEM((depth, LANES), F32),
        pltpu.SemaphoreType.DMA((3,)),
        pltpu.SemaphoreType.DMA((2,)),
        pltpu.SemaphoreType.DMA((2, 3, chans)),
        pltpu.SemaphoreType.DMA((2,)),
        pltpu.SemaphoreType.DMA((2,)),
        pltpu.SemaphoreType.DMA((4 * MICRO,)),
        pltpu.SemaphoreType.DMA((4 * MICRO,)),
        pltpu.SemaphoreType.REGULAR((2,)),
        pltpu.SemaphoreType.DMA((2,)),
        pltpu.SemaphoreType.DMA((2,)),
        pltpu.SemaphoreType.DMA((4,)),
        pltpu.SemaphoreType.DMA((4,)),
        pltpu.SemaphoreType.DMA((2, 3)),
        pltpu.SemaphoreType.DMA((2, 3)),
        pltpu.SemaphoreType.DMA((2, 3)),
        pltpu.SemaphoreType.DMA((2, 3)),
        pltpu.SemaphoreType.DMA((2, 3)),
        pltpu.SemaphoreType.DMA((2, 3)),
    ]
    found = pl.pallas_call(
        functools.partial(body, (groups, chans, own, own_pad, classes)),
        out_shape=[pltpu.VMEM(out.shape, out.dtype) for out in out_shape],
        in_specs=[hbm, vmem, smem, smem, hbm, hbm] + [vmem] * 10,
        out_specs=[vmem] * 10,
        scratch_shapes=scratch,
        compiler_params=pltpu.CompilerParams(
            collective_id=0, has_side_effects=True, vmem_limit_bytes=62 * 2**20
        ),
    )(
        teacher_images,
        student_images,
        pair_index,
        labels,
        teacher_first.reshape(9 * depth, depth),
        teacher_second.reshape(9 * depth, depth),
        teacher_head.T,
        row(teacher_bias),
        turned(conv_first),
        row(gain_first),
        row(shift_first),
        turned(conv_second),
        row(gain_second),
        row(shift_second),
        head_weight,
        row(head_bias),
    )
    found = pl.pallas_call(
        hand_on,
        out_shape=out_shape,
        in_specs=[vmem] * len(out_shape),
        out_specs=[hbm] * len(out_shape),
        scratch_shapes=[pltpu.SemaphoreType.DMA((len(out_shape),))],
    )(*[pltpu.with_memory_space_constraint(x, pltpu.VMEM) for x in found])
    logits, images_grad, first, gain1, shift1, second, gain2, shift2, head, bias = found

    def back(grad):
        return jnp.transpose(grad[:, :own].reshape(3, 3, own, depth), (0, 1, 3, 2))

    return (
        logits,
        images_grad,
        back(first),
        gain1.reshape(-1),
        shift1.reshape(-1),
        back(second),
        gain2.reshape(-1),
        shift2.reshape(-1),
        head,
        bias.reshape(-1),
    )


def solution(mesh):
    in_specs = (
        P(("batch", "chan"), None, None, None),
        P(("batch", "chan"), None, None, None),
        P(("batch", "chan")),
        P(("batch", "chan")),
        P(),
        P(),
        P(),
        P(),
        P(None, None, None, "chan"),
        P("chan"),
        P("chan"),
        P(None, None, None, "chan"),
        P("chan"),
        P("chan"),
        P("chan", None),
        P(),
    )
    out_specs = (
        P("batch", None),
        P(("batch", "chan"), None, None, None),
        P(None, None, None, "chan"),
        P("chan"),
        P("chan"),
        P(None, None, None, "chan"),
        P("chan"),
        P("chan"),
        P("chan", None),
        P(),
    )
    return jax.shard_map(shards, mesh=mesh, in_specs=in_specs, out_specs=out_specs, check_vma=False)
```

```python
import functools

import jax
import jax.numpy as jnp
from jax import lax
from jax.experimental import pallas as pl
from jax.experimental.pallas import tpu as pltpu
from jax.sharding import PartitionSpec as P

MESH = pl.DeviceIdType.MESH
F32 = jnp.float32
BF16 = jnp.bfloat16
HIGHEST = lax.Precision.HIGHEST
MICRO = 2
EPS = 1e-05
TARGET_WEIGHT = 1.0
NONTARGET_WEIGHT = 8.0
SOFTEN = 4.0
GELU_A = 0.7978845608028654
GELU_B = 0.044715
LANES = 128
QUADRATURE = (
    (0.0, 0.5333333333),
    (1.3556261800, 0.2220759220),
    (-1.3556261800, 0.2220759220),
    (2.8569700139, 0.0112574113),
    (-2.8569700139, 0.0112574113),
)


def gelu(x):
    return x * (0.5 + 0.5 * jnp.tanh(GELU_A * (x + GELU_B * (x * x * x))))


def gelu_slope(x):
    square = x * x
    t = jnp.tanh(GELU_A * (x + GELU_B * (x * square)))
    return 0.5 + 0.5 * t + (0.5 * x) * (1.0 - t * t) * (GELU_A + (3.0 * GELU_A * GELU_B) * square)


def column(shape, width):
    return lax.rem(lax.broadcasted_iota(jnp.int32, shape, 0), width)


def spread_columns(dest, lead, top, values, width):
    rows, depth = values.shape
    col = column(values.shape, width)
    left = jnp.where(col == 0, 0.0, pltpu.roll(values, 1, 0))
    right = jnp.where(col == width - 1, 0.0, pltpu.roll(values, rows - 1, 0))
    high = rows // width
    for place, part in enumerate((left, values, right)):
        dest[lead, pl.ds(top, high), :, place * depth : (place + 1) * depth] = part.astype(BF16).reshape(
            high, width, depth
        )


def halves(row):
    return (row[:, :LANES], row[:, LANES:])


def distill_grad(student, teacher, label, classes):
    lane = lax.broadcasted_iota(jnp.int32, student.shape, 1)
    live = lane < classes
    target = lane == label
    other = jnp.logical_and(live, jnp.logical_not(target))
    low = -1e30

    def parts(logits):
        soft = logits / SOFTEN
        whole_top = jnp.max(jnp.where(live, soft, low), axis=1, keepdims=True)
        rest_top = jnp.max(jnp.where(other, soft, low), axis=1, keepdims=True)
        whole_exp = jnp.where(live, jnp.exp(jnp.where(live, soft, whole_top) - whole_top), 0.0)
        rest_exp = jnp.where(other, jnp.exp(jnp.where(other, soft, rest_top) - rest_top), 0.0)
        whole_sum = jnp.sum(whole_exp, axis=1, keepdims=True)
        rest_sum = jnp.sum(rest_exp, axis=1, keepdims=True)
        whole = whole_top + jnp.log(whole_sum)
        rest = rest_top + jnp.log(rest_sum)
        true = jnp.sum(jnp.where(target, soft, 0.0), axis=1, keepdims=True)
        return (whole_exp / whole_sum, rest_exp / rest_sum, true - whole, rest - whole)

    probs, inner, _, _ = parts(student)
    _, inner_t, log_pt, log_rt = parts(teacher)
    p_true, p_rest = jnp.exp(log_pt), jnp.exp(log_rt)
    split_grad = (p_true + p_rest) * probs - jnp.where(target, p_true, 0.0) - p_rest * inner
    inner_grad = jnp.sum(inner_t, axis=1, keepdims=True) * inner - inner_t
    return SOFTEN * (TARGET_WEIGHT * split_grad + NONTARGET_WEIGHT * inner_grad)


def body(
    sizes,
    teacher_hbm,
    images_hbm,
    pair_index,
    labels,
    teacher_first_hbm,
    teacher_second_hbm,
    teacher_head_hbm,
    teacher_bias_hbm,
    first_hbm,
    gain_first_hbm,
    shift_first_hbm,
    second_hbm,
    gain_second_hbm,
    shift_second_hbm,
    head_hbm,
    head_bias_hbm,
    logits_out,
    images_grad,
    first_grad,
    gain_first_grad,
    shift_first_grad,
    second_grad,
    gain_second_grad,
    shift_second_grad,
    head_grad,
    bias_grad,
    stage_first,
    stage_second,
    images,
    teacher_head,
    teacher_bias,
    gain_first,
    shift_first,
    gain_second,
    shift_second,
    head_own,
    head_bias,
    teacher_in,
    teacher_w1,
    teacher_w2,
    teacher_x,
    teacher_h,
    teacher_head_pad,
    image_x,
    hidden_x,
    grad_x,
    w_first,
    w_second,
    own_first,
    own_second,
    y_first,
    y_second,
    slope_first,
    slope_second,
    d_hid,
    image_sib,
    hidden_sib,
    turned,
    turned_sib,
    part_all,
    part_own,
    part_send,
    part_recv,
    cross_all,
    cross_own,
    cross_send,
    cross_recv,
    last_all,
    last_own,
    last_send,
    last_recv,
    line_own,
    line_send,
    line_recv,
    sum_send,
    sum_recv,
    level_send,
    level_recv,
    level_line_send,
    level_line_recv,
    level_column,
    param_send,
    param_all,
    head_send,
    head_all,
    logit_send,
    logit_all,
    wide_send,
    wide_all,
    sync_send,
    sync_all_0,
    sync_all_1,
    sync_all_2,
    sync_all_3,
    sync_all_4,
    sync_all_5,
    sync_all_6,
    sync_all_7,
    head_sum,
    local_sem,
    gather_send,
    gather_recv,
    wide_ssem,
    wide_rsem,
    sync_ssem,
    sync_rsem,
    known,
    plane_ssem,
    plane_rsem,
    swap_ssem,
    swap_rsem,
    part_ssem,
    part_rsem,
    cross_ssem,
    cross_rsem,
    last_ssem,
    last_rsem,
    level_ssem,
    level_rsem,
    level_line_ssem,
    level_line_rsem,
    line_ssem,
    line_rsem,
    sum_ssem,
    sum_rsem,
):
    groups, chans, own, own_pad, classes = sizes
    sync_all = (
        sync_all_0,
        sync_all_1,
        sync_all_2,
        sync_all_3,
        sync_all_4,
        sync_all_5,
        sync_all_6,
        sync_all_7,
    )
    b = lax.axis_index("batch")
    c = lax.axis_index("chan")
    me = b * chans + c
    devices = groups * chans
    sibling = c + 1 - 2 * lax.rem(c, 2)
    extent = images.shape[1]
    cells = extent * extent
    depth = images.shape[3]
    wide = teacher_hbm.shape[1]
    samples = float(devices * cells)
    chips = chans // 2
    chip, core = c // 2, lax.rem(c, 2)

    if groups == 4:
        far_first = [groups - 1 - b, lax.rem(b + 2, groups), b + 1 - 2 * lax.rem(b, 2)]
    else:
        far_first = [lax.rem(b + i, groups) for i in range(1, groups)]

    def each_device(fn):
        for peer_b in far_first + [b]:

            def one(i, carry, peer_b=peer_b):
                fn(peer_b, lax.rem(c + (chans - i), chans))
                return carry

            lax.fori_loop(1 if peer_b is b else 0, chans, one, 0, unroll=chans <= 8)

    def each_chip(fn):
        def one(i, carry):
            fn(lax.rem(chip + i, chips))
            return carry

        lax.fori_loop(1, chips, one, 0, unroll=chips <= 4)

    def each_line(fn):
        for peer_b in far_first:
            fn(peer_b)

    def signal(sem, peer_b, peer_c):
        pl.semaphore_signal(sem, inc=1, device_id=(peer_b, peer_c), device_id_type=MESH)

    def each_plane(fn):
        def one(i, carry):
            fn(lax.rem(c + i, chans))
            return carry

        lax.fori_loop(1, chans, one, 0, unroll=chans <= 8)

    if chips == 4:
        beside = chip + 1 - 2 * lax.rem(chip, 2)
        above = lax.rem(chip + 2, chips)
        near = [beside, above]
    else:
        near = [lax.rem(chip + i, chips) for i in range(1, chips)]
    if groups == 4:
        lines = [[b + 1 - 2 * lax.rem(b, 2)], [lax.rem(b + 2, groups)]]
    else:
        lines = [far_first]
    barrier = pltpu.get_barrier_semaphore()
    for peer in near:
        signal(barrier, b, 2 * peer + core)
    for line in lines:
        for peer in line:
            signal(barrier, peer, c)
    signal(barrier, b, sibling)
    greeted = len(near) + sum(len(line) for line in lines) + 1

    own_rows = own_first.shape[0]
    exact = own_rows == 9 * own
    moves = (
        (first_hbm, own_first if exact else stage_first),
        (images_hbm, images),
        (second_hbm, own_second if exact else stage_second),
        (gain_first_hbm, gain_first),
        (shift_first_hbm, shift_first),
        (gain_second_hbm, gain_second),
        (shift_second_hbm, shift_second),
        (head_hbm, head_own),
        (head_bias_hbm, head_bias),
        (teacher_bias_hbm, teacher_bias),
        (teacher_head_hbm, teacher_head),
        (teacher_hbm, teacher_in),
        (teacher_first_hbm, teacher_w1),
        (teacher_second_hbm, teacher_w2),
    )
    loads = [pltpu.make_async_copy(source, dest, local_sem.at[i]) for i, (source, dest) in enumerate(moves)]
    for load in loads:
        load.start()

    for ref in (image_x, hidden_x, grad_x, teacher_x, teacher_h):
        high = ref.shape[1]
        for lead in range(ref.shape[0]):
            ref[lead, 0] = jnp.zeros(ref.shape[2:], BF16)
            ref[lead, high - 1] = jnp.zeros(ref.shape[2:], BF16)
    for load in loads[:11]:
        load.wait()
    if not exact:
        for source, dest in ((stage_first, own_first), (stage_second, own_second)):
            dest[...] = jnp.zeros(dest.shape, BF16)
            dest[0 : 9 * own, :] = source[...]

    def place_own(param_row):
        at = c * own
        lane0 = lax.rem(at, LANES)
        padded = jnp.concatenate([param_row, jnp.zeros((1, LANES - own), F32)], axis=1)
        moved = pltpu.roll(jnp.broadcast_to(padded, (8, LANES)), lane0, 1)[0:1]
        upper = at >= LANES
        return (jnp.where(upper, 0.0, moved), jnp.where(upper, moved, 0.0))

    for i, ref in enumerate((gain_first, shift_first, gain_second, shift_second)):
        low_half, high_half = place_own(ref[...])
        param_send[2 * i : 2 * i + 1, :] = low_half
        param_send[2 * i + 1 : 2 * i + 2, :] = high_half
    head_send[...] = jnp.zeros(head_send.shape, BF16)
    head_send[0:own, 0:classes] = head_own[...]
    for lead in range(MICRO):
        spread_columns(image_x, lead, 1, images[lead].astype(F32).reshape(cells, depth), extent)

    t_high = 16
    t_steps = wide // t_high
    t_rows = t_high * wide

    def teacher_conv(source, kernel, top):
        total = None
        for row_off in range(3):
            window = source[0, pl.ds(top + row_off, t_high)].reshape(t_rows, 3 * depth)
            term = jnp.dot(
                window, kernel[row_off * 3 * depth : (row_off + 1) * 3 * depth, :], preferred_element_type=F32
            )
            total = term if total is None else total + term
        return total

    def teacher_fill(lead):
        def fill(i, carry):
            top = i * t_high
            values = teacher_in[lead, pl.ds(top, t_high)].astype(F32).reshape(t_rows, depth)
            spread_columns(teacher_x, 0, top + 1, values, wide)
            return carry

        lax.fori_loop(0, t_steps, fill, 0)

    def teacher_one():
        def one(i, carry):
            top = i * t_high
            spread_columns(teacher_h, 0, top + 1, gelu(teacher_conv(teacher_x, teacher_w1, top)), wide)
            return carry

        lax.fori_loop(0, t_steps, one, 0)

    def teacher_two(lead):
        def two(i, total):
            top = i * t_high
            values = teacher_in[lead, pl.ds(top, t_high)].astype(F32).reshape(t_rows, depth)
            act = gelu(teacher_conv(teacher_h, teacher_w2, top) + values)
            return total + jnp.sum(act, axis=0, keepdims=True)

        return lax.fori_loop(0, t_steps, two, jnp.zeros((1, depth), F32))

    loads[11].wait()
    teacher_fill(0)
    loads[12].wait()
    teacher_one()

    pl.semaphore_wait(barrier, greeted)
    rounds = [[(b, sibling)]] + [[(peer, c) for peer in line] for line in lines]
    if chips == 4:
        rounds = [[(b, 2 * beside + core)]] + rounds

    def say(i):
        if i < len(rounds):
            for peer in rounds[i]:
                signal(known.at[i], *peer)

    def hear(i):
        if i < len(rounds):
            pl.semaphore_wait(known.at[i], len(rounds[i]))
            say(i + 1)

    say(0)

    pieces = 3 if 3 * own % 16 == 0 else 1
    piece_rows = own_rows // pieces
    square = chips == 4 and piece_rows % 32 == 0
    held = (w_first, w_second)
    offered = (own_first, own_second)

    def gather_copy(k, rows, sem, shard, target, source=None):
        slot = held[k].at[shard, rows]
        return pltpu.make_async_remote_copy(
            src_ref=slot if source is None else source.at[rows],
            dst_ref=slot,
            send_sem=gather_send.at[k],
            recv_sem=gather_recv.at[k, sem, shard],
            device_id=(b, target),
            device_id_type=MESH,
        )

    def whole_copy(k, piece, shard, target, source=None):
        return gather_copy(k, pl.ds(piece * piece_rows, piece_rows), piece, shard, target, source)

    def half_copy(k, piece, half, shard, target, source=None):
        rows = pl.ds(piece * piece_rows + half * (piece_rows // 2), piece_rows // 2)
        return gather_copy(k, rows, 2 * piece + half, shard, target, source)

    def shard_of(peer):
        return 2 * peer + core

    def gather_start(k):
        if square:
            for late in range(2):
                for piece in range(pieces):
                    half_copy(k, piece, late, c, shard_of(beside), offered[k]).start()
                    half_copy(k, piece, 1 - late, c, shard_of(above), offered[k]).start()
        for piece in range(pieces):
            if not square:
                each_chip(lambda peer, piece=piece: whole_copy(k, piece, c, shard_of(peer), offered[k]).start())
            whole_copy(k, piece, c, sibling, offered[k]).start()
        held[k][c] = offered[k][...]

    def gather_turn(k):
        if square:
            for piece in range(pieces):
                for half, source, target in ((0, beside, above), (1, above, beside)):
                    half_copy(k, piece, half, shard_of(source), sibling).wait_recv()
                    half_copy(k, piece, half, shard_of(source), shard_of(target)).start()

    def gather_forward(k, piece):
        if square:
            half_copy(k, piece, 1, shard_of(beside), sibling).wait_recv()
            half_copy(k, piece, 0, shard_of(above), sibling).wait_recv()
            whole_copy(k, piece, shard_of(beside), sibling).start()
            whole_copy(k, piece, shard_of(above), sibling).start()
            for half in range(2):
                half_copy(k, piece, half, shard_of(3 - chip), sibling).wait_recv()
            whole_copy(k, piece, shard_of(3 - chip), sibling).start()
        else:

            def one(peer):
                whole_copy(k, piece, shard_of(peer), sibling).wait_recv()
                whole_copy(k, piece, shard_of(peer), sibling).start()

            each_chip(one)

    def gather_finish(k, piece):
        def one(i, carry):
            whole_copy(k, piece, 2 * lax.rem(chip + i, chips) + 1 - core, sibling).wait_recv()
            return carry

        lax.fori_loop(0, chips, one, 0, unroll=chips <= 4)

    def bytes_of(sem, many):
        pltpu.make_async_copy(many, many, sem).wait()

    def swap(k, source, dest):
        return pltpu.make_async_remote_copy(
            src_ref=source,
            dst_ref=dest,
            send_sem=swap_ssem.at[k],
            recv_sem=swap_rsem.at[k],
            device_id=(b, sibling),
            device_id_type=MESH,
        )

    def tile_start(send, recv, ssem, rsem):
        def one(pb, pc):
            pltpu.make_async_remote_copy(
                src_ref=send, dst_ref=recv.at[me], send_sem=ssem, recv_sem=rsem, device_id=(pb, pc), device_id_type=MESH
            ).start()

        each_device(one)
        recv[me] = send[...]

    def tile_bytes(sem, recv):
        bytes_of(sem, recv.at[pl.ds(0, devices - 1)])

    def sync_start(stage, micro, rows):
        k = stage * MICRO + micro
        for i, row in enumerate(rows):
            for j, half in enumerate(halves(row)):
                sync_send[k, 2 * i + j : 2 * i + j + 1, :] = half
        tile_start(sync_send.at[k], sync_all[k], sync_ssem.at[k], sync_rsem.at[k])

    def sync_wait(stage, micro):
        k = stage * MICRO + micro
        tile_bytes(sync_rsem.at[k], sync_all[k])
        total = jnp.sum(sync_all[k][...], axis=0)
        return [jnp.concatenate([total[2 * i : 2 * i + 1], total[2 * i + 1 : 2 * i + 2]], axis=1) for i in range(2)]

    def plane_start(k, source, slot):
        def one(pc):
            pltpu.make_async_remote_copy(
                src_ref=source(pc),
                dst_ref=slot(c),
                send_sem=plane_ssem.at[k],
                recv_sem=plane_rsem.at[k],
                device_id=(b, pc),
                device_id_type=MESH,
            ).start()

        each_plane(one)

    def plane_wait(k, many):
        pltpu.make_async_copy(many, many, plane_rsem.at[k]).wait()

    def plane_drain(k, many):
        pltpu.make_async_copy(many, many, plane_ssem.at[k]).wait()

    gather_start(0)
    swaps = [swap(0, image_x, image_sib)]
    swaps[0].start()
    loads[13].wait()
    teacher_rows = [teacher_two(0)]

    hear(0)

    teacher_fill(1)
    hear(1)
    plane_start(0, lambda pc: param_send, lambda s: param_all.at[s])
    plane_start(1, lambda pc: head_send, lambda s: head_all.at[s])
    param_all[c] = param_send[...]
    head_all[c] = head_send[...]
    teacher_one()
    gather_turn(0)
    gather_start(1)
    hear(2)
    teacher_rows.append(teacher_two(1))
    which_t = lax.broadcasted_iota(jnp.int32, (8, depth), 0)
    pooled_t = jnp.zeros((8, depth), F32)
    for m in range(MICRO):
        pooled_t = jnp.where(which_t == m, teacher_rows[m] / float(wide * wide), pooled_t)
    teacher_head_pad[...] = jnp.zeros(teacher_head_pad.shape, F32)
    teacher_head_pad[0:classes, :] = teacher_head[...].astype(F32)
    teacher_logits = lax.dot_general(
        pooled_t, teacher_head_pad[...], (((1,), (1,)), ((), ())), precision=HIGHEST, preferred_element_type=F32
    )
    lane_pad = jnp.zeros((1, LANES - classes), F32)
    teacher_logits = teacher_logits + jnp.concatenate([teacher_bias[...], lane_pad], axis=1)
    image_sum = jnp.zeros((1, depth), F32)
    for m in range(MICRO):
        image_sum = image_sum + jnp.sum(images[m].astype(F32).reshape(cells, depth), axis=0, keepdims=True)
    logit_send[0:MICRO, :] = teacher_logits[0:MICRO]
    for j, half in enumerate(halves(image_sum)):
        logit_send[MICRO + j : MICRO + j + 1, :] = half
    hear(3)
    tile_start(logit_send, logit_all, wide_ssem.at[0], wide_rsem.at[0])

    def picker(shard, block, offset):
        at_row = lax.broadcasted_iota(jnp.int32, (depth, block), 0)
        place = lax.broadcasted_iota(jnp.int32, (depth, block), 1) - offset
        wanted = jnp.logical_and(place >= 0, place < own)
        return jnp.logical_and(wanted, at_row == shard * own + place).astype(BF16)

    def unpack(ref, block, offset):
        def one(shard, total):
            return total + jnp.dot(picker(shard, block, offset), ref[shard], preferred_element_type=F32)

        return lax.fori_loop(0, chans, one, jnp.zeros((depth, ref.shape[2]), F32)).astype(BF16)

    def weights(ref, tap):
        if own_pad == own:
            return ref[:, tap * own : (tap + 1) * own, :].reshape(depth, depth)
        return unpack(ref, own_rows, tap * own)

    def window(source, micro, row_off, col_off):
        return source[micro, row_off : row_off + extent, :, col_off * depth : (col_off + 1) * depth].reshape(
            cells, depth
        )

    def student_conv(source, micro, ref, row_offs):
        total = None
        for row_off in row_offs:
            for col_off in range(3):
                term = lax.dot_general(
                    window(source, micro, row_off, col_off),
                    weights(ref, row_off * 3 + col_off),
                    (((1,), (1,)), ((), ())),
                    preferred_element_type=F32,
                )
                total = term if total is None else total + term
        return total

    def student_back(source, micro, ref):
        total = None
        for row_off in range(3):
            for col_off in range(3):
                term = jnp.dot(
                    window(source, micro, row_off, col_off),
                    weights(ref, (2 - row_off) * 3 + 2 - col_off),
                    preferred_element_type=F32,
                )
                total = term if total is None else total + term
        return total

    def rows_of(m):
        return slice(m * cells, (m + 1) * cells)

    def col_sum(values):
        return jnp.sum(values, axis=0, keepdims=True)

    def moments_start(stage, m, values):
        sync_start(stage, m, (col_sum(values), col_sum(values * values)))

    def moments(stage, m):
        total, square = sync_wait(stage, m)
        center = total / samples
        spread = square / samples - center * center
        return (center, lax.rsqrt(spread + EPS))

    if pieces == 3:
        gather_forward(0, 0)
        gather_forward(0, 1)
        gather_finish(0, 0)
        for m in range(MICRO):
            y_first[rows_of(m), :] = student_conv(image_x, m, w_first, (0,))
        gather_forward(0, 2)
        gather_finish(0, 1)
        for m in range(MICRO):
            y_first[rows_of(m), :] += student_conv(image_x, m, w_first, (1,))
        gather_finish(0, 2)
        for m in range(MICRO):
            values = y_first[rows_of(m), :] + student_conv(image_x, m, w_first, (2,))
            y_first[rows_of(m), :] = values
            moments_start(0, m, values)
    else:
        gather_forward(0, 0)
        gather_finish(0, 0)
        for m in range(MICRO):
            values = student_conv(image_x, m, w_first, range(3))
            y_first[rows_of(m), :] = values
            moments_start(0, m, values)

    plane_wait(0, param_all.at[pl.ds(0, chans - 1)])
    plane_wait(1, head_all.at[pl.ds(0, chans - 1)])
    params = jnp.sum(param_all[...], axis=0)
    gain1, shift1, gain2, shift2 = (
        jnp.concatenate([params[2 * i : 2 * i + 1], params[2 * i + 1 : 2 * i + 2]], axis=1) for i in range(4)
    )
    if own_pad == own:
        head = head_all[...].reshape(depth, LANES)
    else:
        head = unpack(head_all, own_pad, 0)
    gather_turn(1)
    for piece in range(pieces):
        gather_forward(1, piece)
    for piece in range(pieces):
        gather_finish(1, piece)

    def three_parts(values):
        first = values.astype(BF16)
        rest = values - first.astype(F32)
        second = rest.astype(BF16)
        third = (rest - second.astype(F32)).astype(BF16)
        return jnp.concatenate([first, second, third], axis=0)

    def sum_parts(product):
        return product[0:8] + product[8:16] + product[16:24]

    norm1 = []
    for m in range(MICRO):
        center, inv = moments(0, m)
        norm1.append((center, inv))
        normed = (y_first[rows_of(m), :] - center) * (inv * gain1) + shift1
        spread_columns(hidden_x, m, 1, gelu(normed), extent)
        values = student_conv(hidden_x, m, w_second, range(3))
        y_second[rows_of(m), :] = values
        moments_start(1, m, values)
    swaps.append(swap(1, hidden_x, hidden_sib))
    swaps[1].start()
    for m in range(MICRO):
        center, inv = norm1[m]
        slope_first[rows_of(m), :] = gelu_slope((y_first[rows_of(m), :] - center) * (inv * gain1) + shift1)

    per_device = pair_index.shape[0]
    norm2, slope_scale = [], []
    which = lax.broadcasted_iota(jnp.int32, (8, depth), 0)
    which_lane = lax.broadcasted_iota(jnp.int32, (8, LANES), 0)
    for m in range(MICRO):
        center, inv = moments(1, m)
        norm2.append((center, inv))
        spread = y_second[rows_of(m), :] - center
        res = spread * (inv * gain2) + shift2 + images[m].astype(F32).reshape(cells, depth)
        square = res * res
        t = jnp.tanh(GELU_A * (res + GELU_B * (res * square)))
        half = 0.5 + 0.5 * t
        slope = half + (0.5 * res) * (1.0 - t * t) * (GELU_A + (3.0 * GELU_A * GELU_B) * square)
        slope_second[rows_of(m), :] = slope
        pooled = col_sum(res * half) / float(cells)
        slope_sum = col_sum(slope)
        slope_dot = col_sum(slope * spread) * inv
        product = jnp.dot(
            three_parts(jnp.where(which == 0, pooled, 0.0)), head, preferred_element_type=F32
        )
        logits = sum_parts(product)[0:1] + jnp.concatenate([head_bias[...], lane_pad], axis=1)
        if m == 0:
            tile_bytes(wide_rsem.at[0], logit_all)
        paired = pair_index[m]
        teacher_row = logit_all[pl.ds(paired // per_device, 1), pl.ds(lax.rem(paired, per_device), 1), :].reshape(1, LANES)
        grad = distill_grad(logits, teacher_row, labels[m], classes)
        product = lax.dot_general(
            three_parts(jnp.where(which_lane == 0, grad, 0.0)),
            head,
            (((1,), (1,)), ((), ())),
            preferred_element_type=F32,
        )
        scale = sum_parts(product)[0:1] / float(cells)
        slope_scale.append(scale)
        sync_start(2, m, (scale * slope_dot, scale * slope_sum))
        for j, part in enumerate(halves(pooled)):
            wide_send[m * 4 + j : m * 4 + j + 1, :] = part
        wide_send[m * 4 + 2 : m * 4 + 3, :] = grad
        wide_send[m * 4 + 3 : m * 4 + 4, :] = logits
    tile_start(wide_send, wide_all, wide_ssem.at[1], wide_rsem.at[1])

    def own_lanes(low_row, high_row):
        at = c * own
        row = jnp.where(at >= LANES, high_row, low_row)
        turn = lax.rem(LANES - lax.rem(at, LANES), LANES)
        return pltpu.roll(jnp.broadcast_to(row, (8, LANES)), turn, 1)[0:1, 0:own]

    def norm_back(stage, m, gain, norm, grad, y_ref):
        center, inv = norm
        totals = sync_wait(stage, m)
        scale = gain * inv
        slant = scale * inv * (totals[0] / samples)
        level = scale * (totals[1] / samples)
        return (grad * scale - (y_ref[rows_of(m), :] - center) * slant - level, totals)

    def norm_out(totals, gain_out, shift_out):
        for out, i in ((gain_out, 0), (shift_out, 1)):
            row = totals[0][i]
            for m in range(1, MICRO):
                row = row + totals[m][i]
            out[...] = own_lanes(*halves(row))

    def turn(k, m, grad):
        whole = jnp.transpose(grad).astype(BF16)
        if own_pad == own:
            turned[k, m] = whole.reshape(chips, 2, own, cells)
        else:

            def one(shard, carry):
                turned[k, m, shard // 2, lax.rem(shard, 2)] = lax.dot_general(
                    picker(shard, own_pad, 0), whole, (((0,), (0,)), ((), ())), preferred_element_type=F32
                ).astype(BF16)
                return carry

            lax.fori_loop(0, chans, one, 0)
        turns[k, m] = swap(2 + k * MICRO + m, turned.at[k, m, :, 1 - core], turned_sib.at[k, m])
        turns[k, m].start()

    turns = {}
    taps = 3 * own_pad
    per_half = groups // 2
    part_rows = taps // per_half
    part_pad = sum_send.shape[2]
    across = 2

    def send(source, dest, ssem, rsem, peer_b, peer_c):
        pltpu.make_async_remote_copy(
            src_ref=source, dst_ref=dest, send_sem=ssem, recv_sem=rsem, device_id=(peer_b, peer_c), device_id_type=MESH
        ).start()

    def cut(p):
        half, row = p // per_half, (p % per_half) * part_rows
        return slice(row, row + part_rows), slice(half * LANES, (half + 1) * LANES)

    def kernel_grad(k, source, source_sib, mean):
        sides = [(turned[k, m, :, pl.ds(core, 1)].reshape(chips * own_pad, cells), source, m) for m in range(MICRO)]
        for m in range(MICRO):
            turns[k, m].wait_recv()
            sides.append((turned_sib[k, m].reshape(chips * own_pad, cells), source_sib, m))
        level = sum(jnp.sum(grads.astype(F32), axis=1, keepdims=True) for grads, _, _ in sides)
        ones = jnp.ones((8, cells), BF16)
        level_send[k] = sum(
            lax.dot_general(ones, grads, (((1,), (1,)), ((), ())), preferred_element_type=F32) for grads, _, _ in sides
        )[0:1]
        for row_off in (across, 0, 1):
            total = sum(
                jnp.dot(
                    grads,
                    ref[m, row_off : row_off + extent].reshape(cells, 3 * depth),
                    preferred_element_type=F32,
                )
                for grads, ref, m in sides
            )
            for col_off in range(3):
                block = total[:, col_off * depth : (col_off + 1) * depth] - level * mean
                for i in range(chips):
                    part_all[i, col_off * own_pad : (col_off + 1) * own_pad, :] = block[i * own_pad : (i + 1) * own_pad]
            if row_off == across:
                for p in range(groups):
                    rows, lanes = cut(p)
                    cross_all[p, :, 0:part_rows] = part_all[:, rows, lanes]
                    if part_pad != part_rows:
                        cross_all[p, :, part_rows:part_pad] = jnp.zeros((chips, part_pad - part_rows, LANES), F32)
                cross_send[k] = cross_all[...].astype(BF16)
                cross_own[k] = cross_all[pl.ds(b, 1)].reshape(chips, part_pad, LANES)
                each_line(
                    lambda peer: send(
                        cross_send.at[k, peer], cross_recv.at[k, b], cross_ssem.at[k], cross_rsem.at[k], peer, c
                    )
                )
                cross_recv[k, b] = jnp.zeros((chips, part_pad, LANES), BF16)
            else:
                part_send[k, row_off] = part_all[...].astype(BF16)
                part_own[k, row_off] = part_all[pl.ds(chip, 1)].reshape(taps, depth)
                each_chip(
                    lambda peer, row_off=row_off: send(
                        part_send.at[k, row_off, peer],
                        part_recv.at[k, row_off, chip],
                        part_ssem.at[k, row_off],
                        part_rsem.at[k, row_off],
                        b,
                        2 * peer + core,
                    )
                )
                part_recv[k, row_off, chip] = jnp.zeros((taps, depth), BF16)
        each_chip(
            lambda peer: send(
                level_send.at[k], level_recv.at[k, chip], level_ssem.at[k], level_rsem.at[k], b, 2 * peer + core
            )
        )
        level_recv[k, chip] = level_send[k]

    def line_start(k):
        for row_off in range(across):
            bytes_of(part_rsem.at[k, row_off], part_recv.at[k, row_off, pl.ds(0, chips - 1)])
            total = part_own[k, row_off] + jnp.sum(part_recv[k, row_off].astype(F32), axis=0)
            for p in range(groups):
                line_own[k, row_off, p, 0:part_rows] = total[cut(p)]
                if part_pad != part_rows:
                    line_own[k, row_off, p, part_rows:part_pad] = jnp.zeros((part_pad - part_rows, LANES), F32)
            line_send[k, row_off] = line_own[k, row_off].astype(BF16)
            each_line(
                lambda peer, row_off=row_off: send(
                    line_send.at[k, row_off, peer],
                    line_recv.at[k, row_off, b],
                    line_ssem.at[k, row_off],
                    line_rsem.at[k, row_off],
                    peer,
                    c,
                )
            )
            line_recv[k, row_off, b] = jnp.zeros((part_pad, LANES), BF16)
        bytes_of(level_rsem.at[k], level_recv.at[k, pl.ds(0, chips - 1)])
        level_line_send[k] = jnp.sum(level_recv[k], axis=0)
        each_line(
            lambda peer: send(
                level_line_send.at[k], level_line_recv.at[k, b], level_line_ssem.at[k], level_line_rsem.at[k], peer, c
            )
        )
        level_line_recv[k, b] = level_line_send[k]

    def cross_forward(k):
        bytes_of(cross_rsem.at[k], cross_recv.at[k, pl.ds(0, groups - 1)])
        last_all[...] = cross_own[k] + jnp.sum(cross_recv[k].astype(F32), axis=0)
        last_send[k] = last_all[...].astype(BF16)
        last_own[k] = last_all[pl.ds(chip, 1)].reshape(part_pad, LANES)
        each_chip(
            lambda peer: send(
                last_send.at[k, peer], last_recv.at[k, chip], last_ssem.at[k], last_rsem.at[k], b, 2 * peer + core
            )
        )
        last_recv[k, chip] = jnp.zeros((part_pad, LANES), BF16)

    def share(k, row_off, total):
        sum_send[k, row_off] = total.astype(BF16)
        each_line(
            lambda peer: send(
                sum_send.at[k, row_off],
                sum_recv.at[k, row_off, b],
                sum_ssem.at[k, row_off],
                sum_rsem.at[k, row_off],
                peer,
                c,
            )
        )
        sum_recv[k, row_off, b] = sum_send[k, row_off]

    def cross_sum(k):
        bytes_of(last_rsem.at[k], last_recv.at[k, pl.ds(0, chips - 1)])
        share(k, across, last_own[k] + jnp.sum(last_recv[k].astype(F32), axis=0))

    def line_sum(k):
        for row_off in range(across):
            bytes_of(line_rsem.at[k, row_off], line_recv.at[k, row_off, pl.ds(0, groups - 1)])
            share(
                k,
                row_off,
                line_own[k, row_off, pl.ds(b, 1)].reshape(part_pad, LANES)
                + jnp.sum(line_recv[k, row_off].astype(F32), axis=0),
            )

    def sum_finish(k, mean, out):
        bytes_of(level_line_rsem.at[k], level_line_recv.at[k, pl.ds(0, groups - 1)])
        level = jnp.sum(level_line_recv[k], axis=0)
        level_column[...] = jnp.transpose(jnp.broadcast_to(level, (LANES, level.shape[1])))
        column_own = level_column[pl.ds(chip * own_pad, own_pad), :]
        back = [column_own * half for half in halves(mean)]
        for row_off in (0, 1, 2):
            bytes_of(sum_rsem.at[k, row_off], sum_recv.at[k, row_off, pl.ds(0, groups - 1)])
            for half in range(2):
                rows = sum_recv[k, row_off, half * per_half : (half + 1) * per_half, 0:part_rows].astype(F32)
                out[row_off * 3 : row_off * 3 + 3, :, half * LANES : (half + 1) * LANES] = (
                    rows.reshape(3, own_pad, LANES) + back[half][None]
                )

    totals2 = []
    for m in range(MICRO):
        found, totals = norm_back(2, m, gain2, norm2[m], slope_second[rows_of(m), :] * slope_scale[m], y_second)
        totals2.append(totals)
        spread_columns(grad_x, m, 1, found, extent)
        grad = student_back(grad_x, m, w_second) * slope_first[rows_of(m), :]
        d_hid[rows_of(m), :] = grad
        center, inv = norm1[m]
        sync_start(3, m, (col_sum(grad * (y_first[rows_of(m), :] - center)) * inv, col_sum(grad)))
    for m in range(MICRO):
        turn(0, m, grad_x[m, 1 : extent + 1, :, depth : 2 * depth].astype(F32).reshape(cells, depth))
    norm_out(totals2, gain_second_grad, shift_second_grad)

    hidden_mean = jnp.zeros((1, depth), F32)
    for node, weight in QUADRATURE:
        hidden_mean = hidden_mean + weight * gelu(shift1 + gain1 * node)
    image_rows = jnp.sum(logit_all[...], axis=0)
    image_mean = jnp.concatenate([image_rows[MICRO : MICRO + 1], image_rows[MICRO + 1 : MICRO + 2]], axis=1) / (
        MICRO * samples
    )

    swaps[0].wait_recv()
    swaps[1].wait_recv()
    kernel_grad(0, hidden_x, hidden_sib, hidden_mean)

    totals1 = []
    for m in range(MICRO):
        found, totals = norm_back(3, m, gain1, norm1[m], d_hid[rows_of(m), :], y_first)
        totals1.append(totals)
        turn(1, m, found)
        spread_columns(grad_x, m, 1, found, extent)
    kernel_grad(1, image_x, image_sib, image_mean)
    for m in range(MICRO):
        images_grad[m] = (
            student_back(grad_x, m, w_first) + slope_second[rows_of(m), :] * slope_scale[m]
        ).reshape(images_grad.shape[1:])
    norm_out(totals1, gain_first_grad, shift_first_grad)
    line_start(0)
    cross_forward(0)

    tile_bytes(wide_rsem.at[1], wide_all)
    totals = [jnp.zeros((LANES, LANES), F32) for _ in range(2)]
    bias_row = jnp.zeros((1, LANES), F32)
    for m in range(MICRO):
        per_image = wide_all[:, m * 4 + 2, :]
        bias_row = bias_row + col_sum(per_image)
        for j in range(2):
            totals[j] = totals[j] + lax.dot_general(
                wide_all[:, m * 4 + j, :],
                per_image,
                (((0,), (0,)), ((), ())),
                precision=HIGHEST,
                preferred_element_type=F32,
            )
        shown = wide_all[pl.ds(b * chans, chans), m * 4 + 3, :]
        logits_out[pl.ds(m, chans, stride=MICRO), :] = shown[:, 0:classes]
    for j in range(2):
        head_sum[j * LANES : (j + 1) * LANES, :] = totals[j]
    head_grad[...] = head_sum[pl.ds(c * own, own), :][:, 0:classes]
    bias_grad[...] = bias_row[:, 0:classes]

    cross_sum(0)
    line_start(1)
    cross_forward(1)
    line_sum(0)
    cross_sum(1)
    line_sum(1)
    sum_finish(0, hidden_mean, second_grad)
    sum_finish(1, image_mean, first_grad)

    for k in range(2):
        tile_bytes(wide_ssem.at[k], (logit_all, wide_all)[k])
        bytes_of(gather_send.at[k], held[k].at[pl.ds(0, chans - 1)])
    for k in range(4 * MICRO):
        tile_bytes(sync_ssem.at[k], sync_all[k])
    plane_drain(0, param_all.at[pl.ds(0, chans - 1)])
    plane_drain(1, head_all.at[pl.ds(0, chans - 1)])
    for copy in swaps + list(turns.values()):
        copy.wait_send()
    for k in range(2):
        for row_off in range(across):
            bytes_of(part_ssem.at[k, row_off], part_recv.at[k, row_off, pl.ds(0, chips - 1)])
            bytes_of(line_ssem.at[k, row_off], line_recv.at[k, row_off, pl.ds(0, groups - 1)])
        for row_off in range(3):
            bytes_of(sum_ssem.at[k, row_off], sum_recv.at[k, row_off, pl.ds(0, groups - 1)])
        bytes_of(cross_ssem.at[k], cross_recv.at[k, pl.ds(0, groups - 1)])
        bytes_of(last_ssem.at[k], last_recv.at[k, pl.ds(0, chips - 1)])
        bytes_of(level_ssem.at[k], level_recv.at[k, pl.ds(0, chips - 1)])
        bytes_of(level_line_ssem.at[k], level_line_recv.at[k, pl.ds(0, groups - 1)])


def hand_on(*refs):
    count = len(refs) // 2
    copies = [pltpu.make_async_copy(refs[i], refs[count + i], refs[-1].at[i]) for i in range(count)]
    for copy in copies:
        copy.start()
    for copy in copies:
        copy.wait()


def shards(
    teacher_images,
    student_images,
    pair_index,
    labels,
    teacher_first,
    teacher_second,
    teacher_head,
    teacher_bias,
    conv_first,
    gain_first,
    shift_first,
    conv_second,
    gain_second,
    shift_second,
    head_weight,
    head_bias,
):
    groups, chans = lax.axis_size("batch"), lax.axis_size("chan")
    devices = groups * chans
    count, extent, _, depth = student_images.shape
    wide = teacher_images.shape[1]
    own = conv_first.shape[3]
    own_pad = max(own, 16)
    own_rows = -(-9 * own // 16) * 16
    classes = head_bias.shape[0]
    cells = extent * extent
    rows = count * cells
    chips = chans // 2
    taps = 3 * own_pad
    part_rows = 2 * taps // groups
    part_pad = -(-part_rows // 16) * 16

    def turned(kernel):
        return jnp.transpose(kernel, (0, 1, 3, 2)).reshape(9 * own, depth)

    def row(vector):
        return vector.reshape(1, -1)

    vmem = pl.BlockSpec(memory_space=pltpu.VMEM)
    smem = pl.BlockSpec(memory_space=pltpu.SMEM)
    hbm = pl.BlockSpec(memory_space=pl.ANY)
    out_shape = [
        jax.ShapeDtypeStruct((chans * count, classes), F32),
        jax.ShapeDtypeStruct(student_images.shape, F32),
        jax.ShapeDtypeStruct((9, own_pad, depth), F32),
        jax.ShapeDtypeStruct((1, own), F32),
        jax.ShapeDtypeStruct((1, own), F32),
        jax.ShapeDtypeStruct((9, own_pad, depth), F32),
        jax.ShapeDtypeStruct((1, own), F32),
        jax.ShapeDtypeStruct((1, own), F32),
        jax.ShapeDtypeStruct((own, classes), F32),
        jax.ShapeDtypeStruct((1, classes), F32),
    ]
    stage = (16, LANES) if own_rows == 9 * own else (9 * own, depth)
    scratch = [
        pltpu.VMEM(stage, BF16),
        pltpu.VMEM(stage, BF16),
        pltpu.VMEM(student_images.shape, BF16),
        pltpu.VMEM((classes, depth), BF16),
        pltpu.VMEM((1, classes), F32),
        pltpu.VMEM((1, own), F32),
        pltpu.VMEM((1, own), F32),
        pltpu.VMEM((1, own), F32),
        pltpu.VMEM((1, own), F32),
        pltpu.VMEM((own, classes), BF16),
        pltpu.VMEM((1, classes), F32),
        pltpu.VMEM(teacher_images.shape, BF16),
        pltpu.VMEM((9 * depth, depth), BF16),
        pltpu.VMEM((9 * depth, depth), BF16),
        pltpu.VMEM((1, wide + 2, wide, 3 * depth), BF16),
        pltpu.VMEM((1, wide + 2, wide, 3 * depth), BF16),
        pltpu.VMEM((LANES, depth), F32),
        pltpu.VMEM((count, extent + 2, extent, 3 * depth), BF16),
        pltpu.VMEM((count, extent + 2, extent, 3 * depth), BF16),
        pltpu.VMEM((count, extent + 2, extent, 3 * depth), BF16),
        pltpu.VMEM((chans, own_rows, depth), BF16),
        pltpu.VMEM((chans, own_rows, depth), BF16),
        pltpu.VMEM((own_rows, depth), BF16),
        pltpu.VMEM((own_rows, depth), BF16),
        pltpu.VMEM((rows, depth), F32),
        pltpu.VMEM((rows, depth), F32),
        pltpu.VMEM((rows, depth), F32),
        pltpu.VMEM((rows, depth), F32),
        pltpu.VMEM((rows, depth), F32),
        pltpu.VMEM((count, extent + 2, extent, 3 * depth), BF16),
        pltpu.VMEM((count, extent + 2, extent, 3 * depth), BF16),
        pltpu.VMEM((2, count, chips, 2, own_pad, cells), BF16),
        pltpu.VMEM((2, count, chips, own_pad, cells), BF16),
        pltpu.VMEM((chips, taps, depth), F32),
        pltpu.VMEM((2, 2, taps, depth), F32),
        pltpu.VMEM((2, 2, chips, taps, depth), BF16),
        pltpu.VMEM((2, 2, chips, taps, depth), BF16),
        pltpu.VMEM((groups, chips, part_pad, LANES), F32),
        pltpu.VMEM((2, chips, part_pad, LANES), F32),
        pltpu.VMEM((2, groups, chips, part_pad, LANES), BF16),
        pltpu.VMEM((2, groups, chips, part_pad, LANES), BF16),
        pltpu.VMEM((chips, part_pad, LANES), F32),
        pltpu.VMEM((2, part_pad, LANES), F32),
        pltpu.VMEM((2, chips, part_pad, LANES), BF16),
        pltpu.VMEM((2, chips, part_pad, LANES), BF16),
        pltpu.VMEM((2, 2, groups, part_pad, LANES), F32),
        pltpu.VMEM((2, 2, groups, part_pad, LANES), BF16),
        pltpu.VMEM((2, 2, groups, part_pad, LANES), BF16),
        pltpu.VMEM((2, 3, part_pad, LANES), BF16),
        pltpu.VMEM((2, 3, groups, part_pad, LANES), BF16),
        pltpu.VMEM((2, 1, chips * own_pad), F32),
        pltpu.VMEM((2, chips, 1, chips * own_pad), F32),
        pltpu.VMEM((2, 1, chips * own_pad), F32),
        pltpu.VMEM((2, groups, 1, chips * own_pad), F32),
        pltpu.VMEM((chips * own_pad, LANES), F32),
        pltpu.VMEM((8, LANES), F32),
        pltpu.VMEM((chans, 8, LANES), F32),
        pltpu.VMEM((own_pad, LANES), BF16),
        pltpu.VMEM((chans, own_pad, LANES), BF16),
        pltpu.VMEM((4, LANES), F32),
        pltpu.VMEM((devices, 4, LANES), F32),
        pltpu.VMEM((8, LANES), F32),
        pltpu.VMEM((devices, 8, LANES), F32),
        pltpu.VMEM((4 * MICRO, 4, LANES), F32),
        pltpu.VMEM((devices, 4, LANES), F32),
        pltpu.VMEM((devices, 4, LANES), F32),
        pltpu.VMEM((devices, 4, LANES), F32),
        pltpu.VMEM((devices, 4, LANES), F32),
        pltpu.VMEM((devices, 4, LANES), F32),
        pltpu.VMEM((devices, 4, LANES), F32),
        pltpu.VMEM((devices, 4, LANES), F32),
        pltpu.VMEM((devices, 4, LANES), F32),
        pltpu.VMEM((depth, LANES), F32),
        pltpu.SemaphoreType.DMA((14,)),
        pltpu.SemaphoreType.DMA((2,)),
        pltpu.SemaphoreType.DMA((2, 6, chans)),
        pltpu.SemaphoreType.DMA((2,)),
        pltpu.SemaphoreType.DMA((2,)),
        pltpu.SemaphoreType.DMA((4 * MICRO,)),
        pltpu.SemaphoreType.DMA((4 * MICRO,)),
        pltpu.SemaphoreType.REGULAR((4,)),
        pltpu.SemaphoreType.DMA((2,)),
        pltpu.SemaphoreType.DMA((2,)),
        pltpu.SemaphoreType.DMA((2 + 2 * MICRO,)),
        pltpu.SemaphoreType.DMA((2 + 2 * MICRO,)),
        pltpu.SemaphoreType.DMA((2, 2)),
        pltpu.SemaphoreType.DMA((2, 2)),
        pltpu.SemaphoreType.DMA((2,)),
        pltpu.SemaphoreType.DMA((2,)),
        pltpu.SemaphoreType.DMA((2,)),
        pltpu.SemaphoreType.DMA((2,)),
        pltpu.SemaphoreType.DMA((2,)),
        pltpu.SemaphoreType.DMA((2,)),
        pltpu.SemaphoreType.DMA((2,)),
        pltpu.SemaphoreType.DMA((2,)),
        pltpu.SemaphoreType.DMA((2, 2)),
        pltpu.SemaphoreType.DMA((2, 2)),
        pltpu.SemaphoreType.DMA((2, 3)),
        pltpu.SemaphoreType.DMA((2, 3)),
    ]
    found = pl.pallas_call(
        functools.partial(body, (groups, chans, own, own_pad, classes)),
        out_shape=[pltpu.VMEM(out.shape, out.dtype) for out in out_shape],
        in_specs=[hbm, hbm, smem, smem] + [hbm] * 12,
        out_specs=[vmem] * 10,
        scratch_shapes=scratch,
        compiler_params=pltpu.CompilerParams(
            collective_id=0, has_side_effects=True, vmem_limit_bytes=62 * 2**20
        ),
    )(
        teacher_images,
        student_images,
        pair_index,
        labels,
        teacher_first.reshape(9 * depth, depth),
        teacher_second.reshape(9 * depth, depth),
        teacher_head.T,
        row(teacher_bias),
        turned(conv_first),
        row(gain_first),
        row(shift_first),
        turned(conv_second),
        row(gain_second),
        row(shift_second),
        head_weight,
        row(head_bias),
    )
    found = pl.pallas_call(
        hand_on,
        out_shape=out_shape,
        in_specs=[vmem] * len(out_shape),
        out_specs=[hbm] * len(out_shape),
        scratch_shapes=[pltpu.SemaphoreType.DMA((len(out_shape),))],
    )(*[pltpu.with_memory_space_constraint(x, pltpu.VMEM) for x in found])
    logits, images_grad, first, gain1, shift1, second, gain2, shift2, head, bias = found

    def back(grad):
        return jnp.transpose(grad[:, :own].reshape(3, 3, own, depth), (0, 1, 3, 2))

    return (
        logits,
        images_grad,
        back(first),
        gain1.reshape(-1),
        shift1.reshape(-1),
        back(second),
        gain2.reshape(-1),
        shift2.reshape(-1),
        head,
        bias.reshape(-1),
    )


def solution(mesh):
    in_specs = (
        P(("batch", "chan"), None, None, None),
        P(("batch", "chan"), None, None, None),
        P(("batch", "chan")),
        P(("batch", "chan")),
        P(),
        P(),
        P(),
        P(),
        P(None, None, None, "chan"),
        P("chan"),
        P("chan"),
        P(None, None, None, "chan"),
        P("chan"),
        P("chan"),
        P("chan", None),
        P(),
    )
    out_specs = (
        P("batch", None),
        P(("batch", "chan"), None, None, None),
        P(None, None, None, "chan"),
        P("chan"),
        P("chan"),
        P(None, None, None, "chan"),
        P("chan"),
        P("chan"),
        P("chan", None),
        P(),
    )
    return jax.shard_map(shards, mesh=mesh, in_specs=in_specs, out_specs=out_specs, check_vma=False)
```

```python
import functools

import jax
import jax.numpy as jnp
from jax import lax
from jax.experimental import pallas as pl
from jax.experimental.pallas import tpu as pltpu
from jax.sharding import PartitionSpec as P

MESH = pl.DeviceIdType.MESH
F32 = jnp.float32
BF16 = jnp.bfloat16
HIGHEST = lax.Precision.HIGHEST
MICRO = 2
EPS = 1e-05
TARGET_WEIGHT = 1.0
NONTARGET_WEIGHT = 8.0
SOFTEN = 4.0
GELU_A = 0.7978845608028654
GELU_B = 0.044715
LANES = 128
QUADRATURE = (
    (0.0, 0.5333333333),
    (1.3556261800, 0.2220759220),
    (-1.3556261800, 0.2220759220),
    (2.8569700139, 0.0112574113),
    (-2.8569700139, 0.0112574113),
)


def gelu(x):
    return x * (0.5 + 0.5 * jnp.tanh(GELU_A * (x + GELU_B * (x * x * x))))


def gelu_slope(x):
    square = x * x
    t = jnp.tanh(GELU_A * (x + GELU_B * (x * square)))
    return 0.5 + 0.5 * t + (0.5 * x) * (1.0 - t * t) * (GELU_A + (3.0 * GELU_A * GELU_B) * square)


def column(shape, width):
    return lax.rem(lax.broadcasted_iota(jnp.int32, shape, 0), width)


def spread_columns(dest, lead, top, values, width):
    rows, depth = values.shape
    col = column(values.shape, width)
    left = jnp.where(col == 0, 0.0, pltpu.roll(values, 1, 0))
    right = jnp.where(col == width - 1, 0.0, pltpu.roll(values, rows - 1, 0))
    high = rows // width
    for place, part in enumerate((left, values, right)):
        dest[lead, pl.ds(top, high), :, place * depth : (place + 1) * depth] = part.astype(BF16).reshape(
            high, width, depth
        )


def halves(row):
    return (row[:, :LANES], row[:, LANES:])


def distill_grad(student, teacher, label, classes):
    lane = lax.broadcasted_iota(jnp.int32, student.shape, 1)
    live = lane < classes
    target = lane == label
    other = jnp.logical_and(live, jnp.logical_not(target))
    low = -1e30

    def parts(logits):
        soft = logits / SOFTEN
        whole_top = jnp.max(jnp.where(live, soft, low), axis=1, keepdims=True)
        rest_top = jnp.max(jnp.where(other, soft, low), axis=1, keepdims=True)
        whole_exp = jnp.where(live, jnp.exp(jnp.where(live, soft, whole_top) - whole_top), 0.0)
        rest_exp = jnp.where(other, jnp.exp(jnp.where(other, soft, rest_top) - rest_top), 0.0)
        whole_sum = jnp.sum(whole_exp, axis=1, keepdims=True)
        rest_sum = jnp.sum(rest_exp, axis=1, keepdims=True)
        whole = whole_top + jnp.log(whole_sum)
        rest = rest_top + jnp.log(rest_sum)
        true = jnp.sum(jnp.where(target, soft, 0.0), axis=1, keepdims=True)
        return (whole_exp / whole_sum, rest_exp / rest_sum, true - whole, rest - whole)

    probs, inner, _, _ = parts(student)
    _, inner_t, log_pt, log_rt = parts(teacher)
    p_true, p_rest = jnp.exp(log_pt), jnp.exp(log_rt)
    split_grad = (p_true + p_rest) * probs - jnp.where(target, p_true, 0.0) - p_rest * inner
    inner_grad = jnp.sum(inner_t, axis=1, keepdims=True) * inner - inner_t
    return SOFTEN * (TARGET_WEIGHT * split_grad + NONTARGET_WEIGHT * inner_grad)


def body(
    sizes,
    teacher_hbm,
    images_hbm,
    pair_index_hbm,
    labels_hbm,
    teacher_first_hbm,
    teacher_second_hbm,
    teacher_head_hbm,
    teacher_bias_hbm,
    first_hbm,
    gain_first_hbm,
    shift_first_hbm,
    second_hbm,
    gain_second_hbm,
    shift_second_hbm,
    head_hbm,
    head_bias_hbm,
    logits_out,
    images_grad,
    first_grad,
    gain_first_grad,
    shift_first_grad,
    second_grad,
    gain_second_grad,
    shift_second_grad,
    head_grad,
    bias_grad,
    pair_index,
    labels,
    stage_first,
    stage_second,
    images,
    teacher_head,
    teacher_bias,
    gain_first,
    shift_first,
    gain_second,
    shift_second,
    head_own,
    head_bias,
    teacher_in,
    teacher_w1,
    teacher_w2,
    teacher_x,
    teacher_h,
    teacher_head_pad,
    image_x,
    hidden_x,
    grad_x,
    w_first,
    w_second,
    own_first,
    own_second,
    y_first,
    y_second,
    slope_first,
    slope_second,
    d_hid,
    image_sib,
    hidden_sib,
    turned,
    turned_sib,
    part_all,
    part_own,
    part_send,
    part_recv,
    cross_all,
    cross_own,
    cross_send,
    cross_recv,
    last_all,
    last_own,
    last_send,
    last_recv,
    line_own,
    line_send,
    line_recv,
    sum_send,
    sum_recv,
    level_send,
    level_recv,
    level_line_send,
    level_line_recv,
    level_column,
    param_send,
    param_all,
    head_send,
    head_all,
    logit_send,
    logit_all,
    wide_send,
    wide_all,
    sync_send,
    sync_all_0,
    sync_all_1,
    sync_all_2,
    sync_all_3,
    sync_all_4,
    sync_all_5,
    sync_all_6,
    sync_all_7,
    head_sum,
    head_line_send,
    head_line_recv,
    local_sem,
    gather_send,
    gather_recv,
    wide_ssem,
    wide_rsem,
    sync_ssem,
    sync_rsem,
    known,
    plane_ssem,
    plane_rsem,
    swap_ssem,
    swap_rsem,
    part_ssem,
    part_rsem,
    cross_ssem,
    cross_rsem,
    last_ssem,
    last_rsem,
    level_ssem,
    level_rsem,
    level_line_ssem,
    level_line_rsem,
    line_ssem,
    line_rsem,
    sum_ssem,
    sum_rsem,
):
    groups, chans, own, own_pad, classes = sizes
    sync_all = (
        sync_all_0,
        sync_all_1,
        sync_all_2,
        sync_all_3,
        sync_all_4,
        sync_all_5,
        sync_all_6,
        sync_all_7,
    )
    b = lax.axis_index("batch")
    c = lax.axis_index("chan")
    me = b * chans + c
    devices = groups * chans
    sibling = c + 1 - 2 * lax.rem(c, 2)
    extent = images.shape[1]
    cells = extent * extent
    depth = images.shape[3]
    wide = teacher_hbm.shape[1]
    samples = float(devices * cells)
    chips = chans // 2
    chip, core = c // 2, lax.rem(c, 2)

    if groups == 4:
        far_first = [groups - 1 - b, lax.rem(b + 2, groups), b + 1 - 2 * lax.rem(b, 2)]
    else:
        far_first = [lax.rem(b + i, groups) for i in range(1, groups)]

    def each_device(fn):
        for peer_b in far_first + [b]:

            def one(i, carry, peer_b=peer_b):
                fn(peer_b, lax.rem(c + (chans - i), chans))
                return carry

            lax.fori_loop(1 if peer_b is b else 0, chans, one, 0, unroll=chans <= 8)

    def each_chip(fn):
        def one(i, carry):
            fn(lax.rem(chip + i, chips))
            return carry

        lax.fori_loop(1, chips, one, 0, unroll=chips <= 4)

    def each_line(fn):
        for peer_b in far_first:
            fn(peer_b)

    def signal(sem, peer_b, peer_c):
        pl.semaphore_signal(sem, inc=1, device_id=(peer_b, peer_c), device_id_type=MESH)

    def each_plane(fn):
        def one(i, carry):
            fn(lax.rem(c + i, chans))
            return carry

        lax.fori_loop(1, chans, one, 0, unroll=chans <= 8)

    if chips == 4:
        beside = chip + 1 - 2 * lax.rem(chip, 2)
        above = lax.rem(chip + 2, chips)
        near = [beside, above]
    else:
        near = [lax.rem(chip + i, chips) for i in range(1, chips)]
    if groups == 4:
        lines = [[b + 1 - 2 * lax.rem(b, 2)], [lax.rem(b + 2, groups)]]
    else:
        lines = [far_first]
    barrier = pltpu.get_barrier_semaphore()
    for peer in near:
        signal(barrier, b, 2 * peer + core)
    for line in lines:
        for peer in line:
            signal(barrier, peer, c)
    signal(barrier, b, sibling)
    greeted = len(near) + sum(len(line) for line in lines) + 1

    own_rows = own_first.shape[0]
    exact = own_rows == 9 * own
    moves = (
        (first_hbm, own_first if exact else stage_first),
        (images_hbm, images),
        (second_hbm, own_second if exact else stage_second),
        (gain_first_hbm, gain_first),
        (shift_first_hbm, shift_first),
        (gain_second_hbm, gain_second),
        (shift_second_hbm, shift_second),
        (head_hbm, head_own),
        (head_bias_hbm, head_bias),
        (teacher_bias_hbm, teacher_bias),
        (teacher_head_hbm, teacher_head),
        (teacher_hbm, teacher_in),
        (teacher_first_hbm, teacher_w1),
        (teacher_second_hbm, teacher_w2),
        (pair_index_hbm, pair_index),
        (labels_hbm, labels),
    )
    loads = [pltpu.make_async_copy(source, dest, local_sem.at[i]) for i, (source, dest) in enumerate(moves)]
    for load in loads:
        load.start()

    for ref in (image_x, hidden_x, grad_x, teacher_x, teacher_h):
        high = ref.shape[1]
        for lead in range(ref.shape[0]):
            ref[lead, 0] = jnp.zeros(ref.shape[2:], BF16)
            ref[lead, high - 1] = jnp.zeros(ref.shape[2:], BF16)
    for load in loads[:11]:
        load.wait()
    if not exact:
        for source, dest in ((stage_first, own_first), (stage_second, own_second)):
            dest[...] = jnp.zeros(dest.shape, BF16)
            dest[0 : 9 * own, :] = source[...]

    def place_own(param_row):
        at = c * own
        lane0 = lax.rem(at, LANES)
        padded = jnp.concatenate([param_row, jnp.zeros((1, LANES - own), F32)], axis=1)
        moved = pltpu.roll(jnp.broadcast_to(padded, (8, LANES)), lane0, 1)[0:1]
        upper = at >= LANES
        return (jnp.where(upper, 0.0, moved), jnp.where(upper, moved, 0.0))

    for i, ref in enumerate((gain_first, shift_first, gain_second, shift_second)):
        low_half, high_half = place_own(ref[...])
        param_send[2 * i : 2 * i + 1, :] = low_half
        param_send[2 * i + 1 : 2 * i + 2, :] = high_half
    head_send[...] = jnp.zeros(head_send.shape, BF16)
    head_send[0:own, 0:classes] = head_own[...]
    for lead in range(MICRO):
        spread_columns(image_x, lead, 1, images[lead].astype(F32).reshape(cells, depth), extent)

    t_high = 16
    t_steps = wide // t_high
    t_rows = t_high * wide

    def teacher_conv(source, kernel, top):
        total = None
        for row_off in range(3):
            window = source[0, pl.ds(top + row_off, t_high)].reshape(t_rows, 3 * depth)
            term = jnp.dot(
                window, kernel[row_off * 3 * depth : (row_off + 1) * 3 * depth, :], preferred_element_type=F32
            )
            total = term if total is None else total + term
        return total

    def teacher_fill(lead):
        def fill(i, carry):
            top = i * t_high
            values = teacher_in[lead, pl.ds(top, t_high)].astype(F32).reshape(t_rows, depth)
            spread_columns(teacher_x, 0, top + 1, values, wide)
            return carry

        lax.fori_loop(0, t_steps, fill, 0)

    def teacher_one():
        def one(i, carry):
            top = i * t_high
            spread_columns(teacher_h, 0, top + 1, gelu(teacher_conv(teacher_x, teacher_w1, top)), wide)
            return carry

        lax.fori_loop(0, t_steps, one, 0)

    def teacher_two(lead):
        def two(i, total):
            top = i * t_high
            values = teacher_in[lead, pl.ds(top, t_high)].astype(F32).reshape(t_rows, depth)
            act = gelu(teacher_conv(teacher_h, teacher_w2, top) + values)
            return total + jnp.sum(act, axis=0, keepdims=True)

        return lax.fori_loop(0, t_steps, two, jnp.zeros((1, depth), F32))

    loads[11].wait()
    teacher_fill(0)
    loads[12].wait()
    teacher_one()

    pl.semaphore_wait(barrier, greeted)
    rounds = [[(b, sibling)]] + [[(peer, c) for peer in line] for line in lines]
    if chips == 4:
        rounds = [[(b, 2 * beside + core)]] + rounds

    def say(i):
        if i < len(rounds):
            for peer in rounds[i]:
                signal(known.at[i], *peer)

    def hear(i):
        if i < len(rounds):
            pl.semaphore_wait(known.at[i], len(rounds[i]))
            say(i + 1)

    say(0)

    pieces = 3 if 3 * own % 16 == 0 else 1
    piece_rows = own_rows // pieces
    square = chips == 4 and piece_rows % 32 == 0
    held = (w_first, w_second)
    offered = (own_first, own_second)

    def gather_copy(k, rows, sem, shard, target, source=None):
        slot = held[k].at[shard, rows]
        return pltpu.make_async_remote_copy(
            src_ref=slot if source is None else source.at[rows],
            dst_ref=slot,
            send_sem=gather_send.at[k],
            recv_sem=gather_recv.at[k, sem, shard],
            device_id=(b, target),
            device_id_type=MESH,
        )

    def whole_copy(k, piece, shard, target, source=None):
        return gather_copy(k, pl.ds(piece * piece_rows, piece_rows), piece, shard, target, source)

    def half_copy(k, piece, half, shard, target, source=None):
        rows = pl.ds(piece * piece_rows + half * (piece_rows // 2), piece_rows // 2)
        return gather_copy(k, rows, 2 * piece + half, shard, target, source)

    def shard_of(peer):
        return 2 * peer + core

    def gather_start(k):
        if square:
            for late in range(2):
                for piece in range(pieces):
                    half_copy(k, piece, late, c, shard_of(beside), offered[k]).start()
                    half_copy(k, piece, 1 - late, c, shard_of(above), offered[k]).start()
        for piece in range(pieces):
            if not square:
                each_chip(lambda peer, piece=piece: whole_copy(k, piece, c, shard_of(peer), offered[k]).start())
            whole_copy(k, piece, c, sibling, offered[k]).start()
        held[k][c] = offered[k][...]

    def gather_turn(k):
        if square:
            for piece in range(pieces):
                for half, source, target in ((0, beside, above), (1, above, beside)):
                    half_copy(k, piece, half, shard_of(source), sibling).wait_recv()
                    half_copy(k, piece, half, shard_of(source), shard_of(target)).start()

    def gather_forward(k, piece):
        if square:
            half_copy(k, piece, 1, shard_of(beside), sibling).wait_recv()
            half_copy(k, piece, 0, shard_of(above), sibling).wait_recv()
            whole_copy(k, piece, shard_of(beside), sibling).start()
            whole_copy(k, piece, shard_of(above), sibling).start()
            for half in range(2):
                half_copy(k, piece, half, shard_of(3 - chip), sibling).wait_recv()
            whole_copy(k, piece, shard_of(3 - chip), sibling).start()
        else:

            def one(peer):
                whole_copy(k, piece, shard_of(peer), sibling).wait_recv()
                whole_copy(k, piece, shard_of(peer), sibling).start()

            each_chip(one)

    def gather_finish(k, piece):
        def one(i, carry):
            whole_copy(k, piece, 2 * lax.rem(chip + i, chips) + 1 - core, sibling).wait_recv()
            return carry

        lax.fori_loop(0, chips, one, 0, unroll=chips <= 4)

    def bytes_of(sem, many):
        pltpu.make_async_copy(many, many, sem).wait()

    def swap(k, source, dest):
        return pltpu.make_async_remote_copy(
            src_ref=source,
            dst_ref=dest,
            send_sem=swap_ssem.at[k],
            recv_sem=swap_rsem.at[k],
            device_id=(b, sibling),
            device_id_type=MESH,
        )

    def tile_start(send, recv, ssem, rsem):
        def one(pb, pc):
            pltpu.make_async_remote_copy(
                src_ref=send, dst_ref=recv.at[me], send_sem=ssem, recv_sem=rsem, device_id=(pb, pc), device_id_type=MESH
            ).start()

        each_device(one)
        recv[me] = send[...]

    def tile_bytes(sem, recv):
        bytes_of(sem, recv.at[pl.ds(0, devices - 1)])

    def sync_start(stage, micro, rows):
        k = stage * MICRO + micro
        for i, row in enumerate(rows):
            for j, half in enumerate(halves(row)):
                sync_send[k, 2 * i + j : 2 * i + j + 1, :] = half
        tile_start(sync_send.at[k], sync_all[k], sync_ssem.at[k], sync_rsem.at[k])

    def sync_wait(stage, micro):
        k = stage * MICRO + micro
        tile_bytes(sync_rsem.at[k], sync_all[k])
        total = jnp.sum(sync_all[k][...], axis=0)
        return [jnp.concatenate([total[2 * i : 2 * i + 1], total[2 * i + 1 : 2 * i + 2]], axis=1) for i in range(2)]

    def plane_start(k, source, slot):
        def one(pc):
            pltpu.make_async_remote_copy(
                src_ref=source(pc),
                dst_ref=slot(c),
                send_sem=plane_ssem.at[k],
                recv_sem=plane_rsem.at[k],
                device_id=(b, pc),
                device_id_type=MESH,
            ).start()

        each_plane(one)

    def plane_wait(k, many):
        pltpu.make_async_copy(many, many, plane_rsem.at[k]).wait()

    def plane_drain(k, many):
        pltpu.make_async_copy(many, many, plane_ssem.at[k]).wait()

    gather_start(0)
    swaps = [swap(0, image_x, image_sib)]
    swaps[0].start()
    for load in loads[13:]:
        load.wait()
    teacher_rows = [teacher_two(0)]

    hear(0)

    teacher_fill(1)
    hear(1)
    plane_start(0, lambda pc: param_send, lambda s: param_all.at[s])
    plane_start(1, lambda pc: head_send, lambda s: head_all.at[s])
    param_all[c] = param_send[...]
    head_all[c] = head_send[...]
    teacher_one()
    gather_turn(0)
    hear(2)
    teacher_rows.append(teacher_two(1))
    which_t = lax.broadcasted_iota(jnp.int32, (8, depth), 0)
    pooled_t = jnp.zeros((8, depth), F32)
    for m in range(MICRO):
        pooled_t = jnp.where(which_t == m, teacher_rows[m] / float(wide * wide), pooled_t)
    teacher_head_pad[...] = jnp.zeros(teacher_head_pad.shape, F32)
    teacher_head_pad[0:classes, :] = teacher_head[...].astype(F32)
    teacher_logits = lax.dot_general(
        pooled_t, teacher_head_pad[...], (((1,), (1,)), ((), ())), precision=HIGHEST, preferred_element_type=F32
    )
    lane_pad = jnp.zeros((1, LANES - classes), F32)
    teacher_logits = teacher_logits + jnp.concatenate([teacher_bias[...], lane_pad], axis=1)
    image_sum = jnp.zeros((1, depth), F32)
    for m in range(MICRO):
        image_sum = image_sum + jnp.sum(images[m].astype(F32).reshape(cells, depth), axis=0, keepdims=True)
    logit_send[0:MICRO, :] = teacher_logits[0:MICRO]
    for j, half in enumerate(halves(image_sum)):
        logit_send[MICRO + j : MICRO + j + 1, :] = half
    gather_start(1)
    hear(3)
    tile_start(logit_send, logit_all, wide_ssem.at[0], wide_rsem.at[0])

    def picker(shard, block, offset):
        at_row = lax.broadcasted_iota(jnp.int32, (depth, block), 0)
        place = lax.broadcasted_iota(jnp.int32, (depth, block), 1) - offset
        wanted = jnp.logical_and(place >= 0, place < own)
        return jnp.logical_and(wanted, at_row == shard * own + place).astype(BF16)

    def unpack(ref, block, offset):
        def one(shard, total):
            return total + jnp.dot(picker(shard, block, offset), ref[shard], preferred_element_type=F32)

        return lax.fori_loop(0, chans, one, jnp.zeros((depth, ref.shape[2]), F32)).astype(BF16)

    def weights(ref, tap):
        if own_pad == own:
            return ref[:, tap * own : (tap + 1) * own, :].reshape(depth, depth)
        return unpack(ref, own_rows, tap * own)

    def window(source, micro, row_off, col_off):
        return source[micro, row_off : row_off + extent, :, col_off * depth : (col_off + 1) * depth].reshape(
            cells, depth
        )

    def student_conv(source, micro, ref):
        total = None
        for row_off in range(3):
            for col_off in range(3):
                term = lax.dot_general(
                    window(source, micro, row_off, col_off),
                    weights(ref, row_off * 3 + col_off),
                    (((1,), (1,)), ((), ())),
                    preferred_element_type=F32,
                )
                total = term if total is None else total + term
        return total

    def student_back(source, micro, ref):
        total = None
        for row_off in range(3):
            for col_off in range(3):
                term = jnp.dot(
                    window(source, micro, row_off, col_off),
                    weights(ref, (2 - row_off) * 3 + 2 - col_off),
                    preferred_element_type=F32,
                )
                total = term if total is None else total + term
        return total

    def rows_of(m):
        return slice(m * cells, (m + 1) * cells)

    def col_sum(values):
        return jnp.sum(values, axis=0, keepdims=True)

    def moments_start(stage, m, values):
        sync_start(stage, m, (col_sum(values), col_sum(values * values)))

    def moments(stage, m):
        total, square = sync_wait(stage, m)
        center = total / samples
        spread = square / samples - center * center
        return (center, lax.rsqrt(spread + EPS))

    for piece in range(pieces):
        gather_forward(0, piece)
    for piece in range(pieces):
        gather_finish(0, piece)
    total = None
    for row_off in range(3):
        for col_off in range(3):
            term = lax.dot_general(
                image_x[:, row_off : row_off + extent, :, col_off * depth : (col_off + 1) * depth].reshape(
                    MICRO * cells, depth
                ),
                weights(w_first, row_off * 3 + col_off),
                (((1,), (1,)), ((), ())),
                preferred_element_type=F32,
            )
            total = term if total is None else total + term
    y_first[...] = total
    for m in range(MICRO):
        moments_start(0, m, total[rows_of(m), :])

    plane_wait(0, param_all.at[pl.ds(0, chans - 1)])
    plane_wait(1, head_all.at[pl.ds(0, chans - 1)])
    params = jnp.sum(param_all[...], axis=0)
    gain1, shift1, gain2, shift2 = (
        jnp.concatenate([params[2 * i : 2 * i + 1], params[2 * i + 1 : 2 * i + 2]], axis=1) for i in range(4)
    )
    if own_pad == own:
        head = head_all[...].reshape(depth, LANES)
    else:
        head = unpack(head_all, own_pad, 0)
    gather_turn(1)
    for piece in range(pieces):
        gather_forward(1, piece)
    for piece in range(pieces):
        gather_finish(1, piece)

    def three_parts(values):
        first = values.astype(BF16)
        rest = values - first.astype(F32)
        second = rest.astype(BF16)
        third = (rest - second.astype(F32)).astype(BF16)
        return jnp.concatenate([first, second, third], axis=0)

    def sum_parts(product):
        return product[0:8] + product[8:16] + product[16:24]

    norm1 = []
    for m in range(MICRO):
        center, inv = moments(0, m)
        norm1.append((center, inv))
        normed = (y_first[rows_of(m), :] - center) * (inv * gain1) + shift1
        spread_columns(hidden_x, m, 1, gelu(normed), extent)
        values = student_conv(hidden_x, m, w_second)
        y_second[rows_of(m), :] = values
        moments_start(1, m, values)
    swaps.append(swap(1, hidden_x, hidden_sib))
    swaps[1].start()
    for m in range(MICRO):
        center, inv = norm1[m]
        slope_first[rows_of(m), :] = gelu_slope((y_first[rows_of(m), :] - center) * (inv * gain1) + shift1)

    per_device = pair_index.shape[0]
    norm2, slope_scale = [], []
    which = lax.broadcasted_iota(jnp.int32, (8, depth), 0)
    which_lane = lax.broadcasted_iota(jnp.int32, (8, LANES), 0)
    for m in range(MICRO):
        center, inv = moments(1, m)
        norm2.append((center, inv))
        spread = y_second[rows_of(m), :] - center
        res = spread * (inv * gain2) + shift2 + images[m].astype(F32).reshape(cells, depth)
        square = res * res
        t = jnp.tanh(GELU_A * (res + GELU_B * (res * square)))
        half = 0.5 + 0.5 * t
        slope = half + (0.5 * res) * (1.0 - t * t) * (GELU_A + (3.0 * GELU_A * GELU_B) * square)
        slope_second[rows_of(m), :] = slope
        pooled = col_sum(res * half) / float(cells)
        slope_sum = col_sum(slope)
        slope_dot = col_sum(slope * spread) * inv
        product = jnp.dot(
            three_parts(jnp.where(which == 0, pooled, 0.0)), head, preferred_element_type=F32
        )
        logits = sum_parts(product)[0:1] + jnp.concatenate([head_bias[...], lane_pad], axis=1)
        if m == 0:
            tile_bytes(wide_rsem.at[0], logit_all)
        paired = pair_index[m]
        teacher_row = logit_all[pl.ds(paired // per_device, 1), pl.ds(lax.rem(paired, per_device), 1), :].reshape(1, LANES)
        grad = distill_grad(logits, teacher_row, labels[m], classes)
        product = lax.dot_general(
            three_parts(jnp.where(which_lane == 0, grad, 0.0)),
            head,
            (((1,), (1,)), ((), ())),
            preferred_element_type=F32,
        )
        scale = sum_parts(product)[0:1] / float(cells)
        slope_scale.append(scale)
        sync_start(2, m, (scale * slope_dot, scale * slope_sum))
        for j, part in enumerate(halves(pooled)):
            wide_send[m * 4 + j : m * 4 + j + 1, :] = part
        wide_send[m * 4 + 2 : m * 4 + 3, :] = grad
        wide_send[m * 4 + 3 : m * 4 + 4, :] = logits
    plane_start(2, lambda pc: wide_send, lambda s: wide_all.at[s])
    wide_all[c] = wide_send[...]

    def own_lanes(low_row, high_row):
        at = c * own
        row = jnp.where(at >= LANES, high_row, low_row)
        turn = lax.rem(LANES - lax.rem(at, LANES), LANES)
        return pltpu.roll(jnp.broadcast_to(row, (8, LANES)), turn, 1)[0:1, 0:own]

    def norm_back(stage, m, gain, norm, grad, y_ref):
        center, inv = norm
        totals = sync_wait(stage, m)
        scale = gain * inv
        slant = scale * inv * (totals[0] / samples)
        level = scale * (totals[1] / samples)
        return (grad * scale - (y_ref[rows_of(m), :] - center) * slant - level, totals)

    def norm_out(totals, gain_out, shift_out):
        for out, i in ((gain_out, 0), (shift_out, 1)):
            row = totals[0][i]
            for m in range(1, MICRO):
                row = row + totals[m][i]
            out[...] = own_lanes(*halves(row))

    def turn(k, m, grad):
        whole = jnp.transpose(grad).astype(BF16)
        if own_pad == own:
            turned[k, m] = whole.reshape(chips, 2, own, cells)
        else:

            def one(shard, carry):
                turned[k, m, shard // 2, lax.rem(shard, 2)] = lax.dot_general(
                    picker(shard, own_pad, 0), whole, (((0,), (0,)), ((), ())), preferred_element_type=F32
                ).astype(BF16)
                return carry

            lax.fori_loop(0, chans, one, 0)
        turns[k, m] = swap(2 + k * MICRO + m, turned.at[k, m, :, 1 - core], turned_sib.at[k, m])
        turns[k, m].start()

    turns = {}
    taps = 3 * own_pad
    per_half = groups // 2
    part_rows = taps // per_half
    part_pad = sum_send.shape[2]
    across = {0: None, 1: 2}
    planar = {0: (0, 1, 2), 1: (0, 1)}

    def send(source, dest, ssem, rsem, peer_b, peer_c):
        pltpu.make_async_remote_copy(
            src_ref=source, dst_ref=dest, send_sem=ssem, recv_sem=rsem, device_id=(peer_b, peer_c), device_id_type=MESH
        ).start()

    def cut(p):
        half, row = p // per_half, (p % per_half) * part_rows
        return slice(row, row + part_rows), slice(half * LANES, (half + 1) * LANES)

    def kernel_grad(k, source, source_sib, mean):
        mine = [(turned[k, m, :, pl.ds(core, 1)].reshape(chips * own_pad, cells), source, m) for m in range(MICRO)]
        theirs = []

        def products(sides, row_off):
            return sum(
                jnp.dot(
                    grads,
                    ref[m, row_off : row_off + extent].reshape(cells, 3 * depth),
                    preferred_element_type=F32,
                )
                for grads, ref, m in sides
            )

        def levels(sides):
            return sum(jnp.sum(grads.astype(F32), axis=1, keepdims=True) for grads, _, _ in sides)

        level = levels(mine)
        for row_off in (2, 0, 1):
            total = products(mine, row_off)
            if not theirs:
                for m in range(MICRO):
                    turns[k, m].wait_recv()
                    theirs.append((turned_sib[k, m].reshape(chips * own_pad, cells), source_sib, m))
                level = level + levels(theirs)
            total = total + products(theirs, row_off)
            for col_off in range(3):
                block = total[:, col_off * depth : (col_off + 1) * depth] - level * mean
                for i in range(chips):
                    part_all[i, col_off * own_pad : (col_off + 1) * own_pad, :] = block[i * own_pad : (i + 1) * own_pad]
            if row_off == across[k]:
                for p in range(groups):
                    rows, lanes = cut(p)
                    cross_all[p, :, 0:part_rows] = part_all[:, rows, lanes]
                    if part_pad != part_rows:
                        cross_all[p, :, part_rows:part_pad] = jnp.zeros((chips, part_pad - part_rows, LANES), F32)
                cross_send[k] = cross_all[...].astype(BF16)
                cross_own[k] = cross_all[pl.ds(b, 1)].reshape(chips, part_pad, LANES)
                each_line(
                    lambda peer: send(
                        cross_send.at[k, peer], cross_recv.at[k, b], cross_ssem.at[k], cross_rsem.at[k], peer, c
                    )
                )
                cross_recv[k, b] = jnp.zeros((chips, part_pad, LANES), BF16)
            else:
                part_send[k, row_off] = part_all[...].astype(BF16)
                part_own[k, row_off] = part_all[pl.ds(chip, 1)].reshape(taps, depth)
                each_chip(
                    lambda peer, row_off=row_off: send(
                        part_send.at[k, row_off, peer],
                        part_recv.at[k, row_off, chip],
                        part_ssem.at[k, row_off],
                        part_rsem.at[k, row_off],
                        b,
                        2 * peer + core,
                    )
                )
                part_recv[k, row_off, chip] = jnp.zeros((taps, depth), BF16)
        ones = jnp.ones((8, cells), BF16)
        level_send[k] = sum(
            lax.dot_general(ones, grads, (((1,), (1,)), ((), ())), preferred_element_type=F32)
            for grads, _, _ in mine + theirs
        )[0:1]
        each_chip(
            lambda peer: send(
                level_send.at[k], level_recv.at[k, chip], level_ssem.at[k], level_rsem.at[k], b, 2 * peer + core
            )
        )
        level_recv[k, chip] = level_send[k]

    def line_start(k):
        for row_off in planar[k]:
            bytes_of(part_rsem.at[k, row_off], part_recv.at[k, row_off, pl.ds(0, chips - 1)])
            total = part_own[k, row_off] + jnp.sum(part_recv[k, row_off].astype(F32), axis=0)
            for p in range(groups):
                line_own[k, row_off, p, 0:part_rows] = total[cut(p)]
                if part_pad != part_rows:
                    line_own[k, row_off, p, part_rows:part_pad] = jnp.zeros((part_pad - part_rows, LANES), F32)
            line_send[k, row_off] = line_own[k, row_off].astype(BF16)
            each_line(
                lambda peer, row_off=row_off: send(
                    line_send.at[k, row_off, peer],
                    line_recv.at[k, row_off, b],
                    line_ssem.at[k, row_off],
                    line_rsem.at[k, row_off],
                    peer,
                    c,
                )
            )
            line_recv[k, row_off, b] = jnp.zeros((part_pad, LANES), BF16)
        bytes_of(level_rsem.at[k], level_recv.at[k, pl.ds(0, chips - 1)])
        level_line_send[k] = jnp.sum(level_recv[k], axis=0)
        each_line(
            lambda peer: send(
                level_line_send.at[k], level_line_recv.at[k, b], level_line_ssem.at[k], level_line_rsem.at[k], peer, c
            )
        )
        level_line_recv[k, b] = level_line_send[k]

    def cross_forward(k):
        if across[k] is None:
            return
        bytes_of(cross_rsem.at[k], cross_recv.at[k, pl.ds(0, groups - 1)])
        last_all[...] = cross_own[k] + jnp.sum(cross_recv[k].astype(F32), axis=0)
        last_send[k] = last_all[...].astype(BF16)
        last_own[k] = last_all[pl.ds(chip, 1)].reshape(part_pad, LANES)
        each_chip(
            lambda peer: send(
                last_send.at[k, peer], last_recv.at[k, chip], last_ssem.at[k], last_rsem.at[k], b, 2 * peer + core
            )
        )
        last_recv[k, chip] = jnp.zeros((part_pad, LANES), BF16)

    def share(k, row_off, total):
        sum_send[k, row_off] = total.astype(BF16)
        each_line(
            lambda peer: send(
                sum_send.at[k, row_off],
                sum_recv.at[k, row_off, b],
                sum_ssem.at[k, row_off],
                sum_rsem.at[k, row_off],
                peer,
                c,
            )
        )
        sum_recv[k, row_off, b] = sum_send[k, row_off]

    def cross_sum(k):
        if across[k] is None:
            return
        bytes_of(last_rsem.at[k], last_recv.at[k, pl.ds(0, chips - 1)])
        share(k, across[k], last_own[k] + jnp.sum(last_recv[k].astype(F32), axis=0))

    def line_sum(k):
        for row_off in planar[k]:
            bytes_of(line_rsem.at[k, row_off], line_recv.at[k, row_off, pl.ds(0, groups - 1)])
            share(
                k,
                row_off,
                line_own[k, row_off, pl.ds(b, 1)].reshape(part_pad, LANES)
                + jnp.sum(line_recv[k, row_off].astype(F32), axis=0),
            )

    def sum_finish(k, mean, out):
        bytes_of(level_line_rsem.at[k], level_line_recv.at[k, pl.ds(0, groups - 1)])
        level = jnp.sum(level_line_recv[k], axis=0)
        level_column[...] = jnp.transpose(jnp.broadcast_to(level, (LANES, level.shape[1])))
        column_own = level_column[pl.ds(chip * own_pad, own_pad), :]
        back = [column_own * half for half in halves(mean)]
        for row_off in (0, 1, 2):
            bytes_of(sum_rsem.at[k, row_off], sum_recv.at[k, row_off, pl.ds(0, groups - 1)])
            for half in range(2):
                rows = sum_recv[k, row_off, half * per_half : (half + 1) * per_half, 0:part_rows].astype(F32)
                out[row_off * 3 : row_off * 3 + 3, :, half * LANES : (half + 1) * LANES] = (
                    rows.reshape(3, own_pad, LANES) + back[half][None]
                )

    totals2 = []
    for m in range(MICRO):
        found, totals = norm_back(2, m, gain2, norm2[m], slope_second[rows_of(m), :] * slope_scale[m], y_second)
        totals2.append(totals)
        spread_columns(grad_x, m, 1, found, extent)
        grad = student_back(grad_x, m, w_second) * slope_first[rows_of(m), :]
        d_hid[rows_of(m), :] = grad
        center, inv = norm1[m]
        sync_start(3, m, (col_sum(grad * (y_first[rows_of(m), :] - center)) * inv, col_sum(grad)))
    for m in range(MICRO):
        turn(0, m, grad_x[m, 1 : extent + 1, :, depth : 2 * depth].astype(F32).reshape(cells, depth))
    norm_out(totals2, gain_second_grad, shift_second_grad)

    hidden_mean = jnp.zeros((1, depth), F32)
    for node, weight in QUADRATURE:
        hidden_mean = hidden_mean + weight * gelu(shift1 + gain1 * node)
    image_rows = jnp.sum(logit_all[...], axis=0)
    image_mean = jnp.concatenate([image_rows[MICRO : MICRO + 1], image_rows[MICRO + 1 : MICRO + 2]], axis=1) / (
        MICRO * samples
    )

    swaps[0].wait_recv()
    swaps[1].wait_recv()
    kernel_grad(0, hidden_x, hidden_sib, hidden_mean)

    plane_wait(2, wide_all.at[pl.ds(0, chans - 1)])
    totals = [jnp.zeros((LANES, LANES), F32) for _ in range(2)]
    bias_row = jnp.zeros((1, LANES), F32)
    for m in range(MICRO):
        per_image = wide_all[:, m * 4 + 2, :]
        bias_row = bias_row + col_sum(per_image)
        for j in range(2):
            totals[j] = totals[j] + lax.dot_general(
                wide_all[:, m * 4 + j, :],
                per_image,
                (((0,), (0,)), ((), ())),
                precision=HIGHEST,
                preferred_element_type=F32,
            )
        logits_out[pl.ds(m, chans, stride=MICRO), :] = wide_all[:, m * 4 + 3, :][:, 0:classes]
    for j in range(2):
        head_sum[j * LANES : (j + 1) * LANES, :] = totals[j]
    head_line_send[0:own, :] = head_sum[pl.ds(c * own, own), :]
    head_line_send[own : own + 8, :] = jnp.broadcast_to(bias_row, (8, LANES))
    each_line(
        lambda peer: send(head_line_send, head_line_recv.at[b], wide_ssem.at[1], wide_rsem.at[1], peer, c)
    )
    head_line_recv[b] = head_line_send[...]

    totals1 = []
    for m in range(MICRO):
        found, totals = norm_back(3, m, gain1, norm1[m], d_hid[rows_of(m), :], y_first)
        totals1.append(totals)
        turn(1, m, found)
        spread_columns(grad_x, m, 1, found, extent)
    kernel_grad(1, image_x, image_sib, image_mean)
    for m in range(MICRO):
        images_grad[m] = (
            student_back(grad_x, m, w_first) + slope_second[rows_of(m), :] * slope_scale[m]
        ).reshape(images_grad.shape[1:])
    norm_out(totals1, gain_first_grad, shift_first_grad)
    line_start(0)
    cross_forward(0)

    cross_sum(0)
    line_start(1)
    cross_forward(1)
    line_sum(0)
    cross_sum(1)
    line_sum(1)
    bytes_of(wide_rsem.at[1], head_line_recv.at[pl.ds(0, groups - 1)])
    head_total = jnp.sum(head_line_recv[...], axis=0)
    head_grad[...] = head_total[0:own, 0:classes]
    bias_grad[...] = head_total[own : own + 1, 0:classes]
    sum_finish(0, hidden_mean, second_grad)
    sum_finish(1, image_mean, first_grad)

    tile_bytes(wide_ssem.at[0], logit_all)
    bytes_of(wide_ssem.at[1], head_line_recv.at[pl.ds(0, groups - 1)])
    plane_drain(2, wide_all.at[pl.ds(0, chans - 1)])
    for k in range(2):
        bytes_of(gather_send.at[k], held[k].at[pl.ds(0, chans - 1)])
    for k in range(4 * MICRO):
        tile_bytes(sync_ssem.at[k], sync_all[k])
    plane_drain(0, param_all.at[pl.ds(0, chans - 1)])
    plane_drain(1, head_all.at[pl.ds(0, chans - 1)])
    for copy in swaps + list(turns.values()):
        copy.wait_send()
    for k in range(2):
        for row_off in planar[k]:
            bytes_of(part_ssem.at[k, row_off], part_recv.at[k, row_off, pl.ds(0, chips - 1)])
            bytes_of(line_ssem.at[k, row_off], line_recv.at[k, row_off, pl.ds(0, groups - 1)])
        for row_off in range(3):
            bytes_of(sum_ssem.at[k, row_off], sum_recv.at[k, row_off, pl.ds(0, groups - 1)])
        if across[k] is not None:
            bytes_of(cross_ssem.at[k], cross_recv.at[k, pl.ds(0, groups - 1)])
            bytes_of(last_ssem.at[k], last_recv.at[k, pl.ds(0, chips - 1)])
        bytes_of(level_ssem.at[k], level_recv.at[k, pl.ds(0, chips - 1)])
        bytes_of(level_line_ssem.at[k], level_line_recv.at[k, pl.ds(0, groups - 1)])


def hand_on(*refs):
    count = len(refs) // 2
    copies = [pltpu.make_async_copy(refs[i], refs[count + i], refs[-1].at[i]) for i in range(count)]
    for copy in copies:
        copy.start()
    for copy in copies:
        copy.wait()


def shards(
    teacher_images,
    student_images,
    pair_index,
    labels,
    teacher_first,
    teacher_second,
    teacher_head,
    teacher_bias,
    conv_first,
    gain_first,
    shift_first,
    conv_second,
    gain_second,
    shift_second,
    head_weight,
    head_bias,
):
    groups, chans = lax.axis_size("batch"), lax.axis_size("chan")
    devices = groups * chans
    count, extent, _, depth = student_images.shape
    wide = teacher_images.shape[1]
    own = conv_first.shape[3]
    own_pad = max(own, 16)
    own_rows = -(-9 * own // 16) * 16
    classes = head_bias.shape[0]
    cells = extent * extent
    rows = count * cells
    chips = chans // 2
    taps = 3 * own_pad
    part_rows = 2 * taps // groups
    part_pad = -(-part_rows // 16) * 16

    def turned(kernel):
        return jnp.transpose(kernel, (0, 1, 3, 2)).reshape(9 * own, depth)

    def row(vector):
        return vector.reshape(1, -1)

    vmem = pl.BlockSpec(memory_space=pltpu.VMEM)
    hbm = pl.BlockSpec(memory_space=pl.ANY)
    out_shape = [
        jax.ShapeDtypeStruct((chans * count, classes), F32),
        jax.ShapeDtypeStruct(student_images.shape, F32),
        jax.ShapeDtypeStruct((9, own_pad, depth), F32),
        jax.ShapeDtypeStruct((1, own), F32),
        jax.ShapeDtypeStruct((1, own), F32),
        jax.ShapeDtypeStruct((9, own_pad, depth), F32),
        jax.ShapeDtypeStruct((1, own), F32),
        jax.ShapeDtypeStruct((1, own), F32),
        jax.ShapeDtypeStruct((own, classes), F32),
        jax.ShapeDtypeStruct((1, classes), F32),
    ]
    stage = (16, LANES) if own_rows == 9 * own else (9 * own, depth)
    scratch = [
        pltpu.SMEM(pair_index.shape, jnp.int32),
        pltpu.SMEM(labels.shape, jnp.int32),
        pltpu.VMEM(stage, BF16),
        pltpu.VMEM(stage, BF16),
        pltpu.VMEM(student_images.shape, BF16),
        pltpu.VMEM((classes, depth), BF16),
        pltpu.VMEM((1, classes), F32),
        pltpu.VMEM((1, own), F32),
        pltpu.VMEM((1, own), F32),
        pltpu.VMEM((1, own), F32),
        pltpu.VMEM((1, own), F32),
        pltpu.VMEM((own, classes), BF16),
        pltpu.VMEM((1, classes), F32),
        pltpu.VMEM(teacher_images.shape, BF16),
        pltpu.VMEM((9 * depth, depth), BF16),
        pltpu.VMEM((9 * depth, depth), BF16),
        pltpu.VMEM((1, wide + 2, wide, 3 * depth), BF16),
        pltpu.VMEM((1, wide + 2, wide, 3 * depth), BF16),
        pltpu.VMEM((LANES, depth), F32),
        pltpu.VMEM((count, extent + 2, extent, 3 * depth), BF16),
        pltpu.VMEM((count, extent + 2, extent, 3 * depth), BF16),
        pltpu.VMEM((count, extent + 2, extent, 3 * depth), BF16),
        pltpu.VMEM((chans, own_rows, depth), BF16),
        pltpu.VMEM((chans, own_rows, depth), BF16),
        pltpu.VMEM((own_rows, depth), BF16),
        pltpu.VMEM((own_rows, depth), BF16),
        pltpu.VMEM((rows, depth), F32),
        pltpu.VMEM((rows, depth), F32),
        pltpu.VMEM((rows, depth), F32),
        pltpu.VMEM((rows, depth), F32),
        pltpu.VMEM((rows, depth), F32),
        pltpu.VMEM((count, extent + 2, extent, 3 * depth), BF16),
        pltpu.VMEM((count, extent + 2, extent, 3 * depth), BF16),
        pltpu.VMEM((2, count, chips, 2, own_pad, cells), BF16),
        pltpu.VMEM((2, count, chips, own_pad, cells), BF16),
        pltpu.VMEM((chips, taps, depth), F32),
        pltpu.VMEM((2, 3, taps, depth), F32),
        pltpu.VMEM((2, 3, chips, taps, depth), BF16),
        pltpu.VMEM((2, 3, chips, taps, depth), BF16),
        pltpu.VMEM((groups, chips, part_pad, LANES), F32),
        pltpu.VMEM((2, chips, part_pad, LANES), F32),
        pltpu.VMEM((2, groups, chips, part_pad, LANES), BF16),
        pltpu.VMEM((2, groups, chips, part_pad, LANES), BF16),
        pltpu.VMEM((chips, part_pad, LANES), F32),
        pltpu.VMEM((2, part_pad, LANES), F32),
        pltpu.VMEM((2, chips, part_pad, LANES), BF16),
        pltpu.VMEM((2, chips, part_pad, LANES), BF16),
        pltpu.VMEM((2, 3, groups, part_pad, LANES), F32),
        pltpu.VMEM((2, 3, groups, part_pad, LANES), BF16),
        pltpu.VMEM((2, 3, groups, part_pad, LANES), BF16),
        pltpu.VMEM((2, 3, part_pad, LANES), BF16),
        pltpu.VMEM((2, 3, groups, part_pad, LANES), BF16),
        pltpu.VMEM((2, 1, chips * own_pad), F32),
        pltpu.VMEM((2, chips, 1, chips * own_pad), F32),
        pltpu.VMEM((2, 1, chips * own_pad), F32),
        pltpu.VMEM((2, groups, 1, chips * own_pad), F32),
        pltpu.VMEM((chips * own_pad, LANES), F32),
        pltpu.VMEM((8, LANES), F32),
        pltpu.VMEM((chans, 8, LANES), F32),
        pltpu.VMEM((own_pad, LANES), BF16),
        pltpu.VMEM((chans, own_pad, LANES), BF16),
        pltpu.VMEM((4, LANES), F32),
        pltpu.VMEM((devices, 4, LANES), F32),
        pltpu.VMEM((8, LANES), F32),
        pltpu.VMEM((chans, 8, LANES), F32),
        pltpu.VMEM((4 * MICRO, 4, LANES), F32),
        pltpu.VMEM((devices, 4, LANES), F32),
        pltpu.VMEM((devices, 4, LANES), F32),
        pltpu.VMEM((devices, 4, LANES), F32),
        pltpu.VMEM((devices, 4, LANES), F32),
        pltpu.VMEM((devices, 4, LANES), F32),
        pltpu.VMEM((devices, 4, LANES), F32),
        pltpu.VMEM((devices, 4, LANES), F32),
        pltpu.VMEM((devices, 4, LANES), F32),
        pltpu.VMEM((depth, LANES), F32),
        pltpu.VMEM((own + 8, LANES), F32),
        pltpu.VMEM((groups, own + 8, LANES), F32),
        pltpu.SemaphoreType.DMA((16,)),
        pltpu.SemaphoreType.DMA((2,)),
        pltpu.SemaphoreType.DMA((2, 6, chans)),
        pltpu.SemaphoreType.DMA((2,)),
        pltpu.SemaphoreType.DMA((2,)),
        pltpu.SemaphoreType.DMA((4 * MICRO,)),
        pltpu.SemaphoreType.DMA((4 * MICRO,)),
        pltpu.SemaphoreType.REGULAR((4,)),
        pltpu.SemaphoreType.DMA((3,)),
        pltpu.SemaphoreType.DMA((3,)),
        pltpu.SemaphoreType.DMA((2 + 2 * MICRO,)),
        pltpu.SemaphoreType.DMA((2 + 2 * MICRO,)),
        pltpu.SemaphoreType.DMA((2, 3)),
        pltpu.SemaphoreType.DMA((2, 3)),
        pltpu.SemaphoreType.DMA((2,)),
        pltpu.SemaphoreType.DMA((2,)),
        pltpu.SemaphoreType.DMA((2,)),
        pltpu.SemaphoreType.DMA((2,)),
        pltpu.SemaphoreType.DMA((2,)),
        pltpu.SemaphoreType.DMA((2,)),
        pltpu.SemaphoreType.DMA((2,)),
        pltpu.SemaphoreType.DMA((2,)),
        pltpu.SemaphoreType.DMA((2, 3)),
        pltpu.SemaphoreType.DMA((2, 3)),
        pltpu.SemaphoreType.DMA((2, 3)),
        pltpu.SemaphoreType.DMA((2, 3)),
    ]
    found = pl.pallas_call(
        functools.partial(body, (groups, chans, own, own_pad, classes)),
        out_shape=[pltpu.VMEM(out.shape, out.dtype) for out in out_shape],
        in_specs=[hbm] * 16,
        out_specs=[vmem] * 10,
        scratch_shapes=scratch,
        compiler_params=pltpu.CompilerParams(
            collective_id=0, has_side_effects=True, vmem_limit_bytes=62 * 2**20
        ),
    )(
        teacher_images,
        student_images,
        pair_index,
        labels,
        teacher_first.reshape(9 * depth, depth),
        teacher_second.reshape(9 * depth, depth),
        teacher_head.T,
        row(teacher_bias),
        turned(conv_first),
        row(gain_first),
        row(shift_first),
        turned(conv_second),
        row(gain_second),
        row(shift_second),
        head_weight,
        row(head_bias),
    )
    found = pl.pallas_call(
        hand_on,
        out_shape=out_shape,
        in_specs=[vmem] * len(out_shape),
        out_specs=[hbm] * len(out_shape),
        scratch_shapes=[pltpu.SemaphoreType.DMA((len(out_shape),))],
    )(*[pltpu.with_memory_space_constraint(x, pltpu.VMEM) for x in found])
    logits, images_grad, first, gain1, shift1, second, gain2, shift2, head, bias = found

    def back(grad):
        return jnp.transpose(grad[:, :own].reshape(3, 3, own, depth), (0, 1, 3, 2))

    return (
        logits,
        images_grad,
        back(first),
        gain1.reshape(-1),
        shift1.reshape(-1),
        back(second),
        gain2.reshape(-1),
        shift2.reshape(-1),
        head,
        bias.reshape(-1),
    )


def solution(mesh):
    in_specs = (
        P(("batch", "chan"), None, None, None),
        P(("batch", "chan"), None, None, None),
        P(("batch", "chan")),
        P(("batch", "chan")),
        P(),
        P(),
        P(),
        P(),
        P(None, None, None, "chan"),
        P("chan"),
        P("chan"),
        P(None, None, None, "chan"),
        P("chan"),
        P("chan"),
        P("chan", None),
        P(),
    )
    out_specs = (
        P("batch", None),
        P(("batch", "chan"), None, None, None),
        P(None, None, None, "chan"),
        P("chan"),
        P("chan"),
        P(None, None, None, "chan"),
        P("chan"),
        P("chan"),
        P("chan", None),
        P(),
    )
    return jax.shard_map(shards, mesh=mesh, in_specs=in_specs, out_specs=out_specs, check_vma=False)
```

```python
import functools

import jax
import jax.numpy as jnp
from jax import lax
from jax.experimental import pallas as pl
from jax.experimental.pallas import tpu as pltpu
from jax.sharding import PartitionSpec as P

MESH = pl.DeviceIdType.MESH
F32 = jnp.float32
BF16 = jnp.bfloat16
HIGHEST = lax.Precision.HIGHEST
MICRO = 2
EPS = 1e-05
TARGET_WEIGHT = 1.0
NONTARGET_WEIGHT = 8.0
SOFTEN = 4.0
GELU_A = 0.7978845608028654
GELU_B = 0.044715
LANES = 128
QUADRATURE = (
    (0.0, 0.5333333333),
    (1.3556261800, 0.2220759220),
    (-1.3556261800, 0.2220759220),
    (2.8569700139, 0.0112574113),
    (-2.8569700139, 0.0112574113),
)


def gelu(x):
    return x * (0.5 + 0.5 * jnp.tanh(GELU_A * (x + GELU_B * (x * x * x))))


def gelu_slope(x):
    square = x * x
    t = jnp.tanh(GELU_A * (x + GELU_B * (x * square)))
    return 0.5 + 0.5 * t + (0.5 * x) * (1.0 - t * t) * (GELU_A + (3.0 * GELU_A * GELU_B) * square)


def column(shape, width):
    return lax.rem(lax.broadcasted_iota(jnp.int32, shape, 0), width)


def spread_columns(dest, lead, top, values, width):
    rows, depth = values.shape
    col = column(values.shape, width)
    left = jnp.where(col == 0, 0.0, pltpu.roll(values, 1, 0))
    right = jnp.where(col == width - 1, 0.0, pltpu.roll(values, rows - 1, 0))
    high = rows // width
    for place, part in enumerate((left, values, right)):
        dest[lead, pl.ds(top, high), :, place * depth : (place + 1) * depth] = part.astype(BF16).reshape(
            high, width, depth
        )


def halves(row):
    return (row[:, :LANES], row[:, LANES:])


def distill_grad(student, teacher, label, classes):
    lane = lax.broadcasted_iota(jnp.int32, student.shape, 1)
    live = lane < classes
    target = lane == label
    other = jnp.logical_and(live, jnp.logical_not(target))
    low = -1e30

    def parts(logits):
        soft = logits / SOFTEN
        whole_top = jnp.max(jnp.where(live, soft, low), axis=1, keepdims=True)
        rest_top = jnp.max(jnp.where(other, soft, low), axis=1, keepdims=True)
        whole_exp = jnp.where(live, jnp.exp(jnp.where(live, soft, whole_top) - whole_top), 0.0)
        rest_exp = jnp.where(other, jnp.exp(jnp.where(other, soft, rest_top) - rest_top), 0.0)
        whole_sum = jnp.sum(whole_exp, axis=1, keepdims=True)
        rest_sum = jnp.sum(rest_exp, axis=1, keepdims=True)
        whole = whole_top + jnp.log(whole_sum)
        rest = rest_top + jnp.log(rest_sum)
        true = jnp.sum(jnp.where(target, soft, 0.0), axis=1, keepdims=True)
        return (whole_exp / whole_sum, rest_exp / rest_sum, true - whole, rest - whole)

    probs, inner, _, _ = parts(student)
    _, inner_t, log_pt, log_rt = parts(teacher)
    p_true, p_rest = jnp.exp(log_pt), jnp.exp(log_rt)
    split_grad = (p_true + p_rest) * probs - jnp.where(target, p_true, 0.0) - p_rest * inner
    inner_grad = jnp.sum(inner_t, axis=1, keepdims=True) * inner - inner_t
    return SOFTEN * (TARGET_WEIGHT * split_grad + NONTARGET_WEIGHT * inner_grad)


def body(
    sizes,
    teacher_hbm,
    images_hbm,
    pair_index_hbm,
    labels_hbm,
    teacher_first_hbm,
    teacher_second_hbm,
    teacher_head_hbm,
    teacher_bias_hbm,
    first_hbm,
    gain_first_hbm,
    shift_first_hbm,
    second_hbm,
    gain_second_hbm,
    shift_second_hbm,
    head_hbm,
    head_bias_hbm,
    logits_out,
    images_grad,
    first_grad,
    gain_first_grad,
    shift_first_grad,
    second_grad,
    gain_second_grad,
    shift_second_grad,
    head_grad,
    bias_grad,
    pair_index,
    labels,
    stage_first,
    stage_second,
    images,
    teacher_head,
    teacher_bias,
    gain_first,
    shift_first,
    gain_second,
    shift_second,
    head_own,
    head_bias,
    teacher_in,
    teacher_w1,
    teacher_w2,
    teacher_x,
    teacher_h,
    teacher_head_pad,
    image_x,
    hidden_x,
    grad_x,
    w_first,
    w_second,
    own_first,
    own_second,
    y_first,
    y_second,
    slope_first,
    slope_second,
    d_hid,
    image_sib,
    hidden_sib,
    turned,
    turned_sib,
    turned_terms,
    part_all,
    part_own,
    part_send,
    part_recv,
    cross_all,
    cross_own,
    cross_send,
    cross_recv,
    last_all,
    last_own,
    last_send,
    last_recv,
    line_own,
    line_send,
    line_recv,
    sum_send,
    sum_recv,
    level_send,
    level_recv,
    level_line_send,
    level_line_recv,
    level_column,
    param_send,
    param_all,
    head_send,
    head_all,
    logit_send,
    logit_all,
    wide_send,
    wide_all,
    sync_send,
    sync_all_0,
    sync_all_1,
    sync_all_2,
    sync_all_3,
    sync_all_4,
    sync_all_5,
    sync_all_6,
    sync_all_7,
    head_sum,
    head_line_send,
    head_line_recv,
    local_sem,
    gather_send,
    gather_recv,
    wide_ssem,
    wide_rsem,
    sync_ssem,
    sync_rsem,
    known,
    plane_ssem,
    plane_rsem,
    swap_ssem,
    swap_rsem,
    part_ssem,
    part_rsem,
    cross_ssem,
    cross_rsem,
    last_ssem,
    last_rsem,
    level_ssem,
    level_rsem,
    level_line_ssem,
    level_line_rsem,
    line_ssem,
    line_rsem,
    sum_ssem,
    sum_rsem,
):
    groups, chans, own, own_pad, classes = sizes
    sync_all = (
        sync_all_0,
        sync_all_1,
        sync_all_2,
        sync_all_3,
        sync_all_4,
        sync_all_5,
        sync_all_6,
        sync_all_7,
    )
    b = lax.axis_index("batch")
    c = lax.axis_index("chan")
    me = b * chans + c
    devices = groups * chans
    sibling = c + 1 - 2 * lax.rem(c, 2)
    extent = images.shape[1]
    cells = extent * extent
    depth = images.shape[3]
    wide = teacher_hbm.shape[1]
    samples = float(devices * cells)
    chips = chans // 2
    chip, core = c // 2, lax.rem(c, 2)

    if groups == 4:
        far_first = [groups - 1 - b, lax.rem(b + 2, groups), b + 1 - 2 * lax.rem(b, 2)]
    else:
        far_first = [lax.rem(b + i, groups) for i in range(1, groups)]

    def each_device(fn):
        for peer_b in far_first + [b]:

            def one(i, carry, peer_b=peer_b):
                fn(peer_b, lax.rem(c + (chans - i), chans))
                return carry

            lax.fori_loop(1 if peer_b is b else 0, chans, one, 0, unroll=chans <= 8)

    def each_chip(fn):
        def one(i, carry):
            fn(lax.rem(chip + i, chips))
            return carry

        lax.fori_loop(1, chips, one, 0, unroll=chips <= 4)

    def each_line(fn):
        for peer_b in far_first:
            fn(peer_b)

    def signal(sem, peer_b, peer_c):
        pl.semaphore_signal(sem, inc=1, device_id=(peer_b, peer_c), device_id_type=MESH)

    def each_plane(fn):
        def one(i, carry):
            fn(lax.rem(c + i, chans))
            return carry

        lax.fori_loop(1, chans, one, 0, unroll=chans <= 8)

    if chips == 4:
        beside = chip + 1 - 2 * lax.rem(chip, 2)
        above = lax.rem(chip + 2, chips)
        near = [beside, above]
    else:
        near = [lax.rem(chip + i, chips) for i in range(1, chips)]
    if groups == 4:
        lines = [[b + 1 - 2 * lax.rem(b, 2)], [lax.rem(b + 2, groups)]]
    else:
        lines = [far_first]
    barrier = pltpu.get_barrier_semaphore()
    for peer in near:
        signal(barrier, b, 2 * peer + core)
    for line in lines:
        for peer in line:
            signal(barrier, peer, c)
    signal(barrier, b, sibling)
    greeted = len(near) + sum(len(line) for line in lines) + 1

    own_rows = own_first.shape[0]
    exact = own_rows == 9 * own
    moves = (
        (first_hbm, own_first if exact else stage_first),
        (images_hbm, images),
        (second_hbm, own_second if exact else stage_second),
        (gain_first_hbm, gain_first),
        (shift_first_hbm, shift_first),
        (gain_second_hbm, gain_second),
        (shift_second_hbm, shift_second),
        (head_hbm, head_own),
        (head_bias_hbm, head_bias),
        (teacher_bias_hbm, teacher_bias),
        (teacher_head_hbm, teacher_head),
        (teacher_hbm, teacher_in),
        (teacher_first_hbm, teacher_w1),
        (teacher_second_hbm, teacher_w2),
        (pair_index_hbm, pair_index),
        (labels_hbm, labels),
    )
    loads = [pltpu.make_async_copy(source, dest, local_sem.at[i]) for i, (source, dest) in enumerate(moves)]
    for load in loads:
        load.start()

    for ref in (image_x, hidden_x, grad_x, teacher_x, teacher_h):
        high = ref.shape[1]
        for lead in range(ref.shape[0]):
            ref[lead, 0] = jnp.zeros(ref.shape[2:], BF16)
            ref[lead, high - 1] = jnp.zeros(ref.shape[2:], BF16)
    for load in loads[:11]:
        load.wait()
    if not exact:
        for source, dest in ((stage_first, own_first), (stage_second, own_second)):
            dest[...] = jnp.zeros(dest.shape, BF16)
            dest[0 : 9 * own, :] = source[...]

    def place_own(param_row):
        at = c * own
        lane0 = lax.rem(at, LANES)
        padded = jnp.concatenate([param_row, jnp.zeros((1, LANES - own), F32)], axis=1)
        moved = pltpu.roll(jnp.broadcast_to(padded, (8, LANES)), lane0, 1)[0:1]
        upper = at >= LANES
        return (jnp.where(upper, 0.0, moved), jnp.where(upper, moved, 0.0))

    for i, ref in enumerate((gain_first, shift_first, gain_second, shift_second)):
        low_half, high_half = place_own(ref[...])
        param_send[2 * i : 2 * i + 1, :] = low_half
        param_send[2 * i + 1 : 2 * i + 2, :] = high_half
    head_send[...] = jnp.zeros(head_send.shape, BF16)
    head_send[0:own, 0:classes] = head_own[...]
    for lead in range(MICRO):
        spread_columns(image_x, lead, 1, images[lead].astype(F32).reshape(cells, depth), extent)

    t_high = 16
    t_steps = wide // t_high
    t_rows = t_high * wide

    def teacher_conv(source, kernel, top):
        total = None
        for row_off in range(3):
            window = source[0, pl.ds(top + row_off, t_high)].reshape(t_rows, 3 * depth)
            term = jnp.dot(
                window, kernel[row_off * 3 * depth : (row_off + 1) * 3 * depth, :], preferred_element_type=F32
            )
            total = term if total is None else total + term
        return total

    def teacher_fill(lead):
        def fill(i, carry):
            top = i * t_high
            values = teacher_in[lead, pl.ds(top, t_high)].astype(F32).reshape(t_rows, depth)
            spread_columns(teacher_x, 0, top + 1, values, wide)
            return carry

        lax.fori_loop(0, t_steps, fill, 0)

    def teacher_one():
        def one(i, carry):
            top = i * t_high
            spread_columns(teacher_h, 0, top + 1, gelu(teacher_conv(teacher_x, teacher_w1, top)), wide)
            return carry

        lax.fori_loop(0, t_steps, one, 0)

    def teacher_two(lead):
        def two(i, total):
            top = i * t_high
            values = teacher_in[lead, pl.ds(top, t_high)].astype(F32).reshape(t_rows, depth)
            act = gelu(teacher_conv(teacher_h, teacher_w2, top) + values)
            return total + jnp.sum(act, axis=0, keepdims=True)

        return lax.fori_loop(0, t_steps, two, jnp.zeros((1, depth), F32))

    loads[11].wait()
    teacher_fill(0)
    loads[12].wait()
    teacher_one()

    pl.semaphore_wait(barrier, greeted)
    rounds = [[(b, sibling)]] + [[(peer, c) for peer in line] for line in lines]
    if chips == 4:
        rounds = [[(b, 2 * beside + core)]] + rounds

    def say(i):
        if i < len(rounds):
            for peer in rounds[i]:
                signal(known.at[i], *peer)

    def hear(i):
        if i < len(rounds):
            pl.semaphore_wait(known.at[i], len(rounds[i]))
            say(i + 1)

    say(0)

    pieces = 1
    piece_rows = own_rows // pieces
    square = chips == 4 and piece_rows % 32 == 0
    held = (w_first, w_second)
    offered = (own_first, own_second)

    def gather_copy(k, rows, sem, shard, target, source=None):
        slot = held[k].at[shard, rows]
        return pltpu.make_async_remote_copy(
            src_ref=slot if source is None else source.at[rows],
            dst_ref=slot,
            send_sem=gather_send.at[k],
            recv_sem=gather_recv.at[k, sem, shard],
            device_id=(b, target),
            device_id_type=MESH,
        )

    def whole_copy(k, piece, shard, target, source=None):
        return gather_copy(k, pl.ds(piece * piece_rows, piece_rows), piece, shard, target, source)

    def half_copy(k, piece, half, shard, target, source=None):
        rows = pl.ds(piece * piece_rows + half * (piece_rows // 2), piece_rows // 2)
        return gather_copy(k, rows, 2 * piece + half, shard, target, source)

    def shard_of(peer):
        return 2 * peer + core

    def gather_start(k):
        if square:
            for late in range(2):
                for piece in range(pieces):
                    half_copy(k, piece, late, c, shard_of(beside), offered[k]).start()
                    half_copy(k, piece, 1 - late, c, shard_of(above), offered[k]).start()
        for piece in range(pieces):
            if not square:
                each_chip(lambda peer, piece=piece: whole_copy(k, piece, c, shard_of(peer), offered[k]).start())
            whole_copy(k, piece, c, sibling, offered[k]).start()
        held[k][c] = offered[k][...]

    def gather_turn(k):
        if square:
            for piece in range(pieces):
                for half, source, target in ((0, beside, above), (1, above, beside)):
                    half_copy(k, piece, half, shard_of(source), sibling).wait_recv()
                    half_copy(k, piece, half, shard_of(source), shard_of(target)).start()

    def gather_forward(k, piece):
        if square:
            half_copy(k, piece, 1, shard_of(beside), sibling).wait_recv()
            half_copy(k, piece, 0, shard_of(above), sibling).wait_recv()
            whole_copy(k, piece, shard_of(beside), sibling).start()
            whole_copy(k, piece, shard_of(above), sibling).start()
            for half in range(2):
                half_copy(k, piece, half, shard_of(3 - chip), sibling).wait_recv()
            whole_copy(k, piece, shard_of(3 - chip), sibling).start()
        else:

            def one(peer):
                whole_copy(k, piece, shard_of(peer), sibling).wait_recv()
                whole_copy(k, piece, shard_of(peer), sibling).start()

            each_chip(one)

    def gather_finish(k, piece):
        def one(i, carry):
            whole_copy(k, piece, 2 * lax.rem(chip + i, chips) + 1 - core, sibling).wait_recv()
            return carry

        lax.fori_loop(0, chips, one, 0, unroll=chips <= 4)

    def bytes_of(sem, many):
        pltpu.make_async_copy(many, many, sem).wait()

    def swap(k, source, dest):
        return pltpu.make_async_remote_copy(
            src_ref=source,
            dst_ref=dest,
            send_sem=swap_ssem.at[k],
            recv_sem=swap_rsem.at[k],
            device_id=(b, sibling),
            device_id_type=MESH,
        )

    def tile_start(send, recv, ssem, rsem):
        def one(pb, pc):
            pltpu.make_async_remote_copy(
                src_ref=send, dst_ref=recv.at[me], send_sem=ssem, recv_sem=rsem, device_id=(pb, pc), device_id_type=MESH
            ).start()

        each_device(one)
        recv[me] = send[...]

    def tile_bytes(sem, recv):
        bytes_of(sem, recv.at[pl.ds(0, devices - 1)])

    def sync_start(stage, micro, rows):
        k = stage * MICRO + micro
        for i, row in enumerate(rows):
            for j, half in enumerate(halves(row)):
                sync_send[k, 2 * i + j : 2 * i + j + 1, :] = half
        tile_start(sync_send.at[k], sync_all[k], sync_ssem.at[k], sync_rsem.at[k])

    def sync_wait(stage, micro):
        k = stage * MICRO + micro
        tile_bytes(sync_rsem.at[k], sync_all[k])
        total = jnp.sum(sync_all[k][...], axis=0)
        return [jnp.concatenate([total[2 * i : 2 * i + 1], total[2 * i + 1 : 2 * i + 2]], axis=1) for i in range(2)]

    def plane_start(k, source, slot):
        def one(pc):
            pltpu.make_async_remote_copy(
                src_ref=source(pc),
                dst_ref=slot(c),
                send_sem=plane_ssem.at[k],
                recv_sem=plane_rsem.at[k],
                device_id=(b, pc),
                device_id_type=MESH,
            ).start()

        each_plane(one)

    def plane_wait(k, many):
        pltpu.make_async_copy(many, many, plane_rsem.at[k]).wait()

    def plane_drain(k, many):
        pltpu.make_async_copy(many, many, plane_ssem.at[k]).wait()

    gather_start(0)
    swaps = [swap(0, image_x, image_sib)]
    swaps[0].start()
    for load in loads[13:]:
        load.wait()
    teacher_rows = [teacher_two(0)]

    hear(0)

    teacher_fill(1)
    hear(1)
    plane_start(0, lambda pc: param_send, lambda s: param_all.at[s])
    plane_start(1, lambda pc: head_send, lambda s: head_all.at[s])
    param_all[c] = param_send[...]
    head_all[c] = head_send[...]
    teacher_one()
    gather_turn(0)
    hear(2)
    teacher_rows.append(teacher_two(1))
    which_t = lax.broadcasted_iota(jnp.int32, (8, depth), 0)
    pooled_t = jnp.zeros((8, depth), F32)
    for m in range(MICRO):
        pooled_t = jnp.where(which_t == m, teacher_rows[m] / float(wide * wide), pooled_t)
    teacher_head_pad[...] = jnp.zeros(teacher_head_pad.shape, F32)
    teacher_head_pad[0:classes, :] = teacher_head[...].astype(F32)
    teacher_logits = lax.dot_general(
        pooled_t, teacher_head_pad[...], (((1,), (1,)), ((), ())), precision=HIGHEST, preferred_element_type=F32
    )
    lane_pad = jnp.zeros((1, LANES - classes), F32)
    teacher_logits = teacher_logits + jnp.concatenate([teacher_bias[...], lane_pad], axis=1)
    image_sum = jnp.zeros((1, depth), F32)
    for m in range(MICRO):
        image_sum = image_sum + jnp.sum(images[m].astype(F32).reshape(cells, depth), axis=0, keepdims=True)
    logit_send[0:MICRO, :] = teacher_logits[0:MICRO]
    for j, half in enumerate(halves(image_sum)):
        logit_send[MICRO + j : MICRO + j + 1, :] = half
    gather_start(1)
    hear(3)
    tile_start(logit_send, logit_all, wide_ssem.at[0], wide_rsem.at[0])

    def picker(shard, block, offset):
        at_row = lax.broadcasted_iota(jnp.int32, (depth, block), 0)
        place = lax.broadcasted_iota(jnp.int32, (depth, block), 1) - offset
        wanted = jnp.logical_and(place >= 0, place < own)
        return jnp.logical_and(wanted, at_row == shard * own + place).astype(BF16)

    def unpack(ref, block, offset):
        def one(shard, total):
            return total + jnp.dot(picker(shard, block, offset), ref[shard], preferred_element_type=F32)

        return lax.fori_loop(0, chans, one, jnp.zeros((depth, ref.shape[2]), F32)).astype(BF16)

    def weights(ref, tap):
        if own_pad == own:
            return ref[:, tap * own : (tap + 1) * own, :].reshape(depth, depth)
        return unpack(ref, own_rows, tap * own)

    def window(source, micro, row_off, col_off):
        return source[micro, row_off : row_off + extent, :, col_off * depth : (col_off + 1) * depth].reshape(
            cells, depth
        )

    def student_conv(source, micro, ref):
        total = None
        for row_off in range(3):
            for col_off in range(3):
                term = lax.dot_general(
                    window(source, micro, row_off, col_off),
                    weights(ref, row_off * 3 + col_off),
                    (((1,), (1,)), ((), ())),
                    preferred_element_type=F32,
                )
                total = term if total is None else total + term
        return total

    def student_back(source, micro, ref):
        total = None
        for row_off in range(3):
            for col_off in range(3):
                term = jnp.dot(
                    window(source, micro, row_off, col_off),
                    weights(ref, (2 - row_off) * 3 + 2 - col_off),
                    preferred_element_type=F32,
                )
                total = term if total is None else total + term
        return total

    def rows_of(m):
        return slice(m * cells, (m + 1) * cells)

    def col_sum(values):
        return jnp.sum(values, axis=0, keepdims=True)

    def moments_start(stage, m, values):
        sync_start(stage, m, (col_sum(values), col_sum(values * values)))

    def moments(stage, m):
        total, square = sync_wait(stage, m)
        center = total / samples
        spread = square / samples - center * center
        return (center, lax.rsqrt(spread + EPS))

    for piece in range(pieces):
        gather_forward(0, piece)
    for piece in range(pieces):
        gather_finish(0, piece)
    total = None
    for row_off in range(3):
        for col_off in range(3):
            term = lax.dot_general(
                image_x[:, row_off : row_off + extent, :, col_off * depth : (col_off + 1) * depth].reshape(
                    MICRO * cells, depth
                ),
                weights(w_first, row_off * 3 + col_off),
                (((1,), (1,)), ((), ())),
                preferred_element_type=F32,
            )
            total = term if total is None else total + term
    y_first[...] = total
    for m in range(MICRO):
        moments_start(0, m, total[rows_of(m), :])

    plane_wait(0, param_all.at[pl.ds(0, chans - 1)])
    plane_wait(1, head_all.at[pl.ds(0, chans - 1)])
    params = jnp.sum(param_all[...], axis=0)
    gain1, shift1, gain2, shift2 = (
        jnp.concatenate([params[2 * i : 2 * i + 1], params[2 * i + 1 : 2 * i + 2]], axis=1) for i in range(4)
    )
    if own_pad == own:
        head = head_all[...].reshape(depth, LANES)
    else:
        head = unpack(head_all, own_pad, 0)
    gather_turn(1)
    for piece in range(pieces):
        gather_forward(1, piece)
    for piece in range(pieces):
        gather_finish(1, piece)

    def three_parts(values):
        first = values.astype(BF16)
        rest = values - first.astype(F32)
        second = rest.astype(BF16)
        third = (rest - second.astype(F32)).astype(BF16)
        return jnp.concatenate([first, second, third], axis=0)

    def sum_parts(product):
        return product[0:8] + product[8:16] + product[16:24]

    norm1 = []
    for m in range(MICRO):
        center, inv = moments(0, m)
        norm1.append((center, inv))
        normed = (y_first[rows_of(m), :] - center) * (inv * gain1) + shift1
        spread_columns(hidden_x, m, 1, gelu(normed), extent)
        values = student_conv(hidden_x, m, w_second)
        y_second[rows_of(m), :] = values
        moments_start(1, m, values)
    swaps.append(swap(1, hidden_x, hidden_sib))
    swaps[1].start()
    for m in range(MICRO):
        center, inv = norm1[m]
        slope_first[rows_of(m), :] = gelu_slope((y_first[rows_of(m), :] - center) * (inv * gain1) + shift1)

    per_device = pair_index.shape[0]
    norm2, slope_scale = [], []
    which = lax.broadcasted_iota(jnp.int32, (8, depth), 0)
    which_lane = lax.broadcasted_iota(jnp.int32, (8, LANES), 0)
    for m in range(MICRO):
        center, inv = moments(1, m)
        norm2.append((center, inv))
        spread = y_second[rows_of(m), :] - center
        res = spread * (inv * gain2) + shift2 + images[m].astype(F32).reshape(cells, depth)
        square = res * res
        t = jnp.tanh(GELU_A * (res + GELU_B * (res * square)))
        half = 0.5 + 0.5 * t
        slope = half + (0.5 * res) * (1.0 - t * t) * (GELU_A + (3.0 * GELU_A * GELU_B) * square)
        slope_second[rows_of(m), :] = slope
        pooled = col_sum(res * half) / float(cells)
        slope_sum = col_sum(slope)
        slope_dot = col_sum(slope * spread) * inv
        product = jnp.dot(
            three_parts(jnp.where(which == 0, pooled, 0.0)), head, preferred_element_type=F32
        )
        logits = sum_parts(product)[0:1] + jnp.concatenate([head_bias[...], lane_pad], axis=1)
        if m == 0:
            tile_bytes(wide_rsem.at[0], logit_all)
        paired = pair_index[m]
        teacher_row = logit_all[pl.ds(paired // per_device, 1), pl.ds(lax.rem(paired, per_device), 1), :].reshape(1, LANES)
        grad = distill_grad(logits, teacher_row, labels[m], classes)
        product = lax.dot_general(
            three_parts(jnp.where(which_lane == 0, grad, 0.0)),
            head,
            (((1,), (1,)), ((), ())),
            preferred_element_type=F32,
        )
        scale = sum_parts(product)[0:1] / float(cells)
        slope_scale.append(scale)
        sync_start(2, m, (scale * slope_dot, scale * slope_sum))
        for j, part in enumerate(halves(pooled)):
            wide_send[m * 4 + j : m * 4 + j + 1, :] = part
        wide_send[m * 4 + 2 : m * 4 + 3, :] = grad
        wide_send[m * 4 + 3 : m * 4 + 4, :] = logits
    plane_start(2, lambda pc: wide_send, lambda s: wide_all.at[s])
    wide_all[c] = wide_send[...]

    def own_lanes(low_row, high_row):
        at = c * own
        row = jnp.where(at >= LANES, high_row, low_row)
        turn = lax.rem(LANES - lax.rem(at, LANES), LANES)
        return pltpu.roll(jnp.broadcast_to(row, (8, LANES)), turn, 1)[0:1, 0:own]

    def norm_terms(stage, m, gain, norm):
        center, inv = norm
        totals = sync_wait(stage, m)
        scale = gain * inv
        slant = scale * inv * (totals[0] / samples)
        level = scale * (totals[1] / samples)
        return (scale, center, slant, level), totals

    def norm_apply(terms, grad, values):
        scale, center, slant, level = terms
        return grad * scale - (values - center) * slant - level

    def norm_out(totals, gain_out, shift_out):
        for out, i in ((gain_out, 0), (shift_out, 1)):
            row = totals[0][i]
            for m in range(1, MICRO):
                row = row + totals[m][i]
            out[...] = own_lanes(*halves(row))

    def by_core(whole, dest):
        if own_pad == own:
            dest[...] = whole.reshape(dest.shape)
        else:

            def one(shard, carry):
                dest[shard // 2, lax.rem(shard, 2)] = lax.dot_general(
                    picker(shard, own_pad, 0).astype(F32),
                    whole,
                    (((0,), (0,)), ((), ())),
                    precision=HIGHEST,
                    preferred_element_type=F32,
                )
                return carry

            lax.fori_loop(0, chans, one, 0)

    def hand(k, m, grad, values):
        by_core(jnp.transpose(grad), turned.at[k, m, 0])
        by_core(jnp.transpose(values), turned.at[k, m, 1])
        turns[k, m] = swap(2 + k * MICRO + m, turned.at[k, m, :, :, 1 - core], turned_sib.at[k, m])
        turns[k, m].start()

    def low_grads(k, m, terms):
        by_core(
            jnp.transpose(jnp.concatenate(list(terms) + [jnp.zeros((4, depth), F32)], axis=0)), turned_terms
        )
        columns = turned_terms[:, pl.ds(core, 1)].reshape(chips * own_pad, 8)
        scale, center, slant, level = (columns[:, i : i + 1] for i in range(4))
        mine = [turned[k, m, i, :, pl.ds(core, 1)].reshape(chips * own_pad, cells) for i in range(2)]
        turns[k, m].wait_recv()
        theirs = [turned_sib[k, m, i].reshape(chips * own_pad, cells) for i in range(2)]
        return [norm_apply((scale, center, slant, level), *pair).astype(BF16) for pair in (mine, theirs)]

    turns = {}
    taps = 3 * own_pad
    per_half = groups // 2
    part_rows = taps // per_half
    part_pad = sum_send.shape[2]
    across = {0: None, 1: 2}
    planar = {0: (0, 1, 2), 1: (0, 1)}

    def send(source, dest, ssem, rsem, peer_b, peer_c):
        pltpu.make_async_remote_copy(
            src_ref=source, dst_ref=dest, send_sem=ssem, recv_sem=rsem, device_id=(peer_b, peer_c), device_id_type=MESH
        ).start()

    def cut(p):
        half, row = p // per_half, (p % per_half) * part_rows
        return slice(row, row + part_rows), slice(half * LANES, (half + 1) * LANES)

    def kernel_grad(k, grads, source, source_sib, mean):
        sides = [(grads[m][i], ref, m) for m in range(MICRO) for i, ref in enumerate((source, source_sib))]
        level = sum(jnp.sum(low.astype(F32), axis=1, keepdims=True) for low, _, _ in sides)
        for row_off in (2, 0, 1):
            total = sum(
                jnp.dot(
                    low,
                    ref[m, row_off : row_off + extent].reshape(cells, 3 * depth),
                    preferred_element_type=F32,
                )
                for low, ref, m in sides
            )
            for col_off in range(3):
                block = total[:, col_off * depth : (col_off + 1) * depth] - level * mean
                for i in range(chips):
                    part_all[i, col_off * own_pad : (col_off + 1) * own_pad, :] = block[i * own_pad : (i + 1) * own_pad]
            if row_off == across[k]:
                for p in range(groups):
                    rows, lanes = cut(p)
                    cross_all[p, :, 0:part_rows] = part_all[:, rows, lanes]
                    if part_pad != part_rows:
                        cross_all[p, :, part_rows:part_pad] = jnp.zeros((chips, part_pad - part_rows, LANES), F32)
                cross_send[k] = cross_all[...].astype(BF16)
                cross_own[k] = cross_all[pl.ds(b, 1)].reshape(chips, part_pad, LANES)
                each_line(
                    lambda peer: send(
                        cross_send.at[k, peer], cross_recv.at[k, b], cross_ssem.at[k], cross_rsem.at[k], peer, c
                    )
                )
                cross_recv[k, b] = jnp.zeros((chips, part_pad, LANES), BF16)
            else:
                part_send[k, row_off] = part_all[...].astype(BF16)
                part_own[k, row_off] = part_all[pl.ds(chip, 1)].reshape(taps, depth)
                each_chip(
                    lambda peer, row_off=row_off: send(
                        part_send.at[k, row_off, peer],
                        part_recv.at[k, row_off, chip],
                        part_ssem.at[k, row_off],
                        part_rsem.at[k, row_off],
                        b,
                        2 * peer + core,
                    )
                )
                part_recv[k, row_off, chip] = jnp.zeros((taps, depth), BF16)
        ones = jnp.ones((8, cells), BF16)
        level_send[k] = sum(
            lax.dot_general(ones, low, (((1,), (1,)), ((), ())), preferred_element_type=F32) for low, _, _ in sides
        )[0:1]
        each_chip(
            lambda peer: send(
                level_send.at[k], level_recv.at[k, chip], level_ssem.at[k], level_rsem.at[k], b, 2 * peer + core
            )
        )
        level_recv[k, chip] = level_send[k]

    def line_start(k):
        for row_off in planar[k]:
            bytes_of(part_rsem.at[k, row_off], part_recv.at[k, row_off, pl.ds(0, chips - 1)])
            total = part_own[k, row_off] + jnp.sum(part_recv[k, row_off].astype(F32), axis=0)
            for p in range(groups):
                line_own[k, row_off, p, 0:part_rows] = total[cut(p)]
                if part_pad != part_rows:
                    line_own[k, row_off, p, part_rows:part_pad] = jnp.zeros((part_pad - part_rows, LANES), F32)
            line_send[k, row_off] = line_own[k, row_off].astype(BF16)
            each_line(
                lambda peer, row_off=row_off: send(
                    line_send.at[k, row_off, peer],
                    line_recv.at[k, row_off, b],
                    line_ssem.at[k, row_off],
                    line_rsem.at[k, row_off],
                    peer,
                    c,
                )
            )
            line_recv[k, row_off, b] = jnp.zeros((part_pad, LANES), BF16)
        bytes_of(level_rsem.at[k], level_recv.at[k, pl.ds(0, chips - 1)])
        level_line_send[k] = jnp.sum(level_recv[k], axis=0)
        each_line(
            lambda peer: send(
                level_line_send.at[k], level_line_recv.at[k, b], level_line_ssem.at[k], level_line_rsem.at[k], peer, c
            )
        )
        level_line_recv[k, b] = level_line_send[k]

    def cross_forward(k):
        if across[k] is None:
            return
        bytes_of(cross_rsem.at[k], cross_recv.at[k, pl.ds(0, groups - 1)])
        last_all[...] = cross_own[k] + jnp.sum(cross_recv[k].astype(F32), axis=0)
        last_send[k] = last_all[...].astype(BF16)
        last_own[k] = last_all[pl.ds(chip, 1)].reshape(part_pad, LANES)
        each_chip(
            lambda peer: send(
                last_send.at[k, peer], last_recv.at[k, chip], last_ssem.at[k], last_rsem.at[k], b, 2 * peer + core
            )
        )
        last_recv[k, chip] = jnp.zeros((part_pad, LANES), BF16)

    def share(k, row_off, total):
        sum_send[k, row_off] = total.astype(BF16)
        each_line(
            lambda peer: send(
                sum_send.at[k, row_off],
                sum_recv.at[k, row_off, b],
                sum_ssem.at[k, row_off],
                sum_rsem.at[k, row_off],
                peer,
                c,
            )
        )
        sum_recv[k, row_off, b] = sum_send[k, row_off]

    def cross_sum(k):
        if across[k] is None:
            return
        bytes_of(last_rsem.at[k], last_recv.at[k, pl.ds(0, chips - 1)])
        share(k, across[k], last_own[k] + jnp.sum(last_recv[k].astype(F32), axis=0))

    def line_sum(k):
        for row_off in planar[k]:
            bytes_of(line_rsem.at[k, row_off], line_recv.at[k, row_off, pl.ds(0, groups - 1)])
            share(
                k,
                row_off,
                line_own[k, row_off, pl.ds(b, 1)].reshape(part_pad, LANES)
                + jnp.sum(line_recv[k, row_off].astype(F32), axis=0),
            )

    def sum_finish(k, mean, out):
        bytes_of(level_line_rsem.at[k], level_line_recv.at[k, pl.ds(0, groups - 1)])
        level = jnp.sum(level_line_recv[k], axis=0)
        level_column[...] = jnp.transpose(jnp.broadcast_to(level, (LANES, level.shape[1])))
        column_own = level_column[pl.ds(chip * own_pad, own_pad), :]
        back = [column_own * half for half in halves(mean)]
        for row_off in (0, 1, 2):
            bytes_of(sum_rsem.at[k, row_off], sum_recv.at[k, row_off, pl.ds(0, groups - 1)])
            for half in range(2):
                rows = sum_recv[k, row_off, half * per_half : (half + 1) * per_half, 0:part_rows].astype(F32)
                out[row_off * 3 : row_off * 3 + 3, :, half * LANES : (half + 1) * LANES] = (
                    rows.reshape(3, own_pad, LANES) + back[half][None]
                )

    for m in range(MICRO):
        hand(0, m, slope_second[rows_of(m), :] * slope_scale[m], y_second[rows_of(m), :])
    terms2, totals2 = [], []
    for m in range(MICRO):
        terms, totals = norm_terms(2, m, gain2, norm2[m])
        terms2.append(terms)
        totals2.append(totals)
        found = norm_apply(terms, slope_second[rows_of(m), :] * slope_scale[m], y_second[rows_of(m), :])
        spread_columns(grad_x, m, 1, found, extent)
        grad = student_back(grad_x, m, w_second) * slope_first[rows_of(m), :]
        d_hid[rows_of(m), :] = grad
        center, inv = norm1[m]
        sync_start(3, m, (col_sum(grad * (y_first[rows_of(m), :] - center)) * inv, col_sum(grad)))

    hidden_mean = jnp.zeros((1, depth), F32)
    for node, weight in QUADRATURE:
        hidden_mean = hidden_mean + weight * gelu(shift1 + gain1 * node)
    image_rows = jnp.sum(logit_all[...], axis=0)
    image_mean = jnp.concatenate([image_rows[MICRO : MICRO + 1], image_rows[MICRO + 1 : MICRO + 2]], axis=1) / (
        MICRO * samples
    )

    swaps[0].wait_recv()
    swaps[1].wait_recv()
    kernel_grad(0, [low_grads(0, m, terms2[m]) for m in range(MICRO)], hidden_x, hidden_sib, hidden_mean)
    for m in range(MICRO):
        hand(1, m, d_hid[rows_of(m), :], y_first[rows_of(m), :])
    norm_out(totals2, gain_second_grad, shift_second_grad)

    plane_wait(2, wide_all.at[pl.ds(0, chans - 1)])
    totals = [jnp.zeros((LANES, LANES), F32) for _ in range(2)]
    bias_row = jnp.zeros((1, LANES), F32)
    for m in range(MICRO):
        per_image = wide_all[:, m * 4 + 2, :]
        bias_row = bias_row + col_sum(per_image)
        for j in range(2):
            totals[j] = totals[j] + lax.dot_general(
                wide_all[:, m * 4 + j, :],
                per_image,
                (((0,), (0,)), ((), ())),
                precision=HIGHEST,
                preferred_element_type=F32,
            )
        logits_out[pl.ds(m, chans, stride=MICRO), :] = wide_all[:, m * 4 + 3, :][:, 0:classes]
    for j in range(2):
        head_sum[j * LANES : (j + 1) * LANES, :] = totals[j]
    head_line_send[0:own, :] = head_sum[pl.ds(c * own, own), :]
    head_line_send[own : own + 8, :] = jnp.broadcast_to(bias_row, (8, LANES))
    each_line(
        lambda peer: send(head_line_send, head_line_recv.at[b], wide_ssem.at[1], wide_rsem.at[1], peer, c)
    )
    head_line_recv[b] = head_line_send[...]

    terms1, totals1, lows = [], [], []
    for m in range(MICRO):
        terms, totals = norm_terms(3, m, gain1, norm1[m])
        terms1.append(terms)
        totals1.append(totals)
        lows.append(low_grads(1, m, terms))
    kernel_grad(1, lows, image_x, image_sib, image_mean)
    for m in range(MICRO):
        found = norm_apply(terms1[m], d_hid[rows_of(m), :], y_first[rows_of(m), :])
        spread_columns(grad_x, m, 1, found, extent)
        images_grad[m] = (
            student_back(grad_x, m, w_first) + slope_second[rows_of(m), :] * slope_scale[m]
        ).reshape(images_grad.shape[1:])
    norm_out(totals1, gain_first_grad, shift_first_grad)
    line_start(0)
    cross_forward(0)

    cross_sum(0)
    line_start(1)
    cross_forward(1)
    line_sum(0)
    cross_sum(1)
    line_sum(1)
    bytes_of(wide_rsem.at[1], head_line_recv.at[pl.ds(0, groups - 1)])
    head_total = jnp.sum(head_line_recv[...], axis=0)
    head_grad[...] = head_total[0:own, 0:classes]
    bias_grad[...] = head_total[own : own + 1, 0:classes]
    sum_finish(0, hidden_mean, second_grad)
    sum_finish(1, image_mean, first_grad)

    tile_bytes(wide_ssem.at[0], logit_all)
    bytes_of(wide_ssem.at[1], head_line_recv.at[pl.ds(0, groups - 1)])
    plane_drain(2, wide_all.at[pl.ds(0, chans - 1)])
    for k in range(2):
        bytes_of(gather_send.at[k], held[k].at[pl.ds(0, chans - 1)])
    for k in range(4 * MICRO):
        tile_bytes(sync_ssem.at[k], sync_all[k])
    plane_drain(0, param_all.at[pl.ds(0, chans - 1)])
    plane_drain(1, head_all.at[pl.ds(0, chans - 1)])
    for copy in swaps + list(turns.values()):
        copy.wait_send()
    for k in range(2):
        for row_off in planar[k]:
            bytes_of(part_ssem.at[k, row_off], part_recv.at[k, row_off, pl.ds(0, chips - 1)])
            bytes_of(line_ssem.at[k, row_off], line_recv.at[k, row_off, pl.ds(0, groups - 1)])
        for row_off in range(3):
            bytes_of(sum_ssem.at[k, row_off], sum_recv.at[k, row_off, pl.ds(0, groups - 1)])
        if across[k] is not None:
            bytes_of(cross_ssem.at[k], cross_recv.at[k, pl.ds(0, groups - 1)])
            bytes_of(last_ssem.at[k], last_recv.at[k, pl.ds(0, chips - 1)])
        bytes_of(level_ssem.at[k], level_recv.at[k, pl.ds(0, chips - 1)])
        bytes_of(level_line_ssem.at[k], level_line_recv.at[k, pl.ds(0, groups - 1)])


def hand_on(*refs):
    count = len(refs) // 2
    copies = [pltpu.make_async_copy(refs[i], refs[count + i], refs[-1].at[i]) for i in range(count)]
    for copy in copies:
        copy.start()
    for copy in copies:
        copy.wait()


def shards(
    teacher_images,
    student_images,
    pair_index,
    labels,
    teacher_first,
    teacher_second,
    teacher_head,
    teacher_bias,
    conv_first,
    gain_first,
    shift_first,
    conv_second,
    gain_second,
    shift_second,
    head_weight,
    head_bias,
):
    groups, chans = lax.axis_size("batch"), lax.axis_size("chan")
    devices = groups * chans
    count, extent, _, depth = student_images.shape
    wide = teacher_images.shape[1]
    own = conv_first.shape[3]
    own_pad = max(own, 16)
    own_rows = -(-9 * own // 16) * 16
    classes = head_bias.shape[0]
    cells = extent * extent
    rows = count * cells
    chips = chans // 2
    taps = 3 * own_pad
    part_rows = 2 * taps // groups
    part_pad = -(-part_rows // 16) * 16

    def turned(kernel):
        return jnp.transpose(kernel, (0, 1, 3, 2)).reshape(9 * own, depth)

    def row(vector):
        return vector.reshape(1, -1)

    vmem = pl.BlockSpec(memory_space=pltpu.VMEM)
    hbm = pl.BlockSpec(memory_space=pl.ANY)
    out_shape = [
        jax.ShapeDtypeStruct((chans * count, classes), F32),
        jax.ShapeDtypeStruct(student_images.shape, F32),
        jax.ShapeDtypeStruct((9, own_pad, depth), F32),
        jax.ShapeDtypeStruct((1, own), F32),
        jax.ShapeDtypeStruct((1, own), F32),
        jax.ShapeDtypeStruct((9, own_pad, depth), F32),
        jax.ShapeDtypeStruct((1, own), F32),
        jax.ShapeDtypeStruct((1, own), F32),
        jax.ShapeDtypeStruct((own, classes), F32),
        jax.ShapeDtypeStruct((1, classes), F32),
    ]
    stage = (16, LANES) if own_rows == 9 * own else (9 * own, depth)
    scratch = [
        pltpu.SMEM(pair_index.shape, jnp.int32),
        pltpu.SMEM(labels.shape, jnp.int32),
        pltpu.VMEM(stage, BF16),
        pltpu.VMEM(stage, BF16),
        pltpu.VMEM(student_images.shape, BF16),
        pltpu.VMEM((classes, depth), BF16),
        pltpu.VMEM((1, classes), F32),
        pltpu.VMEM((1, own), F32),
        pltpu.VMEM((1, own), F32),
        pltpu.VMEM((1, own), F32),
        pltpu.VMEM((1, own), F32),
        pltpu.VMEM((own, classes), BF16),
        pltpu.VMEM((1, classes), F32),
        pltpu.VMEM(teacher_images.shape, BF16),
        pltpu.VMEM((9 * depth, depth), BF16),
        pltpu.VMEM((9 * depth, depth), BF16),
        pltpu.VMEM((1, wide + 2, wide, 3 * depth), BF16),
        pltpu.VMEM((1, wide + 2, wide, 3 * depth), BF16),
        pltpu.VMEM((LANES, depth), F32),
        pltpu.VMEM((count, extent + 2, extent, 3 * depth), BF16),
        pltpu.VMEM((count, extent + 2, extent, 3 * depth), BF16),
        pltpu.VMEM((count, extent + 2, extent, 3 * depth), BF16),
        pltpu.VMEM((chans, own_rows, depth), BF16),
        pltpu.VMEM((chans, own_rows, depth), BF16),
        pltpu.VMEM((own_rows, depth), BF16),
        pltpu.VMEM((own_rows, depth), BF16),
        pltpu.VMEM((rows, depth), F32),
        pltpu.VMEM((rows, depth), F32),
        pltpu.VMEM((rows, depth), F32),
        pltpu.VMEM((rows, depth), F32),
        pltpu.VMEM((rows, depth), F32),
        pltpu.VMEM((count, extent + 2, extent, 3 * depth), BF16),
        pltpu.VMEM((count, extent + 2, extent, 3 * depth), BF16),
        pltpu.VMEM((2, count, 2, chips, 2, own_pad, cells), F32),
        pltpu.VMEM((2, count, 2, chips, own_pad, cells), F32),
        pltpu.VMEM((chips, 2, own_pad, 8), F32),
        pltpu.VMEM((chips, taps, depth), F32),
        pltpu.VMEM((2, 3, taps, depth), F32),
        pltpu.VMEM((2, 3, chips, taps, depth), BF16),
        pltpu.VMEM((2, 3, chips, taps, depth), BF16),
        pltpu.VMEM((groups, chips, part_pad, LANES), F32),
        pltpu.VMEM((2, chips, part_pad, LANES), F32),
        pltpu.VMEM((2, groups, chips, part_pad, LANES), BF16),
        pltpu.VMEM((2, groups, chips, part_pad, LANES), BF16),
        pltpu.VMEM((chips, part_pad, LANES), F32),
        pltpu.VMEM((2, part_pad, LANES), F32),
        pltpu.VMEM((2, chips, part_pad, LANES), BF16),
        pltpu.VMEM((2, chips, part_pad, LANES), BF16),
        pltpu.VMEM((2, 3, groups, part_pad, LANES), F32),
        pltpu.VMEM((2, 3, groups, part_pad, LANES), BF16),
        pltpu.VMEM((2, 3, groups, part_pad, LANES), BF16),
        pltpu.VMEM((2, 3, part_pad, LANES), BF16),
        pltpu.VMEM((2, 3, groups, part_pad, LANES), BF16),
        pltpu.VMEM((2, 1, chips * own_pad), F32),
        pltpu.VMEM((2, chips, 1, chips * own_pad), F32),
        pltpu.VMEM((2, 1, chips * own_pad), F32),
        pltpu.VMEM((2, groups, 1, chips * own_pad), F32),
        pltpu.VMEM((chips * own_pad, LANES), F32),
        pltpu.VMEM((8, LANES), F32),
        pltpu.VMEM((chans, 8, LANES), F32),
        pltpu.VMEM((own_pad, LANES), BF16),
        pltpu.VMEM((chans, own_pad, LANES), BF16),
        pltpu.VMEM((4, LANES), F32),
        pltpu.VMEM((devices, 4, LANES), F32),
        pltpu.VMEM((8, LANES), F32),
        pltpu.VMEM((chans, 8, LANES), F32),
        pltpu.VMEM((4 * MICRO, 4, LANES), F32),
        pltpu.VMEM((devices, 4, LANES), F32),
        pltpu.VMEM((devices, 4, LANES), F32),
        pltpu.VMEM((devices, 4, LANES), F32),
        pltpu.VMEM((devices, 4, LANES), F32),
        pltpu.VMEM((devices, 4, LANES), F32),
        pltpu.VMEM((devices, 4, LANES), F32),
        pltpu.VMEM((devices, 4, LANES), F32),
        pltpu.VMEM((devices, 4, LANES), F32),
        pltpu.VMEM((depth, LANES), F32),
        pltpu.VMEM((own + 8, LANES), F32),
        pltpu.VMEM((groups, own + 8, LANES), F32),
        pltpu.SemaphoreType.DMA((16,)),
        pltpu.SemaphoreType.DMA((2,)),
        pltpu.SemaphoreType.DMA((2, 6, chans)),
        pltpu.SemaphoreType.DMA((2,)),
        pltpu.SemaphoreType.DMA((2,)),
        pltpu.SemaphoreType.DMA((4 * MICRO,)),
        pltpu.SemaphoreType.DMA((4 * MICRO,)),
        pltpu.SemaphoreType.REGULAR((4,)),
        pltpu.SemaphoreType.DMA((3,)),
        pltpu.SemaphoreType.DMA((3,)),
        pltpu.SemaphoreType.DMA((2 + 2 * MICRO,)),
        pltpu.SemaphoreType.DMA((2 + 2 * MICRO,)),
        pltpu.SemaphoreType.DMA((2, 3)),
        pltpu.SemaphoreType.DMA((2, 3)),
        pltpu.SemaphoreType.DMA((2,)),
        pltpu.SemaphoreType.DMA((2,)),
        pltpu.SemaphoreType.DMA((2,)),
        pltpu.SemaphoreType.DMA((2,)),
        pltpu.SemaphoreType.DMA((2,)),
        pltpu.SemaphoreType.DMA((2,)),
        pltpu.SemaphoreType.DMA((2,)),
        pltpu.SemaphoreType.DMA((2,)),
        pltpu.SemaphoreType.DMA((2, 3)),
        pltpu.SemaphoreType.DMA((2, 3)),
        pltpu.SemaphoreType.DMA((2, 3)),
        pltpu.SemaphoreType.DMA((2, 3)),
    ]
    found = pl.pallas_call(
        functools.partial(body, (groups, chans, own, own_pad, classes)),
        out_shape=[pltpu.VMEM(out.shape, out.dtype) for out in out_shape],
        in_specs=[hbm] * 16,
        out_specs=[vmem] * 10,
        scratch_shapes=scratch,
        compiler_params=pltpu.CompilerParams(
            collective_id=0, has_side_effects=True, vmem_limit_bytes=62 * 2**20
        ),
    )(
        teacher_images,
        student_images,
        pair_index,
        labels,
        teacher_first.reshape(9 * depth, depth),
        teacher_second.reshape(9 * depth, depth),
        teacher_head.T,
        row(teacher_bias),
        turned(conv_first),
        row(gain_first),
        row(shift_first),
        turned(conv_second),
        row(gain_second),
        row(shift_second),
        head_weight,
        row(head_bias),
    )
    found = pl.pallas_call(
        hand_on,
        out_shape=out_shape,
        in_specs=[vmem] * len(out_shape),
        out_specs=[hbm] * len(out_shape),
        scratch_shapes=[pltpu.SemaphoreType.DMA((len(out_shape),))],
    )(*[pltpu.with_memory_space_constraint(x, pltpu.VMEM) for x in found])
    logits, images_grad, first, gain1, shift1, second, gain2, shift2, head, bias = found

    def back(grad):
        return jnp.transpose(grad[:, :own].reshape(3, 3, own, depth), (0, 1, 3, 2))

    return (
        logits,
        images_grad,
        back(first),
        gain1.reshape(-1),
        shift1.reshape(-1),
        back(second),
        gain2.reshape(-1),
        shift2.reshape(-1),
        head,
        bias.reshape(-1),
    )


def solution(mesh):
    in_specs = (
        P(("batch", "chan"), None, None, None),
        P(("batch", "chan"), None, None, None),
        P(("batch", "chan")),
        P(("batch", "chan")),
        P(),
        P(),
        P(),
        P(),
        P(None, None, None, "chan"),
        P("chan"),
        P("chan"),
        P(None, None, None, "chan"),
        P("chan"),
        P("chan"),
        P("chan", None),
        P(),
    )
    out_specs = (
        P("batch", None),
        P(("batch", "chan"), None, None, None),
        P(None, None, None, "chan"),
        P("chan"),
        P("chan"),
        P(None, None, None, "chan"),
        P("chan"),
        P("chan"),
        P("chan", None),
        P(),
    )
    return jax.shard_map(shards, mesh=mesh, in_specs=in_specs, out_specs=out_specs, check_vma=False)
```

```python
import functools

import jax
import jax.numpy as jnp
from jax import lax
from jax.experimental import pallas as pl
from jax.experimental.pallas import tpu as pltpu
from jax.sharding import PartitionSpec as P

MESH = pl.DeviceIdType.MESH
F32 = jnp.float32
BF16 = jnp.bfloat16
HIGHEST = lax.Precision.HIGHEST
MICRO = 2
EPS = 1e-05
TARGET_WEIGHT = 1.0
NONTARGET_WEIGHT = 8.0
SOFTEN = 4.0
GELU_A = 0.7978845608028654
GELU_B = 0.044715
LANES = 128
QUADRATURE = (
    (0.0, 0.5333333333),
    (1.3556261800, 0.2220759220),
    (-1.3556261800, 0.2220759220),
    (2.8569700139, 0.0112574113),
    (-2.8569700139, 0.0112574113),
)


def gelu(x):
    return x * (0.5 + 0.5 * jnp.tanh(GELU_A * (x + GELU_B * (x * x * x))))


def gelu_slope(x):
    square = x * x
    t = jnp.tanh(GELU_A * (x + GELU_B * (x * square)))
    return 0.5 + 0.5 * t + (0.5 * x) * (1.0 - t * t) * (GELU_A + (3.0 * GELU_A * GELU_B) * square)


def column(shape, width):
    return lax.rem(lax.broadcasted_iota(jnp.int32, shape, 0), width)


def spread_columns(dest, lead, top, values, width):
    rows, depth = values.shape
    col = column(values.shape, width)
    left = jnp.where(col == 0, 0.0, pltpu.roll(values, 1, 0))
    right = jnp.where(col == width - 1, 0.0, pltpu.roll(values, rows - 1, 0))
    high = rows // width
    for place, part in enumerate((left, values, right)):
        dest[lead, pl.ds(top, high), :, place * depth : (place + 1) * depth] = part.astype(BF16).reshape(
            high, width, depth
        )


def halves(row):
    return (row[:, :LANES], row[:, LANES:])


def soft_parts(logits, label, classes):
    lane = lax.broadcasted_iota(jnp.int32, logits.shape, 1)
    live = lane < classes
    target = lane == label
    other = jnp.logical_and(live, jnp.logical_not(target))
    low = -1e30
    soft = logits / SOFTEN
    whole_top = jnp.max(jnp.where(live, soft, low), axis=1, keepdims=True)
    rest_top = jnp.max(jnp.where(other, soft, low), axis=1, keepdims=True)
    whole_exp = jnp.where(live, jnp.exp(jnp.where(live, soft, whole_top) - whole_top), 0.0)
    rest_exp = jnp.where(other, jnp.exp(jnp.where(other, soft, rest_top) - rest_top), 0.0)
    whole_sum = jnp.sum(whole_exp, axis=1, keepdims=True)
    rest_sum = jnp.sum(rest_exp, axis=1, keepdims=True)
    whole = whole_top + jnp.log(whole_sum)
    rest = rest_top + jnp.log(rest_sum)
    true = jnp.sum(jnp.where(target, soft, 0.0), axis=1, keepdims=True)
    return (whole_exp / whole_sum, rest_exp / rest_sum, true - whole, rest - whole, target)


def teacher_terms(teacher, label, classes):
    _, inner, log_true, log_rest, target = soft_parts(teacher, label, classes)
    true, rest = jnp.exp(log_true), jnp.exp(log_rest)
    fixed = TARGET_WEIGHT * jnp.where(target, true, 0.0) + NONTARGET_WEIGHT * inner
    return (
        SOFTEN * TARGET_WEIGHT * (true + rest),
        SOFTEN * (NONTARGET_WEIGHT * jnp.sum(inner, axis=1, keepdims=True) - TARGET_WEIGHT * rest),
        SOFTEN * fixed,
    )


def distill_grad(student, terms, label, classes):
    probs, inner, _, _, _ = soft_parts(student, label, classes)
    whole, rest, fixed = terms
    return whole * probs + rest * inner - fixed


def body(
    sizes,
    teacher_hbm,
    images_hbm,
    pair_index_hbm,
    labels_hbm,
    teacher_first_hbm,
    teacher_second_hbm,
    teacher_head_hbm,
    teacher_bias_hbm,
    first_hbm,
    gain_first_hbm,
    shift_first_hbm,
    second_hbm,
    gain_second_hbm,
    shift_second_hbm,
    head_hbm,
    head_bias_hbm,
    logits_out,
    images_grad,
    first_grad,
    gain_first_grad,
    shift_first_grad,
    second_grad,
    gain_second_grad,
    shift_second_grad,
    head_grad,
    bias_grad,
    pair_index,
    labels,
    stage_first,
    stage_second,
    images,
    teacher_head,
    teacher_bias,
    gain_first,
    shift_first,
    gain_second,
    shift_second,
    head_own,
    head_bias,
    teacher_in,
    teacher_w1,
    teacher_w2,
    teacher_x,
    teacher_h,
    teacher_head_pad,
    image_x,
    hidden_x,
    grad_x,
    w_first,
    w_second,
    own_first,
    own_second,
    y_first,
    y_second,
    slope_first,
    slope_second,
    d_hid,
    image_sib,
    hidden_sib,
    turned,
    turned_sib,
    turned_terms,
    part_all,
    part_own,
    part_send,
    part_recv,
    cross_all,
    cross_own,
    cross_send,
    cross_recv,
    last_all,
    last_own,
    last_send,
    last_recv,
    line_own,
    line_send,
    line_recv,
    sum_send,
    sum_recv,
    level_send,
    level_recv,
    level_line_send,
    level_line_recv,
    level_column,
    param_send,
    param_all,
    head_send,
    head_all,
    logit_send,
    logit_all,
    wide_send,
    wide_all,
    sync_send,
    sync_all_0,
    sync_all_1,
    sync_all_2,
    sync_all_3,
    sync_all_4,
    sync_all_5,
    sync_all_6,
    sync_all_7,
    head_sum,
    head_line_send,
    head_line_recv,
    local_sem,
    gather_send,
    gather_recv,
    wide_ssem,
    wide_rsem,
    sync_ssem,
    sync_rsem,
    known,
    plane_ssem,
    plane_rsem,
    swap_ssem,
    swap_rsem,
    part_ssem,
    part_rsem,
    cross_ssem,
    cross_rsem,
    last_ssem,
    last_rsem,
    level_ssem,
    level_rsem,
    level_line_ssem,
    level_line_rsem,
    line_ssem,
    line_rsem,
    sum_ssem,
    sum_rsem,
):
    groups, chans, own, own_pad, classes = sizes
    sync_all = (
        sync_all_0,
        sync_all_1,
        sync_all_2,
        sync_all_3,
        sync_all_4,
        sync_all_5,
        sync_all_6,
        sync_all_7,
    )
    b = lax.axis_index("batch")
    c = lax.axis_index("chan")
    me = b * chans + c
    devices = groups * chans
    sibling = c + 1 - 2 * lax.rem(c, 2)
    extent = images.shape[1]
    cells = extent * extent
    depth = images.shape[3]
    wide = teacher_hbm.shape[1]
    samples = float(devices * cells)
    chips = chans // 2
    chip, core = c // 2, lax.rem(c, 2)

    if groups == 4:
        far_first = [groups - 1 - b, lax.rem(b + 2, groups), b + 1 - 2 * lax.rem(b, 2)]
    else:
        far_first = [lax.rem(b + i, groups) for i in range(1, groups)]

    def each_device(fn):
        for peer_b in far_first + [b]:

            def one(i, carry, peer_b=peer_b):
                fn(peer_b, lax.rem(c + (chans - i), chans))
                return carry

            lax.fori_loop(1 if peer_b is b else 0, chans, one, 0, unroll=chans <= 8)

    def each_chip(fn):
        def one(i, carry):
            fn(lax.rem(chip + i, chips))
            return carry

        lax.fori_loop(1, chips, one, 0, unroll=chips <= 4)

    def each_line(fn):
        for peer_b in far_first:
            fn(peer_b)

    def signal(sem, peer_b, peer_c):
        pl.semaphore_signal(sem, inc=1, device_id=(peer_b, peer_c), device_id_type=MESH)

    def each_plane(fn):
        def one(i, carry):
            fn(lax.rem(c + i, chans))
            return carry

        lax.fori_loop(1, chans, one, 0, unroll=chans <= 8)

    if chips == 4:
        beside = chip + 1 - 2 * lax.rem(chip, 2)
        above = lax.rem(chip + 2, chips)
        near = [beside, above]
    else:
        near = [lax.rem(chip + i, chips) for i in range(1, chips)]
    if groups == 4:
        lines = [[b + 1 - 2 * lax.rem(b, 2)], [lax.rem(b + 2, groups)]]
    else:
        lines = [far_first]
    barrier = pltpu.get_barrier_semaphore()
    for peer in near:
        signal(barrier, b, 2 * peer + core)
    for line in lines:
        for peer in line:
            signal(barrier, peer, c)
    signal(barrier, b, sibling)
    greeted = len(near) + sum(len(line) for line in lines) + 1

    own_rows = own_first.shape[0]
    exact = own_rows == 9 * own
    moves = (
        (first_hbm, own_first if exact else stage_first),
        (images_hbm, images),
        (second_hbm, own_second if exact else stage_second),
        (gain_first_hbm, gain_first),
        (shift_first_hbm, shift_first),
        (gain_second_hbm, gain_second),
        (shift_second_hbm, shift_second),
        (head_hbm, head_own),
        (head_bias_hbm, head_bias),
        (teacher_bias_hbm, teacher_bias),
        (teacher_head_hbm, teacher_head),
        (teacher_hbm, teacher_in),
        (teacher_first_hbm, teacher_w1),
        (teacher_second_hbm, teacher_w2),
        (pair_index_hbm, pair_index),
        (labels_hbm, labels),
    )
    loads = [pltpu.make_async_copy(source, dest, local_sem.at[i]) for i, (source, dest) in enumerate(moves)]
    for load in loads:
        load.start()

    for ref in (image_x, hidden_x, grad_x, teacher_x, teacher_h):
        high = ref.shape[1]
        for lead in range(ref.shape[0]):
            ref[lead, 0] = jnp.zeros(ref.shape[2:], BF16)
            ref[lead, high - 1] = jnp.zeros(ref.shape[2:], BF16)
    for load in loads[:11]:
        load.wait()
    if not exact:
        for source, dest in ((stage_first, own_first), (stage_second, own_second)):
            dest[...] = jnp.zeros(dest.shape, BF16)
            dest[0 : 9 * own, :] = source[...]

    def place_own(param_row):
        at = c * own
        lane0 = lax.rem(at, LANES)
        padded = jnp.concatenate([param_row, jnp.zeros((1, LANES - own), F32)], axis=1)
        moved = pltpu.roll(jnp.broadcast_to(padded, (8, LANES)), lane0, 1)[0:1]
        upper = at >= LANES
        return (jnp.where(upper, 0.0, moved), jnp.where(upper, moved, 0.0))

    for i, ref in enumerate((gain_first, shift_first, gain_second, shift_second)):
        low_half, high_half = place_own(ref[...])
        param_send[2 * i : 2 * i + 1, :] = low_half
        param_send[2 * i + 1 : 2 * i + 2, :] = high_half
    head_send[...] = jnp.zeros(head_send.shape, BF16)
    head_send[0:own, 0:classes] = head_own[...]
    for lead in range(MICRO):
        spread_columns(image_x, lead, 1, images[lead].astype(F32).reshape(cells, depth), extent)

    t_high = 16
    t_steps = wide // t_high
    t_rows = t_high * wide

    def teacher_conv(source, kernel, top):
        total = None
        for row_off in range(3):
            window = source[0, pl.ds(top + row_off, t_high)].reshape(t_rows, 3 * depth)
            term = jnp.dot(
                window, kernel[row_off * 3 * depth : (row_off + 1) * 3 * depth, :], preferred_element_type=F32
            )
            total = term if total is None else total + term
        return total

    def teacher_fill(lead):
        def fill(i, carry):
            top = i * t_high
            values = teacher_in[lead, pl.ds(top, t_high)].astype(F32).reshape(t_rows, depth)
            spread_columns(teacher_x, 0, top + 1, values, wide)
            return carry

        lax.fori_loop(0, t_steps, fill, 0)

    def teacher_one():
        def one(i, carry):
            top = i * t_high
            spread_columns(teacher_h, 0, top + 1, gelu(teacher_conv(teacher_x, teacher_w1, top)), wide)
            return carry

        lax.fori_loop(0, t_steps, one, 0)

    def teacher_two(lead):
        def two(i, total):
            top = i * t_high
            values = teacher_in[lead, pl.ds(top, t_high)].astype(F32).reshape(t_rows, depth)
            act = gelu(teacher_conv(teacher_h, teacher_w2, top) + values)
            return total + jnp.sum(act, axis=0, keepdims=True)

        return lax.fori_loop(0, t_steps, two, jnp.zeros((1, depth), F32))

    loads[11].wait()
    teacher_fill(0)
    loads[12].wait()
    teacher_one()

    pl.semaphore_wait(barrier, greeted)
    rounds = [[(b, sibling)]] + [[(peer, c) for peer in line] for line in lines]
    if chips == 4:
        rounds = [[(b, 2 * beside + core)]] + rounds

    def say(i):
        if i < len(rounds):
            for peer in rounds[i]:
                signal(known.at[i], *peer)

    def hear(i):
        if i < len(rounds):
            pl.semaphore_wait(known.at[i], len(rounds[i]))
            say(i + 1)

    say(0)

    pieces = 1
    piece_rows = own_rows // pieces
    square = chips == 4 and piece_rows % 32 == 0
    held = (w_first, w_second)
    offered = (own_first, own_second)

    def gather_copy(k, rows, sem, shard, target, source=None):
        slot = held[k].at[shard, rows]
        return pltpu.make_async_remote_copy(
            src_ref=slot if source is None else source.at[rows],
            dst_ref=slot,
            send_sem=gather_send.at[k],
            recv_sem=gather_recv.at[k, sem, shard],
            device_id=(b, target),
            device_id_type=MESH,
        )

    def whole_copy(k, piece, shard, target, source=None):
        return gather_copy(k, pl.ds(piece * piece_rows, piece_rows), piece, shard, target, source)

    def half_copy(k, piece, half, shard, target, source=None):
        rows = pl.ds(piece * piece_rows + half * (piece_rows // 2), piece_rows // 2)
        return gather_copy(k, rows, 2 * piece + half, shard, target, source)

    def shard_of(peer):
        return 2 * peer + core

    def gather_start(k):
        if square:
            for late in range(2):
                for piece in range(pieces):
                    half_copy(k, piece, late, c, shard_of(beside), offered[k]).start()
                    half_copy(k, piece, 1 - late, c, shard_of(above), offered[k]).start()
        for piece in range(pieces):
            if not square:
                each_chip(lambda peer, piece=piece: whole_copy(k, piece, c, shard_of(peer), offered[k]).start())
            whole_copy(k, piece, c, sibling, offered[k]).start()
        held[k][c] = offered[k][...]

    def gather_turn(k):
        if square:
            for piece in range(pieces):
                for half, source, target in ((0, beside, above), (1, above, beside)):
                    half_copy(k, piece, half, shard_of(source), sibling).wait_recv()
                    half_copy(k, piece, half, shard_of(source), shard_of(target)).start()

    def gather_forward(k, piece):
        if square:
            half_copy(k, piece, 1, shard_of(beside), sibling).wait_recv()
            half_copy(k, piece, 0, shard_of(above), sibling).wait_recv()
            whole_copy(k, piece, shard_of(beside), sibling).start()
            whole_copy(k, piece, shard_of(above), sibling).start()
            for half in range(2):
                half_copy(k, piece, half, shard_of(3 - chip), sibling).wait_recv()
            whole_copy(k, piece, shard_of(3 - chip), sibling).start()
        else:

            def one(peer):
                whole_copy(k, piece, shard_of(peer), sibling).wait_recv()
                whole_copy(k, piece, shard_of(peer), sibling).start()

            each_chip(one)

    def gather_finish(k, piece):
        def one(i, carry):
            whole_copy(k, piece, 2 * lax.rem(chip + i, chips) + 1 - core, sibling).wait_recv()
            return carry

        lax.fori_loop(0, chips, one, 0, unroll=chips <= 4)

    def bytes_of(sem, many):
        pltpu.make_async_copy(many, many, sem).wait()

    def swap(k, source, dest):
        return pltpu.make_async_remote_copy(
            src_ref=source,
            dst_ref=dest,
            send_sem=swap_ssem.at[k],
            recv_sem=swap_rsem.at[k],
            device_id=(b, sibling),
            device_id_type=MESH,
        )

    def tile_start(send, recv, ssem, rsem):
        def one(pb, pc):
            pltpu.make_async_remote_copy(
                src_ref=send, dst_ref=recv.at[me], send_sem=ssem, recv_sem=rsem, device_id=(pb, pc), device_id_type=MESH
            ).start()

        each_device(one)
        recv[me] = send[...]

    def tile_bytes(sem, recv):
        bytes_of(sem, recv.at[pl.ds(0, devices - 1)])

    def sync_start(stage, micro, rows):
        k = stage * MICRO + micro
        for i, row in enumerate(rows):
            for j, half in enumerate(halves(row)):
                sync_send[k, 2 * i + j : 2 * i + j + 1, :] = half
        tile_start(sync_send.at[k], sync_all[k], sync_ssem.at[k], sync_rsem.at[k])

    def sync_wait(stage, micro):
        k = stage * MICRO + micro
        tile_bytes(sync_rsem.at[k], sync_all[k])
        total = jnp.sum(sync_all[k][...], axis=0)
        return [jnp.concatenate([total[2 * i : 2 * i + 1], total[2 * i + 1 : 2 * i + 2]], axis=1) for i in range(2)]

    def plane_start(k, source, slot):
        def one(pc):
            pltpu.make_async_remote_copy(
                src_ref=source(pc),
                dst_ref=slot(c),
                send_sem=plane_ssem.at[k],
                recv_sem=plane_rsem.at[k],
                device_id=(b, pc),
                device_id_type=MESH,
            ).start()

        each_plane(one)

    def plane_wait(k, many):
        pltpu.make_async_copy(many, many, plane_rsem.at[k]).wait()

    def plane_drain(k, many):
        pltpu.make_async_copy(many, many, plane_ssem.at[k]).wait()

    gather_start(0)
    swaps = [swap(0, image_x, image_sib)]
    swaps[0].start()
    for load in loads[13:]:
        load.wait()
    teacher_rows = [teacher_two(0)]

    hear(0)

    teacher_fill(1)
    hear(1)
    plane_start(0, lambda pc: param_send, lambda s: param_all.at[s])
    plane_start(1, lambda pc: head_send, lambda s: head_all.at[s])
    param_all[c] = param_send[...]
    head_all[c] = head_send[...]
    teacher_one()
    gather_turn(0)
    hear(2)
    teacher_rows.append(teacher_two(1))
    which_t = lax.broadcasted_iota(jnp.int32, (8, depth), 0)
    pooled_t = jnp.zeros((8, depth), F32)
    for m in range(MICRO):
        pooled_t = jnp.where(which_t == m, teacher_rows[m] / float(wide * wide), pooled_t)
    teacher_head_pad[...] = jnp.zeros(teacher_head_pad.shape, F32)
    teacher_head_pad[0:classes, :] = teacher_head[...].astype(F32)
    teacher_logits = lax.dot_general(
        pooled_t, teacher_head_pad[...], (((1,), (1,)), ((), ())), precision=HIGHEST, preferred_element_type=F32
    )
    lane_pad = jnp.zeros((1, LANES - classes), F32)
    teacher_logits = teacher_logits + jnp.concatenate([teacher_bias[...], lane_pad], axis=1)
    image_sum = jnp.zeros((1, depth), F32)
    for m in range(MICRO):
        image_sum = image_sum + jnp.sum(images[m].astype(F32).reshape(cells, depth), axis=0, keepdims=True)
    logit_send[0:MICRO, :] = teacher_logits[0:MICRO]
    for j, half in enumerate(halves(image_sum)):
        logit_send[MICRO + j : MICRO + j + 1, :] = half
    gather_start(1)
    hear(3)
    tile_start(logit_send, logit_all, wide_ssem.at[0], wide_rsem.at[0])

    def picker(shard, block, offset):
        at_row = lax.broadcasted_iota(jnp.int32, (depth, block), 0)
        place = lax.broadcasted_iota(jnp.int32, (depth, block), 1) - offset
        wanted = jnp.logical_and(place >= 0, place < own)
        return jnp.logical_and(wanted, at_row == shard * own + place).astype(BF16)

    def unpack(ref, block, offset):
        def one(shard, total):
            return total + jnp.dot(picker(shard, block, offset), ref[shard], preferred_element_type=F32)

        return lax.fori_loop(0, chans, one, jnp.zeros((depth, ref.shape[2]), F32)).astype(BF16)

    def weights(ref, tap):
        if own_pad == own:
            return ref[:, tap * own : (tap + 1) * own, :].reshape(depth, depth)
        return unpack(ref, own_rows, tap * own)

    def window(source, micro, row_off, col_off):
        return source[micro, row_off : row_off + extent, :, col_off * depth : (col_off + 1) * depth].reshape(
            cells, depth
        )

    def student_conv(source, micro, ref):
        total = None
        for row_off in range(3):
            for col_off in range(3):
                term = lax.dot_general(
                    window(source, micro, row_off, col_off),
                    weights(ref, row_off * 3 + col_off),
                    (((1,), (1,)), ((), ())),
                    preferred_element_type=F32,
                )
                total = term if total is None else total + term
        return total

    def student_back(source, micro, ref):
        total = None
        for row_off in range(3):
            for col_off in range(3):
                term = jnp.dot(
                    window(source, micro, row_off, col_off),
                    weights(ref, (2 - row_off) * 3 + 2 - col_off),
                    preferred_element_type=F32,
                )
                total = term if total is None else total + term
        return total

    def rows_of(m):
        return slice(m * cells, (m + 1) * cells)

    def col_sum(values):
        return jnp.sum(values, axis=0, keepdims=True)

    def moments_start(stage, m, values):
        sync_start(stage, m, (col_sum(values), col_sum(values * values)))

    def moments(stage, m):
        total, square = sync_wait(stage, m)
        center = total / samples
        spread = square / samples - center * center
        return (center, lax.rsqrt(spread + EPS))

    for piece in range(pieces):
        gather_forward(0, piece)
    for piece in range(pieces):
        gather_finish(0, piece)
    total = None
    for row_off in range(3):
        for col_off in range(3):
            term = lax.dot_general(
                image_x[:, row_off : row_off + extent, :, col_off * depth : (col_off + 1) * depth].reshape(
                    MICRO * cells, depth
                ),
                weights(w_first, row_off * 3 + col_off),
                (((1,), (1,)), ((), ())),
                preferred_element_type=F32,
            )
            total = term if total is None else total + term
    y_first[...] = total
    for m in range(MICRO):
        moments_start(0, m, total[rows_of(m), :])

    plane_wait(0, param_all.at[pl.ds(0, chans - 1)])
    plane_wait(1, head_all.at[pl.ds(0, chans - 1)])
    params = jnp.sum(param_all[...], axis=0)
    gain1, shift1, gain2, shift2 = (
        jnp.concatenate([params[2 * i : 2 * i + 1], params[2 * i + 1 : 2 * i + 2]], axis=1) for i in range(4)
    )
    if own_pad == own:
        head = head_all[...].reshape(depth, LANES)
    else:
        head = unpack(head_all, own_pad, 0)
    gather_turn(1)
    for piece in range(pieces):
        gather_forward(1, piece)
    for piece in range(pieces):
        gather_finish(1, piece)

    def three_parts(values):
        first = values.astype(BF16)
        rest = values - first.astype(F32)
        second = rest.astype(BF16)
        third = (rest - second.astype(F32)).astype(BF16)
        return jnp.concatenate([first, second, third], axis=0)

    def sum_parts(product):
        return product[0:8] + product[8:16] + product[16:24]

    norm1 = []
    for m in range(MICRO):
        center, inv = moments(0, m)
        norm1.append((center, inv))
        normed = (y_first[rows_of(m), :] - center) * (inv * gain1) + shift1
        spread_columns(hidden_x, m, 1, gelu(normed), extent)
        values = student_conv(hidden_x, m, w_second)
        y_second[rows_of(m), :] = values
        moments_start(1, m, values)
    swaps.append(swap(1, hidden_x, hidden_sib))
    swaps[1].start()
    for m in range(MICRO):
        center, inv = norm1[m]
        slope_first[rows_of(m), :] = gelu_slope((y_first[rows_of(m), :] - center) * (inv * gain1) + shift1)

    per_device = pair_index.shape[0]
    norm2, slope_scale = [], []
    tile_bytes(wide_rsem.at[0], logit_all)
    taught = []
    for m in range(MICRO):
        paired = pair_index[m]
        teacher_row = logit_all[pl.ds(paired // per_device, 1), pl.ds(lax.rem(paired, per_device), 1), :]
        taught.append(teacher_terms(teacher_row.reshape(1, LANES), labels[m], classes))
    which = lax.broadcasted_iota(jnp.int32, (8, depth), 0)
    which_lane = lax.broadcasted_iota(jnp.int32, (8, LANES), 0)
    for m in range(MICRO):
        center, inv = moments(1, m)
        norm2.append((center, inv))
        spread = y_second[rows_of(m), :] - center
        res = spread * (inv * gain2) + shift2 + images[m].astype(F32).reshape(cells, depth)
        square = res * res
        t = jnp.tanh(GELU_A * (res + GELU_B * (res * square)))
        half = 0.5 + 0.5 * t
        slope = half + (0.5 * res) * (1.0 - t * t) * (GELU_A + (3.0 * GELU_A * GELU_B) * square)
        slope_second[rows_of(m), :] = slope
        pooled = col_sum(res * half) / float(cells)
        slope_sum = col_sum(slope)
        slope_dot = col_sum(slope * spread) * inv
        product = jnp.dot(
            three_parts(jnp.where(which == 0, pooled, 0.0)), head, preferred_element_type=F32
        )
        logits = sum_parts(product)[0:1] + jnp.concatenate([head_bias[...], lane_pad], axis=1)
        grad = distill_grad(logits, taught[m], labels[m], classes)
        product = lax.dot_general(
            three_parts(jnp.where(which_lane == 0, grad, 0.0)),
            head,
            (((1,), (1,)), ((), ())),
            preferred_element_type=F32,
        )
        scale = sum_parts(product)[0:1] / float(cells)
        slope_scale.append(scale)
        sync_start(2, m, (scale * slope_dot, scale * slope_sum))
        for j, part in enumerate(halves(pooled)):
            wide_send[m * 4 + j : m * 4 + j + 1, :] = part
        wide_send[m * 4 + 2 : m * 4 + 3, :] = grad
        wide_send[m * 4 + 3 : m * 4 + 4, :] = logits
    plane_start(2, lambda pc: wide_send, lambda s: wide_all.at[s])
    wide_all[c] = wide_send[...]

    def own_lanes(low_row, high_row):
        at = c * own
        row = jnp.where(at >= LANES, high_row, low_row)
        turn = lax.rem(LANES - lax.rem(at, LANES), LANES)
        return pltpu.roll(jnp.broadcast_to(row, (8, LANES)), turn, 1)[0:1, 0:own]

    def norm_terms(stage, m, gain, norm):
        center, inv = norm
        totals = sync_wait(stage, m)
        scale = gain * inv
        slant = scale * inv * (totals[0] / samples)
        level = scale * (totals[1] / samples)
        return (scale, center, slant, level), totals

    def norm_apply(terms, grad, values):
        scale, center, slant, level = terms
        return grad * scale - (values - center) * slant - level

    def norm_out(totals, gain_out, shift_out):
        for out, i in ((gain_out, 0), (shift_out, 1)):
            row = totals[0][i]
            for m in range(1, MICRO):
                row = row + totals[m][i]
            out[...] = own_lanes(*halves(row))

    def by_core(whole, dest):
        if own_pad == own:
            dest[...] = whole.reshape(dest.shape)
        else:

            def one(shard, carry):
                dest[shard // 2, lax.rem(shard, 2)] = lax.dot_general(
                    picker(shard, own_pad, 0).astype(F32),
                    whole,
                    (((0,), (0,)), ((), ())),
                    precision=HIGHEST,
                    preferred_element_type=F32,
                )
                return carry

            lax.fori_loop(0, chans, one, 0)

    def hand(k, m, grad, values):
        by_core(jnp.transpose(grad), turned.at[k, m, 0])
        by_core(jnp.transpose(values), turned.at[k, m, 1])
        turns[k, m] = swap(2 + k * MICRO + m, turned.at[k, m, :, :, 1 - core], turned_sib.at[k, m])
        turns[k, m].start()

    def low_grads(k, m, terms):
        by_core(
            jnp.transpose(jnp.concatenate(list(terms) + [jnp.zeros((4, depth), F32)], axis=0)), turned_terms
        )
        columns = turned_terms[:, pl.ds(core, 1)].reshape(chips * own_pad, 8)
        scale, center, slant, level = (columns[:, i : i + 1] for i in range(4))
        mine = [turned[k, m, i, :, pl.ds(core, 1)].reshape(chips * own_pad, cells) for i in range(2)]
        turns[k, m].wait_recv()
        theirs = [turned_sib[k, m, i].reshape(chips * own_pad, cells) for i in range(2)]
        return [norm_apply((scale, center, slant, level), *pair).astype(BF16) for pair in (mine, theirs)]

    turns = {}
    taps = 3 * own_pad
    per_half = groups // 2
    part_rows = taps // per_half
    part_pad = sum_send.shape[2]
    across = {0: None, 1: 2}
    planar = {0: (0, 1, 2), 1: (0, 1)}

    def send(source, dest, ssem, rsem, peer_b, peer_c):
        pltpu.make_async_remote_copy(
            src_ref=source, dst_ref=dest, send_sem=ssem, recv_sem=rsem, device_id=(peer_b, peer_c), device_id_type=MESH
        ).start()

    def cut(p):
        half, row = p // per_half, (p % per_half) * part_rows
        return slice(row, row + part_rows), slice(half * LANES, (half + 1) * LANES)

    def kernel_grad(k, grads, source, source_sib, mean):
        sides = [(grads[m][i], ref, m) for m in range(MICRO) for i, ref in enumerate((source, source_sib))]
        level = sum(jnp.sum(low.astype(F32), axis=1, keepdims=True) for low, _, _ in sides)
        for row_off in (2, 0, 1):
            total = sum(
                jnp.dot(
                    low,
                    ref[m, row_off : row_off + extent].reshape(cells, 3 * depth),
                    preferred_element_type=F32,
                )
                for low, ref, m in sides
            )
            for col_off in range(3):
                block = total[:, col_off * depth : (col_off + 1) * depth] - level * mean
                for i in range(chips):
                    part_all[i, col_off * own_pad : (col_off + 1) * own_pad, :] = block[i * own_pad : (i + 1) * own_pad]
            if row_off == across[k]:
                for p in range(groups):
                    rows, lanes = cut(p)
                    cross_all[p, :, 0:part_rows] = part_all[:, rows, lanes]
                    if part_pad != part_rows:
                        cross_all[p, :, part_rows:part_pad] = jnp.zeros((chips, part_pad - part_rows, LANES), F32)
                cross_send[k] = cross_all[...].astype(BF16)
                cross_own[k] = cross_all[pl.ds(b, 1)].reshape(chips, part_pad, LANES)
                each_line(
                    lambda peer: send(
                        cross_send.at[k, peer], cross_recv.at[k, b], cross_ssem.at[k], cross_rsem.at[k], peer, c
                    )
                )
                cross_recv[k, b] = jnp.zeros((chips, part_pad, LANES), BF16)
            else:
                part_send[k, row_off] = part_all[...].astype(BF16)
                part_own[k, row_off] = part_all[pl.ds(chip, 1)].reshape(taps, depth)
                each_chip(
                    lambda peer, row_off=row_off: send(
                        part_send.at[k, row_off, peer],
                        part_recv.at[k, row_off, chip],
                        part_ssem.at[k, row_off],
                        part_rsem.at[k, row_off],
                        b,
                        2 * peer + core,
                    )
                )
                part_recv[k, row_off, chip] = jnp.zeros((taps, depth), BF16)
        ones = jnp.ones((8, cells), BF16)
        level_send[k] = sum(
            lax.dot_general(ones, low, (((1,), (1,)), ((), ())), preferred_element_type=F32) for low, _, _ in sides
        )[0:1]
        each_chip(
            lambda peer: send(
                level_send.at[k], level_recv.at[k, chip], level_ssem.at[k], level_rsem.at[k], b, 2 * peer + core
            )
        )
        level_recv[k, chip] = level_send[k]

    def line_start(k):
        for row_off in planar[k]:
            bytes_of(part_rsem.at[k, row_off], part_recv.at[k, row_off, pl.ds(0, chips - 1)])
            total = part_own[k, row_off] + jnp.sum(part_recv[k, row_off].astype(F32), axis=0)
            for p in range(groups):
                line_own[k, row_off, p, 0:part_rows] = total[cut(p)]
                if part_pad != part_rows:
                    line_own[k, row_off, p, part_rows:part_pad] = jnp.zeros((part_pad - part_rows, LANES), F32)
            line_send[k, row_off] = line_own[k, row_off].astype(BF16)
            each_line(
                lambda peer, row_off=row_off: send(
                    line_send.at[k, row_off, peer],
                    line_recv.at[k, row_off, b],
                    line_ssem.at[k, row_off],
                    line_rsem.at[k, row_off],
                    peer,
                    c,
                )
            )
            line_recv[k, row_off, b] = jnp.zeros((part_pad, LANES), BF16)
        bytes_of(level_rsem.at[k], level_recv.at[k, pl.ds(0, chips - 1)])
        level_line_send[k] = jnp.sum(level_recv[k], axis=0)
        each_line(
            lambda peer: send(
                level_line_send.at[k], level_line_recv.at[k, b], level_line_ssem.at[k], level_line_rsem.at[k], peer, c
            )
        )
        level_line_recv[k, b] = level_line_send[k]

    def cross_forward(k):
        if across[k] is None:
            return
        bytes_of(cross_rsem.at[k], cross_recv.at[k, pl.ds(0, groups - 1)])
        last_all[...] = cross_own[k] + jnp.sum(cross_recv[k].astype(F32), axis=0)
        last_send[k] = last_all[...].astype(BF16)
        last_own[k] = last_all[pl.ds(chip, 1)].reshape(part_pad, LANES)
        each_chip(
            lambda peer: send(
                last_send.at[k, peer], last_recv.at[k, chip], last_ssem.at[k], last_rsem.at[k], b, 2 * peer + core
            )
        )
        last_recv[k, chip] = jnp.zeros((part_pad, LANES), BF16)

    def share(k, row_off, total):
        sum_send[k, row_off] = total.astype(BF16)
        each_line(
            lambda peer: send(
                sum_send.at[k, row_off],
                sum_recv.at[k, row_off, b],
                sum_ssem.at[k, row_off],
                sum_rsem.at[k, row_off],
                peer,
                c,
            )
        )
        sum_recv[k, row_off, b] = sum_send[k, row_off]

    def cross_sum(k):
        if across[k] is None:
            return
        bytes_of(last_rsem.at[k], last_recv.at[k, pl.ds(0, chips - 1)])
        share(k, across[k], last_own[k] + jnp.sum(last_recv[k].astype(F32), axis=0))

    def line_sum(k):
        for row_off in planar[k]:
            bytes_of(line_rsem.at[k, row_off], line_recv.at[k, row_off, pl.ds(0, groups - 1)])
            share(
                k,
                row_off,
                line_own[k, row_off, pl.ds(b, 1)].reshape(part_pad, LANES)
                + jnp.sum(line_recv[k, row_off].astype(F32), axis=0),
            )

    def sum_finish(k, mean, out):
        bytes_of(level_line_rsem.at[k], level_line_recv.at[k, pl.ds(0, groups - 1)])
        level = jnp.sum(level_line_recv[k], axis=0)
        level_column[...] = jnp.transpose(jnp.broadcast_to(level, (LANES, level.shape[1])))
        column_own = level_column[pl.ds(chip * own_pad, own_pad), :]
        back = [column_own * half for half in halves(mean)]
        for row_off in (0, 1, 2):
            bytes_of(sum_rsem.at[k, row_off], sum_recv.at[k, row_off, pl.ds(0, groups - 1)])
            for half in range(2):
                rows = sum_recv[k, row_off, half * per_half : (half + 1) * per_half, 0:part_rows].astype(F32)
                out[row_off * 3 : row_off * 3 + 3, :, half * LANES : (half + 1) * LANES] = (
                    rows.reshape(3, own_pad, LANES) + back[half][None]
                )

    for m in range(MICRO):
        hand(0, m, slope_second[rows_of(m), :] * slope_scale[m], y_second[rows_of(m), :])
    terms2, totals2 = [], []
    for m in range(MICRO):
        terms, totals = norm_terms(2, m, gain2, norm2[m])
        terms2.append(terms)
        totals2.append(totals)
        found = norm_apply(terms, slope_second[rows_of(m), :] * slope_scale[m], y_second[rows_of(m), :])
        spread_columns(grad_x, m, 1, found, extent)
        grad = student_back(grad_x, m, w_second) * slope_first[rows_of(m), :]
        d_hid[rows_of(m), :] = grad
        center, inv = norm1[m]
        sync_start(3, m, (col_sum(grad * (y_first[rows_of(m), :] - center)) * inv, col_sum(grad)))

    hidden_mean = jnp.zeros((1, depth), F32)
    for node, weight in QUADRATURE:
        hidden_mean = hidden_mean + weight * gelu(shift1 + gain1 * node)
    image_rows = jnp.sum(logit_all[...], axis=0)
    image_mean = jnp.concatenate([image_rows[MICRO : MICRO + 1], image_rows[MICRO + 1 : MICRO + 2]], axis=1) / (
        MICRO * samples
    )

    swaps[0].wait_recv()
    swaps[1].wait_recv()
    kernel_grad(0, [low_grads(0, m, terms2[m]) for m in range(MICRO)], hidden_x, hidden_sib, hidden_mean)
    for m in range(MICRO):
        hand(1, m, d_hid[rows_of(m), :], y_first[rows_of(m), :])
    norm_out(totals2, gain_second_grad, shift_second_grad)

    plane_wait(2, wide_all.at[pl.ds(0, chans - 1)])
    totals = [jnp.zeros((LANES, LANES), F32) for _ in range(2)]
    bias_row = jnp.zeros((1, LANES), F32)
    for m in range(MICRO):
        per_image = wide_all[:, m * 4 + 2, :]
        bias_row = bias_row + col_sum(per_image)
        for j in range(2):
            totals[j] = totals[j] + lax.dot_general(
                wide_all[:, m * 4 + j, :],
                per_image,
                (((0,), (0,)), ((), ())),
                precision=HIGHEST,
                preferred_element_type=F32,
            )
        for j in range(chans):
            logits_out[j * MICRO + m : j * MICRO + m + 1, :] = wide_all[j, m * 4 + 3 : m * 4 + 4, 0:classes]
    for j in range(2):
        head_sum[j * LANES : (j + 1) * LANES, :] = totals[j]
    head_line_send[0:own, :] = head_sum[pl.ds(c * own, own), :]
    head_line_send[own : own + 8, :] = jnp.broadcast_to(bias_row, (8, LANES))
    each_line(
        lambda peer: send(head_line_send, head_line_recv.at[b], wide_ssem.at[1], wide_rsem.at[1], peer, c)
    )
    head_line_recv[b] = head_line_send[...]

    terms1, totals1, lows = [], [], []
    for m in range(MICRO):
        terms, totals = norm_terms(3, m, gain1, norm1[m])
        terms1.append(terms)
        totals1.append(totals)
        lows.append(low_grads(1, m, terms))
    kernel_grad(1, lows, image_x, image_sib, image_mean)
    for m in range(MICRO):
        found = norm_apply(terms1[m], d_hid[rows_of(m), :], y_first[rows_of(m), :])
        spread_columns(grad_x, m, 1, found, extent)
        images_grad[m] = (
            student_back(grad_x, m, w_first) + slope_second[rows_of(m), :] * slope_scale[m]
        ).reshape(images_grad.shape[1:])
    norm_out(totals1, gain_first_grad, shift_first_grad)
    line_start(0)
    cross_forward(0)

    cross_sum(0)
    line_start(1)
    cross_forward(1)
    line_sum(0)
    cross_sum(1)
    line_sum(1)
    bytes_of(wide_rsem.at[1], head_line_recv.at[pl.ds(0, groups - 1)])
    head_total = jnp.sum(head_line_recv[...], axis=0)
    head_grad[...] = head_total[0:own, 0:classes]
    bias_grad[...] = head_total[own : own + 1, 0:classes]
    sum_finish(0, hidden_mean, second_grad)
    sum_finish(1, image_mean, first_grad)

    tile_bytes(wide_ssem.at[0], logit_all)
    bytes_of(wide_ssem.at[1], head_line_recv.at[pl.ds(0, groups - 1)])
    plane_drain(2, wide_all.at[pl.ds(0, chans - 1)])
    for k in range(2):
        bytes_of(gather_send.at[k], held[k].at[pl.ds(0, chans - 1)])
    for k in range(4 * MICRO):
        tile_bytes(sync_ssem.at[k], sync_all[k])
    plane_drain(0, param_all.at[pl.ds(0, chans - 1)])
    plane_drain(1, head_all.at[pl.ds(0, chans - 1)])
    for copy in swaps + list(turns.values()):
        copy.wait_send()
    for k in range(2):
        for row_off in planar[k]:
            bytes_of(part_ssem.at[k, row_off], part_recv.at[k, row_off, pl.ds(0, chips - 1)])
            bytes_of(line_ssem.at[k, row_off], line_recv.at[k, row_off, pl.ds(0, groups - 1)])
        for row_off in range(3):
            bytes_of(sum_ssem.at[k, row_off], sum_recv.at[k, row_off, pl.ds(0, groups - 1)])
        if across[k] is not None:
            bytes_of(cross_ssem.at[k], cross_recv.at[k, pl.ds(0, groups - 1)])
            bytes_of(last_ssem.at[k], last_recv.at[k, pl.ds(0, chips - 1)])
        bytes_of(level_ssem.at[k], level_recv.at[k, pl.ds(0, chips - 1)])
        bytes_of(level_line_ssem.at[k], level_line_recv.at[k, pl.ds(0, groups - 1)])


def hand_on(*refs):
    count = len(refs) // 2
    copies = [pltpu.make_async_copy(refs[i], refs[count + i], refs[-1].at[i]) for i in range(count)]
    for copy in copies:
        copy.start()
    for copy in copies:
        copy.wait()


def shards(
    teacher_images,
    student_images,
    pair_index,
    labels,
    teacher_first,
    teacher_second,
    teacher_head,
    teacher_bias,
    conv_first,
    gain_first,
    shift_first,
    conv_second,
    gain_second,
    shift_second,
    head_weight,
    head_bias,
):
    groups, chans = lax.axis_size("batch"), lax.axis_size("chan")
    devices = groups * chans
    count, extent, _, depth = student_images.shape
    wide = teacher_images.shape[1]
    own = conv_first.shape[3]
    own_pad = max(own, 16)
    own_rows = -(-9 * own // 16) * 16
    classes = head_bias.shape[0]
    cells = extent * extent
    rows = count * cells
    chips = chans // 2
    taps = 3 * own_pad
    part_rows = 2 * taps // groups
    part_pad = -(-part_rows // 16) * 16

    def turned(kernel):
        return jnp.transpose(kernel, (0, 1, 3, 2)).reshape(9 * own, depth)

    def row(vector):
        return vector.reshape(1, -1)

    vmem = pl.BlockSpec(memory_space=pltpu.VMEM)
    hbm = pl.BlockSpec(memory_space=pl.ANY)
    out_shape = [
        jax.ShapeDtypeStruct((chans * count, classes), F32),
        jax.ShapeDtypeStruct(student_images.shape, F32),
        jax.ShapeDtypeStruct((9, own_pad, depth), F32),
        jax.ShapeDtypeStruct((1, own), F32),
        jax.ShapeDtypeStruct((1, own), F32),
        jax.ShapeDtypeStruct((9, own_pad, depth), F32),
        jax.ShapeDtypeStruct((1, own), F32),
        jax.ShapeDtypeStruct((1, own), F32),
        jax.ShapeDtypeStruct((own, classes), F32),
        jax.ShapeDtypeStruct((1, classes), F32),
    ]
    stage = (16, LANES) if own_rows == 9 * own else (9 * own, depth)
    scratch = [
        pltpu.SMEM(pair_index.shape, jnp.int32),
        pltpu.SMEM(labels.shape, jnp.int32),
        pltpu.VMEM(stage, BF16),
        pltpu.VMEM(stage, BF16),
        pltpu.VMEM(student_images.shape, BF16),
        pltpu.VMEM((classes, depth), BF16),
        pltpu.VMEM((1, classes), F32),
        pltpu.VMEM((1, own), F32),
        pltpu.VMEM((1, own), F32),
        pltpu.VMEM((1, own), F32),
        pltpu.VMEM((1, own), F32),
        pltpu.VMEM((own, classes), BF16),
        pltpu.VMEM((1, classes), F32),
        pltpu.VMEM(teacher_images.shape, BF16),
        pltpu.VMEM((9 * depth, depth), BF16),
        pltpu.VMEM((9 * depth, depth), BF16),
        pltpu.VMEM((1, wide + 2, wide, 3 * depth), BF16),
        pltpu.VMEM((1, wide + 2, wide, 3 * depth), BF16),
        pltpu.VMEM((LANES, depth), F32),
        pltpu.VMEM((count, extent + 2, extent, 3 * depth), BF16),
        pltpu.VMEM((count, extent + 2, extent, 3 * depth), BF16),
        pltpu.VMEM((count, extent + 2, extent, 3 * depth), BF16),
        pltpu.VMEM((chans, own_rows, depth), BF16),
        pltpu.VMEM((chans, own_rows, depth), BF16),
        pltpu.VMEM((own_rows, depth), BF16),
        pltpu.VMEM((own_rows, depth), BF16),
        pltpu.VMEM((rows, depth), F32),
        pltpu.VMEM((rows, depth), F32),
        pltpu.VMEM((rows, depth), F32),
        pltpu.VMEM((rows, depth), F32),
        pltpu.VMEM((rows, depth), F32),
        pltpu.VMEM((count, extent + 2, extent, 3 * depth), BF16),
        pltpu.VMEM((count, extent + 2, extent, 3 * depth), BF16),
        pltpu.VMEM((2, count, 2, chips, 2, own_pad, cells), F32),
        pltpu.VMEM((2, count, 2, chips, own_pad, cells), F32),
        pltpu.VMEM((chips, 2, own_pad, 8), F32),
        pltpu.VMEM((chips, taps, depth), F32),
        pltpu.VMEM((2, 3, taps, depth), F32),
        pltpu.VMEM((2, 3, chips, taps, depth), BF16),
        pltpu.VMEM((2, 3, chips, taps, depth), BF16),
        pltpu.VMEM((groups, chips, part_pad, LANES), F32),
        pltpu.VMEM((2, chips, part_pad, LANES), F32),
        pltpu.VMEM((2, groups, chips, part_pad, LANES), BF16),
        pltpu.VMEM((2, groups, chips, part_pad, LANES), BF16),
        pltpu.VMEM((chips, part_pad, LANES), F32),
        pltpu.VMEM((2, part_pad, LANES), F32),
        pltpu.VMEM((2, chips, part_pad, LANES), BF16),
        pltpu.VMEM((2, chips, part_pad, LANES), BF16),
        pltpu.VMEM((2, 3, groups, part_pad, LANES), F32),
        pltpu.VMEM((2, 3, groups, part_pad, LANES), BF16),
        pltpu.VMEM((2, 3, groups, part_pad, LANES), BF16),
        pltpu.VMEM((2, 3, part_pad, LANES), BF16),
        pltpu.VMEM((2, 3, groups, part_pad, LANES), BF16),
        pltpu.VMEM((2, 1, chips * own_pad), F32),
        pltpu.VMEM((2, chips, 1, chips * own_pad), F32),
        pltpu.VMEM((2, 1, chips * own_pad), F32),
        pltpu.VMEM((2, groups, 1, chips * own_pad), F32),
        pltpu.VMEM((chips * own_pad, LANES), F32),
        pltpu.VMEM((8, LANES), F32),
        pltpu.VMEM((chans, 8, LANES), F32),
        pltpu.VMEM((own_pad, LANES), BF16),
        pltpu.VMEM((chans, own_pad, LANES), BF16),
        pltpu.VMEM((4, LANES), F32),
        pltpu.VMEM((devices, 4, LANES), F32),
        pltpu.VMEM((8, LANES), F32),
        pltpu.VMEM((chans, 8, LANES), F32),
        pltpu.VMEM((4 * MICRO, 4, LANES), F32),
        pltpu.VMEM((devices, 4, LANES), F32),
        pltpu.VMEM((devices, 4, LANES), F32),
        pltpu.VMEM((devices, 4, LANES), F32),
        pltpu.VMEM((devices, 4, LANES), F32),
        pltpu.VMEM((devices, 4, LANES), F32),
        pltpu.VMEM((devices, 4, LANES), F32),
        pltpu.VMEM((devices, 4, LANES), F32),
        pltpu.VMEM((devices, 4, LANES), F32),
        pltpu.VMEM((depth, LANES), F32),
        pltpu.VMEM((own + 8, LANES), F32),
        pltpu.VMEM((groups, own + 8, LANES), F32),
        pltpu.SemaphoreType.DMA((16,)),
        pltpu.SemaphoreType.DMA((2,)),
        pltpu.SemaphoreType.DMA((2, 6, chans)),
        pltpu.SemaphoreType.DMA((2,)),
        pltpu.SemaphoreType.DMA((2,)),
        pltpu.SemaphoreType.DMA((4 * MICRO,)),
        pltpu.SemaphoreType.DMA((4 * MICRO,)),
        pltpu.SemaphoreType.REGULAR((4,)),
        pltpu.SemaphoreType.DMA((3,)),
        pltpu.SemaphoreType.DMA((3,)),
        pltpu.SemaphoreType.DMA((2 + 2 * MICRO,)),
        pltpu.SemaphoreType.DMA((2 + 2 * MICRO,)),
        pltpu.SemaphoreType.DMA((2, 3)),
        pltpu.SemaphoreType.DMA((2, 3)),
        pltpu.SemaphoreType.DMA((2,)),
        pltpu.SemaphoreType.DMA((2,)),
        pltpu.SemaphoreType.DMA((2,)),
        pltpu.SemaphoreType.DMA((2,)),
        pltpu.SemaphoreType.DMA((2,)),
        pltpu.SemaphoreType.DMA((2,)),
        pltpu.SemaphoreType.DMA((2,)),
        pltpu.SemaphoreType.DMA((2,)),
        pltpu.SemaphoreType.DMA((2, 3)),
        pltpu.SemaphoreType.DMA((2, 3)),
        pltpu.SemaphoreType.DMA((2, 3)),
        pltpu.SemaphoreType.DMA((2, 3)),
    ]
    found = pl.pallas_call(
        functools.partial(body, (groups, chans, own, own_pad, classes)),
        out_shape=[pltpu.VMEM(out.shape, out.dtype) for out in out_shape],
        in_specs=[hbm] * 16,
        out_specs=[vmem] * 10,
        scratch_shapes=scratch,
        compiler_params=pltpu.CompilerParams(
            collective_id=0, has_side_effects=True, vmem_limit_bytes=62 * 2**20
        ),
    )(
        teacher_images,
        student_images,
        pair_index,
        labels,
        teacher_first.reshape(9 * depth, depth),
        teacher_second.reshape(9 * depth, depth),
        teacher_head.T,
        row(teacher_bias),
        turned(conv_first),
        row(gain_first),
        row(shift_first),
        turned(conv_second),
        row(gain_second),
        row(shift_second),
        head_weight,
        row(head_bias),
    )
    found = pl.pallas_call(
        hand_on,
        out_shape=out_shape,
        in_specs=[vmem] * len(out_shape),
        out_specs=[hbm] * len(out_shape),
        scratch_shapes=[pltpu.SemaphoreType.DMA((len(out_shape),))],
    )(*[pltpu.with_memory_space_constraint(x, pltpu.VMEM) for x in found])
    logits, images_grad, first, gain1, shift1, second, gain2, shift2, head, bias = found

    def back(grad):
        return jnp.transpose(grad[:, :own].reshape(3, 3, own, depth), (0, 1, 3, 2))

    return (
        logits,
        images_grad,
        back(first),
        gain1.reshape(-1),
        shift1.reshape(-1),
        back(second),
        gain2.reshape(-1),
        shift2.reshape(-1),
        head,
        bias.reshape(-1),
    )


def solution(mesh):
    in_specs = (
        P(("batch", "chan"), None, None, None),
        P(("batch", "chan"), None, None, None),
        P(("batch", "chan")),
        P(("batch", "chan")),
        P(),
        P(),
        P(),
        P(),
        P(None, None, None, "chan"),
        P("chan"),
        P("chan"),
        P(None, None, None, "chan"),
        P("chan"),
        P("chan"),
        P("chan", None),
        P(),
    )
    out_specs = (
        P("batch", None),
        P(("batch", "chan"), None, None, None),
        P(None, None, None, "chan"),
        P("chan"),
        P("chan"),
        P(None, None, None, "chan"),
        P("chan"),
        P("chan"),
        P("chan", None),
        P(),
    )
    return jax.shard_map(shards, mesh=mesh, in_specs=in_specs, out_specs=out_specs, check_vma=False)
```

```python
import functools

import jax
import jax.numpy as jnp
from jax import lax
from jax.experimental import pallas as pl
from jax.experimental.pallas import tpu as pltpu
from jax.sharding import PartitionSpec as P

MESH = pl.DeviceIdType.MESH
F32 = jnp.float32
BF16 = jnp.bfloat16
HIGHEST = lax.Precision.HIGHEST
MICRO = 2
EPS = 1e-05
TARGET_WEIGHT = 1.0
NONTARGET_WEIGHT = 8.0
SOFTEN = 4.0
GELU_A = 0.7978845608028654
GELU_B = 0.044715
LANES = 128
QUADRATURE = (
    (0.0, 0.5333333333),
    (1.3556261800, 0.2220759220),
    (-1.3556261800, 0.2220759220),
    (2.8569700139, 0.0112574113),
    (-2.8569700139, 0.0112574113),
)


def gelu(x):
    return x * (0.5 + 0.5 * jnp.tanh(GELU_A * (x + GELU_B * (x * x * x))))


def gelu_slope(x):
    square = x * x
    t = jnp.tanh(GELU_A * (x + GELU_B * (x * square)))
    return 0.5 + 0.5 * t + (0.5 * x) * (1.0 - t * t) * (GELU_A + (3.0 * GELU_A * GELU_B) * square)


def column(shape, width):
    return lax.rem(lax.broadcasted_iota(jnp.int32, shape, 0), width)


def spread_columns(dest, lead, top, values, width):
    rows, depth = values.shape
    col = column(values.shape, width)
    left = jnp.where(col == 0, 0.0, pltpu.roll(values, 1, 0))
    right = jnp.where(col == width - 1, 0.0, pltpu.roll(values, rows - 1, 0))
    high = rows // width
    for place, part in enumerate((left, values, right)):
        dest[lead, pl.ds(top, high), :, place * depth : (place + 1) * depth] = part.astype(BF16).reshape(
            high, width, depth
        )


def halves(row):
    return (row[:, :LANES], row[:, LANES:])


def soft_parts(logits, label, classes):
    lane = lax.broadcasted_iota(jnp.int32, logits.shape, 1)
    live = lane < classes
    target = lane == label
    other = jnp.logical_and(live, jnp.logical_not(target))
    low = -1e30
    soft = logits / SOFTEN
    whole_top = jnp.max(jnp.where(live, soft, low), axis=1, keepdims=True)
    rest_top = jnp.max(jnp.where(other, soft, low), axis=1, keepdims=True)
    whole_exp = jnp.where(live, jnp.exp(jnp.where(live, soft, whole_top) - whole_top), 0.0)
    rest_exp = jnp.where(other, jnp.exp(jnp.where(other, soft, rest_top) - rest_top), 0.0)
    whole_sum = jnp.sum(whole_exp, axis=1, keepdims=True)
    rest_sum = jnp.sum(rest_exp, axis=1, keepdims=True)
    whole = whole_top + jnp.log(whole_sum)
    rest = rest_top + jnp.log(rest_sum)
    true = jnp.sum(jnp.where(target, soft, 0.0), axis=1, keepdims=True)
    return (whole_exp / whole_sum, rest_exp / rest_sum, true - whole, rest - whole, target)


def teacher_terms(teacher, label, classes):
    _, inner, log_true, log_rest, target = soft_parts(teacher, label, classes)
    true, rest = jnp.exp(log_true), jnp.exp(log_rest)
    fixed = TARGET_WEIGHT * jnp.where(target, true, 0.0) + NONTARGET_WEIGHT * inner
    return (
        SOFTEN * TARGET_WEIGHT * (true + rest),
        SOFTEN * (NONTARGET_WEIGHT * jnp.sum(inner, axis=1, keepdims=True) - TARGET_WEIGHT * rest),
        SOFTEN * fixed,
    )


def distill_grad(student, terms, label, classes):
    probs, inner, _, _, _ = soft_parts(student, label, classes)
    whole, rest, fixed = terms
    return whole * probs + rest * inner - fixed


def body(
    sizes,
    teacher_hbm,
    images_hbm,
    pair_index_hbm,
    labels_hbm,
    teacher_first_hbm,
    teacher_second_hbm,
    teacher_head_hbm,
    teacher_bias_hbm,
    first_hbm,
    gain_first_hbm,
    shift_first_hbm,
    second_hbm,
    gain_second_hbm,
    shift_second_hbm,
    head_hbm,
    head_bias_hbm,
    logits_out,
    images_grad,
    first_grad,
    gain_first_grad,
    shift_first_grad,
    second_grad,
    gain_second_grad,
    shift_second_grad,
    head_grad,
    bias_grad,
    pair_index,
    labels,
    stage_first,
    stage_second,
    images,
    teacher_head,
    teacher_bias,
    gain_first,
    shift_first,
    gain_second,
    shift_second,
    head_own,
    head_bias,
    teacher_in,
    teacher_w1,
    teacher_w2,
    teacher_x,
    teacher_h,
    teacher_head_pad,
    image_x,
    hidden_x,
    grad_x,
    w_first,
    w_second,
    own_first,
    own_second,
    y_first,
    y_second,
    slope_first,
    slope_second,
    d_hid,
    image_sib,
    hidden_sib,
    turned,
    turned_sib,
    turned_terms,
    part_all,
    part_own,
    part_send,
    part_recv,
    cross_all,
    cross_own,
    cross_send,
    cross_recv,
    last_all,
    last_own,
    last_send,
    last_recv,
    line_own,
    line_send,
    line_recv,
    sum_send,
    sum_recv,
    level_send,
    level_recv,
    level_line_send,
    level_line_recv,
    level_column,
    param_send,
    param_all,
    head_send,
    head_all,
    logit_send,
    logit_all,
    wide_send,
    wide_all,
    sync_send,
    sync_all_0,
    sync_all_1,
    sync_all_2,
    sync_all_3,
    sync_all_4,
    sync_all_5,
    sync_all_6,
    sync_all_7,
    head_sum,
    head_line_send,
    head_line_recv,
    local_sem,
    gather_send,
    gather_recv,
    wide_ssem,
    wide_rsem,
    sync_ssem,
    sync_rsem,
    known,
    plane_ssem,
    plane_rsem,
    swap_ssem,
    swap_rsem,
    part_ssem,
    part_rsem,
    cross_ssem,
    cross_rsem,
    last_ssem,
    last_rsem,
    level_ssem,
    level_rsem,
    level_line_ssem,
    level_line_rsem,
    line_ssem,
    line_rsem,
    sum_ssem,
    sum_rsem,
):
    groups, chans, own, own_pad, classes = sizes
    sync_all = (
        sync_all_0,
        sync_all_1,
        sync_all_2,
        sync_all_3,
        sync_all_4,
        sync_all_5,
        sync_all_6,
        sync_all_7,
    )
    b = lax.axis_index("batch")
    c = lax.axis_index("chan")
    me = b * chans + c
    devices = groups * chans
    sibling = c + 1 - 2 * lax.rem(c, 2)
    extent = images.shape[1]
    cells = extent * extent
    depth = images.shape[3]
    wide = teacher_hbm.shape[1]
    samples = float(devices * cells)
    chips = chans // 2
    chip, core = c // 2, lax.rem(c, 2)

    if groups == 4:
        far_first = [groups - 1 - b, lax.rem(b + 2, groups), b + 1 - 2 * lax.rem(b, 2)]
    else:
        far_first = [lax.rem(b + i, groups) for i in range(1, groups)]

    def each_device(fn):
        for peer_b in far_first + [b]:

            def one(i, carry, peer_b=peer_b):
                fn(peer_b, lax.rem(c + (chans - i), chans))
                return carry

            lax.fori_loop(1 if peer_b is b else 0, chans, one, 0, unroll=chans <= 8)

    def each_chip(fn):
        def one(i, carry):
            fn(lax.rem(chip + i, chips))
            return carry

        lax.fori_loop(1, chips, one, 0, unroll=chips <= 4)

    def each_line(fn):
        for peer_b in far_first:
            fn(peer_b)

    def signal(sem, peer_b, peer_c):
        pl.semaphore_signal(sem, inc=1, device_id=(peer_b, peer_c), device_id_type=MESH)

    def each_plane(fn):
        def one(i, carry):
            fn(lax.rem(c + i, chans))
            return carry

        lax.fori_loop(1, chans, one, 0, unroll=chans <= 8)

    if chips == 4:
        beside = chip + 1 - 2 * lax.rem(chip, 2)
        above = lax.rem(chip + 2, chips)
        near = [beside, above]
    else:
        near = [lax.rem(chip + i, chips) for i in range(1, chips)]
    if groups == 4:
        lines = [[b + 1 - 2 * lax.rem(b, 2)], [lax.rem(b + 2, groups)]]
    else:
        lines = [far_first]
    barrier = pltpu.get_barrier_semaphore()
    for peer in near:
        signal(barrier, b, 2 * peer + core)
    for line in lines:
        for peer in line:
            signal(barrier, peer, c)
    signal(barrier, b, sibling)
    greeted = len(near) + sum(len(line) for line in lines) + 1

    own_rows = own_first.shape[0]
    exact = own_rows == 9 * own
    moves = (
        (first_hbm, own_first if exact else stage_first),
        (images_hbm, images),
        (second_hbm, own_second if exact else stage_second),
        (gain_first_hbm, gain_first),
        (shift_first_hbm, shift_first),
        (gain_second_hbm, gain_second),
        (shift_second_hbm, shift_second),
        (head_hbm, head_own),
        (head_bias_hbm, head_bias),
        (teacher_bias_hbm, teacher_bias),
        (teacher_head_hbm, teacher_head),
        (teacher_hbm, teacher_in),
        (teacher_first_hbm, teacher_w1),
        (teacher_second_hbm, teacher_w2),
        (pair_index_hbm, pair_index),
        (labels_hbm, labels),
    )
    loads = [pltpu.make_async_copy(source, dest, local_sem.at[i]) for i, (source, dest) in enumerate(moves)]
    for load in loads:
        load.start()

    for ref in (image_x, hidden_x, grad_x, teacher_x, teacher_h):
        high = ref.shape[1]
        for lead in range(ref.shape[0]):
            ref[lead, 0] = jnp.zeros(ref.shape[2:], BF16)
            ref[lead, high - 1] = jnp.zeros(ref.shape[2:], BF16)
    for load in loads[:11]:
        load.wait()
    if not exact:
        for source, dest in ((stage_first, own_first), (stage_second, own_second)):
            dest[...] = jnp.zeros(dest.shape, BF16)
            dest[0 : 9 * own, :] = source[...]

    def place_own(param_row):
        at = c * own
        lane0 = lax.rem(at, LANES)
        padded = jnp.concatenate([param_row, jnp.zeros((1, LANES - own), F32)], axis=1)
        moved = pltpu.roll(jnp.broadcast_to(padded, (8, LANES)), lane0, 1)[0:1]
        upper = at >= LANES
        return (jnp.where(upper, 0.0, moved), jnp.where(upper, moved, 0.0))

    for i, ref in enumerate((gain_first, shift_first, gain_second, shift_second)):
        low_half, high_half = place_own(ref[...])
        param_send[2 * i : 2 * i + 1, :] = low_half
        param_send[2 * i + 1 : 2 * i + 2, :] = high_half
    head_send[...] = jnp.zeros(head_send.shape, BF16)
    head_send[0:own, 0:classes] = head_own[...]
    for lead in range(MICRO):
        spread_columns(image_x, lead, 1, images[lead].astype(F32).reshape(cells, depth), extent)

    t_high = 16
    t_steps = wide // t_high
    t_rows = t_high * wide

    def teacher_conv(source, kernel, top):
        total = None
        for row_off in range(3):
            window = source[0, pl.ds(top + row_off, t_high)].reshape(t_rows, 3 * depth)
            term = jnp.dot(
                window, kernel[row_off * 3 * depth : (row_off + 1) * 3 * depth, :], preferred_element_type=F32
            )
            total = term if total is None else total + term
        return total

    def teacher_fill(lead):
        def fill(i, carry):
            top = i * t_high
            values = teacher_in[lead, pl.ds(top, t_high)].astype(F32).reshape(t_rows, depth)
            spread_columns(teacher_x, 0, top + 1, values, wide)
            return carry

        lax.fori_loop(0, t_steps, fill, 0)

    def teacher_one():
        def one(i, carry):
            top = i * t_high
            spread_columns(teacher_h, 0, top + 1, gelu(teacher_conv(teacher_x, teacher_w1, top)), wide)
            return carry

        lax.fori_loop(0, t_steps, one, 0)

    def teacher_two(lead):
        def two(i, total):
            top = i * t_high
            values = teacher_in[lead, pl.ds(top, t_high)].astype(F32).reshape(t_rows, depth)
            act = gelu(teacher_conv(teacher_h, teacher_w2, top) + values)
            return total + jnp.sum(act, axis=0, keepdims=True)

        return lax.fori_loop(0, t_steps, two, jnp.zeros((1, depth), F32))

    loads[11].wait()
    teacher_fill(0)
    loads[12].wait()
    teacher_one()

    pl.semaphore_wait(barrier, greeted)
    rounds = [[(b, sibling)]] + [[(peer, c) for peer in line] for line in lines]
    if chips == 4:
        rounds = [[(b, 2 * beside + core)]] + rounds

    def say(i):
        if i < len(rounds):
            for peer in rounds[i]:
                signal(known.at[i], *peer)

    def hear(i):
        if i < len(rounds):
            pl.semaphore_wait(known.at[i], len(rounds[i]))
            say(i + 1)

    say(0)

    pieces = 1
    piece_rows = own_rows // pieces
    square = chips == 4 and piece_rows % 32 == 0
    held = (w_first, w_second)
    offered = (own_first, own_second)

    def gather_copy(k, rows, sem, shard, target, source=None):
        slot = held[k].at[shard, rows]
        return pltpu.make_async_remote_copy(
            src_ref=slot if source is None else source.at[rows],
            dst_ref=slot,
            send_sem=gather_send.at[k],
            recv_sem=gather_recv.at[k, sem, shard],
            device_id=(b, target),
            device_id_type=MESH,
        )

    def whole_copy(k, piece, shard, target, source=None):
        return gather_copy(k, pl.ds(piece * piece_rows, piece_rows), piece, shard, target, source)

    def half_copy(k, piece, half, shard, target, source=None):
        rows = pl.ds(piece * piece_rows + half * (piece_rows // 2), piece_rows // 2)
        return gather_copy(k, rows, 2 * piece + half, shard, target, source)

    def shard_of(peer):
        return 2 * peer + core

    def gather_start(k):
        if square:
            for late in range(2):
                for piece in range(pieces):
                    half_copy(k, piece, late, c, shard_of(beside), offered[k]).start()
                    half_copy(k, piece, 1 - late, c, shard_of(above), offered[k]).start()
        for piece in range(pieces):
            if not square:
                each_chip(lambda peer, piece=piece: whole_copy(k, piece, c, shard_of(peer), offered[k]).start())
            whole_copy(k, piece, c, sibling, offered[k]).start()
        held[k][c] = offered[k][...]

    def gather_turn(k):
        if square:
            for piece in range(pieces):
                for half, source, target in ((0, beside, above), (1, above, beside)):
                    half_copy(k, piece, half, shard_of(source), sibling).wait_recv()
                    half_copy(k, piece, half, shard_of(source), shard_of(target)).start()

    def gather_forward(k, piece):
        if square:
            half_copy(k, piece, 1, shard_of(beside), sibling).wait_recv()
            half_copy(k, piece, 0, shard_of(above), sibling).wait_recv()
            whole_copy(k, piece, shard_of(beside), sibling).start()
            whole_copy(k, piece, shard_of(above), sibling).start()
            for half in range(2):
                half_copy(k, piece, half, shard_of(3 - chip), sibling).wait_recv()
            whole_copy(k, piece, shard_of(3 - chip), sibling).start()
        else:

            def one(peer):
                whole_copy(k, piece, shard_of(peer), sibling).wait_recv()
                whole_copy(k, piece, shard_of(peer), sibling).start()

            each_chip(one)

    def gather_finish(k, piece):
        def one(i, carry):
            whole_copy(k, piece, 2 * lax.rem(chip + i, chips) + 1 - core, sibling).wait_recv()
            return carry

        lax.fori_loop(0, chips, one, 0, unroll=chips <= 4)

    def bytes_of(sem, many):
        pltpu.make_async_copy(many, many, sem).wait()

    def swap(k, source, dest):
        return pltpu.make_async_remote_copy(
            src_ref=source,
            dst_ref=dest,
            send_sem=swap_ssem.at[k],
            recv_sem=swap_rsem.at[k],
            device_id=(b, sibling),
            device_id_type=MESH,
        )

    def tile_start(send, recv, ssem, rsem):
        def one(pb, pc):
            pltpu.make_async_remote_copy(
                src_ref=send, dst_ref=recv.at[me], send_sem=ssem, recv_sem=rsem, device_id=(pb, pc), device_id_type=MESH
            ).start()

        each_device(one)
        recv[me] = send[...]

    def tile_bytes(sem, recv):
        bytes_of(sem, recv.at[pl.ds(0, devices - 1)])

    def sync_start(stage, micro, rows):
        k = stage * MICRO + micro
        for i, row in enumerate(rows):
            for j, half in enumerate(halves(row)):
                sync_send[k, 2 * i + j : 2 * i + j + 1, :] = half
        tile_start(sync_send.at[k], sync_all[k], sync_ssem.at[k], sync_rsem.at[k])

    def sync_wait(stage, micro):
        k = stage * MICRO + micro
        tile_bytes(sync_rsem.at[k], sync_all[k])
        total = jnp.sum(sync_all[k][...], axis=0)
        return [jnp.concatenate([total[2 * i : 2 * i + 1], total[2 * i + 1 : 2 * i + 2]], axis=1) for i in range(2)]

    def plane_start(k, source, slot):
        def one(pc):
            pltpu.make_async_remote_copy(
                src_ref=source(pc),
                dst_ref=slot(c),
                send_sem=plane_ssem.at[k],
                recv_sem=plane_rsem.at[k],
                device_id=(b, pc),
                device_id_type=MESH,
            ).start()

        each_plane(one)

    def plane_wait(k, many):
        pltpu.make_async_copy(many, many, plane_rsem.at[k]).wait()

    def plane_drain(k, many):
        pltpu.make_async_copy(many, many, plane_ssem.at[k]).wait()

    gather_start(0)
    swaps = [swap(0, image_x, image_sib)]
    swaps[0].start()
    for load in loads[13:]:
        load.wait()
    teacher_rows = [teacher_two(0)]

    hear(0)

    teacher_fill(1)
    hear(1)
    plane_start(0, lambda pc: param_send, lambda s: param_all.at[s])
    plane_start(1, lambda pc: head_send, lambda s: head_all.at[s])
    param_all[c] = param_send[...]
    head_all[c] = head_send[...]
    teacher_one()
    gather_turn(0)
    hear(2)
    teacher_rows.append(teacher_two(1))
    which_t = lax.broadcasted_iota(jnp.int32, (8, depth), 0)
    pooled_t = jnp.zeros((8, depth), F32)
    for m in range(MICRO):
        pooled_t = jnp.where(which_t == m, teacher_rows[m] / float(wide * wide), pooled_t)
    teacher_head_pad[...] = jnp.zeros(teacher_head_pad.shape, F32)
    teacher_head_pad[0:classes, :] = teacher_head[...].astype(F32)
    teacher_logits = lax.dot_general(
        pooled_t, teacher_head_pad[...], (((1,), (1,)), ((), ())), precision=HIGHEST, preferred_element_type=F32
    )
    lane_pad = jnp.zeros((1, LANES - classes), F32)
    teacher_logits = teacher_logits + jnp.concatenate([teacher_bias[...], lane_pad], axis=1)
    image_sum = jnp.zeros((1, depth), F32)
    for m in range(MICRO):
        image_sum = image_sum + jnp.sum(images[m].astype(F32).reshape(cells, depth), axis=0, keepdims=True)
    logit_send[0:MICRO, :] = teacher_logits[0:MICRO]
    for j, half in enumerate(halves(image_sum)):
        logit_send[MICRO + j : MICRO + j + 1, :] = half
    gather_start(1)
    hear(3)
    tile_start(logit_send, logit_all, wide_ssem.at[0], wide_rsem.at[0])

    def picker(shard, block, offset):
        at_row = lax.broadcasted_iota(jnp.int32, (depth, block), 0)
        place = lax.broadcasted_iota(jnp.int32, (depth, block), 1) - offset
        wanted = jnp.logical_and(place >= 0, place < own)
        return jnp.logical_and(wanted, at_row == shard * own + place).astype(BF16)

    def unpack(ref, block, offset):
        def one(shard, total):
            return total + jnp.dot(picker(shard, block, offset), ref[shard], preferred_element_type=F32)

        return lax.fori_loop(0, chans, one, jnp.zeros((depth, ref.shape[2]), F32)).astype(BF16)

    def weights(ref, tap):
        if own_pad == own:
            return ref[:, tap * own : (tap + 1) * own, :].reshape(depth, depth)
        return unpack(ref, own_rows, tap * own)

    def window(source, micro, row_off):
        return source[micro, row_off : row_off + extent].reshape(cells, 3 * depth)

    def tap_row(ref, row_off, back):
        if back:
            return jnp.concatenate([weights(ref, (2 - row_off) * 3 + 2 - i) for i in range(3)], axis=0)
        return jnp.concatenate([weights(ref, row_off * 3 + i) for i in range(3)], axis=1)

    def student_conv(source, micro, ref):
        total = None
        for row_off in range(3):
            term = lax.dot_general(
                window(source, micro, row_off),
                tap_row(ref, row_off, False),
                (((1,), (1,)), ((), ())),
                preferred_element_type=F32,
            )
            total = term if total is None else total + term
        return total

    def student_back(source, micro, ref):
        total = None
        for row_off in range(3):
            term = jnp.dot(
                window(source, micro, row_off), tap_row(ref, row_off, True), preferred_element_type=F32
            )
            total = term if total is None else total + term
        return total

    def rows_of(m):
        return slice(m * cells, (m + 1) * cells)

    def col_sum(values):
        return jnp.sum(values, axis=0, keepdims=True)

    def moments_start(stage, m, values):
        sync_start(stage, m, (col_sum(values), col_sum(values * values)))

    def moments(stage, m):
        total, square = sync_wait(stage, m)
        center = total / samples
        spread = square / samples - center * center
        return (center, lax.rsqrt(spread + EPS))

    for piece in range(pieces):
        gather_forward(0, piece)
    for piece in range(pieces):
        gather_finish(0, piece)
    total = None
    for row_off in range(3):
        term = lax.dot_general(
            image_x[:, row_off : row_off + extent].reshape(MICRO * cells, 3 * depth),
            tap_row(w_first, row_off, False),
            (((1,), (1,)), ((), ())),
            preferred_element_type=F32,
        )
        total = term if total is None else total + term
    y_first[...] = total
    for m in range(MICRO):
        moments_start(0, m, total[rows_of(m), :])

    plane_wait(0, param_all.at[pl.ds(0, chans - 1)])
    plane_wait(1, head_all.at[pl.ds(0, chans - 1)])
    params = jnp.sum(param_all[...], axis=0)
    gain1, shift1, gain2, shift2 = (
        jnp.concatenate([params[2 * i : 2 * i + 1], params[2 * i + 1 : 2 * i + 2]], axis=1) for i in range(4)
    )
    if own_pad == own:
        head = head_all[...].reshape(depth, LANES)
    else:
        head = unpack(head_all, own_pad, 0)
    gather_turn(1)
    for piece in range(pieces):
        gather_forward(1, piece)
    for piece in range(pieces):
        gather_finish(1, piece)

    def three_parts(values):
        first = values.astype(BF16)
        rest = values - first.astype(F32)
        second = rest.astype(BF16)
        third = (rest - second.astype(F32)).astype(BF16)
        return jnp.concatenate([first, second, third], axis=0)

    def sum_parts(product):
        return product[0:8] + product[8:16] + product[16:24]

    norm1 = []
    for m in range(MICRO):
        center, inv = moments(0, m)
        norm1.append((center, inv))
        normed = (y_first[rows_of(m), :] - center) * (inv * gain1) + shift1
        spread_columns(hidden_x, m, 1, gelu(normed), extent)
        values = student_conv(hidden_x, m, w_second)
        y_second[rows_of(m), :] = values
        moments_start(1, m, values)
    swaps.append(swap(1, hidden_x, hidden_sib))
    swaps[1].start()
    for m in range(MICRO):
        center, inv = norm1[m]
        slope_first[rows_of(m), :] = gelu_slope((y_first[rows_of(m), :] - center) * (inv * gain1) + shift1)

    per_device = pair_index.shape[0]
    norm2, slope_scale = [], []
    tile_bytes(wide_rsem.at[0], logit_all)
    taught = []
    for m in range(MICRO):
        paired = pair_index[m]
        teacher_row = logit_all[pl.ds(paired // per_device, 1), pl.ds(lax.rem(paired, per_device), 1), :]
        taught.append(teacher_terms(teacher_row.reshape(1, LANES), labels[m], classes))
    which = lax.broadcasted_iota(jnp.int32, (8, depth), 0)
    which_lane = lax.broadcasted_iota(jnp.int32, (8, LANES), 0)
    for m in range(MICRO):
        center, inv = moments(1, m)
        norm2.append((center, inv))
        spread = y_second[rows_of(m), :] - center
        res = spread * (inv * gain2) + shift2 + images[m].astype(F32).reshape(cells, depth)
        square = res * res
        t = jnp.tanh(GELU_A * (res + GELU_B * (res * square)))
        half = 0.5 + 0.5 * t
        slope = half + (0.5 * res) * (1.0 - t * t) * (GELU_A + (3.0 * GELU_A * GELU_B) * square)
        slope_second[rows_of(m), :] = slope
        pooled = col_sum(res * half) / float(cells)
        slope_sum = col_sum(slope)
        slope_dot = col_sum(slope * spread) * inv
        product = jnp.dot(
            three_parts(jnp.where(which == 0, pooled, 0.0)), head, preferred_element_type=F32
        )
        logits = sum_parts(product)[0:1] + jnp.concatenate([head_bias[...], lane_pad], axis=1)
        grad = distill_grad(logits, taught[m], labels[m], classes)
        product = lax.dot_general(
            three_parts(jnp.where(which_lane == 0, grad, 0.0)),
            head,
            (((1,), (1,)), ((), ())),
            preferred_element_type=F32,
        )
        scale = sum_parts(product)[0:1] / float(cells)
        slope_scale.append(scale)
        sync_start(2, m, (scale * slope_dot, scale * slope_sum))
        for j, part in enumerate(halves(pooled)):
            wide_send[m * 4 + j : m * 4 + j + 1, :] = part
        wide_send[m * 4 + 2 : m * 4 + 3, :] = grad
        wide_send[m * 4 + 3 : m * 4 + 4, :] = logits
    plane_start(2, lambda pc: wide_send, lambda s: wide_all.at[s])
    wide_all[c] = wide_send[...]

    def own_lanes(low_row, high_row):
        at = c * own
        row = jnp.where(at >= LANES, high_row, low_row)
        turn = lax.rem(LANES - lax.rem(at, LANES), LANES)
        return pltpu.roll(jnp.broadcast_to(row, (8, LANES)), turn, 1)[0:1, 0:own]

    def norm_terms(stage, m, gain, norm):
        center, inv = norm
        totals = sync_wait(stage, m)
        scale = gain * inv
        slant = scale * inv * (totals[0] / samples)
        level = scale * (totals[1] / samples)
        return (scale, center, slant, level), totals

    def norm_apply(terms, grad, values):
        scale, center, slant, level = terms
        return grad * scale - (values - center) * slant - level

    def norm_out(totals, gain_out, shift_out):
        for out, i in ((gain_out, 0), (shift_out, 1)):
            row = totals[0][i]
            for m in range(1, MICRO):
                row = row + totals[m][i]
            out[...] = own_lanes(*halves(row))

    def by_core(whole, dest):
        if own_pad == own:
            dest[...] = whole.reshape(dest.shape)
        else:

            def one(shard, carry):
                dest[shard // 2, lax.rem(shard, 2)] = lax.dot_general(
                    picker(shard, own_pad, 0).astype(F32),
                    whole,
                    (((0,), (0,)), ((), ())),
                    precision=HIGHEST,
                    preferred_element_type=F32,
                )
                return carry

            lax.fori_loop(0, chans, one, 0)

    def hand(k, m, grad, values):
        by_core(jnp.transpose(grad), turned.at[k, m, 0])
        by_core(jnp.transpose(values), turned.at[k, m, 1])
        turns[k, m] = swap(2 + k * MICRO + m, turned.at[k, m, :, :, 1 - core], turned_sib.at[k, m])
        turns[k, m].start()

    def low_grads(k, m, terms):
        by_core(
            jnp.transpose(jnp.concatenate(list(terms) + [jnp.zeros((4, depth), F32)], axis=0)), turned_terms
        )
        columns = turned_terms[:, pl.ds(core, 1)].reshape(chips * own_pad, 8)
        scale, center, slant, level = (columns[:, i : i + 1] for i in range(4))
        mine = [turned[k, m, i, :, pl.ds(core, 1)].reshape(chips * own_pad, cells) for i in range(2)]
        turns[k, m].wait_recv()
        theirs = [turned_sib[k, m, i].reshape(chips * own_pad, cells) for i in range(2)]
        return [norm_apply((scale, center, slant, level), *pair).astype(BF16) for pair in (mine, theirs)]

    turns = {}
    taps = 3 * own_pad
    per_half = groups // 2
    part_rows = taps // per_half
    part_pad = sum_send.shape[2]
    across = {0: None, 1: 2}
    planar = {0: (0, 1, 2), 1: (0, 1)}

    def send(source, dest, ssem, rsem, peer_b, peer_c):
        pltpu.make_async_remote_copy(
            src_ref=source, dst_ref=dest, send_sem=ssem, recv_sem=rsem, device_id=(peer_b, peer_c), device_id_type=MESH
        ).start()

    def cut(p):
        half, row = p // per_half, (p % per_half) * part_rows
        return slice(row, row + part_rows), slice(half * LANES, (half + 1) * LANES)

    def kernel_grad(k, grads, source, source_sib, mean):
        sides = [(grads[m][i], ref, m) for m in range(MICRO) for i, ref in enumerate((source, source_sib))]
        level = sum(jnp.sum(low.astype(F32), axis=1, keepdims=True) for low, _, _ in sides)
        for row_off in (2, 0, 1):
            total = sum(
                jnp.dot(
                    low,
                    ref[m, row_off : row_off + extent].reshape(cells, 3 * depth),
                    preferred_element_type=F32,
                )
                for low, ref, m in sides
            )
            for col_off in range(3):
                block = total[:, col_off * depth : (col_off + 1) * depth] - level * mean
                for i in range(chips):
                    part_all[i, col_off * own_pad : (col_off + 1) * own_pad, :] = block[i * own_pad : (i + 1) * own_pad]
            if row_off == across[k]:
                for p in range(groups):
                    rows, lanes = cut(p)
                    cross_all[p, :, 0:part_rows] = part_all[:, rows, lanes]
                    if part_pad != part_rows:
                        cross_all[p, :, part_rows:part_pad] = jnp.zeros((chips, part_pad - part_rows, LANES), F32)
                cross_send[k] = cross_all[...].astype(BF16)
                cross_own[k] = cross_all[pl.ds(b, 1)].reshape(chips, part_pad, LANES)
                each_line(
                    lambda peer: send(
                        cross_send.at[k, peer], cross_recv.at[k, b], cross_ssem.at[k], cross_rsem.at[k], peer, c
                    )
                )
                cross_recv[k, b] = jnp.zeros((chips, part_pad, LANES), BF16)
            else:
                part_send[k, row_off] = part_all[...].astype(BF16)
                part_own[k, row_off] = part_all[pl.ds(chip, 1)].reshape(taps, depth)
                each_chip(
                    lambda peer, row_off=row_off: send(
                        part_send.at[k, row_off, peer],
                        part_recv.at[k, row_off, chip],
                        part_ssem.at[k, row_off],
                        part_rsem.at[k, row_off],
                        b,
                        2 * peer + core,
                    )
                )
                part_recv[k, row_off, chip] = jnp.zeros((taps, depth), BF16)
        ones = jnp.ones((8, cells), BF16)
        level_send[k] = sum(
            lax.dot_general(ones, low, (((1,), (1,)), ((), ())), preferred_element_type=F32) for low, _, _ in sides
        )[0:1]
        each_chip(
            lambda peer: send(
                level_send.at[k], level_recv.at[k, chip], level_ssem.at[k], level_rsem.at[k], b, 2 * peer + core
            )
        )
        level_recv[k, chip] = level_send[k]

    def line_start(k):
        for row_off in planar[k]:
            bytes_of(part_rsem.at[k, row_off], part_recv.at[k, row_off, pl.ds(0, chips - 1)])
            total = part_own[k, row_off] + jnp.sum(part_recv[k, row_off].astype(F32), axis=0)
            for p in range(groups):
                line_own[k, row_off, p, 0:part_rows] = total[cut(p)]
                if part_pad != part_rows:
                    line_own[k, row_off, p, part_rows:part_pad] = jnp.zeros((part_pad - part_rows, LANES), F32)
            line_send[k, row_off] = line_own[k, row_off].astype(BF16)
            each_line(
                lambda peer, row_off=row_off: send(
                    line_send.at[k, row_off, peer],
                    line_recv.at[k, row_off, b],
                    line_ssem.at[k, row_off],
                    line_rsem.at[k, row_off],
                    peer,
                    c,
                )
            )
            line_recv[k, row_off, b] = jnp.zeros((part_pad, LANES), BF16)
        bytes_of(level_rsem.at[k], level_recv.at[k, pl.ds(0, chips - 1)])
        level_line_send[k] = jnp.sum(level_recv[k], axis=0)
        each_line(
            lambda peer: send(
                level_line_send.at[k], level_line_recv.at[k, b], level_line_ssem.at[k], level_line_rsem.at[k], peer, c
            )
        )
        level_line_recv[k, b] = level_line_send[k]

    def cross_forward(k):
        if across[k] is None:
            return
        bytes_of(cross_rsem.at[k], cross_recv.at[k, pl.ds(0, groups - 1)])
        last_all[...] = cross_own[k] + jnp.sum(cross_recv[k].astype(F32), axis=0)
        last_send[k] = last_all[...].astype(BF16)
        last_own[k] = last_all[pl.ds(chip, 1)].reshape(part_pad, LANES)
        each_chip(
            lambda peer: send(
                last_send.at[k, peer], last_recv.at[k, chip], last_ssem.at[k], last_rsem.at[k], b, 2 * peer + core
            )
        )
        last_recv[k, chip] = jnp.zeros((part_pad, LANES), BF16)

    def share(k, row_off, total):
        sum_send[k, row_off] = total.astype(BF16)
        each_line(
            lambda peer: send(
                sum_send.at[k, row_off],
                sum_recv.at[k, row_off, b],
                sum_ssem.at[k, row_off],
                sum_rsem.at[k, row_off],
                peer,
                c,
            )
        )
        sum_recv[k, row_off, b] = sum_send[k, row_off]

    def cross_sum(k):
        if across[k] is None:
            return
        bytes_of(last_rsem.at[k], last_recv.at[k, pl.ds(0, chips - 1)])
        share(k, across[k], last_own[k] + jnp.sum(last_recv[k].astype(F32), axis=0))

    def line_sum(k):
        for row_off in planar[k]:
            bytes_of(line_rsem.at[k, row_off], line_recv.at[k, row_off, pl.ds(0, groups - 1)])
            share(
                k,
                row_off,
                line_own[k, row_off, pl.ds(b, 1)].reshape(part_pad, LANES)
                + jnp.sum(line_recv[k, row_off].astype(F32), axis=0),
            )

    def sum_finish(k, mean, out):
        bytes_of(level_line_rsem.at[k], level_line_recv.at[k, pl.ds(0, groups - 1)])
        level = jnp.sum(level_line_recv[k], axis=0)
        level_column[...] = jnp.transpose(jnp.broadcast_to(level, (LANES, level.shape[1])))
        column_own = level_column[pl.ds(chip * own_pad, own_pad), :]
        back = [column_own * half for half in halves(mean)]
        for row_off in (0, 1, 2):
            bytes_of(sum_rsem.at[k, row_off], sum_recv.at[k, row_off, pl.ds(0, groups - 1)])
            for half in range(2):
                rows = sum_recv[k, row_off, half * per_half : (half + 1) * per_half, 0:part_rows].astype(F32)
                out[row_off * 3 : row_off * 3 + 3, :, half * LANES : (half + 1) * LANES] = (
                    rows.reshape(3, own_pad, LANES) + back[half][None]
                )

    for m in range(MICRO):
        hand(0, m, slope_second[rows_of(m), :] * slope_scale[m], y_second[rows_of(m), :])
    terms2, totals2 = [], []
    for m in range(MICRO):
        terms, totals = norm_terms(2, m, gain2, norm2[m])
        terms2.append(terms)
        totals2.append(totals)
        found = norm_apply(terms, slope_second[rows_of(m), :] * slope_scale[m], y_second[rows_of(m), :])
        spread_columns(grad_x, m, 1, found, extent)
        grad = student_back(grad_x, m, w_second) * slope_first[rows_of(m), :]
        d_hid[rows_of(m), :] = grad
        center, inv = norm1[m]
        sync_start(3, m, (col_sum(grad * (y_first[rows_of(m), :] - center)) * inv, col_sum(grad)))

    hidden_mean = jnp.zeros((1, depth), F32)
    for node, weight in QUADRATURE:
        hidden_mean = hidden_mean + weight * gelu(shift1 + gain1 * node)
    image_rows = jnp.sum(logit_all[...], axis=0)
    image_mean = jnp.concatenate([image_rows[MICRO : MICRO + 1], image_rows[MICRO + 1 : MICRO + 2]], axis=1) / (
        MICRO * samples
    )

    swaps[0].wait_recv()
    swaps[1].wait_recv()
    kernel_grad(0, [low_grads(0, m, terms2[m]) for m in range(MICRO)], hidden_x, hidden_sib, hidden_mean)
    for m in range(MICRO):
        hand(1, m, d_hid[rows_of(m), :], y_first[rows_of(m), :])
    norm_out(totals2, gain_second_grad, shift_second_grad)

    plane_wait(2, wide_all.at[pl.ds(0, chans - 1)])
    totals = [jnp.zeros((LANES, LANES), F32) for _ in range(2)]
    bias_row = jnp.zeros((1, LANES), F32)
    for m in range(MICRO):
        per_image = wide_all[:, m * 4 + 2, :]
        bias_row = bias_row + col_sum(per_image)
        for j in range(2):
            totals[j] = totals[j] + lax.dot_general(
                wide_all[:, m * 4 + j, :],
                per_image,
                (((0,), (0,)), ((), ())),
                precision=HIGHEST,
                preferred_element_type=F32,
            )
        for j in range(chans):
            logits_out[j * MICRO + m : j * MICRO + m + 1, :] = wide_all[j, m * 4 + 3 : m * 4 + 4, 0:classes]
    for j in range(2):
        head_sum[j * LANES : (j + 1) * LANES, :] = totals[j]
    head_line_send[0:own, :] = head_sum[pl.ds(c * own, own), :]
    head_line_send[own : own + 8, :] = jnp.broadcast_to(bias_row, (8, LANES))
    each_line(
        lambda peer: send(head_line_send, head_line_recv.at[b], wide_ssem.at[1], wide_rsem.at[1], peer, c)
    )
    head_line_recv[b] = head_line_send[...]

    terms1, totals1, lows = [], [], []
    for m in range(MICRO):
        terms, totals = norm_terms(3, m, gain1, norm1[m])
        terms1.append(terms)
        totals1.append(totals)
        lows.append(low_grads(1, m, terms))
    kernel_grad(1, lows, image_x, image_sib, image_mean)
    for m in range(MICRO):
        found = norm_apply(terms1[m], d_hid[rows_of(m), :], y_first[rows_of(m), :])
        spread_columns(grad_x, m, 1, found, extent)
        images_grad[m] = (
            student_back(grad_x, m, w_first) + slope_second[rows_of(m), :] * slope_scale[m]
        ).reshape(images_grad.shape[1:])
    norm_out(totals1, gain_first_grad, shift_first_grad)
    line_start(0)
    cross_forward(0)

    cross_sum(0)
    line_start(1)
    cross_forward(1)
    line_sum(0)
    cross_sum(1)
    line_sum(1)
    bytes_of(wide_rsem.at[1], head_line_recv.at[pl.ds(0, groups - 1)])
    head_total = jnp.sum(head_line_recv[...], axis=0)
    head_grad[...] = head_total[0:own, 0:classes]
    bias_grad[...] = head_total[own : own + 1, 0:classes]
    sum_finish(0, hidden_mean, second_grad)
    sum_finish(1, image_mean, first_grad)

    tile_bytes(wide_ssem.at[0], logit_all)
    bytes_of(wide_ssem.at[1], head_line_recv.at[pl.ds(0, groups - 1)])
    plane_drain(2, wide_all.at[pl.ds(0, chans - 1)])
    for k in range(2):
        bytes_of(gather_send.at[k], held[k].at[pl.ds(0, chans - 1)])
    for k in range(4 * MICRO):
        tile_bytes(sync_ssem.at[k], sync_all[k])
    plane_drain(0, param_all.at[pl.ds(0, chans - 1)])
    plane_drain(1, head_all.at[pl.ds(0, chans - 1)])
    for copy in swaps + list(turns.values()):
        copy.wait_send()
    for k in range(2):
        for row_off in planar[k]:
            bytes_of(part_ssem.at[k, row_off], part_recv.at[k, row_off, pl.ds(0, chips - 1)])
            bytes_of(line_ssem.at[k, row_off], line_recv.at[k, row_off, pl.ds(0, groups - 1)])
        for row_off in range(3):
            bytes_of(sum_ssem.at[k, row_off], sum_recv.at[k, row_off, pl.ds(0, groups - 1)])
        if across[k] is not None:
            bytes_of(cross_ssem.at[k], cross_recv.at[k, pl.ds(0, groups - 1)])
            bytes_of(last_ssem.at[k], last_recv.at[k, pl.ds(0, chips - 1)])
        bytes_of(level_ssem.at[k], level_recv.at[k, pl.ds(0, chips - 1)])
        bytes_of(level_line_ssem.at[k], level_line_recv.at[k, pl.ds(0, groups - 1)])


def hand_on(*refs):
    count = len(refs) // 2
    copies = [pltpu.make_async_copy(refs[i], refs[count + i], refs[-1].at[i]) for i in range(count)]
    for copy in copies:
        copy.start()
    for copy in copies:
        copy.wait()


def shards(
    teacher_images,
    student_images,
    pair_index,
    labels,
    teacher_first,
    teacher_second,
    teacher_head,
    teacher_bias,
    conv_first,
    gain_first,
    shift_first,
    conv_second,
    gain_second,
    shift_second,
    head_weight,
    head_bias,
):
    groups, chans = lax.axis_size("batch"), lax.axis_size("chan")
    devices = groups * chans
    count, extent, _, depth = student_images.shape
    wide = teacher_images.shape[1]
    own = conv_first.shape[3]
    own_pad = max(own, 16)
    own_rows = -(-9 * own // 16) * 16
    classes = head_bias.shape[0]
    cells = extent * extent
    rows = count * cells
    chips = chans // 2
    taps = 3 * own_pad
    part_rows = 2 * taps // groups
    part_pad = -(-part_rows // 16) * 16

    def turned(kernel):
        return jnp.transpose(kernel, (0, 1, 3, 2)).reshape(9 * own, depth)

    def row(vector):
        return vector.reshape(1, -1)

    vmem = pl.BlockSpec(memory_space=pltpu.VMEM)
    hbm = pl.BlockSpec(memory_space=pl.ANY)
    out_shape = [
        jax.ShapeDtypeStruct((chans * count, classes), F32),
        jax.ShapeDtypeStruct(student_images.shape, F32),
        jax.ShapeDtypeStruct((9, own_pad, depth), F32),
        jax.ShapeDtypeStruct((1, own), F32),
        jax.ShapeDtypeStruct((1, own), F32),
        jax.ShapeDtypeStruct((9, own_pad, depth), F32),
        jax.ShapeDtypeStruct((1, own), F32),
        jax.ShapeDtypeStruct((1, own), F32),
        jax.ShapeDtypeStruct((own, classes), F32),
        jax.ShapeDtypeStruct((1, classes), F32),
    ]
    stage = (16, LANES) if own_rows == 9 * own else (9 * own, depth)
    scratch = [
        pltpu.SMEM(pair_index.shape, jnp.int32),
        pltpu.SMEM(labels.shape, jnp.int32),
        pltpu.VMEM(stage, BF16),
        pltpu.VMEM(stage, BF16),
        pltpu.VMEM(student_images.shape, BF16),
        pltpu.VMEM((classes, depth), BF16),
        pltpu.VMEM((1, classes), F32),
        pltpu.VMEM((1, own), F32),
        pltpu.VMEM((1, own), F32),
        pltpu.VMEM((1, own), F32),
        pltpu.VMEM((1, own), F32),
        pltpu.VMEM((own, classes), BF16),
        pltpu.VMEM((1, classes), F32),
        pltpu.VMEM(teacher_images.shape, BF16),
        pltpu.VMEM((9 * depth, depth), BF16),
        pltpu.VMEM((9 * depth, depth), BF16),
        pltpu.VMEM((1, wide + 2, wide, 3 * depth), BF16),
        pltpu.VMEM((1, wide + 2, wide, 3 * depth), BF16),
        pltpu.VMEM((LANES, depth), F32),
        pltpu.VMEM((count, extent + 2, extent, 3 * depth), BF16),
        pltpu.VMEM((count, extent + 2, extent, 3 * depth), BF16),
        pltpu.VMEM((count, extent + 2, extent, 3 * depth), BF16),
        pltpu.VMEM((chans, own_rows, depth), BF16),
        pltpu.VMEM((chans, own_rows, depth), BF16),
        pltpu.VMEM((own_rows, depth), BF16),
        pltpu.VMEM((own_rows, depth), BF16),
        pltpu.VMEM((rows, depth), F32),
        pltpu.VMEM((rows, depth), F32),
        pltpu.VMEM((rows, depth), F32),
        pltpu.VMEM((rows, depth), F32),
        pltpu.VMEM((rows, depth), F32),
        pltpu.VMEM((count, extent + 2, extent, 3 * depth), BF16),
        pltpu.VMEM((count, extent + 2, extent, 3 * depth), BF16),
        pltpu.VMEM((2, count, 2, chips, 2, own_pad, cells), F32),
        pltpu.VMEM((2, count, 2, chips, own_pad, cells), F32),
        pltpu.VMEM((chips, 2, own_pad, 8), F32),
        pltpu.VMEM((chips, taps, depth), F32),
        pltpu.VMEM((2, 3, taps, depth), F32),
        pltpu.VMEM((2, 3, chips, taps, depth), BF16),
        pltpu.VMEM((2, 3, chips, taps, depth), BF16),
        pltpu.VMEM((groups, chips, part_pad, LANES), F32),
        pltpu.VMEM((2, chips, part_pad, LANES), F32),
        pltpu.VMEM((2, groups, chips, part_pad, LANES), BF16),
        pltpu.VMEM((2, groups, chips, part_pad, LANES), BF16),
        pltpu.VMEM((chips, part_pad, LANES), F32),
        pltpu.VMEM((2, part_pad, LANES), F32),
        pltpu.VMEM((2, chips, part_pad, LANES), BF16),
        pltpu.VMEM((2, chips, part_pad, LANES), BF16),
        pltpu.VMEM((2, 3, groups, part_pad, LANES), F32),
        pltpu.VMEM((2, 3, groups, part_pad, LANES), BF16),
        pltpu.VMEM((2, 3, groups, part_pad, LANES), BF16),
        pltpu.VMEM((2, 3, part_pad, LANES), BF16),
        pltpu.VMEM((2, 3, groups, part_pad, LANES), BF16),
        pltpu.VMEM((2, 1, chips * own_pad), F32),
        pltpu.VMEM((2, chips, 1, chips * own_pad), F32),
        pltpu.VMEM((2, 1, chips * own_pad), F32),
        pltpu.VMEM((2, groups, 1, chips * own_pad), F32),
        pltpu.VMEM((chips * own_pad, LANES), F32),
        pltpu.VMEM((8, LANES), F32),
        pltpu.VMEM((chans, 8, LANES), F32),
        pltpu.VMEM((own_pad, LANES), BF16),
        pltpu.VMEM((chans, own_pad, LANES), BF16),
        pltpu.VMEM((4, LANES), F32),
        pltpu.VMEM((devices, 4, LANES), F32),
        pltpu.VMEM((8, LANES), F32),
        pltpu.VMEM((chans, 8, LANES), F32),
        pltpu.VMEM((4 * MICRO, 4, LANES), F32),
        pltpu.VMEM((devices, 4, LANES), F32),
        pltpu.VMEM((devices, 4, LANES), F32),
        pltpu.VMEM((devices, 4, LANES), F32),
        pltpu.VMEM((devices, 4, LANES), F32),
        pltpu.VMEM((devices, 4, LANES), F32),
        pltpu.VMEM((devices, 4, LANES), F32),
        pltpu.VMEM((devices, 4, LANES), F32),
        pltpu.VMEM((devices, 4, LANES), F32),
        pltpu.VMEM((depth, LANES), F32),
        pltpu.VMEM((own + 8, LANES), F32),
        pltpu.VMEM((groups, own + 8, LANES), F32),
        pltpu.SemaphoreType.DMA((16,)),
        pltpu.SemaphoreType.DMA((2,)),
        pltpu.SemaphoreType.DMA((2, 6, chans)),
        pltpu.SemaphoreType.DMA((2,)),
        pltpu.SemaphoreType.DMA((2,)),
        pltpu.SemaphoreType.DMA((4 * MICRO,)),
        pltpu.SemaphoreType.DMA((4 * MICRO,)),
        pltpu.SemaphoreType.REGULAR((4,)),
        pltpu.SemaphoreType.DMA((3,)),
        pltpu.SemaphoreType.DMA((3,)),
        pltpu.SemaphoreType.DMA((2 + 2 * MICRO,)),
        pltpu.SemaphoreType.DMA((2 + 2 * MICRO,)),
        pltpu.SemaphoreType.DMA((2, 3)),
        pltpu.SemaphoreType.DMA((2, 3)),
        pltpu.SemaphoreType.DMA((2,)),
        pltpu.SemaphoreType.DMA((2,)),
        pltpu.SemaphoreType.DMA((2,)),
        pltpu.SemaphoreType.DMA((2,)),
        pltpu.SemaphoreType.DMA((2,)),
        pltpu.SemaphoreType.DMA((2,)),
        pltpu.SemaphoreType.DMA((2,)),
        pltpu.SemaphoreType.DMA((2,)),
        pltpu.SemaphoreType.DMA((2, 3)),
        pltpu.SemaphoreType.DMA((2, 3)),
        pltpu.SemaphoreType.DMA((2, 3)),
        pltpu.SemaphoreType.DMA((2, 3)),
    ]
    found = pl.pallas_call(
        functools.partial(body, (groups, chans, own, own_pad, classes)),
        out_shape=[pltpu.VMEM(out.shape, out.dtype) for out in out_shape],
        in_specs=[hbm] * 16,
        out_specs=[vmem] * 10,
        scratch_shapes=scratch,
        compiler_params=pltpu.CompilerParams(
            collective_id=0, has_side_effects=True, vmem_limit_bytes=62 * 2**20
        ),
    )(
        teacher_images,
        student_images,
        pair_index,
        labels,
        teacher_first.reshape(9 * depth, depth),
        teacher_second.reshape(9 * depth, depth),
        teacher_head.T,
        row(teacher_bias),
        turned(conv_first),
        row(gain_first),
        row(shift_first),
        turned(conv_second),
        row(gain_second),
        row(shift_second),
        head_weight,
        row(head_bias),
    )
    found = pl.pallas_call(
        hand_on,
        out_shape=out_shape,
        in_specs=[vmem] * len(out_shape),
        out_specs=[hbm] * len(out_shape),
        scratch_shapes=[pltpu.SemaphoreType.DMA((len(out_shape),))],
    )(*[pltpu.with_memory_space_constraint(x, pltpu.VMEM) for x in found])
    logits, images_grad, first, gain1, shift1, second, gain2, shift2, head, bias = found

    def back(grad):
        return jnp.transpose(grad[:, :own].reshape(3, 3, own, depth), (0, 1, 3, 2))

    return (
        logits,
        images_grad,
        back(first),
        gain1.reshape(-1),
        shift1.reshape(-1),
        back(second),
        gain2.reshape(-1),
        shift2.reshape(-1),
        head,
        bias.reshape(-1),
    )


def solution(mesh):
    in_specs = (
        P(("batch", "chan"), None, None, None),
        P(("batch", "chan"), None, None, None),
        P(("batch", "chan")),
        P(("batch", "chan")),
        P(),
        P(),
        P(),
        P(),
        P(None, None, None, "chan"),
        P("chan"),
        P("chan"),
        P(None, None, None, "chan"),
        P("chan"),
        P("chan"),
        P("chan", None),
        P(),
    )
    out_specs = (
        P("batch", None),
        P(("batch", "chan"), None, None, None),
        P(None, None, None, "chan"),
        P("chan"),
        P("chan"),
        P(None, None, None, "chan"),
        P("chan"),
        P("chan"),
        P("chan", None),
        P(),
    )
    return jax.shard_map(shards, mesh=mesh, in_specs=in_specs, out_specs=out_specs, check_vma=False)
```

```python
import functools

import jax
import jax.numpy as jnp
from jax import lax
from jax.experimental import pallas as pl
from jax.experimental.pallas import tpu as pltpu
from jax.sharding import PartitionSpec as P

MESH = pl.DeviceIdType.MESH
F32 = jnp.float32
BF16 = jnp.bfloat16
HIGHEST = lax.Precision.HIGHEST
MICRO = 2
EPS = 1e-05
TARGET_WEIGHT = 1.0
NONTARGET_WEIGHT = 8.0
SOFTEN = 4.0
GELU_A = 0.7978845608028654
GELU_B = 0.044715
LANES = 128
QUADRATURE = (
    (0.0, 0.5333333333),
    (1.3556261800, 0.2220759220),
    (-1.3556261800, 0.2220759220),
    (2.8569700139, 0.0112574113),
    (-2.8569700139, 0.0112574113),
)


def gelu(x):
    return x * (0.5 + 0.5 * jnp.tanh(GELU_A * (x + GELU_B * (x * x * x))))


def gelu_slope(x):
    square = x * x
    t = jnp.tanh(GELU_A * (x + GELU_B * (x * square)))
    return 0.5 + 0.5 * t + (0.5 * x) * (1.0 - t * t) * (GELU_A + (3.0 * GELU_A * GELU_B) * square)


def column(shape, width):
    return lax.rem(lax.broadcasted_iota(jnp.int32, shape, 0), width)


def spread_columns(dest, lead, top, values, width):
    rows, depth = values.shape
    col = column(values.shape, width)
    left = jnp.where(col == 0, 0.0, pltpu.roll(values, 1, 0))
    right = jnp.where(col == width - 1, 0.0, pltpu.roll(values, rows - 1, 0))
    high = rows // width
    for place, part in enumerate((left, values, right)):
        dest[lead, pl.ds(top, high), :, place * depth : (place + 1) * depth] = part.astype(BF16).reshape(
            high, width, depth
        )


def halves(row):
    return (row[:, :LANES], row[:, LANES:])


def soft_parts(logits, label, classes):
    lane = lax.broadcasted_iota(jnp.int32, logits.shape, 1)
    live = lane < classes
    target = lane == label
    other = jnp.logical_and(live, jnp.logical_not(target))
    low = -1e30
    soft = logits / SOFTEN
    whole_top = jnp.max(jnp.where(live, soft, low), axis=1, keepdims=True)
    rest_top = jnp.max(jnp.where(other, soft, low), axis=1, keepdims=True)
    whole_exp = jnp.where(live, jnp.exp(jnp.where(live, soft, whole_top) - whole_top), 0.0)
    rest_exp = jnp.where(other, jnp.exp(jnp.where(other, soft, rest_top) - rest_top), 0.0)
    whole_sum = jnp.sum(whole_exp, axis=1, keepdims=True)
    rest_sum = jnp.sum(rest_exp, axis=1, keepdims=True)
    whole = whole_top + jnp.log(whole_sum)
    rest = rest_top + jnp.log(rest_sum)
    true = jnp.sum(jnp.where(target, soft, 0.0), axis=1, keepdims=True)
    return (whole_exp / whole_sum, rest_exp / rest_sum, true - whole, rest - whole, target)


def teacher_terms(teacher, label, classes):
    _, inner, log_true, log_rest, target = soft_parts(teacher, label, classes)
    true, rest = jnp.exp(log_true), jnp.exp(log_rest)
    fixed = TARGET_WEIGHT * jnp.where(target, true, 0.0) + NONTARGET_WEIGHT * inner
    return (
        SOFTEN * TARGET_WEIGHT * (true + rest),
        SOFTEN * (NONTARGET_WEIGHT * jnp.sum(inner, axis=1, keepdims=True) - TARGET_WEIGHT * rest),
        SOFTEN * fixed,
    )


def distill_grad(student, terms, label, classes):
    probs, inner, _, _, _ = soft_parts(student, label, classes)
    whole, rest, fixed = terms
    return whole * probs + rest * inner - fixed


def body(
    sizes,
    teacher_hbm,
    images_hbm,
    pair_index_hbm,
    labels_hbm,
    teacher_first_hbm,
    teacher_second_hbm,
    teacher_head_hbm,
    teacher_bias_hbm,
    first_hbm,
    gain_first_hbm,
    shift_first_hbm,
    second_hbm,
    gain_second_hbm,
    shift_second_hbm,
    head_hbm,
    head_bias_hbm,
    logits_out,
    images_grad,
    first_grad,
    gain_first_grad,
    shift_first_grad,
    second_grad,
    gain_second_grad,
    shift_second_grad,
    head_grad,
    bias_grad,
    pair_index,
    labels,
    stage_first,
    stage_second,
    images,
    teacher_head,
    teacher_bias,
    gain_first,
    shift_first,
    gain_second,
    shift_second,
    head_own,
    head_bias,
    teacher_in,
    teacher_w1,
    teacher_w2,
    teacher_x,
    teacher_h,
    teacher_head_pad,
    image_x,
    hidden_x,
    grad_x,
    w_first,
    w_second,
    own_first,
    own_second,
    y_first,
    y_second,
    slope_first,
    slope_second,
    d_hid,
    image_sib,
    hidden_sib,
    turned,
    turned_sib,
    turned_terms,
    part_all,
    part_own,
    part_send,
    part_recv,
    cross_all,
    cross_own,
    cross_send,
    cross_recv,
    last_all,
    last_own,
    last_send,
    last_recv,
    line_own,
    line_send,
    line_recv,
    sum_send,
    sum_recv,
    level_send,
    level_recv,
    level_line_send,
    level_line_recv,
    level_column,
    param_send,
    param_all,
    head_send,
    head_all,
    logit_send,
    logit_all,
    wide_send,
    wide_all,
    sync_send,
    sync_all_0,
    sync_all_1,
    sync_all_2,
    sync_all_3,
    sync_all_4,
    sync_all_5,
    sync_all_6,
    sync_all_7,
    head_sum,
    head_line_send,
    head_line_recv,
    local_sem,
    gather_send,
    gather_recv,
    wide_ssem,
    wide_rsem,
    sync_ssem,
    sync_rsem,
    known,
    plane_ssem,
    plane_rsem,
    swap_ssem,
    swap_rsem,
    part_ssem,
    part_rsem,
    cross_ssem,
    cross_rsem,
    last_ssem,
    last_rsem,
    level_ssem,
    level_rsem,
    level_line_ssem,
    level_line_rsem,
    line_ssem,
    line_rsem,
    sum_ssem,
    sum_rsem,
):
    groups, chans, own, own_pad, classes = sizes
    sync_all = (
        sync_all_0,
        sync_all_1,
        sync_all_2,
        sync_all_3,
        sync_all_4,
        sync_all_5,
        sync_all_6,
        sync_all_7,
    )
    b = lax.axis_index("batch")
    c = lax.axis_index("chan")
    me = b * chans + c
    devices = groups * chans
    sibling = c + 1 - 2 * lax.rem(c, 2)
    extent = images.shape[1]
    cells = extent * extent
    depth = images.shape[3]
    wide = teacher_hbm.shape[1]
    samples = float(devices * cells)
    chips = chans // 2
    chip, core = c // 2, lax.rem(c, 2)

    if groups == 4:
        far_first = [groups - 1 - b, lax.rem(b + 2, groups), b + 1 - 2 * lax.rem(b, 2)]
    else:
        far_first = [lax.rem(b + i, groups) for i in range(1, groups)]

    def each_device(fn):
        for peer_b in far_first + [b]:

            def one(i, carry, peer_b=peer_b):
                fn(peer_b, lax.rem(c + (chans - i), chans))
                return carry

            lax.fori_loop(1 if peer_b is b else 0, chans, one, 0, unroll=chans <= 8)

    def each_chip(fn):
        def one(i, carry):
            fn(lax.rem(chip + i, chips))
            return carry

        lax.fori_loop(1, chips, one, 0, unroll=chips <= 4)

    def each_line(fn):
        for peer_b in far_first:
            fn(peer_b)

    def signal(sem, peer_b, peer_c):
        pl.semaphore_signal(sem, inc=1, device_id=(peer_b, peer_c), device_id_type=MESH)

    def each_plane(fn):
        def one(i, carry):
            fn(lax.rem(c + i, chans))
            return carry

        lax.fori_loop(1, chans, one, 0, unroll=chans <= 8)

    if chips == 4:
        beside = chip + 1 - 2 * lax.rem(chip, 2)
        above = lax.rem(chip + 2, chips)
        near = [beside, above]
    else:
        near = [lax.rem(chip + i, chips) for i in range(1, chips)]
    if groups == 4:
        lines = [[b + 1 - 2 * lax.rem(b, 2)], [lax.rem(b + 2, groups)]]
    else:
        lines = [far_first]
    barrier = pltpu.get_barrier_semaphore()
    for peer in near:
        signal(barrier, b, 2 * peer + core)
    for line in lines:
        for peer in line:
            signal(barrier, peer, c)
    signal(barrier, b, sibling)
    greeted = len(near) + sum(len(line) for line in lines) + 1

    own_rows = own_first.shape[0]
    exact = own_rows == 9 * own
    moves = (
        (first_hbm, own_first if exact else stage_first),
        (images_hbm, images),
        (second_hbm, own_second if exact else stage_second),
        (gain_first_hbm, gain_first),
        (shift_first_hbm, shift_first),
        (gain_second_hbm, gain_second),
        (shift_second_hbm, shift_second),
        (head_hbm, head_own),
        (head_bias_hbm, head_bias),
        (teacher_bias_hbm, teacher_bias),
        (teacher_head_hbm, teacher_head),
        (teacher_hbm, teacher_in),
        (teacher_first_hbm, teacher_w1),
        (teacher_second_hbm, teacher_w2),
        (pair_index_hbm, pair_index),
        (labels_hbm, labels),
    )
    loads = [pltpu.make_async_copy(source, dest, local_sem.at[i]) for i, (source, dest) in enumerate(moves)]
    for load in loads:
        load.start()

    for ref in (image_x, hidden_x, grad_x, teacher_x, teacher_h):
        high = ref.shape[1]
        for lead in range(ref.shape[0]):
            ref[lead, 0] = jnp.zeros(ref.shape[2:], BF16)
            ref[lead, high - 1] = jnp.zeros(ref.shape[2:], BF16)
    for load in loads[:11]:
        load.wait()
    if not exact:
        for source, dest in ((stage_first, own_first), (stage_second, own_second)):
            dest[...] = jnp.zeros(dest.shape, BF16)
            dest[0 : 9 * own, :] = source[...]

    def place_own(param_row):
        at = c * own
        lane0 = lax.rem(at, LANES)
        padded = jnp.concatenate([param_row, jnp.zeros((1, LANES - own), F32)], axis=1)
        moved = pltpu.roll(jnp.broadcast_to(padded, (8, LANES)), lane0, 1)[0:1]
        upper = at >= LANES
        return (jnp.where(upper, 0.0, moved), jnp.where(upper, moved, 0.0))

    for i, ref in enumerate((gain_first, shift_first, gain_second, shift_second)):
        low_half, high_half = place_own(ref[...])
        param_send[2 * i : 2 * i + 1, :] = low_half
        param_send[2 * i + 1 : 2 * i + 2, :] = high_half
    head_send[...] = jnp.zeros(head_send.shape, BF16)
    head_send[0:own, 0:classes] = head_own[...]
    for lead in range(MICRO):
        spread_columns(image_x, lead, 1, images[lead].astype(F32).reshape(cells, depth), extent)

    t_high = 16
    t_steps = wide // t_high
    t_rows = t_high * wide

    def teacher_conv(source, kernel, top):
        total = None
        for row_off in range(3):
            window = source[0, pl.ds(top + row_off, t_high)].reshape(t_rows, 3 * depth)
            term = jnp.dot(
                window, kernel[row_off * 3 * depth : (row_off + 1) * 3 * depth, :], preferred_element_type=F32
            )
            total = term if total is None else total + term
        return total

    def teacher_fill(lead):
        def fill(i, carry):
            top = i * t_high
            values = teacher_in[lead, pl.ds(top, t_high)].astype(F32).reshape(t_rows, depth)
            spread_columns(teacher_x, 0, top + 1, values, wide)
            return carry

        lax.fori_loop(0, t_steps, fill, 0)

    def teacher_one():
        def one(i, carry):
            top = i * t_high
            spread_columns(teacher_h, 0, top + 1, gelu(teacher_conv(teacher_x, teacher_w1, top)), wide)
            return carry

        lax.fori_loop(0, t_steps, one, 0)

    def teacher_two(lead):
        def two(i, total):
            top = i * t_high
            values = teacher_in[lead, pl.ds(top, t_high)].astype(F32).reshape(t_rows, depth)
            act = gelu(teacher_conv(teacher_h, teacher_w2, top) + values)
            return total + jnp.sum(act, axis=0, keepdims=True)

        return lax.fori_loop(0, t_steps, two, jnp.zeros((1, depth), F32))

    loads[11].wait()
    teacher_fill(0)
    loads[12].wait()
    teacher_one()

    pl.semaphore_wait(barrier, greeted)
    rounds = [[(b, sibling)]] + [[(peer, c) for peer in line] for line in lines]
    if chips == 4:
        rounds = [[(b, 2 * beside + core)]] + rounds

    def say(i):
        if i < len(rounds):
            for peer in rounds[i]:
                signal(known.at[i], *peer)

    def hear(i):
        if i < len(rounds):
            pl.semaphore_wait(known.at[i], len(rounds[i]))
            say(i + 1)

    say(0)

    pieces = 1
    piece_rows = own_rows // pieces
    square = chips == 4 and piece_rows % 32 == 0
    held = (w_first, w_second)
    offered = (own_first, own_second)

    def gather_copy(k, rows, sem, shard, target, source=None):
        slot = held[k].at[shard, rows]
        return pltpu.make_async_remote_copy(
            src_ref=slot if source is None else source.at[rows],
            dst_ref=slot,
            send_sem=gather_send.at[k],
            recv_sem=gather_recv.at[k, sem, shard],
            device_id=(b, target),
            device_id_type=MESH,
        )

    def whole_copy(k, piece, shard, target, source=None):
        return gather_copy(k, pl.ds(piece * piece_rows, piece_rows), piece, shard, target, source)

    def half_copy(k, piece, half, shard, target, source=None):
        rows = pl.ds(piece * piece_rows + half * (piece_rows // 2), piece_rows // 2)
        return gather_copy(k, rows, 2 * piece + half, shard, target, source)

    def shard_of(peer):
        return 2 * peer + core

    def gather_start(k):
        if square:
            for late in range(2):
                for piece in range(pieces):
                    half_copy(k, piece, late, c, shard_of(beside), offered[k]).start()
                    half_copy(k, piece, 1 - late, c, shard_of(above), offered[k]).start()
        for piece in range(pieces):
            if not square:
                each_chip(lambda peer, piece=piece: whole_copy(k, piece, c, shard_of(peer), offered[k]).start())
            whole_copy(k, piece, c, sibling, offered[k]).start()
        held[k][c] = offered[k][...]

    def gather_turn(k):
        if square:
            for piece in range(pieces):
                for half, source, target in ((0, beside, above), (1, above, beside)):
                    half_copy(k, piece, half, shard_of(source), sibling).wait_recv()
                    half_copy(k, piece, half, shard_of(source), shard_of(target)).start()

    def gather_forward(k, piece):
        if square:
            half_copy(k, piece, 1, shard_of(beside), sibling).wait_recv()
            half_copy(k, piece, 0, shard_of(above), sibling).wait_recv()
            whole_copy(k, piece, shard_of(beside), sibling).start()
            whole_copy(k, piece, shard_of(above), sibling).start()
            for half in range(2):
                half_copy(k, piece, half, shard_of(3 - chip), sibling).wait_recv()
            whole_copy(k, piece, shard_of(3 - chip), sibling).start()
        else:

            def one(peer):
                whole_copy(k, piece, shard_of(peer), sibling).wait_recv()
                whole_copy(k, piece, shard_of(peer), sibling).start()

            each_chip(one)

    def gather_finish(k, piece):
        def one(i, carry):
            whole_copy(k, piece, 2 * lax.rem(chip + i, chips) + 1 - core, sibling).wait_recv()
            return carry

        lax.fori_loop(0, chips, one, 0, unroll=chips <= 4)

    def bytes_of(sem, many):
        pltpu.make_async_copy(many, many, sem).wait()

    def swap(k, source, dest):
        return pltpu.make_async_remote_copy(
            src_ref=source,
            dst_ref=dest,
            send_sem=swap_ssem.at[k],
            recv_sem=swap_rsem.at[k],
            device_id=(b, sibling),
            device_id_type=MESH,
        )

    def tile_start(send, recv, ssem, rsem):
        def one(pb, pc):
            pltpu.make_async_remote_copy(
                src_ref=send, dst_ref=recv.at[me], send_sem=ssem, recv_sem=rsem, device_id=(pb, pc), device_id_type=MESH
            ).start()

        each_device(one)
        recv[me] = send[...]

    def tile_bytes(sem, recv):
        bytes_of(sem, recv.at[pl.ds(0, devices - 1)])

    def sync_start(stage, micro, rows):
        k = stage * MICRO + micro
        for i, row in enumerate(rows):
            for j, half in enumerate(halves(row)):
                sync_send[k, 2 * i + j : 2 * i + j + 1, :] = half
        tile_start(sync_send.at[k], sync_all[k], sync_ssem.at[k], sync_rsem.at[k])

    def sync_wait(stage, micro):
        k = stage * MICRO + micro
        tile_bytes(sync_rsem.at[k], sync_all[k])
        total = jnp.sum(sync_all[k][...], axis=0)
        return [jnp.concatenate([total[2 * i : 2 * i + 1], total[2 * i + 1 : 2 * i + 2]], axis=1) for i in range(2)]

    def plane_start(k, source, slot):
        def one(pc):
            pltpu.make_async_remote_copy(
                src_ref=source(pc),
                dst_ref=slot(c),
                send_sem=plane_ssem.at[k],
                recv_sem=plane_rsem.at[k],
                device_id=(b, pc),
                device_id_type=MESH,
            ).start()

        each_plane(one)

    def plane_wait(k, many):
        pltpu.make_async_copy(many, many, plane_rsem.at[k]).wait()

    def plane_drain(k, many):
        pltpu.make_async_copy(many, many, plane_ssem.at[k]).wait()

    gather_start(0)
    swaps = [swap(0, image_x, image_sib)]
    swaps[0].start()
    for load in loads[13:]:
        load.wait()
    teacher_rows = [teacher_two(0)]

    hear(0)

    teacher_fill(1)
    hear(1)
    plane_start(0, lambda pc: param_send, lambda s: param_all.at[s])
    plane_start(1, lambda pc: head_send, lambda s: head_all.at[s])
    param_all[c] = param_send[...]
    head_all[c] = head_send[...]
    teacher_one()
    gather_turn(0)
    hear(2)
    teacher_rows.append(teacher_two(1))
    which_t = lax.broadcasted_iota(jnp.int32, (8, depth), 0)
    pooled_t = jnp.zeros((8, depth), F32)
    for m in range(MICRO):
        pooled_t = jnp.where(which_t == m, teacher_rows[m] / float(wide * wide), pooled_t)
    teacher_head_pad[...] = jnp.zeros(teacher_head_pad.shape, F32)
    teacher_head_pad[0:classes, :] = teacher_head[...].astype(F32)
    teacher_logits = lax.dot_general(
        pooled_t, teacher_head_pad[...], (((1,), (1,)), ((), ())), precision=HIGHEST, preferred_element_type=F32
    )
    lane_pad = jnp.zeros((1, LANES - classes), F32)
    teacher_logits = teacher_logits + jnp.concatenate([teacher_bias[...], lane_pad], axis=1)
    image_sum = jnp.zeros((1, depth), F32)
    for m in range(MICRO):
        image_sum = image_sum + jnp.sum(images[m].astype(F32).reshape(cells, depth), axis=0, keepdims=True)
    logit_send[0:MICRO, :] = teacher_logits[0:MICRO]
    for j, half in enumerate(halves(image_sum)):
        logit_send[MICRO + j : MICRO + j + 1, :] = half
    gather_start(1)
    hear(3)
    tile_start(logit_send, logit_all, wide_ssem.at[0], wide_rsem.at[0])

    def picker(shard, block, offset):
        at_row = lax.broadcasted_iota(jnp.int32, (depth, block), 0)
        place = lax.broadcasted_iota(jnp.int32, (depth, block), 1) - offset
        wanted = jnp.logical_and(place >= 0, place < own)
        return jnp.logical_and(wanted, at_row == shard * own + place).astype(BF16)

    def unpack(ref, block, offset):
        def one(shard, total):
            return total + jnp.dot(picker(shard, block, offset), ref[shard], preferred_element_type=F32)

        return lax.fori_loop(0, chans, one, jnp.zeros((depth, ref.shape[2]), F32)).astype(BF16)

    def weights(ref, tap):
        if own_pad == own:
            return ref[:, tap * own : (tap + 1) * own, :].reshape(depth, depth)
        return unpack(ref, own_rows, tap * own)

    def window(source, micro, row_off):
        return source[micro, row_off : row_off + extent].reshape(cells, 3 * depth)

    def tap_row(ref, row_off, back):
        if back:
            return jnp.concatenate([weights(ref, (2 - row_off) * 3 + 2 - i) for i in range(3)], axis=0)
        return jnp.concatenate([weights(ref, row_off * 3 + i) for i in range(3)], axis=1)

    def student_conv(source, micro, ref):
        total = None
        for row_off in range(3):
            term = lax.dot_general(
                window(source, micro, row_off),
                tap_row(ref, row_off, False),
                (((1,), (1,)), ((), ())),
                preferred_element_type=F32,
            )
            total = term if total is None else total + term
        return total

    def student_back(source, micro, ref):
        total = None
        for row_off in range(3):
            term = jnp.dot(
                window(source, micro, row_off), tap_row(ref, row_off, True), preferred_element_type=F32
            )
            total = term if total is None else total + term
        return total

    def rows_of(m):
        return slice(m * cells, (m + 1) * cells)

    def col_sum(values):
        return jnp.sum(values, axis=0, keepdims=True)

    def moments_start(stage, m, values):
        sync_start(stage, m, (col_sum(values), col_sum(values * values)))

    def moments(stage, m):
        total, square = sync_wait(stage, m)
        center = total / samples
        spread = square / samples - center * center
        return (center, lax.rsqrt(spread + EPS))

    for piece in range(pieces):
        gather_forward(0, piece)
    for piece in range(pieces):
        gather_finish(0, piece)
    total = None
    for row_off in range(3):
        term = lax.dot_general(
            image_x[:, row_off : row_off + extent].reshape(MICRO * cells, 3 * depth),
            tap_row(w_first, row_off, False),
            (((1,), (1,)), ((), ())),
            preferred_element_type=F32,
        )
        total = term if total is None else total + term
    y_first[...] = total
    for m in range(MICRO):
        moments_start(0, m, total[rows_of(m), :])

    plane_wait(0, param_all.at[pl.ds(0, chans - 1)])
    plane_wait(1, head_all.at[pl.ds(0, chans - 1)])
    params = jnp.sum(param_all[...], axis=0)
    gain1, shift1, gain2, shift2 = (
        jnp.concatenate([params[2 * i : 2 * i + 1], params[2 * i + 1 : 2 * i + 2]], axis=1) for i in range(4)
    )
    if own_pad == own:
        head = head_all[...].reshape(depth, LANES)
    else:
        head = unpack(head_all, own_pad, 0)
    gather_turn(1)
    for piece in range(pieces):
        gather_forward(1, piece)
    for piece in range(pieces):
        gather_finish(1, piece)

    def three_parts(values):
        first = values.astype(BF16)
        rest = values - first.astype(F32)
        second = rest.astype(BF16)
        third = (rest - second.astype(F32)).astype(BF16)
        return jnp.concatenate([first, second, third], axis=0)

    def sum_parts(product):
        return product[0:8] + product[8:16] + product[16:24]

    norm1 = []
    for m in range(MICRO):
        center, inv = moments(0, m)
        norm1.append((center, inv))
        normed = (y_first[rows_of(m), :] - center) * (inv * gain1) + shift1
        spread_columns(hidden_x, m, 1, gelu(normed), extent)
        values = student_conv(hidden_x, m, w_second)
        y_second[rows_of(m), :] = values
        moments_start(1, m, values)
    swaps.append(swap(1, hidden_x, hidden_sib))
    swaps[1].start()
    for m in range(MICRO):
        center, inv = norm1[m]
        slope_first[rows_of(m), :] = gelu_slope((y_first[rows_of(m), :] - center) * (inv * gain1) + shift1)

    per_device = pair_index.shape[0]
    norm2, slope_scale = [], []
    tile_bytes(wide_rsem.at[0], logit_all)
    taught = []
    for m in range(MICRO):
        paired = pair_index[m]
        teacher_row = logit_all[pl.ds(paired // per_device, 1), pl.ds(lax.rem(paired, per_device), 1), :]
        taught.append(teacher_terms(teacher_row.reshape(1, LANES), labels[m], classes))
    which = lax.broadcasted_iota(jnp.int32, (8, depth), 0)
    which_lane = lax.broadcasted_iota(jnp.int32, (8, LANES), 0)
    for m in range(MICRO):
        center, inv = moments(1, m)
        norm2.append((center, inv))
        spread = y_second[rows_of(m), :] - center
        res = spread * (inv * gain2) + shift2 + images[m].astype(F32).reshape(cells, depth)
        square = res * res
        t = jnp.tanh(GELU_A * (res + GELU_B * (res * square)))
        half = 0.5 + 0.5 * t
        slope = half + (0.5 * res) * (1.0 - t * t) * (GELU_A + (3.0 * GELU_A * GELU_B) * square)
        slope_second[rows_of(m), :] = slope
        pooled = col_sum(res * half) / float(cells)
        slope_sum = col_sum(slope)
        slope_dot = col_sum(slope * spread) * inv
        product = jnp.dot(
            three_parts(jnp.where(which == 0, pooled, 0.0)), head, preferred_element_type=F32
        )
        logits = sum_parts(product)[0:1] + jnp.concatenate([head_bias[...], lane_pad], axis=1)
        grad = distill_grad(logits, taught[m], labels[m], classes)
        product = lax.dot_general(
            three_parts(jnp.where(which_lane == 0, grad, 0.0)),
            head,
            (((1,), (1,)), ((), ())),
            preferred_element_type=F32,
        )
        scale = sum_parts(product)[0:1] / float(cells)
        slope_scale.append(scale)
        sync_start(2, m, (scale * slope_dot, scale * slope_sum))
        for j, part in enumerate(halves(pooled)):
            wide_send[m * 4 + j : m * 4 + j + 1, :] = part
        wide_send[m * 4 + 2 : m * 4 + 3, :] = grad
        wide_send[m * 4 + 3 : m * 4 + 4, :] = logits
    plane_start(2, lambda pc: wide_send, lambda s: wide_all.at[s])
    wide_all[c] = wide_send[...]

    def own_lanes(low_row, high_row):
        at = c * own
        row = jnp.where(at >= LANES, high_row, low_row)
        turn = lax.rem(LANES - lax.rem(at, LANES), LANES)
        return pltpu.roll(jnp.broadcast_to(row, (8, LANES)), turn, 1)[0:1, 0:own]

    def norm_terms(stage, m, gain, norm):
        center, inv = norm
        totals = sync_wait(stage, m)
        scale = gain * inv
        slant = scale * inv * (totals[0] / samples)
        level = scale * (totals[1] / samples)
        return (scale, center, slant, level), totals

    def norm_apply(terms, grad, values):
        scale, center, slant, level = terms
        return grad * scale - (values - center) * slant - level

    def norm_out(totals, gain_out, shift_out):
        for out, i in ((gain_out, 0), (shift_out, 1)):
            row = totals[0][i]
            for m in range(1, MICRO):
                row = row + totals[m][i]
            out[...] = own_lanes(*halves(row))

    def by_core(whole, dest):
        if own_pad == own:
            dest[...] = whole.reshape(dest.shape)
        else:

            def one(shard, carry):
                dest[shard // 2, lax.rem(shard, 2)] = lax.dot_general(
                    picker(shard, own_pad, 0).astype(F32),
                    whole,
                    (((0,), (0,)), ((), ())),
                    precision=HIGHEST,
                    preferred_element_type=F32,
                )
                return carry

            lax.fori_loop(0, chans, one, 0)

    def hand(k, m, grad, values):
        by_core(jnp.transpose(grad), turned.at[k, m, 0])
        by_core(jnp.transpose(values), turned.at[k, m, 1])
        turns[k, m] = swap(2 + k * MICRO + m, turned.at[k, m, :, :, 1 - core], turned_sib.at[k, m])
        turns[k, m].start()

    def low_grads(k, m, terms):
        by_core(
            jnp.transpose(jnp.concatenate(list(terms) + [jnp.zeros((4, depth), F32)], axis=0)), turned_terms
        )
        columns = turned_terms[:, pl.ds(core, 1)].reshape(chips * own_pad, 8)
        scale, center, slant, level = (columns[:, i : i + 1] for i in range(4))
        mine = [turned[k, m, i, :, pl.ds(core, 1)].reshape(chips * own_pad, cells) for i in range(2)]
        turns[k, m].wait_recv()
        theirs = [turned_sib[k, m, i].reshape(chips * own_pad, cells) for i in range(2)]
        return [norm_apply((scale, center, slant, level), *pair).astype(BF16) for pair in (mine, theirs)]

    turns = {}
    taps = 3 * own_pad
    per_half = groups // 2
    part_rows = taps // per_half
    part_pad = sum_send.shape[2]
    across = {0: None, 1: 2}
    planar = {0: (0, 1, 2), 1: (0, 1)}

    def send(source, dest, ssem, rsem, peer_b, peer_c):
        pltpu.make_async_remote_copy(
            src_ref=source, dst_ref=dest, send_sem=ssem, recv_sem=rsem, device_id=(peer_b, peer_c), device_id_type=MESH
        ).start()

    def cut(p):
        half, row = p // per_half, (p % per_half) * part_rows
        return slice(row, row + part_rows), slice(half * LANES, (half + 1) * LANES)

    def kernel_grad(k, grads, source, source_sib, mean):
        sides = [(grads[m][i], ref, m) for m in range(MICRO) for i, ref in enumerate((source, source_sib))]
        level = sum(jnp.sum(low.astype(F32), axis=1, keepdims=True) for low, _, _ in sides)
        for row_off in (2, 0, 1):
            total = sum(
                jnp.dot(
                    low,
                    ref[m, row_off : row_off + extent].reshape(cells, 3 * depth),
                    preferred_element_type=F32,
                )
                for low, ref, m in sides
            )
            for col_off in range(3):
                block = total[:, col_off * depth : (col_off + 1) * depth] - level * mean
                for i in range(chips):
                    part_all[i, col_off * own_pad : (col_off + 1) * own_pad, :] = block[i * own_pad : (i + 1) * own_pad]
            if row_off == across[k]:
                for p in range(groups):
                    rows, lanes = cut(p)
                    cross_all[p, :, 0:part_rows] = part_all[:, rows, lanes]
                    if part_pad != part_rows:
                        cross_all[p, :, part_rows:part_pad] = jnp.zeros((chips, part_pad - part_rows, LANES), F32)
                cross_send[k] = cross_all[...].astype(BF16)
                cross_own[k] = cross_all[pl.ds(b, 1)].reshape(chips, part_pad, LANES)
                each_line(
                    lambda peer: send(
                        cross_send.at[k, peer], cross_recv.at[k, b], cross_ssem.at[k], cross_rsem.at[k], peer, c
                    )
                )
                cross_recv[k, b] = jnp.zeros((chips, part_pad, LANES), BF16)
            else:
                part_send[k, row_off] = part_all[...].astype(BF16)
                part_own[k, row_off] = part_all[pl.ds(chip, 1)].reshape(taps, depth)
                each_chip(
                    lambda peer, row_off=row_off: send(
                        part_send.at[k, row_off, peer],
                        part_recv.at[k, row_off, chip],
                        part_ssem.at[k, row_off],
                        part_rsem.at[k, row_off],
                        b,
                        2 * peer + core,
                    )
                )
                part_recv[k, row_off, chip] = jnp.zeros((taps, depth), BF16)
        ones = jnp.ones((8, cells), BF16)
        level_send[k] = sum(
            lax.dot_general(ones, low, (((1,), (1,)), ((), ())), preferred_element_type=F32) for low, _, _ in sides
        )[0:1]
        each_chip(
            lambda peer: send(
                level_send.at[k], level_recv.at[k, chip], level_ssem.at[k], level_rsem.at[k], b, 2 * peer + core
            )
        )
        level_recv[k, chip] = level_send[k]

    def line_start(k):
        for row_off in planar[k]:
            bytes_of(part_rsem.at[k, row_off], part_recv.at[k, row_off, pl.ds(0, chips - 1)])
            total = part_own[k, row_off] + jnp.sum(part_recv[k, row_off].astype(F32), axis=0)
            for p in range(groups):
                line_own[k, row_off, p, 0:part_rows] = total[cut(p)]
                if part_pad != part_rows:
                    line_own[k, row_off, p, part_rows:part_pad] = jnp.zeros((part_pad - part_rows, LANES), F32)
            line_send[k, row_off] = line_own[k, row_off].astype(BF16)
            each_line(
                lambda peer, row_off=row_off: send(
                    line_send.at[k, row_off, peer],
                    line_recv.at[k, row_off, b],
                    line_ssem.at[k, row_off],
                    line_rsem.at[k, row_off],
                    peer,
                    c,
                )
            )
            line_recv[k, row_off, b] = jnp.zeros((part_pad, LANES), BF16)
        bytes_of(level_rsem.at[k], level_recv.at[k, pl.ds(0, chips - 1)])
        level_line_send[k] = jnp.sum(level_recv[k], axis=0)
        each_line(
            lambda peer: send(
                level_line_send.at[k], level_line_recv.at[k, b], level_line_ssem.at[k], level_line_rsem.at[k], peer, c
            )
        )
        level_line_recv[k, b] = level_line_send[k]

    def cross_forward(k):
        if across[k] is None:
            return
        bytes_of(cross_rsem.at[k], cross_recv.at[k, pl.ds(0, groups - 1)])
        last_all[...] = cross_own[k] + jnp.sum(cross_recv[k].astype(F32), axis=0)
        last_send[k] = last_all[...].astype(BF16)
        last_own[k] = last_all[pl.ds(chip, 1)].reshape(part_pad, LANES)
        each_chip(
            lambda peer: send(
                last_send.at[k, peer], last_recv.at[k, chip], last_ssem.at[k], last_rsem.at[k], b, 2 * peer + core
            )
        )
        last_recv[k, chip] = jnp.zeros((part_pad, LANES), BF16)

    def share(k, row_off, total):
        sum_send[k, row_off] = total.astype(BF16)
        each_line(
            lambda peer: send(
                sum_send.at[k, row_off],
                sum_recv.at[k, row_off, b],
                sum_ssem.at[k, row_off],
                sum_rsem.at[k, row_off],
                peer,
                c,
            )
        )
        sum_recv[k, row_off, b] = sum_send[k, row_off]

    def cross_sum(k):
        if across[k] is None:
            return
        bytes_of(last_rsem.at[k], last_recv.at[k, pl.ds(0, chips - 1)])
        share(k, across[k], last_own[k] + jnp.sum(last_recv[k].astype(F32), axis=0))

    def line_sum(k):
        for row_off in planar[k]:
            bytes_of(line_rsem.at[k, row_off], line_recv.at[k, row_off, pl.ds(0, groups - 1)])
            share(
                k,
                row_off,
                line_own[k, row_off, pl.ds(b, 1)].reshape(part_pad, LANES)
                + jnp.sum(line_recv[k, row_off].astype(F32), axis=0),
            )

    def sum_finish(k, mean, out):
        bytes_of(level_line_rsem.at[k], level_line_recv.at[k, pl.ds(0, groups - 1)])
        level = jnp.sum(level_line_recv[k], axis=0)
        level_column[...] = jnp.transpose(jnp.broadcast_to(level, (LANES, level.shape[1])))
        column_own = level_column[pl.ds(chip * own_pad, own_pad), :]
        back = [column_own * half for half in halves(mean)]
        for row_off in (0, 1, 2):
            bytes_of(sum_rsem.at[k, row_off], sum_recv.at[k, row_off, pl.ds(0, groups - 1)])
            for half in range(2):
                rows = sum_recv[k, row_off, half * per_half : (half + 1) * per_half, 0:part_rows].astype(F32)
                out[row_off * 3 : row_off * 3 + 3, :, half * LANES : (half + 1) * LANES] = (
                    rows.reshape(3, own_pad, LANES) + back[half][None]
                )

    for m in range(MICRO):
        hand(0, m, slope_second[rows_of(m), :] * slope_scale[m], y_second[rows_of(m), :])
    terms2, totals2 = [], []
    for m in range(MICRO):
        terms, totals = norm_terms(2, m, gain2, norm2[m])
        terms2.append(terms)
        totals2.append(totals)
        found = norm_apply(terms, slope_second[rows_of(m), :] * slope_scale[m], y_second[rows_of(m), :])
        spread_columns(grad_x, m, 1, found, extent)
        grad = student_back(grad_x, m, w_second) * slope_first[rows_of(m), :]
        d_hid[rows_of(m), :] = grad
        center, inv = norm1[m]
        sync_start(3, m, (col_sum(grad * (y_first[rows_of(m), :] - center)) * inv, col_sum(grad)))

    hidden_mean = jnp.zeros((1, depth), F32)
    for node, weight in QUADRATURE:
        hidden_mean = hidden_mean + weight * gelu(shift1 + gain1 * node)
    image_rows = jnp.sum(logit_all[...], axis=0)
    image_mean = jnp.concatenate([image_rows[MICRO : MICRO + 1], image_rows[MICRO + 1 : MICRO + 2]], axis=1) / (
        MICRO * samples
    )

    swaps[0].wait_recv()
    swaps[1].wait_recv()
    kernel_grad(0, [low_grads(0, m, terms2[m]) for m in range(MICRO)], hidden_x, hidden_sib, hidden_mean)
    for m in range(MICRO):
        hand(1, m, d_hid[rows_of(m), :], y_first[rows_of(m), :])
    norm_out(totals2, gain_second_grad, shift_second_grad)

    plane_wait(2, wide_all.at[pl.ds(0, chans - 1)])
    totals = [jnp.zeros((LANES, LANES), F32) for _ in range(2)]
    bias_row = jnp.zeros((1, LANES), F32)
    for m in range(MICRO):
        per_image = wide_all[:, m * 4 + 2, :]
        bias_row = bias_row + col_sum(per_image)
        for j in range(2):
            totals[j] = totals[j] + lax.dot_general(
                wide_all[:, m * 4 + j, :],
                per_image,
                (((0,), (0,)), ((), ())),
                precision=HIGHEST,
                preferred_element_type=F32,
            )
        for j in range(chans):
            logits_out[j * MICRO + m : j * MICRO + m + 1, :] = wide_all[j, m * 4 + 3 : m * 4 + 4, 0:classes]
    for j in range(2):
        head_sum[j * LANES : (j + 1) * LANES, :] = totals[j]
    head_line_send[0:own, :] = head_sum[pl.ds(c * own, own), :]
    head_line_send[own : own + 8, :] = jnp.broadcast_to(bias_row, (8, LANES))
    each_line(
        lambda peer: send(head_line_send, head_line_recv.at[b], wide_ssem.at[1], wide_rsem.at[1], peer, c)
    )
    head_line_recv[b] = head_line_send[...]

    terms1, totals1, lows = [], [], []
    for m in range(MICRO):
        terms, totals = norm_terms(3, m, gain1, norm1[m])
        terms1.append(terms)
        totals1.append(totals)
        lows.append(low_grads(1, m, terms))
    kernel_grad(1, lows, image_x, image_sib, image_mean)
    for m in range(MICRO):
        found = norm_apply(terms1[m], d_hid[rows_of(m), :], y_first[rows_of(m), :])
        spread_columns(grad_x, m, 1, found, extent)
        images_grad[m] = (
            student_back(grad_x, m, w_first) + slope_second[rows_of(m), :] * slope_scale[m]
        ).reshape(images_grad.shape[1:])
    norm_out(totals1, gain_first_grad, shift_first_grad)
    line_start(0)
    cross_forward(0)

    cross_sum(0)
    line_start(1)
    cross_forward(1)
    line_sum(0)
    cross_sum(1)
    line_sum(1)
    tile_bytes(wide_ssem.at[0], logit_all)
    bytes_of(wide_ssem.at[1], head_line_recv.at[pl.ds(0, groups - 1)])
    plane_drain(2, wide_all.at[pl.ds(0, chans - 1)])
    for k in range(2):
        bytes_of(gather_send.at[k], held[k].at[pl.ds(0, chans - 1)])
    for k in range(4 * MICRO):
        tile_bytes(sync_ssem.at[k], sync_all[k])
    plane_drain(0, param_all.at[pl.ds(0, chans - 1)])
    plane_drain(1, head_all.at[pl.ds(0, chans - 1)])
    for copy in swaps + list(turns.values()):
        copy.wait_send()
    for k in range(2):
        for row_off in planar[k]:
            bytes_of(part_ssem.at[k, row_off], part_recv.at[k, row_off, pl.ds(0, chips - 1)])
            bytes_of(line_ssem.at[k, row_off], line_recv.at[k, row_off, pl.ds(0, groups - 1)])
        if across[k] is not None:
            bytes_of(cross_ssem.at[k], cross_recv.at[k, pl.ds(0, groups - 1)])
            bytes_of(last_ssem.at[k], last_recv.at[k, pl.ds(0, chips - 1)])
        bytes_of(level_ssem.at[k], level_recv.at[k, pl.ds(0, chips - 1)])
        bytes_of(level_line_ssem.at[k], level_line_recv.at[k, pl.ds(0, groups - 1)])
    bytes_of(wide_rsem.at[1], head_line_recv.at[pl.ds(0, groups - 1)])
    head_total = jnp.sum(head_line_recv[...], axis=0)
    head_grad[...] = head_total[0:own, 0:classes]
    bias_grad[...] = head_total[own : own + 1, 0:classes]
    sum_finish(0, hidden_mean, second_grad)
    sum_finish(1, image_mean, first_grad)
    for k in range(2):
        for row_off in range(3):
            bytes_of(sum_ssem.at[k, row_off], sum_recv.at[k, row_off, pl.ds(0, groups - 1)])


def hand_on(*refs):
    count = len(refs) // 2
    copies = [pltpu.make_async_copy(refs[i], refs[count + i], refs[-1].at[i]) for i in range(count)]
    for copy in copies:
        copy.start()
    for copy in copies:
        copy.wait()


def shards(
    teacher_images,
    student_images,
    pair_index,
    labels,
    teacher_first,
    teacher_second,
    teacher_head,
    teacher_bias,
    conv_first,
    gain_first,
    shift_first,
    conv_second,
    gain_second,
    shift_second,
    head_weight,
    head_bias,
):
    groups, chans = lax.axis_size("batch"), lax.axis_size("chan")
    devices = groups * chans
    count, extent, _, depth = student_images.shape
    wide = teacher_images.shape[1]
    own = conv_first.shape[3]
    own_pad = max(own, 16)
    own_rows = -(-9 * own // 16) * 16
    classes = head_bias.shape[0]
    cells = extent * extent
    rows = count * cells
    chips = chans // 2
    taps = 3 * own_pad
    part_rows = 2 * taps // groups
    part_pad = -(-part_rows // 16) * 16

    def turned(kernel):
        return jnp.transpose(kernel, (0, 1, 3, 2)).reshape(9 * own, depth)

    def row(vector):
        return vector.reshape(1, -1)

    vmem = pl.BlockSpec(memory_space=pltpu.VMEM)
    hbm = pl.BlockSpec(memory_space=pl.ANY)
    out_shape = [
        jax.ShapeDtypeStruct((chans * count, classes), F32),
        jax.ShapeDtypeStruct(student_images.shape, F32),
        jax.ShapeDtypeStruct((9, own_pad, depth), F32),
        jax.ShapeDtypeStruct((1, own), F32),
        jax.ShapeDtypeStruct((1, own), F32),
        jax.ShapeDtypeStruct((9, own_pad, depth), F32),
        jax.ShapeDtypeStruct((1, own), F32),
        jax.ShapeDtypeStruct((1, own), F32),
        jax.ShapeDtypeStruct((own, classes), F32),
        jax.ShapeDtypeStruct((1, classes), F32),
    ]
    stage = (16, LANES) if own_rows == 9 * own else (9 * own, depth)
    scratch = [
        pltpu.SMEM(pair_index.shape, jnp.int32),
        pltpu.SMEM(labels.shape, jnp.int32),
        pltpu.VMEM(stage, BF16),
        pltpu.VMEM(stage, BF16),
        pltpu.VMEM(student_images.shape, BF16),
        pltpu.VMEM((classes, depth), BF16),
        pltpu.VMEM((1, classes), F32),
        pltpu.VMEM((1, own), F32),
        pltpu.VMEM((1, own), F32),
        pltpu.VMEM((1, own), F32),
        pltpu.VMEM((1, own), F32),
        pltpu.VMEM((own, classes), BF16),
        pltpu.VMEM((1, classes), F32),
        pltpu.VMEM(teacher_images.shape, BF16),
        pltpu.VMEM((9 * depth, depth), BF16),
        pltpu.VMEM((9 * depth, depth), BF16),
        pltpu.VMEM((1, wide + 2, wide, 3 * depth), BF16),
        pltpu.VMEM((1, wide + 2, wide, 3 * depth), BF16),
        pltpu.VMEM((LANES, depth), F32),
        pltpu.VMEM((count, extent + 2, extent, 3 * depth), BF16),
        pltpu.VMEM((count, extent + 2, extent, 3 * depth), BF16),
        pltpu.VMEM((count, extent + 2, extent, 3 * depth), BF16),
        pltpu.VMEM((chans, own_rows, depth), BF16),
        pltpu.VMEM((chans, own_rows, depth), BF16),
        pltpu.VMEM((own_rows, depth), BF16),
        pltpu.VMEM((own_rows, depth), BF16),
        pltpu.VMEM((rows, depth), F32),
        pltpu.VMEM((rows, depth), F32),
        pltpu.VMEM((rows, depth), F32),
        pltpu.VMEM((rows, depth), F32),
        pltpu.VMEM((rows, depth), F32),
        pltpu.VMEM((count, extent + 2, extent, 3 * depth), BF16),
        pltpu.VMEM((count, extent + 2, extent, 3 * depth), BF16),
        pltpu.VMEM((2, count, 2, chips, 2, own_pad, cells), F32),
        pltpu.VMEM((2, count, 2, chips, own_pad, cells), F32),
        pltpu.VMEM((chips, 2, own_pad, 8), F32),
        pltpu.VMEM((chips, taps, depth), F32),
        pltpu.VMEM((2, 3, taps, depth), F32),
        pltpu.VMEM((2, 3, chips, taps, depth), BF16),
        pltpu.VMEM((2, 3, chips, taps, depth), BF16),
        pltpu.VMEM((groups, chips, part_pad, LANES), F32),
        pltpu.VMEM((2, chips, part_pad, LANES), F32),
        pltpu.VMEM((2, groups, chips, part_pad, LANES), BF16),
        pltpu.VMEM((2, groups, chips, part_pad, LANES), BF16),
        pltpu.VMEM((chips, part_pad, LANES), F32),
        pltpu.VMEM((2, part_pad, LANES), F32),
        pltpu.VMEM((2, chips, part_pad, LANES), BF16),
        pltpu.VMEM((2, chips, part_pad, LANES), BF16),
        pltpu.VMEM((2, 3, groups, part_pad, LANES), F32),
        pltpu.VMEM((2, 3, groups, part_pad, LANES), BF16),
        pltpu.VMEM((2, 3, groups, part_pad, LANES), BF16),
        pltpu.VMEM((2, 3, part_pad, LANES), BF16),
        pltpu.VMEM((2, 3, groups, part_pad, LANES), BF16),
        pltpu.VMEM((2, 1, chips * own_pad), F32),
        pltpu.VMEM((2, chips, 1, chips * own_pad), F32),
        pltpu.VMEM((2, 1, chips * own_pad), F32),
        pltpu.VMEM((2, groups, 1, chips * own_pad), F32),
        pltpu.VMEM((chips * own_pad, LANES), F32),
        pltpu.VMEM((8, LANES), F32),
        pltpu.VMEM((chans, 8, LANES), F32),
        pltpu.VMEM((own_pad, LANES), BF16),
        pltpu.VMEM((chans, own_pad, LANES), BF16),
        pltpu.VMEM((4, LANES), F32),
        pltpu.VMEM((devices, 4, LANES), F32),
        pltpu.VMEM((8, LANES), F32),
        pltpu.VMEM((chans, 8, LANES), F32),
        pltpu.VMEM((4 * MICRO, 4, LANES), F32),
        pltpu.VMEM((devices, 4, LANES), F32),
        pltpu.VMEM((devices, 4, LANES), F32),
        pltpu.VMEM((devices, 4, LANES), F32),
        pltpu.VMEM((devices, 4, LANES), F32),
        pltpu.VMEM((devices, 4, LANES), F32),
        pltpu.VMEM((devices, 4, LANES), F32),
        pltpu.VMEM((devices, 4, LANES), F32),
        pltpu.VMEM((devices, 4, LANES), F32),
        pltpu.VMEM((depth, LANES), F32),
        pltpu.VMEM((own + 8, LANES), F32),
        pltpu.VMEM((groups, own + 8, LANES), F32),
        pltpu.SemaphoreType.DMA((16,)),
        pltpu.SemaphoreType.DMA((2,)),
        pltpu.SemaphoreType.DMA((2, 6, chans)),
        pltpu.SemaphoreType.DMA((2,)),
        pltpu.SemaphoreType.DMA((2,)),
        pltpu.SemaphoreType.DMA((4 * MICRO,)),
        pltpu.SemaphoreType.DMA((4 * MICRO,)),
        pltpu.SemaphoreType.REGULAR((4,)),
        pltpu.SemaphoreType.DMA((3,)),
        pltpu.SemaphoreType.DMA((3,)),
        pltpu.SemaphoreType.DMA((2 + 2 * MICRO,)),
        pltpu.SemaphoreType.DMA((2 + 2 * MICRO,)),
        pltpu.SemaphoreType.DMA((2, 3)),
        pltpu.SemaphoreType.DMA((2, 3)),
        pltpu.SemaphoreType.DMA((2,)),
        pltpu.SemaphoreType.DMA((2,)),
        pltpu.SemaphoreType.DMA((2,)),
        pltpu.SemaphoreType.DMA((2,)),
        pltpu.SemaphoreType.DMA((2,)),
        pltpu.SemaphoreType.DMA((2,)),
        pltpu.SemaphoreType.DMA((2,)),
        pltpu.SemaphoreType.DMA((2,)),
        pltpu.SemaphoreType.DMA((2, 3)),
        pltpu.SemaphoreType.DMA((2, 3)),
        pltpu.SemaphoreType.DMA((2, 3)),
        pltpu.SemaphoreType.DMA((2, 3)),
    ]
    found = pl.pallas_call(
        functools.partial(body, (groups, chans, own, own_pad, classes)),
        out_shape=[pltpu.VMEM(out.shape, out.dtype) for out in out_shape],
        in_specs=[hbm] * 16,
        out_specs=[vmem] * 10,
        scratch_shapes=scratch,
        compiler_params=pltpu.CompilerParams(
            collective_id=0, has_side_effects=True, vmem_limit_bytes=62 * 2**20
        ),
    )(
        teacher_images,
        student_images,
        pair_index,
        labels,
        teacher_first.reshape(9 * depth, depth),
        teacher_second.reshape(9 * depth, depth),
        teacher_head.T,
        row(teacher_bias),
        turned(conv_first),
        row(gain_first),
        row(shift_first),
        turned(conv_second),
        row(gain_second),
        row(shift_second),
        head_weight,
        row(head_bias),
    )
    found = pl.pallas_call(
        hand_on,
        out_shape=out_shape,
        in_specs=[vmem] * len(out_shape),
        out_specs=[hbm] * len(out_shape),
        scratch_shapes=[pltpu.SemaphoreType.DMA((len(out_shape),))],
    )(*[pltpu.with_memory_space_constraint(x, pltpu.VMEM) for x in found])
    logits, images_grad, first, gain1, shift1, second, gain2, shift2, head, bias = found

    def back(grad):
        return jnp.transpose(grad[:, :own].reshape(3, 3, own, depth), (0, 1, 3, 2))

    return (
        logits,
        images_grad,
        back(first),
        gain1.reshape(-1),
        shift1.reshape(-1),
        back(second),
        gain2.reshape(-1),
        shift2.reshape(-1),
        head,
        bias.reshape(-1),
    )


def solution(mesh):
    in_specs = (
        P(("batch", "chan"), None, None, None),
        P(("batch", "chan"), None, None, None),
        P(("batch", "chan")),
        P(("batch", "chan")),
        P(),
        P(),
        P(),
        P(),
        P(None, None, None, "chan"),
        P("chan"),
        P("chan"),
        P(None, None, None, "chan"),
        P("chan"),
        P("chan"),
        P("chan", None),
        P(),
    )
    out_specs = (
        P("batch", None),
        P(("batch", "chan"), None, None, None),
        P(None, None, None, "chan"),
        P("chan"),
        P("chan"),
        P(None, None, None, "chan"),
        P("chan"),
        P("chan"),
        P("chan", None),
        P(),
    )
    return jax.shard_map(shards, mesh=mesh, in_specs=in_specs, out_specs=out_specs, check_vma=False)
```

```python
import functools

import jax
import jax.numpy as jnp
from jax import lax
from jax.experimental import pallas as pl
from jax.experimental.pallas import tpu as pltpu
from jax.sharding import PartitionSpec as P

MESH = pl.DeviceIdType.MESH
F32 = jnp.float32
BF16 = jnp.bfloat16
HIGHEST = lax.Precision.HIGHEST
MICRO = 2
EPS = 1e-05
TARGET_WEIGHT = 1.0
NONTARGET_WEIGHT = 8.0
SOFTEN = 4.0
GELU_A = 0.7978845608028654
GELU_B = 0.044715
LANES = 128
QUADRATURE = (
    (0.0, 0.5333333333),
    (1.3556261800, 0.2220759220),
    (-1.3556261800, 0.2220759220),
    (2.8569700139, 0.0112574113),
    (-2.8569700139, 0.0112574113),
)


def gelu(x):
    return x * (0.5 + 0.5 * jnp.tanh(GELU_A * (x + GELU_B * (x * x * x))))


def gelu_slope(x):
    square = x * x
    t = jnp.tanh(GELU_A * (x + GELU_B * (x * square)))
    return 0.5 + 0.5 * t + (0.5 * x) * (1.0 - t * t) * (GELU_A + (3.0 * GELU_A * GELU_B) * square)


def column(shape, width):
    return lax.rem(lax.broadcasted_iota(jnp.int32, shape, 0), width)


def spread_columns(dest, lead, top, values, width):
    rows, depth = values.shape
    col = column(values.shape, width)
    left = jnp.where(col == 0, 0.0, pltpu.roll(values, 1, 0))
    right = jnp.where(col == width - 1, 0.0, pltpu.roll(values, rows - 1, 0))
    high = rows // width
    for place, part in enumerate((left, values, right)):
        dest[lead, pl.ds(top, high), :, place * depth : (place + 1) * depth] = part.astype(BF16).reshape(
            high, width, depth
        )


def halves(row):
    return (row[:, :LANES], row[:, LANES:])


def soft_parts(logits, label, classes):
    lane = lax.broadcasted_iota(jnp.int32, logits.shape, 1)
    live = lane < classes
    target = lane == label
    other = jnp.logical_and(live, jnp.logical_not(target))
    low = -1e30
    soft = logits / SOFTEN
    whole_top = jnp.max(jnp.where(live, soft, low), axis=1, keepdims=True)
    rest_top = jnp.max(jnp.where(other, soft, low), axis=1, keepdims=True)
    whole_exp = jnp.where(live, jnp.exp(jnp.where(live, soft, whole_top) - whole_top), 0.0)
    rest_exp = jnp.where(other, jnp.exp(jnp.where(other, soft, rest_top) - rest_top), 0.0)
    whole_sum = jnp.sum(whole_exp, axis=1, keepdims=True)
    rest_sum = jnp.sum(rest_exp, axis=1, keepdims=True)
    whole = whole_top + jnp.log(whole_sum)
    rest = rest_top + jnp.log(rest_sum)
    true = jnp.sum(jnp.where(target, soft, 0.0), axis=1, keepdims=True)
    return (whole_exp / whole_sum, rest_exp / rest_sum, true - whole, rest - whole, target)


def teacher_terms(teacher, label, classes):
    _, inner, log_true, log_rest, target = soft_parts(teacher, label, classes)
    true, rest = jnp.exp(log_true), jnp.exp(log_rest)
    fixed = TARGET_WEIGHT * jnp.where(target, true, 0.0) + NONTARGET_WEIGHT * inner
    return (
        SOFTEN * TARGET_WEIGHT * (true + rest),
        SOFTEN * (NONTARGET_WEIGHT * jnp.sum(inner, axis=1, keepdims=True) - TARGET_WEIGHT * rest),
        SOFTEN * fixed,
    )


def distill_grad(student, terms, label, classes):
    probs, inner, _, _, _ = soft_parts(student, label, classes)
    whole, rest, fixed = terms
    return whole * probs + rest * inner - fixed


def body(
    sizes,
    teacher_hbm,
    images_hbm,
    pair_index_hbm,
    labels_hbm,
    teacher_first_hbm,
    teacher_second_hbm,
    teacher_head_hbm,
    teacher_bias_hbm,
    first_hbm,
    gain_first_hbm,
    shift_first_hbm,
    second_hbm,
    gain_second_hbm,
    shift_second_hbm,
    head_hbm,
    head_bias_hbm,
    logits_out,
    images_grad,
    first_grad,
    gain_first_grad,
    shift_first_grad,
    second_grad,
    gain_second_grad,
    shift_second_grad,
    head_grad,
    bias_grad,
    pair_index,
    labels,
    stage_first,
    stage_second,
    images,
    teacher_head,
    teacher_bias,
    gain_first,
    shift_first,
    gain_second,
    shift_second,
    head_own,
    head_bias,
    teacher_in,
    teacher_w1,
    teacher_w2,
    teacher_x,
    teacher_h,
    teacher_head_pad,
    image_x,
    hidden_x,
    grad_x,
    w_first,
    w_second,
    own_first,
    own_second,
    y_first,
    y_second,
    slope_first,
    slope_second,
    d_hid,
    image_sib,
    hidden_sib,
    turned,
    turned_sib,
    turned_terms,
    part_all,
    part_own,
    part_send,
    part_recv,
    cross_all,
    cross_own,
    cross_send,
    cross_recv,
    last_all,
    last_own,
    last_send,
    last_recv,
    line_own,
    line_send,
    line_recv,
    sum_send,
    sum_recv,
    level_send,
    level_recv,
    level_line_send,
    level_line_recv,
    level_column,
    param_send,
    param_all,
    head_send,
    head_all,
    logit_send,
    logit_all,
    wide_send,
    wide_all,
    sync_send,
    sync_all_0,
    sync_all_1,
    sync_all_2,
    sync_all_3,
    sync_all_4,
    sync_all_5,
    sync_all_6,
    sync_all_7,
    head_sum,
    head_line_send,
    head_line_recv,
    local_sem,
    gather_send,
    gather_recv,
    wide_ssem,
    wide_rsem,
    sync_ssem,
    sync_rsem,
    known,
    plane_ssem,
    plane_rsem,
    swap_ssem,
    swap_rsem,
    part_ssem,
    part_rsem,
    cross_ssem,
    cross_rsem,
    last_ssem,
    last_rsem,
    level_ssem,
    level_rsem,
    level_line_ssem,
    level_line_rsem,
    line_ssem,
    line_rsem,
    sum_ssem,
    sum_rsem,
):
    groups, chans, own, own_pad, classes = sizes
    sync_all = (
        sync_all_0,
        sync_all_1,
        sync_all_2,
        sync_all_3,
        sync_all_4,
        sync_all_5,
        sync_all_6,
        sync_all_7,
    )
    b = lax.axis_index("batch")
    c = lax.axis_index("chan")
    me = b * chans + c
    devices = groups * chans
    sibling = c + 1 - 2 * lax.rem(c, 2)
    extent = images.shape[1]
    cells = extent * extent
    depth = images.shape[3]
    wide = teacher_hbm.shape[1]
    samples = float(devices * cells)
    chips = chans // 2
    chip, core = c // 2, lax.rem(c, 2)

    if groups == 4:
        far_first = [groups - 1 - b, lax.rem(b + 2, groups), b + 1 - 2 * lax.rem(b, 2)]
    else:
        far_first = [lax.rem(b + i, groups) for i in range(1, groups)]

    def each_device(fn):
        for peer_b in far_first + [b]:

            def one(i, carry, peer_b=peer_b):
                fn(peer_b, lax.rem(c + (chans - i), chans))
                return carry

            lax.fori_loop(1 if peer_b is b else 0, chans, one, 0, unroll=chans <= 8)

    def each_chip(fn):
        if chips == 4:
            for peer in (3 - chip, chip + 1 - 2 * lax.rem(chip, 2), lax.rem(chip + 2, chips)):
                fn(peer)
            return

        def one(i, carry):
            fn(lax.rem(chip + i, chips))
            return carry

        lax.fori_loop(1, chips, one, 0, unroll=chips <= 4)

    def each_line(fn):
        for peer_b in far_first:
            fn(peer_b)

    def signal(sem, peer_b, peer_c):
        pl.semaphore_signal(sem, inc=1, device_id=(peer_b, peer_c), device_id_type=MESH)

    def each_plane(fn):
        def one(i, carry):
            fn(lax.rem(c + i, chans))
            return carry

        lax.fori_loop(1, chans, one, 0, unroll=chans <= 8)

    if chips == 4:
        beside = chip + 1 - 2 * lax.rem(chip, 2)
        above = lax.rem(chip + 2, chips)
        near = [beside, above]
    else:
        near = [lax.rem(chip + i, chips) for i in range(1, chips)]
    if groups == 4:
        lines = [[b + 1 - 2 * lax.rem(b, 2)], [lax.rem(b + 2, groups)]]
    else:
        lines = [far_first]
    barrier = pltpu.get_barrier_semaphore()
    for peer in near:
        signal(barrier, b, 2 * peer + core)
    for line in lines:
        for peer in line:
            signal(barrier, peer, c)
    signal(barrier, b, sibling)
    greeted = len(near) + sum(len(line) for line in lines) + 1

    own_rows = own_first.shape[0]
    exact = own_rows == 9 * own
    moves = (
        (first_hbm, own_first if exact else stage_first),
        (images_hbm, images),
        (second_hbm, own_second if exact else stage_second),
        (gain_first_hbm, gain_first),
        (shift_first_hbm, shift_first),
        (gain_second_hbm, gain_second),
        (shift_second_hbm, shift_second),
        (head_hbm, head_own),
        (head_bias_hbm, head_bias),
        (teacher_bias_hbm, teacher_bias),
        (teacher_head_hbm, teacher_head),
        (teacher_hbm, teacher_in),
        (teacher_first_hbm, teacher_w1),
        (teacher_second_hbm, teacher_w2),
        (pair_index_hbm, pair_index),
        (labels_hbm, labels),
    )
    loads = [pltpu.make_async_copy(source, dest, local_sem.at[i]) for i, (source, dest) in enumerate(moves)]
    for load in loads:
        load.start()

    for ref in (image_x, hidden_x, grad_x, teacher_x, teacher_h):
        high = ref.shape[1]
        for lead in range(ref.shape[0]):
            ref[lead, 0] = jnp.zeros(ref.shape[2:], BF16)
            ref[lead, high - 1] = jnp.zeros(ref.shape[2:], BF16)
    for load in loads[:11]:
        load.wait()
    if not exact:
        for source, dest in ((stage_first, own_first), (stage_second, own_second)):
            dest[...] = jnp.zeros(dest.shape, BF16)
            dest[0 : 9 * own, :] = source[...]

    def place_own(param_row):
        at = c * own
        lane0 = lax.rem(at, LANES)
        padded = jnp.concatenate([param_row, jnp.zeros((1, LANES - own), F32)], axis=1)
        moved = pltpu.roll(jnp.broadcast_to(padded, (8, LANES)), lane0, 1)[0:1]
        upper = at >= LANES
        return (jnp.where(upper, 0.0, moved), jnp.where(upper, moved, 0.0))

    for i, ref in enumerate((gain_first, shift_first, gain_second, shift_second)):
        low_half, high_half = place_own(ref[...])
        param_send[2 * i : 2 * i + 1, :] = low_half
        param_send[2 * i + 1 : 2 * i + 2, :] = high_half
    head_send[...] = jnp.zeros(head_send.shape, BF16)
    head_send[0:own, 0:classes] = head_own[...]
    for lead in range(MICRO):
        spread_columns(image_x, lead, 1, images[lead].astype(F32).reshape(cells, depth), extent)

    t_high = 16
    t_steps = wide // t_high
    t_rows = t_high * wide

    def teacher_conv(source, kernel, top):
        total = None
        for row_off in range(3):
            window = source[0, pl.ds(top + row_off, t_high)].reshape(t_rows, 3 * depth)
            term = jnp.dot(
                window, kernel[row_off * 3 * depth : (row_off + 1) * 3 * depth, :], preferred_element_type=F32
            )
            total = term if total is None else total + term
        return total

    def teacher_fill(lead):
        def fill(i, carry):
            top = i * t_high
            values = teacher_in[lead, pl.ds(top, t_high)].astype(F32).reshape(t_rows, depth)
            spread_columns(teacher_x, 0, top + 1, values, wide)
            return carry

        lax.fori_loop(0, t_steps, fill, 0)

    def teacher_one():
        def one(i, carry):
            top = i * t_high
            spread_columns(teacher_h, 0, top + 1, gelu(teacher_conv(teacher_x, teacher_w1, top)), wide)
            return carry

        lax.fori_loop(0, t_steps, one, 0)

    def teacher_two(lead):
        def two(i, total):
            top = i * t_high
            values = teacher_in[lead, pl.ds(top, t_high)].astype(F32).reshape(t_rows, depth)
            act = gelu(teacher_conv(teacher_h, teacher_w2, top) + values)
            return total + jnp.sum(act, axis=0, keepdims=True)

        return lax.fori_loop(0, t_steps, two, jnp.zeros((1, depth), F32))

    loads[11].wait()
    teacher_fill(0)
    loads[12].wait()
    teacher_one()

    pl.semaphore_wait(barrier, greeted)
    rounds = [[(b, sibling)]] + [[(peer, c) for peer in line] for line in lines]
    if chips == 4:
        rounds = [[(b, 2 * beside + core)]] + rounds

    def say(i):
        if i < len(rounds):
            for peer in rounds[i]:
                signal(known.at[i], *peer)

    def hear(i):
        if i < len(rounds):
            pl.semaphore_wait(known.at[i], len(rounds[i]))
            say(i + 1)

    say(0)

    pieces = 1
    piece_rows = own_rows // pieces
    square = chips == 4 and piece_rows % 32 == 0
    held = (w_first, w_second)
    offered = (own_first, own_second)

    def gather_copy(k, rows, sem, shard, target, source=None):
        slot = held[k].at[shard, rows]
        return pltpu.make_async_remote_copy(
            src_ref=slot if source is None else source.at[rows],
            dst_ref=slot,
            send_sem=gather_send.at[k],
            recv_sem=gather_recv.at[k, sem, shard],
            device_id=(b, target),
            device_id_type=MESH,
        )

    def whole_copy(k, piece, shard, target, source=None):
        return gather_copy(k, pl.ds(piece * piece_rows, piece_rows), piece, shard, target, source)

    def half_copy(k, piece, half, shard, target, source=None):
        rows = pl.ds(piece * piece_rows + half * (piece_rows // 2), piece_rows // 2)
        return gather_copy(k, rows, 2 * piece + half, shard, target, source)

    def shard_of(peer):
        return 2 * peer + core

    def gather_start(k):
        if square:
            for late in range(2):
                for piece in range(pieces):
                    half_copy(k, piece, late, c, shard_of(beside), offered[k]).start()
                    half_copy(k, piece, 1 - late, c, shard_of(above), offered[k]).start()
        for piece in range(pieces):
            if not square:
                each_chip(lambda peer, piece=piece: whole_copy(k, piece, c, shard_of(peer), offered[k]).start())
            whole_copy(k, piece, c, sibling, offered[k]).start()
        held[k][c] = offered[k][...]

    def gather_turn(k):
        if square:
            for piece in range(pieces):
                for half, source, target in ((0, beside, above), (1, above, beside)):
                    half_copy(k, piece, half, shard_of(source), sibling).wait_recv()
                    half_copy(k, piece, half, shard_of(source), shard_of(target)).start()

    def gather_forward(k, piece):
        if square:
            half_copy(k, piece, 1, shard_of(beside), sibling).wait_recv()
            half_copy(k, piece, 0, shard_of(above), sibling).wait_recv()
            whole_copy(k, piece, shard_of(beside), sibling).start()
            whole_copy(k, piece, shard_of(above), sibling).start()
            for half in range(2):
                half_copy(k, piece, half, shard_of(3 - chip), sibling).wait_recv()
            whole_copy(k, piece, shard_of(3 - chip), sibling).start()
        else:

            def one(peer):
                whole_copy(k, piece, shard_of(peer), sibling).wait_recv()
                whole_copy(k, piece, shard_of(peer), sibling).start()

            each_chip(one)

    def gather_finish(k, piece):
        def one(i, carry):
            whole_copy(k, piece, 2 * lax.rem(chip + i, chips) + 1 - core, sibling).wait_recv()
            return carry

        lax.fori_loop(0, chips, one, 0, unroll=chips <= 4)

    def bytes_of(sem, many):
        pltpu.make_async_copy(many, many, sem).wait()

    def swap(k, source, dest):
        return pltpu.make_async_remote_copy(
            src_ref=source,
            dst_ref=dest,
            send_sem=swap_ssem.at[k],
            recv_sem=swap_rsem.at[k],
            device_id=(b, sibling),
            device_id_type=MESH,
        )

    def tile_start(send, recv, ssem, rsem):
        def one(pb, pc):
            pltpu.make_async_remote_copy(
                src_ref=send, dst_ref=recv.at[me], send_sem=ssem, recv_sem=rsem, device_id=(pb, pc), device_id_type=MESH
            ).start()

        each_device(one)
        recv[me] = send[...]

    def tile_bytes(sem, recv):
        bytes_of(sem, recv.at[pl.ds(0, devices - 1)])

    def sync_start(stage, micro, rows):
        k = stage * MICRO + micro
        for i, row in enumerate(rows):
            for j, half in enumerate(halves(row)):
                sync_send[k, 2 * i + j : 2 * i + j + 1, :] = half
        tile_start(sync_send.at[k], sync_all[k], sync_ssem.at[k], sync_rsem.at[k])

    def sync_wait(stage, micro):
        k = stage * MICRO + micro
        tile_bytes(sync_rsem.at[k], sync_all[k])
        total = jnp.sum(sync_all[k][...], axis=0)
        return [jnp.concatenate([total[2 * i : 2 * i + 1], total[2 * i + 1 : 2 * i + 2]], axis=1) for i in range(2)]

    def plane_start(k, source, slot):
        def one(pc):
            pltpu.make_async_remote_copy(
                src_ref=source(pc),
                dst_ref=slot(c),
                send_sem=plane_ssem.at[k],
                recv_sem=plane_rsem.at[k],
                device_id=(b, pc),
                device_id_type=MESH,
            ).start()

        each_plane(one)

    def plane_wait(k, many):
        pltpu.make_async_copy(many, many, plane_rsem.at[k]).wait()

    def plane_drain(k, many):
        pltpu.make_async_copy(many, many, plane_ssem.at[k]).wait()

    gather_start(0)
    swaps = [swap(0, image_x, image_sib)]
    swaps[0].start()
    for load in loads[13:]:
        load.wait()
    teacher_rows = [teacher_two(0)]

    hear(0)

    teacher_fill(1)
    hear(1)
    plane_start(0, lambda pc: param_send, lambda s: param_all.at[s])
    plane_start(1, lambda pc: head_send, lambda s: head_all.at[s])
    param_all[c] = param_send[...]
    head_all[c] = head_send[...]
    teacher_one()
    gather_turn(0)
    hear(2)
    teacher_rows.append(teacher_two(1))
    which_t = lax.broadcasted_iota(jnp.int32, (8, depth), 0)
    pooled_t = jnp.zeros((8, depth), F32)
    for m in range(MICRO):
        pooled_t = jnp.where(which_t == m, teacher_rows[m] / float(wide * wide), pooled_t)
    teacher_head_pad[...] = jnp.zeros(teacher_head_pad.shape, F32)
    teacher_head_pad[0:classes, :] = teacher_head[...].astype(F32)
    teacher_logits = lax.dot_general(
        pooled_t, teacher_head_pad[...], (((1,), (1,)), ((), ())), precision=HIGHEST, preferred_element_type=F32
    )
    lane_pad = jnp.zeros((1, LANES - classes), F32)
    teacher_logits = teacher_logits + jnp.concatenate([teacher_bias[...], lane_pad], axis=1)
    image_sum = jnp.zeros((1, depth), F32)
    for m in range(MICRO):
        image_sum = image_sum + jnp.sum(images[m].astype(F32).reshape(cells, depth), axis=0, keepdims=True)
    logit_send[0:MICRO, :] = teacher_logits[0:MICRO]
    for j, half in enumerate(halves(image_sum)):
        logit_send[MICRO + j : MICRO + j + 1, :] = half
    gather_start(1)
    hear(3)
    tile_start(logit_send, logit_all, wide_ssem.at[0], wide_rsem.at[0])

    def picker(shard, block, offset):
        at_row = lax.broadcasted_iota(jnp.int32, (depth, block), 0)
        place = lax.broadcasted_iota(jnp.int32, (depth, block), 1) - offset
        wanted = jnp.logical_and(place >= 0, place < own)
        return jnp.logical_and(wanted, at_row == shard * own + place).astype(BF16)

    def unpack(ref, block, offset):
        def one(shard, total):
            return total + jnp.dot(picker(shard, block, offset), ref[shard], preferred_element_type=F32)

        return lax.fori_loop(0, chans, one, jnp.zeros((depth, ref.shape[2]), F32)).astype(BF16)

    def weights(ref, tap):
        if own_pad == own:
            return ref[:, tap * own : (tap + 1) * own, :].reshape(depth, depth)
        return unpack(ref, own_rows, tap * own)

    def window(source, micro, row_off):
        return source[micro, row_off : row_off + extent].reshape(cells, 3 * depth)

    def tap_row(ref, row_off, back):
        if back:
            return jnp.concatenate([weights(ref, (2 - row_off) * 3 + 2 - i) for i in range(3)], axis=0)
        return jnp.concatenate([weights(ref, row_off * 3 + i) for i in range(3)], axis=1)

    def student_conv(source, micro, ref):
        total = None
        for row_off in range(3):
            term = lax.dot_general(
                window(source, micro, row_off),
                tap_row(ref, row_off, False),
                (((1,), (1,)), ((), ())),
                preferred_element_type=F32,
            )
            total = term if total is None else total + term
        return total

    def student_back(source, micro, ref):
        total = None
        for row_off in range(3):
            term = jnp.dot(
                window(source, micro, row_off), tap_row(ref, row_off, True), preferred_element_type=F32
            )
            total = term if total is None else total + term
        return total

    def rows_of(m):
        return slice(m * cells, (m + 1) * cells)

    def col_sum(values):
        return jnp.sum(values, axis=0, keepdims=True)

    def moments_start(stage, m, values):
        sync_start(stage, m, (col_sum(values), col_sum(values * values)))

    def moments(stage, m):
        total, square = sync_wait(stage, m)
        center = total / samples
        spread = square / samples - center * center
        return (center, lax.rsqrt(spread + EPS))

    for piece in range(pieces):
        gather_forward(0, piece)
    for piece in range(pieces):
        gather_finish(0, piece)
    total = None
    for row_off in range(3):
        term = lax.dot_general(
            image_x[:, row_off : row_off + extent].reshape(MICRO * cells, 3 * depth),
            tap_row(w_first, row_off, False),
            (((1,), (1,)), ((), ())),
            preferred_element_type=F32,
        )
        total = term if total is None else total + term
    y_first[...] = total
    for m in range(MICRO):
        moments_start(0, m, total[rows_of(m), :])

    plane_wait(0, param_all.at[pl.ds(0, chans - 1)])
    plane_wait(1, head_all.at[pl.ds(0, chans - 1)])
    params = jnp.sum(param_all[...], axis=0)
    gain1, shift1, gain2, shift2 = (
        jnp.concatenate([params[2 * i : 2 * i + 1], params[2 * i + 1 : 2 * i + 2]], axis=1) for i in range(4)
    )
    if own_pad == own:
        head = head_all[...].reshape(depth, LANES)
    else:
        head = unpack(head_all, own_pad, 0)
    gather_turn(1)
    for piece in range(pieces):
        gather_forward(1, piece)
    for piece in range(pieces):
        gather_finish(1, piece)

    def three_parts(values):
        first = values.astype(BF16)
        rest = values - first.astype(F32)
        second = rest.astype(BF16)
        third = (rest - second.astype(F32)).astype(BF16)
        return jnp.concatenate([first, second, third], axis=0)

    def sum_parts(product):
        return product[0:8] + product[8:16] + product[16:24]

    norm1 = []
    for m in range(MICRO):
        center, inv = moments(0, m)
        norm1.append((center, inv))
        normed = (y_first[rows_of(m), :] - center) * (inv * gain1) + shift1
        spread_columns(hidden_x, m, 1, gelu(normed), extent)
        values = student_conv(hidden_x, m, w_second)
        y_second[rows_of(m), :] = values
        moments_start(1, m, values)
    swaps.append(swap(1, hidden_x, hidden_sib))
    swaps[1].start()
    for m in range(MICRO):
        center, inv = norm1[m]
        slope_first[rows_of(m), :] = gelu_slope((y_first[rows_of(m), :] - center) * (inv * gain1) + shift1)

    per_device = pair_index.shape[0]
    norm2, slope_scale = [], []
    tile_bytes(wide_rsem.at[0], logit_all)
    taught = []
    for m in range(MICRO):
        paired = pair_index[m]
        teacher_row = logit_all[pl.ds(paired // per_device, 1), pl.ds(lax.rem(paired, per_device), 1), :]
        taught.append(teacher_terms(teacher_row.reshape(1, LANES), labels[m], classes))
    which = lax.broadcasted_iota(jnp.int32, (8, depth), 0)
    which_lane = lax.broadcasted_iota(jnp.int32, (8, LANES), 0)
    for m in range(MICRO):
        center, inv = moments(1, m)
        norm2.append((center, inv))
        spread = y_second[rows_of(m), :] - center
        res = spread * (inv * gain2) + shift2 + images[m].astype(F32).reshape(cells, depth)
        square = res * res
        t = jnp.tanh(GELU_A * (res + GELU_B * (res * square)))
        half = 0.5 + 0.5 * t
        slope = half + (0.5 * res) * (1.0 - t * t) * (GELU_A + (3.0 * GELU_A * GELU_B) * square)
        slope_second[rows_of(m), :] = slope
        pooled = col_sum(res * half) / float(cells)
        slope_sum = col_sum(slope)
        slope_dot = col_sum(slope * spread) * inv
        product = jnp.dot(
            three_parts(jnp.where(which == 0, pooled, 0.0)), head, preferred_element_type=F32
        )
        logits = sum_parts(product)[0:1] + jnp.concatenate([head_bias[...], lane_pad], axis=1)
        grad = distill_grad(logits, taught[m], labels[m], classes)
        product = lax.dot_general(
            three_parts(jnp.where(which_lane == 0, grad, 0.0)),
            head,
            (((1,), (1,)), ((), ())),
            preferred_element_type=F32,
        )
        scale = sum_parts(product)[0:1] / float(cells)
        slope_scale.append(scale)
        sync_start(2, m, (scale * slope_dot, scale * slope_sum))
        for j, part in enumerate(halves(pooled)):
            wide_send[m * 4 + j : m * 4 + j + 1, :] = part
        wide_send[m * 4 + 2 : m * 4 + 3, :] = grad
        wide_send[m * 4 + 3 : m * 4 + 4, :] = logits
    plane_start(2, lambda pc: wide_send, lambda s: wide_all.at[s])
    wide_all[c] = wide_send[...]

    def own_lanes(low_row, high_row):
        at = c * own
        row = jnp.where(at >= LANES, high_row, low_row)
        turn = lax.rem(LANES - lax.rem(at, LANES), LANES)
        return pltpu.roll(jnp.broadcast_to(row, (8, LANES)), turn, 1)[0:1, 0:own]

    def norm_terms(stage, m, gain, norm):
        center, inv = norm
        totals = sync_wait(stage, m)
        scale = gain * inv
        slant = scale * inv * (totals[0] / samples)
        level = scale * (totals[1] / samples)
        return (scale, center, slant, level), totals

    def norm_apply(terms, grad, values):
        scale, center, slant, level = terms
        return grad * scale - (values - center) * slant - level

    def norm_out(totals, gain_out, shift_out):
        for out, i in ((gain_out, 0), (shift_out, 1)):
            row = totals[0][i]
            for m in range(1, MICRO):
                row = row + totals[m][i]
            out[...] = own_lanes(*halves(row))

    def by_core(whole, dest):
        if own_pad == own:
            dest[...] = whole.reshape(dest.shape)
        else:

            def one(shard, carry):
                dest[shard // 2, lax.rem(shard, 2)] = lax.dot_general(
                    picker(shard, own_pad, 0).astype(F32),
                    whole,
                    (((0,), (0,)), ((), ())),
                    precision=HIGHEST,
                    preferred_element_type=F32,
                )
                return carry

            lax.fori_loop(0, chans, one, 0)

    def hand(k, m, grad, values):
        by_core(jnp.transpose(grad), turned.at[k, m, 0])
        by_core(jnp.transpose(values), turned.at[k, m, 1])
        turns[k, m] = swap(2 + k * MICRO + m, turned.at[k, m, :, :, 1 - core], turned_sib.at[k, m])
        turns[k, m].start()

    def low_grads(k, m, terms):
        by_core(
            jnp.transpose(jnp.concatenate(list(terms) + [jnp.zeros((4, depth), F32)], axis=0)), turned_terms
        )
        columns = turned_terms[:, pl.ds(core, 1)].reshape(chips * own_pad, 8)
        scale, center, slant, level = (columns[:, i : i + 1] for i in range(4))
        mine = [turned[k, m, i, :, pl.ds(core, 1)].reshape(chips * own_pad, cells) for i in range(2)]
        turns[k, m].wait_recv()
        theirs = [turned_sib[k, m, i].reshape(chips * own_pad, cells) for i in range(2)]
        return [norm_apply((scale, center, slant, level), *pair).astype(BF16) for pair in (mine, theirs)]

    turns = {}
    taps = 3 * own_pad
    per_half = groups // 2
    part_rows = taps // per_half
    part_pad = sum_send.shape[2]
    across = {0: None, 1: 2}
    planar = {0: (0, 1, 2), 1: (0, 1)}

    def send(source, dest, ssem, rsem, peer_b, peer_c):
        pltpu.make_async_remote_copy(
            src_ref=source, dst_ref=dest, send_sem=ssem, recv_sem=rsem, device_id=(peer_b, peer_c), device_id_type=MESH
        ).start()

    def cut(p):
        half, row = p // per_half, (p % per_half) * part_rows
        return slice(row, row + part_rows), slice(half * LANES, (half + 1) * LANES)

    def kernel_grad(k, grads, source, source_sib, mean):
        sides = [(grads[m][i], ref, m) for m in range(MICRO) for i, ref in enumerate((source, source_sib))]
        level = sum(jnp.sum(low.astype(F32), axis=1, keepdims=True) for low, _, _ in sides)
        for row_off in (2, 0, 1):
            total = sum(
                jnp.dot(
                    low,
                    ref[m, row_off : row_off + extent].reshape(cells, 3 * depth),
                    preferred_element_type=F32,
                )
                for low, ref, m in sides
            )
            blocks = [total[:, i * depth : (i + 1) * depth] - level * mean for i in range(3)]

            def keep():
                for col_off, block in enumerate(blocks):
                    for i in range(chips):
                        part_all[i, col_off * own_pad : (col_off + 1) * own_pad, :] = block[
                            i * own_pad : (i + 1) * own_pad
                        ]

            if row_off == across[k]:

                def cut_all():
                    for p in range(groups):
                        rows, lanes = cut(p)
                        cross_all[p, :, 0:part_rows] = part_all[:, rows, lanes]
                        if part_pad != part_rows:
                            cross_all[p, :, part_rows:part_pad] = jnp.zeros((chips, part_pad - part_rows, LANES), F32)

                if part_pad == part_rows:
                    for p in range(groups):
                        rows, lanes = cut(p)
                        for col_off, block in enumerate(blocks):
                            low = max(rows.start, col_off * own_pad)
                            high = min(rows.stop, (col_off + 1) * own_pad)
                            for i in range(chips if high > low else 0):
                                at = (i - col_off) * own_pad
                                cross_send[k, p, i, low - rows.start : high - rows.start, :] = block[
                                    at + low : at + high, lanes
                                ].astype(BF16)
                else:
                    keep()
                    cut_all()
                    cross_send[k] = cross_all[...].astype(BF16)
                each_line(
                    lambda peer: send(
                        cross_send.at[k, peer], cross_recv.at[k, b], cross_ssem.at[k], cross_rsem.at[k], peer, c
                    )
                )
                if part_pad == part_rows:
                    keep()
                    cut_all()
                cross_own[k] = cross_all[pl.ds(b, 1)].reshape(chips, part_pad, LANES)
                cross_recv[k, b] = jnp.zeros((chips, part_pad, LANES), BF16)
            else:
                for col_off, block in enumerate(blocks):
                    for i in range(chips):
                        part_send[k, row_off, i, col_off * own_pad : (col_off + 1) * own_pad, :] = block[
                            i * own_pad : (i + 1) * own_pad
                        ].astype(BF16)
                each_chip(
                    lambda peer, row_off=row_off: send(
                        part_send.at[k, row_off, peer],
                        part_recv.at[k, row_off, chip],
                        part_ssem.at[k, row_off],
                        part_rsem.at[k, row_off],
                        b,
                        2 * peer + core,
                    )
                )
                keep()
                part_own[k, row_off] = part_all[pl.ds(chip, 1)].reshape(taps, depth)
                part_recv[k, row_off, chip] = jnp.zeros((taps, depth), BF16)
        ones = jnp.ones((8, cells), BF16)
        level_send[k] = sum(
            lax.dot_general(ones, low, (((1,), (1,)), ((), ())), preferred_element_type=F32) for low, _, _ in sides
        )[0:1]
        each_chip(
            lambda peer: send(
                level_send.at[k], level_recv.at[k, chip], level_ssem.at[k], level_rsem.at[k], b, 2 * peer + core
            )
        )
        level_recv[k, chip] = level_send[k]

    def line_start(k):
        for row_off in planar[k]:
            bytes_of(part_rsem.at[k, row_off], part_recv.at[k, row_off, pl.ds(0, chips - 1)])
            total = part_own[k, row_off] + jnp.sum(part_recv[k, row_off].astype(F32), axis=0)
            for p in range(groups):
                line_own[k, row_off, p, 0:part_rows] = total[cut(p)]
                if part_pad != part_rows:
                    line_own[k, row_off, p, part_rows:part_pad] = jnp.zeros((part_pad - part_rows, LANES), F32)
            line_send[k, row_off] = line_own[k, row_off].astype(BF16)
            each_line(
                lambda peer, row_off=row_off: send(
                    line_send.at[k, row_off, peer],
                    line_recv.at[k, row_off, b],
                    line_ssem.at[k, row_off],
                    line_rsem.at[k, row_off],
                    peer,
                    c,
                )
            )
            line_recv[k, row_off, b] = jnp.zeros((part_pad, LANES), BF16)
        bytes_of(level_rsem.at[k], level_recv.at[k, pl.ds(0, chips - 1)])
        level_line_send[k] = jnp.sum(level_recv[k], axis=0)
        each_line(
            lambda peer: send(
                level_line_send.at[k], level_line_recv.at[k, b], level_line_ssem.at[k], level_line_rsem.at[k], peer, c
            )
        )
        level_line_recv[k, b] = level_line_send[k]

    def cross_forward(k):
        if across[k] is None:
            return
        bytes_of(cross_rsem.at[k], cross_recv.at[k, pl.ds(0, groups - 1)])
        last_all[...] = cross_own[k] + jnp.sum(cross_recv[k].astype(F32), axis=0)
        last_send[k] = last_all[...].astype(BF16)
        last_own[k] = last_all[pl.ds(chip, 1)].reshape(part_pad, LANES)
        each_chip(
            lambda peer: send(
                last_send.at[k, peer], last_recv.at[k, chip], last_ssem.at[k], last_rsem.at[k], b, 2 * peer + core
            )
        )
        last_recv[k, chip] = jnp.zeros((part_pad, LANES), BF16)

    def share(k, row_off, total):
        sum_send[k, row_off] = total.astype(BF16)
        each_line(
            lambda peer: send(
                sum_send.at[k, row_off],
                sum_recv.at[k, row_off, b],
                sum_ssem.at[k, row_off],
                sum_rsem.at[k, row_off],
                peer,
                c,
            )
        )
        sum_recv[k, row_off, b] = sum_send[k, row_off]

    def cross_sum(k):
        if across[k] is None:
            return
        bytes_of(last_rsem.at[k], last_recv.at[k, pl.ds(0, chips - 1)])
        share(k, across[k], last_own[k] + jnp.sum(last_recv[k].astype(F32), axis=0))

    def line_sum(k):
        for row_off in planar[k]:
            bytes_of(line_rsem.at[k, row_off], line_recv.at[k, row_off, pl.ds(0, groups - 1)])
            share(
                k,
                row_off,
                line_own[k, row_off, pl.ds(b, 1)].reshape(part_pad, LANES)
                + jnp.sum(line_recv[k, row_off].astype(F32), axis=0),
            )

    def sum_finish(k, mean, out):
        bytes_of(level_line_rsem.at[k], level_line_recv.at[k, pl.ds(0, groups - 1)])
        level = jnp.sum(level_line_recv[k], axis=0)
        level_column[...] = jnp.transpose(jnp.broadcast_to(level, (LANES, level.shape[1])))
        column_own = level_column[pl.ds(chip * own_pad, own_pad), :]
        back = [column_own * half for half in halves(mean)]
        for row_off in (0, 1, 2):
            bytes_of(sum_rsem.at[k, row_off], sum_recv.at[k, row_off, pl.ds(0, groups - 1)])
            for half in range(2):
                rows = sum_recv[k, row_off, half * per_half : (half + 1) * per_half, 0:part_rows].astype(F32)
                out[row_off * 3 : row_off * 3 + 3, :, half * LANES : (half + 1) * LANES] = (
                    rows.reshape(3, own_pad, LANES) + back[half][None]
                )

    for m in range(MICRO):
        hand(0, m, slope_second[rows_of(m), :] * slope_scale[m], y_second[rows_of(m), :])
    terms2, totals2 = [], []
    for m in range(MICRO):
        terms, totals = norm_terms(2, m, gain2, norm2[m])
        terms2.append(terms)
        totals2.append(totals)
        found = norm_apply(terms, slope_second[rows_of(m), :] * slope_scale[m], y_second[rows_of(m), :])
        spread_columns(grad_x, m, 1, found, extent)
        grad = student_back(grad_x, m, w_second) * slope_first[rows_of(m), :]
        d_hid[rows_of(m), :] = grad
        center, inv = norm1[m]
        sync_start(3, m, (col_sum(grad * (y_first[rows_of(m), :] - center)) * inv, col_sum(grad)))

    hidden_mean = jnp.zeros((1, depth), F32)
    for node, weight in QUADRATURE:
        hidden_mean = hidden_mean + weight * gelu(shift1 + gain1 * node)
    image_rows = jnp.sum(logit_all[...], axis=0)
    image_mean = jnp.concatenate([image_rows[MICRO : MICRO + 1], image_rows[MICRO + 1 : MICRO + 2]], axis=1) / (
        MICRO * samples
    )

    swaps[0].wait_recv()
    swaps[1].wait_recv()
    kernel_grad(0, [low_grads(0, m, terms2[m]) for m in range(MICRO)], hidden_x, hidden_sib, hidden_mean)
    for m in range(MICRO):
        hand(1, m, d_hid[rows_of(m), :], y_first[rows_of(m), :])
    norm_out(totals2, gain_second_grad, shift_second_grad)

    plane_wait(2, wide_all.at[pl.ds(0, chans - 1)])
    totals = [jnp.zeros((LANES, LANES), F32) for _ in range(2)]
    bias_row = jnp.zeros((1, LANES), F32)
    for m in range(MICRO):
        per_image = wide_all[:, m * 4 + 2, :]
        bias_row = bias_row + col_sum(per_image)
        for j in range(2):
            totals[j] = totals[j] + lax.dot_general(
                wide_all[:, m * 4 + j, :],
                per_image,
                (((0,), (0,)), ((), ())),
                precision=HIGHEST,
                preferred_element_type=F32,
            )
        for j in range(chans):
            logits_out[j * MICRO + m : j * MICRO + m + 1, :] = wide_all[j, m * 4 + 3 : m * 4 + 4, 0:classes]
    for j in range(2):
        head_sum[j * LANES : (j + 1) * LANES, :] = totals[j]
    head_line_send[0:own, :] = head_sum[pl.ds(c * own, own), :]
    head_line_send[own : own + 8, :] = jnp.broadcast_to(bias_row, (8, LANES))
    each_line(
        lambda peer: send(head_line_send, head_line_recv.at[b], wide_ssem.at[1], wide_rsem.at[1], peer, c)
    )
    head_line_recv[b] = head_line_send[...]

    terms1, totals1, lows = [], [], []
    for m in range(MICRO):
        terms, totals = norm_terms(3, m, gain1, norm1[m])
        terms1.append(terms)
        totals1.append(totals)
        lows.append(low_grads(1, m, terms))
    kernel_grad(1, lows, image_x, image_sib, image_mean)
    for m in range(MICRO):
        found = norm_apply(terms1[m], d_hid[rows_of(m), :], y_first[rows_of(m), :])
        spread_columns(grad_x, m, 1, found, extent)
        images_grad[m] = (
            student_back(grad_x, m, w_first) + slope_second[rows_of(m), :] * slope_scale[m]
        ).reshape(images_grad.shape[1:])
    norm_out(totals1, gain_first_grad, shift_first_grad)
    line_start(0)
    cross_forward(0)

    cross_sum(0)
    line_start(1)
    cross_forward(1)
    line_sum(0)
    cross_sum(1)
    line_sum(1)
    tile_bytes(wide_ssem.at[0], logit_all)
    bytes_of(wide_ssem.at[1], head_line_recv.at[pl.ds(0, groups - 1)])
    plane_drain(2, wide_all.at[pl.ds(0, chans - 1)])
    for k in range(2):
        bytes_of(gather_send.at[k], held[k].at[pl.ds(0, chans - 1)])
    for k in range(4 * MICRO):
        tile_bytes(sync_ssem.at[k], sync_all[k])
    plane_drain(0, param_all.at[pl.ds(0, chans - 1)])
    plane_drain(1, head_all.at[pl.ds(0, chans - 1)])
    for copy in swaps + list(turns.values()):
        copy.wait_send()
    for k in range(2):
        for row_off in planar[k]:
            bytes_of(part_ssem.at[k, row_off], part_recv.at[k, row_off, pl.ds(0, chips - 1)])
            bytes_of(line_ssem.at[k, row_off], line_recv.at[k, row_off, pl.ds(0, groups - 1)])
        if across[k] is not None:
            bytes_of(cross_ssem.at[k], cross_recv.at[k, pl.ds(0, groups - 1)])
            bytes_of(last_ssem.at[k], last_recv.at[k, pl.ds(0, chips - 1)])
        bytes_of(level_ssem.at[k], level_recv.at[k, pl.ds(0, chips - 1)])
        bytes_of(level_line_ssem.at[k], level_line_recv.at[k, pl.ds(0, groups - 1)])
    bytes_of(wide_rsem.at[1], head_line_recv.at[pl.ds(0, groups - 1)])
    head_total = jnp.sum(head_line_recv[...], axis=0)
    head_grad[...] = head_total[0:own, 0:classes]
    bias_grad[...] = head_total[own : own + 1, 0:classes]
    sum_finish(0, hidden_mean, second_grad)
    sum_finish(1, image_mean, first_grad)
    for k in range(2):
        for row_off in range(3):
            bytes_of(sum_ssem.at[k, row_off], sum_recv.at[k, row_off, pl.ds(0, groups - 1)])


def hand_on(*refs):
    count = len(refs) // 2
    copies = [pltpu.make_async_copy(refs[i], refs[count + i], refs[-1].at[i]) for i in range(count)]
    for copy in copies:
        copy.start()
    for copy in copies:
        copy.wait()


def shards(
    teacher_images,
    student_images,
    pair_index,
    labels,
    teacher_first,
    teacher_second,
    teacher_head,
    teacher_bias,
    conv_first,
    gain_first,
    shift_first,
    conv_second,
    gain_second,
    shift_second,
    head_weight,
    head_bias,
):
    groups, chans = lax.axis_size("batch"), lax.axis_size("chan")
    devices = groups * chans
    count, extent, _, depth = student_images.shape
    wide = teacher_images.shape[1]
    own = conv_first.shape[3]
    own_pad = max(own, 16)
    own_rows = -(-9 * own // 16) * 16
    classes = head_bias.shape[0]
    cells = extent * extent
    rows = count * cells
    chips = chans // 2
    taps = 3 * own_pad
    part_rows = 2 * taps // groups
    part_pad = -(-part_rows // 16) * 16

    def turned(kernel):
        return jnp.transpose(kernel, (0, 1, 3, 2)).reshape(9 * own, depth)

    def row(vector):
        return vector.reshape(1, -1)

    vmem = pl.BlockSpec(memory_space=pltpu.VMEM)
    hbm = pl.BlockSpec(memory_space=pl.ANY)
    out_shape = [
        jax.ShapeDtypeStruct((chans * count, classes), F32),
        jax.ShapeDtypeStruct(student_images.shape, F32),
        jax.ShapeDtypeStruct((9, own_pad, depth), F32),
        jax.ShapeDtypeStruct((1, own), F32),
        jax.ShapeDtypeStruct((1, own), F32),
        jax.ShapeDtypeStruct((9, own_pad, depth), F32),
        jax.ShapeDtypeStruct((1, own), F32),
        jax.ShapeDtypeStruct((1, own), F32),
        jax.ShapeDtypeStruct((own, classes), F32),
        jax.ShapeDtypeStruct((1, classes), F32),
    ]
    stage = (16, LANES) if own_rows == 9 * own else (9 * own, depth)
    scratch = [
        pltpu.SMEM(pair_index.shape, jnp.int32),
        pltpu.SMEM(labels.shape, jnp.int32),
        pltpu.VMEM(stage, BF16),
        pltpu.VMEM(stage, BF16),
        pltpu.VMEM(student_images.shape, BF16),
        pltpu.VMEM((classes, depth), BF16),
        pltpu.VMEM((1, classes), F32),
        pltpu.VMEM((1, own), F32),
        pltpu.VMEM((1, own), F32),
        pltpu.VMEM((1, own), F32),
        pltpu.VMEM((1, own), F32),
        pltpu.VMEM((own, classes), BF16),
        pltpu.VMEM((1, classes), F32),
        pltpu.VMEM(teacher_images.shape, BF16),
        pltpu.VMEM((9 * depth, depth), BF16),
        pltpu.VMEM((9 * depth, depth), BF16),
        pltpu.VMEM((1, wide + 2, wide, 3 * depth), BF16),
        pltpu.VMEM((1, wide + 2, wide, 3 * depth), BF16),
        pltpu.VMEM((LANES, depth), F32),
        pltpu.VMEM((count, extent + 2, extent, 3 * depth), BF16),
        pltpu.VMEM((count, extent + 2, extent, 3 * depth), BF16),
        pltpu.VMEM((count, extent + 2, extent, 3 * depth), BF16),
        pltpu.VMEM((chans, own_rows, depth), BF16),
        pltpu.VMEM((chans, own_rows, depth), BF16),
        pltpu.VMEM((own_rows, depth), BF16),
        pltpu.VMEM((own_rows, depth), BF16),
        pltpu.VMEM((rows, depth), F32),
        pltpu.VMEM((rows, depth), F32),
        pltpu.VMEM((rows, depth), F32),
        pltpu.VMEM((rows, depth), F32),
        pltpu.VMEM((rows, depth), F32),
        pltpu.VMEM((count, extent + 2, extent, 3 * depth), BF16),
        pltpu.VMEM((count, extent + 2, extent, 3 * depth), BF16),
        pltpu.VMEM((2, count, 2, chips, 2, own_pad, cells), F32),
        pltpu.VMEM((2, count, 2, chips, own_pad, cells), F32),
        pltpu.VMEM((chips, 2, own_pad, 8), F32),
        pltpu.VMEM((chips, taps, depth), F32),
        pltpu.VMEM((2, 3, taps, depth), F32),
        pltpu.VMEM((2, 3, chips, taps, depth), BF16),
        pltpu.VMEM((2, 3, chips, taps, depth), BF16),
        pltpu.VMEM((groups, chips, part_pad, LANES), F32),
        pltpu.VMEM((2, chips, part_pad, LANES), F32),
        pltpu.VMEM((2, groups, chips, part_pad, LANES), BF16),
        pltpu.VMEM((2, groups, chips, part_pad, LANES), BF16),
        pltpu.VMEM((chips, part_pad, LANES), F32),
        pltpu.VMEM((2, part_pad, LANES), F32),
        pltpu.VMEM((2, chips, part_pad, LANES), BF16),
        pltpu.VMEM((2, chips, part_pad, LANES), BF16),
        pltpu.VMEM((2, 3, groups, part_pad, LANES), F32),
        pltpu.VMEM((2, 3, groups, part_pad, LANES), BF16),
        pltpu.VMEM((2, 3, groups, part_pad, LANES), BF16),
        pltpu.VMEM((2, 3, part_pad, LANES), BF16),
        pltpu.VMEM((2, 3, groups, part_pad, LANES), BF16),
        pltpu.VMEM((2, 1, chips * own_pad), F32),
        pltpu.VMEM((2, chips, 1, chips * own_pad), F32),
        pltpu.VMEM((2, 1, chips * own_pad), F32),
        pltpu.VMEM((2, groups, 1, chips * own_pad), F32),
        pltpu.VMEM((chips * own_pad, LANES), F32),
        pltpu.VMEM((8, LANES), F32),
        pltpu.VMEM((chans, 8, LANES), F32),
        pltpu.VMEM((own_pad, LANES), BF16),
        pltpu.VMEM((chans, own_pad, LANES), BF16),
        pltpu.VMEM((4, LANES), F32),
        pltpu.VMEM((devices, 4, LANES), F32),
        pltpu.VMEM((8, LANES), F32),
        pltpu.VMEM((chans, 8, LANES), F32),
        pltpu.VMEM((4 * MICRO, 4, LANES), F32),
        pltpu.VMEM((devices, 4, LANES), F32),
        pltpu.VMEM((devices, 4, LANES), F32),
        pltpu.VMEM((devices, 4, LANES), F32),
        pltpu.VMEM((devices, 4, LANES), F32),
        pltpu.VMEM((devices, 4, LANES), F32),
        pltpu.VMEM((devices, 4, LANES), F32),
        pltpu.VMEM((devices, 4, LANES), F32),
        pltpu.VMEM((devices, 4, LANES), F32),
        pltpu.VMEM((depth, LANES), F32),
        pltpu.VMEM((own + 8, LANES), F32),
        pltpu.VMEM((groups, own + 8, LANES), F32),
        pltpu.SemaphoreType.DMA((16,)),
        pltpu.SemaphoreType.DMA((2,)),
        pltpu.SemaphoreType.DMA((2, 6, chans)),
        pltpu.SemaphoreType.DMA((2,)),
        pltpu.SemaphoreType.DMA((2,)),
        pltpu.SemaphoreType.DMA((4 * MICRO,)),
        pltpu.SemaphoreType.DMA((4 * MICRO,)),
        pltpu.SemaphoreType.REGULAR((4,)),
        pltpu.SemaphoreType.DMA((3,)),
        pltpu.SemaphoreType.DMA((3,)),
        pltpu.SemaphoreType.DMA((2 + 2 * MICRO,)),
        pltpu.SemaphoreType.DMA((2 + 2 * MICRO,)),
        pltpu.SemaphoreType.DMA((2, 3)),
        pltpu.SemaphoreType.DMA((2, 3)),
        pltpu.SemaphoreType.DMA((2,)),
        pltpu.SemaphoreType.DMA((2,)),
        pltpu.SemaphoreType.DMA((2,)),
        pltpu.SemaphoreType.DMA((2,)),
        pltpu.SemaphoreType.DMA((2,)),
        pltpu.SemaphoreType.DMA((2,)),
        pltpu.SemaphoreType.DMA((2,)),
        pltpu.SemaphoreType.DMA((2,)),
        pltpu.SemaphoreType.DMA((2, 3)),
        pltpu.SemaphoreType.DMA((2, 3)),
        pltpu.SemaphoreType.DMA((2, 3)),
        pltpu.SemaphoreType.DMA((2, 3)),
    ]
    found = pl.pallas_call(
        functools.partial(body, (groups, chans, own, own_pad, classes)),
        out_shape=[pltpu.VMEM(out.shape, out.dtype) for out in out_shape],
        in_specs=[hbm] * 16,
        out_specs=[vmem] * 10,
        scratch_shapes=scratch,
        compiler_params=pltpu.CompilerParams(
            collective_id=0, has_side_effects=True, vmem_limit_bytes=62 * 2**20
        ),
    )(
        teacher_images,
        student_images,
        pair_index,
        labels,
        teacher_first.reshape(9 * depth, depth),
        teacher_second.reshape(9 * depth, depth),
        teacher_head.T,
        row(teacher_bias),
        turned(conv_first),
        row(gain_first),
        row(shift_first),
        turned(conv_second),
        row(gain_second),
        row(shift_second),
        head_weight,
        row(head_bias),
    )
    found = pl.pallas_call(
        hand_on,
        out_shape=out_shape,
        in_specs=[vmem] * len(out_shape),
        out_specs=[hbm] * len(out_shape),
        scratch_shapes=[pltpu.SemaphoreType.DMA((len(out_shape),))],
    )(*[pltpu.with_memory_space_constraint(x, pltpu.VMEM) for x in found])
    logits, images_grad, first, gain1, shift1, second, gain2, shift2, head, bias = found

    def back(grad):
        return jnp.transpose(grad[:, :own].reshape(3, 3, own, depth), (0, 1, 3, 2))

    return (
        logits,
        images_grad,
        back(first),
        gain1.reshape(-1),
        shift1.reshape(-1),
        back(second),
        gain2.reshape(-1),
        shift2.reshape(-1),
        head,
        bias.reshape(-1),
    )


def solution(mesh):
    in_specs = (
        P(("batch", "chan"), None, None, None),
        P(("batch", "chan"), None, None, None),
        P(("batch", "chan")),
        P(("batch", "chan")),
        P(),
        P(),
        P(),
        P(),
        P(None, None, None, "chan"),
        P("chan"),
        P("chan"),
        P(None, None, None, "chan"),
        P("chan"),
        P("chan"),
        P("chan", None),
        P(),
    )
    out_specs = (
        P("batch", None),
        P(("batch", "chan"), None, None, None),
        P(None, None, None, "chan"),
        P("chan"),
        P("chan"),
        P(None, None, None, "chan"),
        P("chan"),
        P("chan"),
        P("chan", None),
        P(),
    )
    return jax.shard_map(shards, mesh=mesh, in_specs=in_specs, out_specs=out_specs, check_vma=False)
```
